128 devices in a mesh: ctx: 8 (over x, z_lo), fsdp: 16 (over z_hi, y, core).
Axes of the slice: x: 4, y: 4, z: 4 (z_hi: 2, z_lo: 2; z = z_hi * 2 + z_lo), core: 2. Of those that a mesh axis runs over, the one named last changes fastest.
Arguments:
- tokens: bfloat16 [16, 2048, 768], P('fsdp', 'ctx'), may hold values from -6 to 6
- prev_logits: float32 [16, 2048, 12], P('fsdp', 'ctx'), may hold values from -4 to 4
- routes: int32 [16, 2048, 2], P('fsdp', 'ctx'), may hold values from 0 to 11, all different within a row; in each aligned block of 256 rows (0 to 255, 256 to 511, ..., all dimensions but the last counted through in order) at most 81 rows name the same one
- segments: int32 [16, 2048], P('fsdp', 'ctx'), may hold values from 0 to 5, as said below
- rank_order: int32 [16, 8, 256], P('fsdp', 'ctx'), may hold values from 0 to 255, each once within a row
- norm_first: bfloat16 [768], P(('ctx', 'fsdp')), may hold values from 0.5 to 1.5
- w_query: bfloat16 [768, 768], P(('ctx', 'fsdp')), may hold values from -0.21875 to 0.21875
- w_key: bfloat16 [768, 768], P(('ctx', 'fsdp')), may hold values from -0.21875 to 0.21875
- w_value: bfloat16 [768, 768], P(('ctx', 'fsdp')), may hold values from -0.21875 to 0.21875
- w_output: bfloat16 [768, 768], P(('ctx', 'fsdp')), may hold values from -1.25 to 1.25
- norm_second: bfloat16 [768], P(('ctx', 'fsdp')), may hold values from 0.5 to 1.5
- w_router: bfloat16 [768, 12], P(('ctx', 'fsdp')), may hold values from -0.21875 to 0.21875
- w_residual: float32 [12, 12], replicated, may hold values from -1.75 to 1.75
- w_constant: bfloat16 [768, 4], P(('ctx', 'fsdp')), may hold values from -0.21875 to 0.21875
- v_constant: bfloat16 [768, 2], P(('ctx', 'fsdp')), may hold values from -6 to 6
- w_gate: bfloat16 [16, 768, 1024], P('fsdp', 'ctx'), may hold values from -0.21875 to 0.21875
- w_up: bfloat16 [16, 768, 1024], P('fsdp', 'ctx'), may hold values from -0.21875 to 0.21875
- w_down: bfloat16 [16, 1024, 768], P('fsdp', 'ctx'), may hold values from -0.125 to 0.125
- cotangent: bfloat16 [16, 2048, 768], P('fsdp', 'ctx'), may hold values from -6 to 6
Outputs:
- block_out: bfloat16 [16, 2048, 768], P('fsdp', 'ctx')
- grad_tokens: float32 [16, 2048, 768], P('fsdp', 'ctx')
- grad_prev: float32 [16, 2048, 12], P('fsdp', 'ctx')
- grad_norm_first: float32 [768], P(('ctx', 'fsdp'))
- grad_query: float32 [768, 768], P(('ctx', 'fsdp'))
- grad_key: float32 [768, 768], P(('ctx', 'fsdp'))
- grad_value: float32 [768, 768], P(('ctx', 'fsdp'))
- grad_output: float32 [768, 768], P(('ctx', 'fsdp'))
- grad_norm_second: float32 [768], P(('ctx', 'fsdp'))
- grad_router: float32 [768, 12], P(('ctx', 'fsdp'))
- grad_residual: float32 [12, 12], replicated
- grad_constant: float32 [768, 4], P(('ctx', 'fsdp'))
- grad_vectors: float32 [768, 2], P(('ctx', 'fsdp'))
- grad_gate: float32 [16, 768, 1024], P('fsdp', 'ctx')
- grad_up: float32 [16, 768, 1024], P('fsdp', 'ctx')
- grad_down: float32 [16, 1024, 768], P('fsdp', 'ctx')
The draws below stay inside these ranges and needn't reach their ends.
Inputs may be any that keep to these rules, and one draw needn't show every extreme that they name: `routes`: each token names two different experts. In each aligned block of 256 rows no expert is named by more than 81 rows, and one is named by exactly that many in some blocks. `segments`: one sequence, which one drawn from the seed, is a single document: all its numbers are 0. In every other sequence the numbers start at 0, never fall, rise by one at each document start and end at 5; each of its documents holds between two thirds and four thirds of 341 positions, the last up to 5 more. `rank_order`: each device's 256 ranks are a permutation.
All inputs are finite; a program needn't handle non-finite values.
Results may differ from the reference program's by a relative error of at most 0.025.
Values may be sent and summed in bfloat16 or wider, within the bound.
A program may use at most 128 MiB of HBM per device.

```python
import math
import jax
import jax.numpy as jnp
import numpy as np
from jax import lax

D = 768
HEADS = 12
HDIM = 64
FF = 2048
EXPERTS = 8
BLK = 256
NALL = 12
CAP = 54
HALVES = 2
FFH = 1024
SEQS = 16
LEN = 2048
CUTS = 5
N_CTX = 8


def draw_segments(key, part):
    key = jax.random.fold_in(key, 7)
    spacing = LEN // (CUTS + 1)
    reach = spacing // 6
    moves = jax.random.randint(key, (SEQS, CUTS), -reach, reach + 1)
    all_cuts = (jnp.arange(1, CUTS + 1, dtype=jnp.int32) * spacing)[None, :] + moves
    positions = jnp.arange(LEN, dtype=jnp.int32)
    numbers = jnp.sum((all_cuts[:, None, :] <= positions[None, :, None]).astype(jnp.int32), axis=-1).astype(jnp.int32)
    single = jax.random.randint(jax.random.fold_in(key, 11), (), 0, SEQS)
    whole_doc = (jnp.arange(SEQS, dtype=jnp.int32) == single)[:, None]
    return jnp.where(whole_doc, jnp.zeros_like(numbers), numbers).astype(jnp.int32)


def level_of(own_key, shape, cuts, least, high):
    level = 1.0
    for position, shards_of in cuts:
        draws = jax.random.uniform(jax.random.fold_in(jax.random.fold_in(own_key, 6), position), (shards_of,), jnp.float32, least / len(cuts), high / len(cuts))
        level = level * jnp.repeat(jnp.exp(draws), shape[position] // shards_of).reshape((-1,) + (1,) * (len(shape) - 1 - position))
    return level


def deal_out(rng, own, number, rows, amount, top, bound, skew):
    sequence = jax.random.permutation(rng, amount)
    heavy_load, usual = load_shares(amount, rows * top, bound, skew, True), load_shares(amount, rows * top, bound, skew, False)
    places = jnp.arange(amount)

    def named(sizes, rotation):
        used = int((sizes > 0).sum())
        fixed = max(1, used // 4)
        moved = fixed + (places - fixed + rotation * (used - fixed)) % max(1, amount - fixed)
        return jnp.zeros((amount,), jnp.int32).at[sequence[jnp.where(places < fixed, places, moved)]].set(jnp.asarray(sizes, jnp.int32))

    sizes = jnp.where(number % 4 == 0, named(heavy_load, number // 4), named(usual, number - number // 4 - 1))
    mixed = jax.random.permutation(jax.random.fold_in(own, 3), amount)
    source_of, receiver = mixed[0:amount // 2 * 2:2], mixed[1:amount // 2 * 2:2]
    room = jnp.minimum(sizes[source_of] - 1, bound - sizes[receiver]) // 2
    room = jnp.where((source_of == sequence[0]) | (receiver == sequence[0]) | (sizes[receiver] == 0), 0, jnp.maximum(room, 0))
    moved = jax.random.randint(jax.random.fold_in(own, 4), (amount // 2,), 0, 1 << 20) % (room + 1)
    sizes = sizes.at[source_of].add(-moved).at[receiver].add(moved)
    items = jnp.searchsorted(jnp.cumsum(sizes), jnp.arange(rows * top), side="right").astype(jnp.int32)
    table = items.reshape(top, rows).T
    table = table[jax.random.permutation(jax.random.fold_in(own, 1), rows)]
    rotation = jax.random.randint(jax.random.fold_in(own, 2), (rows, 1), 0, top)
    return jnp.take_along_axis(table, (jnp.arange(top)[None, :] + rotation) % top, axis=1)


def load_shares(amount, total, limit, skew, full):
    weights = [(1 << 20) // math.isqrt(rank ** skew) + 1 for rank in range(1, amount + 1)]
    largest = limit if full else min(limit, max(-(-total // amount), total * weights[0] // sum(weights)))
    least = 1 if total - largest >= amount - 1 else 0
    given, rest = [largest] + [least] * (amount - 1), total - largest - least * (amount - 1)
    while rest > 0:
        candidates = [i for i in range(1, amount) if given[i] < largest] or [i for i in range(1, amount) if given[i] < limit]
        whole, remaining = sum([weights[i] for i in candidates]), rest
        for i in candidates:
            extra = min(limit - given[i], max(1, remaining * weights[i] // whole), rest)
            given[i] = given[i] + extra
            rest = rest - extra
    return np.array(given)


def noise(key, extent, scale, limit, pieces=(), held_as=jnp.bfloat16):
    factor_of = level_of(key, extent, pieces, -0.22, 0.18) if pieces else 1.0
    result = jax.random.normal(key, extent, jnp.float32) * scale * factor_of
    return jnp.minimum(jnp.maximum(result, -limit), limit).astype(held_as)


def setup_inputs(seed: int = 0) -> dict:
    arg_keys = jax.random.split(jax.random.key(seed), 20)
    tokens = noise(arg_keys[0], (SEQS, LEN, D), 1.0, 6.0, ((0, 16), (1, 8)))
    prev_logits = noise(arg_keys[1], (SEQS, LEN, NALL), 0.5, 4.0, ((0, 16), (1, 8)), jnp.float32)
    routes_keys = jax.random.split(jax.random.fold_in(arg_keys[2], 1), SEQS * LEN // BLK)
    routes_turns = jax.random.permutation(jax.random.fold_in(arg_keys[2], 3), SEQS * LEN // BLK)
    routes = jax.vmap(lambda own, number: deal_out(jax.random.fold_in(arg_keys[2], 2), own, number, BLK, NALL, 2, CAP + CAP // 2, 1))(routes_keys, routes_turns).reshape((SEQS, LEN, 2))
    segments = draw_segments(jax.random.fold_in(arg_keys[19], 71), 0)
    rank_order = jax.vmap(lambda own: jax.random.permutation(own, BLK))(jax.random.split(arg_keys[4], SEQS * N_CTX)).reshape((SEQS, N_CTX, BLK)).astype(jnp.int32)
    norm_first = jnp.clip(1.0 + 0.1 * jax.random.normal(arg_keys[5], (D,), jnp.float32), 0.5, 1.5).astype(jnp.bfloat16)
    w_query = noise(arg_keys[6], (D, D), D ** -0.5, 0.21875, ((0, 128),))
    w_key = noise(arg_keys[7], (D, D), D ** -0.5, 0.21875, ((0, 128),))
    w_value = noise(arg_keys[8], (D, D), D ** -0.5, 0.21875, ((0, 128),))
    w_output = noise(arg_keys[9], (D, D), (D // 32) ** -0.5, 1.25, ((0, 128),))
    norm_second = jnp.clip(1.0 + 0.1 * jax.random.normal(arg_keys[10], (D,), jnp.float32), 0.5, 1.5).astype(jnp.bfloat16)
    w_router = noise(arg_keys[11], (D, NALL), D ** -0.5, 0.21875, ((0, 128),))
    w_residual = noise(arg_keys[12], (NALL, NALL), NALL ** -0.5, 1.75, (), jnp.float32)
    w_constant = noise(arg_keys[13], (D, 4), D ** -0.5, 0.21875, ((0, 128),))
    v_constant = noise(arg_keys[14], (D, 2), 1.0, 6.0, ((0, 128),))
    w_gate = noise(arg_keys[15], (EXPERTS * HALVES, D, FFH), D ** -0.5, 0.21875, ((0, 16), (1, 8)))
    w_up = noise(arg_keys[16], (EXPERTS * HALVES, D, FFH), D ** -0.5, 0.21875, ((0, 16), (1, 8)))
    w_down = noise(arg_keys[17], (EXPERTS * HALVES, FFH, D), FF ** -0.5, 0.125, ((0, 16), (1, 8)))
    cotangent = noise(arg_keys[18], (SEQS, LEN, D), 1.0, 6.0, ((0, 16), (1, 8)))
    return dict(tokens=tokens, prev_logits=prev_logits, routes=routes, segments=segments, rank_order=rank_order, norm_first=norm_first, w_query=w_query, w_key=w_key, w_value=w_value, w_output=w_output, norm_second=norm_second, w_router=w_router, w_residual=w_residual, w_constant=w_constant, v_constant=v_constant, w_gate=w_gate, w_up=w_up, w_down=w_down, cotangent=cotangent)


@jax.custom_vjp
def low(v):
    return lax.optimization_barrier(v.astype(jnp.bfloat16)).astype(jnp.float32)

@jax.custom_vjp
def low_back(v):
    return v

def low_keep(v):
    return (low(v), None)

def low_pass(kept, grad):
    return (grad,)

def back_keep(v):
    return (v, None)

def back_low(kept, grad):
    return (low(grad),)
low.defvjp(low_keep, low_pass)
low_back.defvjp(back_keep, back_low)
highest = lax.Precision.HIGHEST
masked_score = -1e+30

def product(left, right):
    return jnp.dot(left, right, precision=highest, preferred_element_type=jnp.float32)

def rms_norm(values, gain_vec):
    scaling = lax.rsqrt(lax.optimization_barrier(jnp.mean(values * values, axis=-1, keepdims=True)) + 1e-06)
    return values * scaling * gain_vec

def rotary(values, positions):
    half_dim = values.shape[-1] // 2
    frequency = jnp.exp(-jnp.log(10000.0) * jnp.arange(half_dim, dtype=jnp.float32) * 2.0 / values.shape[-1])
    phases = positions.astype(jnp.float32)[:, None] * frequency[None, :]
    cosine = jnp.cos(phases)[:, None, :]
    sine_table = jnp.sin(phases)[:, None, :]
    lower_half = values[..., :half_dim]
    upper_half = values[..., half_dim:]
    return jnp.concatenate([lower_half * cosine - upper_half * sine_table, upper_half * cosine + lower_half * sine_table], axis=-1)

def attention(normed, w_query, w_key, w_value, w_output, segment_ids):
    length = normed.shape[0]
    positions = jnp.arange(length, dtype=jnp.int32)
    queries = low(rotary(low_back(product(normed, w_query).reshape(length, HEADS, HDIM)), positions))
    keys_rot = low(rotary(low_back(product(normed, w_key).reshape(length, HEADS, HDIM)), positions))
    values_proj = low(low_back(product(normed, w_value).reshape(length, HEADS, HDIM)))
    scores = low_back(jnp.einsum('qhd,khd->hqk', queries, keys_rot, precision=highest) * HDIM ** (-0.5))
    allowed = (positions[None, :] <= positions[:, None]) & (segment_ids[None, :] == segment_ids[:, None])
    scores = jnp.where(allowed[None], scores, masked_score)
    top_score = lax.optimization_barrier(jnp.max(scores, axis=-1, keepdims=True))
    weights = jnp.exp(scores - top_score)
    weights = weights / lax.optimization_barrier(jnp.sum(weights, axis=-1, keepdims=True))
    attended = jnp.einsum('hqk,khd->qhd', low(weights), values_proj, precision=highest).reshape(length, HEADS * HDIM)
    return product(low(low_back(attended)), w_output)

def block_tables(route_blk, rank_blk):
    onehot = (route_blk[:, :, None] == jnp.arange(NALL, dtype=jnp.int32)[None, None, :]).astype(jnp.float32)
    earlier = (rank_blk[None, :] < rank_blk[:, None]).astype(jnp.float32)
    slot_table = product(earlier, lax.optimization_barrier(jnp.sum(onehot, axis=1))).astype(jnp.int32)
    pair_slot = jnp.take_along_axis(slot_table, route_blk, axis=1)
    kept_pairs = (route_blk < EXPERTS) & (pair_slot < CAP)
    target = jnp.where(kept_pairs, route_blk * CAP + pair_slot, -1)
    slot_ids = jnp.arange(EXPERTS * CAP, dtype=jnp.int32)
    return (target[None, :, :] == slot_ids[:, None, None]).astype(jnp.float32)

def mixture(normed, prev_rows, route_rows, rank_rows, w_router, w_residual, w_constant, v_constant, w_gate, w_up, w_down):
    logits = product(normed, w_router) + product(prev_rows, w_residual)
    chosen = jnp.take_along_axis(logits, route_rows, axis=1)
    chosen = jnp.exp(chosen - lax.optimization_barrier(jnp.max(chosen, axis=1, keepdims=True)))
    gate_values = chosen / lax.optimization_barrier(jnp.sum(chosen, axis=1, keepdims=True))
    blocks = normed.reshape(N_CTX, BLK, D)
    tables = jax.vmap(block_tables)(route_rows.reshape(N_CTX, BLK, 2), rank_rows)
    dispatched = jnp.einsum('cjtk,ctd->cjd', tables, blocks, precision=highest).reshape(N_CTX, EXPERTS, CAP, D)
    owner = jnp.arange(EXPERTS * HALVES, dtype=jnp.int32) // HALVES
    inputs = low_back(dispatched[:, owner])
    gate_proj = low_back(jnp.einsum('cjsd,jdf->cjsf', inputs, w_gate, precision=highest))
    up_proj = low_back(jnp.einsum('cjsd,jdf->cjsf', inputs, w_up, precision=highest))
    hidden = low(gate_proj * jax.nn.sigmoid(gate_proj) * up_proj)
    piece_out = low(jnp.einsum('cjsf,jfd->cjsd', hidden, w_down, precision=highest))
    expert_rows = low_back(lax.optimization_barrier(jnp.sum(piece_out.reshape(N_CTX, EXPERTS, HALVES, CAP, D), axis=2))).reshape(N_CTX, EXPERTS * CAP, D)
    ffn_pairs = jnp.einsum('cjtk,cjd->ctkd', tables, expert_rows, precision=highest).reshape(N_CTX * BLK, 2, D)
    mix_weights = product(normed, w_constant).reshape(N_CTX * BLK, 2, 2)
    mix_weights = jnp.exp(mix_weights - lax.optimization_barrier(jnp.max(mix_weights, axis=2, keepdims=True)))
    mix_weights = mix_weights / lax.optimization_barrier(jnp.sum(mix_weights, axis=2, keepdims=True))
    constant_out = mix_weights[:, :, 0:1] * normed[:, None, :] + mix_weights[:, :, 1:2] * v_constant.T[None, :, :]
    route_ids = route_rows[:, :, None]
    pairs = ffn_pairs + (route_ids == EXPERTS + 1).astype(jnp.float32) * normed[:, None, :]
    pairs = pairs + (route_ids == EXPERTS + 2).astype(jnp.float32) * constant_out[:, 0:1, :]
    pairs = pairs + (route_ids == EXPERTS + 3).astype(jnp.float32) * constant_out[:, 1:2, :]
    return lax.optimization_barrier(jnp.sum(gate_values[:, :, None] * pairs, axis=1))

def block_layer(params, inputs_wide, prev_rows, segment_ids, route_rows, rank_rows):
    norm_first, w_query, w_key, w_value, w_output, norm_second, w_router, w_residual, w_constant, v_constant, w_gate, w_up, w_down = params
    normed_one = low(rms_norm(inputs_wide, norm_first))
    residual_state = inputs_wide + attention(normed_one, w_query, w_key, w_value, w_output, segment_ids)
    normed_two = low(rms_norm(residual_state, norm_second))
    return residual_state + mixture(normed_two, prev_rows, route_rows, rank_rows, w_router, w_residual, w_constant, v_constant, w_gate, w_up, w_down)

def reference(tokens, prev_logits, routes, segments, rank_order, norm_first, w_query, w_key, w_value, w_output, norm_second, w_router, w_residual, w_constant, v_constant, w_gate, w_up, w_down, cotangent):
    params = tuple((weight.astype(jnp.float32) for weight in (norm_first, w_query, w_key, w_value, w_output, norm_second, w_router, w_residual, w_constant, v_constant, w_gate, w_up, w_down)))

    def forward(params, tokens_all, prev_all):

        def scan_step(running, block_items):
            inputs_wide, prev_rows, segment_ids, route_rows, rank_rows = block_items
            return (running, jax.checkpoint(block_layer)(params, inputs_wide, prev_rows, segment_ids, route_rows, rank_rows))
        unused, outputs = lax.scan(scan_step, jnp.zeros((), jnp.float32), (tokens_all, prev_all, segments, routes, rank_order))
        return outputs
    outputs, pullback = jax.vjp(forward, params, tokens.astype(jnp.float32), prev_logits.astype(jnp.float32))
    param_grads, grad_tokens, grad_prev = pullback(cotangent.astype(jnp.float32))
    grad_norm_first, grad_query, grad_key, grad_value, grad_output, grad_norm_second, grad_router, grad_residual, grad_constant, grad_vectors, grad_gate, grad_up, grad_down = param_grads
    return (outputs.astype(jnp.bfloat16), grad_tokens, grad_prev, grad_norm_first, grad_query, grad_key, grad_value, grad_output, grad_norm_second, grad_router, grad_residual, grad_constant, grad_vectors, grad_gate, grad_up, grad_down)
```

```python
import functools

import jax
import jax.numpy as jnp
import numpy as np
from jax import lax
from jax.experimental import pallas as pl
from jax.experimental.pallas import tpu as pltpu
from jax.sharding import PartitionSpec as P

HEADS = 12
HDIM = 64
EXPERTS = 8
NALL = 12
CAP = 54
WIDTH = HEADS * HDIM

MESH = pl.DeviceIdType.MESH
PART_LANES = (512, 384, 384)
PART_START = (0, 512, 896)
PART_ORDER = ((0, 1, 2), (1, 2, 0), (2, 0, 1))


def place():
    ctx = lax.axis_index("ctx")
    fsdp = lax.axis_index("fsdp")
    return ctx // 2, (ctx % 2) * 2 + fsdp // 8, (fsdp // 2) % 4, fsdp % 2


def device_at(x, z, y, core):
    return {"ctx": x * 2 + z // 2, "fsdp": (z % 2) * 8 + y * 2 + core}


def shifted(spot, axis, by):
    moved = list(spot)
    moved[axis] = (moved[axis] + by) % 4
    return tuple(moved)


def greet(devices):
    barrier = pltpu.get_barrier_semaphore()
    for device in devices:
        pl.semaphore_signal(barrier, inc=1, device_id=device, device_id_type=MESH)
    pl.semaphore_wait(barrier, len(devices))


def torus_peers(spot, core):
    peers = [device_at(*shifted(spot, axis, by), core) for axis in range(3) for by in (1, 2, 3)]
    return peers + [device_at(*spot, 1 - core)]


def region(ref, spot, core, whole):
    return ref.at[
        tuple(slice(None) if axis in whole else spot[axis] for axis in range(3)) + (core,)
    ]


def gather_kernel(own_ref, *refs):
    parts = refs[:3]
    net_send, net_recv, twin_send, twin_recv, own_sem = refs[3:]
    *spot, core = place()
    spot = tuple(spot)
    twin = device_at(*spot, 1 - core)
    greet(torus_peers(spot, core))

    def net(part, step, by, source, target):
        axis = PART_ORDER[part][step]
        return pltpu.make_async_remote_copy(
            src_ref=source,
            dst_ref=target,
            send_sem=net_send.at[part, step, by - 1],
            recv_sem=net_recv.at[part, step, by - 1],
            device_id=device_at(*shifted(spot, axis, by), core),
            device_id_type=MESH,
        )

    def share(part, slot, source, target):
        return pltpu.make_async_remote_copy(
            src_ref=source,
            dst_ref=target,
            send_sem=twin_send.at[part, slot],
            recv_sem=twin_recv.at[part, slot],
            device_id=twin,
            device_id_type=MESH,
        )

    started = []
    kept = []
    for part in range(3):
        own = own_ref.at[:, pl.ds(PART_START[part], PART_LANES[part])]
        mine = region(parts[part], spot, core, ())
        for by in (1, 2, 3):
            copy = net(part, 0, by, own, mine)
            copy.start()
            started.append(copy)
    for part in range(3):
        own = own_ref.at[:, pl.ds(PART_START[part], PART_LANES[part])]
        mine = region(parts[part], spot, core, ())
        copy = pltpu.make_async_copy(own, mine, own_sem.at[part])
        copy.start()
        kept.append(copy)
        copy = share(part, 0, own, mine)
        copy.start()
        started.append(copy)
    for copy in kept:
        copy.wait()
    for step in range(3):
        for part in range(3):
            order = PART_ORDER[part]
            axis = order[step]
            whole = order[:step]
            for by in (1, 2, 3):
                came = region(parts[part], shifted(spot, axis, -by), core, whole)
                net(part, step, by, came, came).wait_recv()
                copy = share(part, 1 + step * 3 + by - 1, came, came)
                copy.start()
                started.append(copy)
            if step < 2:
                held = region(parts[part], spot, core, order[: step + 1])
                for by in (1, 2, 3):
                    copy = net(part, step + 1, by, held, held)
                    copy.start()
                    started.append(copy)
    for part in range(3):
        order = PART_ORDER[part]
        first = region(parts[part], spot, 1 - core, ())
        share(part, 0, first, first).wait_recv()
        for step in range(3):
            for by in (1, 2, 3):
                came = region(
                    parts[part], shifted(spot, order[step], -by), 1 - core, order[:step]
                )
                share(part, 1 + step * 3 + by - 1, came, came).wait_recv()
    for copy in started:
        copy.wait_send()


def gather_shards(own):
    return pl.pallas_call(
        gather_kernel,
        out_shape=[
            jax.ShapeDtypeStruct((4, 4, 4, 2, 16, lanes), jnp.bfloat16) for lanes in PART_LANES
        ],
        in_specs=[pl.BlockSpec(memory_space=pltpu.VMEM)],
        out_specs=[pl.BlockSpec(memory_space=pl.ANY)] * 3,
        scratch_shapes=[
            pltpu.SemaphoreType.DMA((3, 3, 3)),
            pltpu.SemaphoreType.DMA((3, 3, 3)),
            pltpu.SemaphoreType.DMA((3, 10)),
            pltpu.SemaphoreType.DMA((3, 10)),
            pltpu.SemaphoreType.DMA((3,)),
        ],
        name="gather_shards",
        compiler_params=pltpu.CompilerParams(collective_id=1, has_side_effects=True),
    )(own)


def scatter_kernel(grads_ref, small_ref, out_ref, total_ref, *refs):
    twin_in, held = refs[0:3], refs[3:6]
    in_one, in_two, in_three = refs[6:9], refs[9:12], refs[12:15]
    sum_one, sum_two = refs[15:18], refs[18:21]
    small_in, small_sum, net_send, net_recv, twin_send, twin_recv, small_send, small_recv = refs[21:]
    *spot, core = place()
    spot = tuple(spot)
    twin = device_at(*spot, 1 - core)
    greet(torus_peers(spot, core))
    started = []

    def net(part, step, by, source, target):
        axis = PART_ORDER[part][2 - step]
        return pltpu.make_async_remote_copy(
            src_ref=source,
            dst_ref=target,
            send_sem=net_send.at[part, step, by - 1],
            recv_sem=net_recv.at[part, step, by - 1],
            device_id=device_at(*shifted(spot, axis, by), core),
            device_id_type=MESH,
        )

    def share(part):
        lanes = pl.ds(PART_START[part], PART_LANES[part])
        return pltpu.make_async_remote_copy(
            src_ref=grads_ref.at[:, :, :, 1 - core, :, lanes],
            dst_ref=twin_in[part],
            send_sem=twin_send.at[part],
            recv_sem=twin_recv.at[part],
            device_id=twin,
            device_id_type=MESH,
        )

    def small(axis, by, source, slot):
        device = twin if axis == 3 else device_at(*shifted(spot, axis, by), core)
        return pltpu.make_async_remote_copy(
            src_ref=source,
            dst_ref=small_in.at[axis, slot],
            send_sem=small_send.at[axis, by - 1],
            recv_sem=small_recv.at[axis, by - 1],
            device_id=device,
            device_id_type=MESH,
        )

    for part in range(3):
        copy = share(part)
        copy.start()
        started.append(copy)
    copy = small(3, 1, small_ref, core)
    copy.start()
    started.append(copy)

    def add_pairs(part):
        start, lanes = PART_START[part], PART_LANES[part]

        def step(index, carry):
            x, z, y = index // 16, (index // 4) % 4, index % 4
            held[part][x, z, y] = (
                grads_ref[x, z, y, core, :, start : start + lanes].astype(jnp.float32)
                + twin_in[part][x, z, y].astype(jnp.float32)
            ).astype(jnp.bfloat16)
            return carry

        lax.fori_loop(0, 64, step, 0, unroll=2)

    def cut(spots, axis, at):
        return tuple(at if a == axis else slice(None) for a in spots)

    for part in range(3):
        share(part).wait_recv()
        add_pairs(part)
        axis = PART_ORDER[part][2]
        for by in (1, 2, 3):
            index = cut((0, 1, 2), axis, shifted(spot, axis, by)[axis])
            copy = net(part, 0, by, held[part].at[index], in_one[part].at[by - 1])
            copy.start()
            started.append(copy)

    small(3, 1, small_ref, 1 - core).wait_recv()
    small_in[3, core] = small_ref[...]
    small_sum[0] = small_in[3, 0] + small_in[3, 1]
    for by in (1, 2, 3):
        copy = small(0, by, small_sum.at[0], spot[0])
        copy.start()
        started.append(copy)

    def small_step(axis):
        for by in (1, 2, 3):
            small(axis, by, small_sum.at[axis], shifted(spot, axis, -by)[axis]).wait_recv()
        small_in[axis, spot[axis]] = small_sum[axis]
        total = small_in[axis, 0] + small_in[axis, 1] + small_in[axis, 2] + small_in[axis, 3]
        if axis == 2:
            total_ref[...] = total
            return
        small_sum[axis + 1] = total
        for by in (1, 2, 3):
            copy = small(axis + 1, by, small_sum.at[axis + 1], spot[axis + 1])
            copy.start()
            started.append(copy)

    for part in range(3):
        first, second, third = PART_ORDER[part]
        for by in (1, 2, 3):
            net(part, 0, by, in_one[part].at[by - 1], in_one[part].at[by - 1]).wait_recv()
        rest = tuple(a for a in (0, 1, 2) if a != third)

        def add_four(index, carry, part=part, third=third, rest=rest):
            at = {rest[0]: index // 4, rest[1]: index % 4, third: spot[third]}
            total = held[part][at[0], at[1], at[2]].astype(jnp.float32)
            for by in range(3):
                total = total + in_one[part][by, index // 4, index % 4].astype(jnp.float32)
            sum_one[part][index // 4, index % 4] = total.astype(jnp.bfloat16)
            return carry

        lax.fori_loop(0, 16, add_four, 0, unroll=2)
        for by in (1, 2, 3):
            at = shifted(spot, second, by)[second]
            source = sum_one[part].at[at] if second == rest[0] else sum_one[part].at[:, at]
            copy = net(part, 1, by, source, in_two[part].at[by - 1])
            copy.start()
            started.append(copy)
    small_step(0)
    for part in range(3):
        first, second, third = PART_ORDER[part]
        for by in (1, 2, 3):
            net(part, 1, by, in_two[part].at[by - 1], in_two[part].at[by - 1]).wait_recv()
        rest = tuple(a for a in (0, 1, 2) if a != third)
        for index in range(4):
            if second == rest[0]:
                total = sum_one[part][spot[second], index].astype(jnp.float32)
            else:
                total = sum_one[part][index, spot[second]].astype(jnp.float32)
            for by in range(3):
                total = total + in_two[part][by, index].astype(jnp.float32)
            sum_two[part][index] = total.astype(jnp.bfloat16)
        for by in (1, 2, 3):
            at = shifted(spot, first, by)[first]
            copy = net(part, 2, by, sum_two[part].at[at], in_three[part].at[by - 1])
            copy.start()
            started.append(copy)
    small_step(1)
    for part in range(3):
        first = PART_ORDER[part][0]
        for by in (1, 2, 3):
            net(part, 2, by, in_three[part].at[by - 1], in_three[part].at[by - 1]).wait_recv()
        total = sum_two[part][spot[first]].astype(jnp.float32)
        for by in range(3):
            total = total + in_three[part][by].astype(jnp.float32)
        out_ref[:, PART_START[part] : PART_START[part] + PART_LANES[part]] = total
    small_step(2)
    for copy in started:
        copy.wait_send()


def scatter_shards(grads, small):
    by_part = lambda *lead: [pltpu.VMEM((*lead, 16, lanes), jnp.bfloat16) for lanes in PART_LANES]
    return pl.pallas_call(
        scatter_kernel,
        out_shape=[
            jax.ShapeDtypeStruct((16, 1280), jnp.float32),
            jax.ShapeDtypeStruct((16, 128), jnp.float32),
        ],
        in_specs=[pl.BlockSpec(memory_space=pltpu.VMEM)] * 2,
        out_specs=[pl.BlockSpec(memory_space=pltpu.VMEM)] * 2,
        scratch_shapes=[
            *by_part(4, 4, 4),
            *by_part(4, 4, 4),
            *by_part(3, 4, 4),
            *by_part(3, 4),
            *by_part(3),
            *by_part(4, 4),
            *by_part(4),
            pltpu.VMEM((4, 4, 16, 128), jnp.float32),
            pltpu.VMEM((3, 16, 128), jnp.float32),
            pltpu.SemaphoreType.DMA((3, 3, 3)),
            pltpu.SemaphoreType.DMA((3, 3, 3)),
            pltpu.SemaphoreType.DMA((3,)),
            pltpu.SemaphoreType.DMA((3,)),
            pltpu.SemaphoreType.DMA((4, 3)),
            pltpu.SemaphoreType.DMA((4, 3)),
        ],
        name="scatter_shards",
        compiler_params=pltpu.CompilerParams(
            collective_id=2, has_side_effects=True, vmem_limit_bytes=40 * 2**20
        ),
    )(grads, small)


def placing_tables():
    left = np.zeros((192, 256), np.float32)
    right = np.zeros((192, 256), np.float32)
    small = np.zeros((48, 128), np.float32)
    for device in range(8):
        for weight in range(4):
            for row in range(6):
                at, line = weight * 48 + device * 6 + row, weight * 6 + row
                if line < 16:
                    left[at, device * 16 + line] = right[at, device * 16 + line] = 1
                else:
                    left[at, 128 + device * 16 + line - 16] = 1
                    right[at, 128 + device * 16 + line - 8] = 1
        for row in range(6):
            small[device * 6 + row, device * 16 + row] = 1
    return left, right, small


def unpack_kernel(a_ref, b_ref, c_ref, left_ref, right_ref, small_ref, weights_ref, smalls_ref):
    a, b, c = a_ref[0], b_ref[0], c_ref[0]
    tail = jnp.concatenate([b[:, 256:], c[:, :256]], axis=1)
    left = jnp.dot(
        left_ref[...],
        jnp.concatenate([a[:, :384], tail], axis=0),
        preferred_element_type=jnp.float32,
    )
    right = jnp.dot(
        right_ref[...],
        jnp.concatenate([jnp.concatenate([a[:, 384:], b[:, :256]], axis=1), tail], axis=0),
        preferred_element_type=jnp.float32,
    )
    for weight in range(4):
        rows = slice(weight * 48, weight * 48 + 48)
        weights_ref[weight, :, :384] = left[rows].astype(jnp.bfloat16)
        weights_ref[weight, :, 384:] = right[rows].astype(jnp.bfloat16)
    smalls_ref[...] = jnp.dot(
        small_ref[...], c[:, 256:], preferred_element_type=jnp.float32
    ).astype(jnp.bfloat16)


def unpack_shards(parts):
    left, right, small = (jnp.asarray(t, jnp.bfloat16) for t in placing_tables())
    whole = lambda t: pl.BlockSpec(t.shape, lambda g: (0, 0))
    return pl.pallas_call(
        unpack_kernel,
        grid=(16,),
        out_shape=[
            jax.ShapeDtypeStruct((4, WIDTH, WIDTH), jnp.bfloat16),
            jax.ShapeDtypeStruct((WIDTH, 128), jnp.bfloat16),
        ],
        in_specs=[
            *(pl.BlockSpec((1, 128, lanes), lambda g: (g, 0, 0)) for lanes in PART_LANES),
            whole(left),
            whole(right),
            whole(small),
        ],
        out_specs=[
            pl.BlockSpec((4, 48, WIDTH), lambda g: (0, g, 0)),
            pl.BlockSpec((48, 128), lambda g: (g, 0)),
        ],
        name="unpack_shards",
        compiler_params=pltpu.CompilerParams(vmem_limit_bytes=24 * 2**20),
    )(*(part.reshape(16, 128, -1) for part in parts), left, right, small)


def pack_kernel(weights_ref, smalls_ref, left_ref, right_ref, small_ref, out_ref):
    left = jnp.concatenate([weights_ref[w, :, :384] for w in range(4)], axis=0).astype(jnp.bfloat16)
    right = jnp.concatenate([weights_ref[w, :, 384:] for w in range(4)], axis=0).astype(jnp.bfloat16)
    from_left = jnp.dot(left_ref[...], left, preferred_element_type=jnp.float32)
    from_right = jnp.dot(right_ref[...], right, preferred_element_type=jnp.float32)
    out_ref[0, :, :384] = from_left[:128].astype(jnp.bfloat16)
    out_ref[0, :, 384:768] = from_right[:128].astype(jnp.bfloat16)
    out_ref[0, :, 768:1152] = (from_left[128:] + from_right[128:]).astype(jnp.bfloat16)
    out_ref[0, :, 1152:] = jnp.dot(
        small_ref[...], smalls_ref[...].astype(jnp.bfloat16), preferred_element_type=jnp.float32
    ).astype(jnp.bfloat16)


def pack_shards(weights, smalls):
    left, right, small = (jnp.asarray(t.T, jnp.bfloat16) for t in placing_tables())
    whole = lambda t: pl.BlockSpec(t.shape, lambda g: (0, 0))
    return pl.pallas_call(
        pack_kernel,
        grid=(16,),
        out_shape=jax.ShapeDtypeStruct((16, 128, 1280), jnp.bfloat16),
        in_specs=[
            pl.BlockSpec((4, 48, WIDTH), lambda g: (0, g, 0)),
            pl.BlockSpec((48, 128), lambda g: (g, 0)),
            whole(left),
            whole(right),
            whole(small),
        ],
        out_specs=pl.BlockSpec((1, 128, 1280), lambda g: (g, 0, 0)),
        name="pack_shards",
        compiler_params=pltpu.CompilerParams(vmem_limit_bytes=24 * 2**20),
    )(weights, smalls, left, right, small).reshape(4, 4, 4, 2, 16, 1280)


def pack_own(weights, smalls):
    rows = jnp.concatenate(weights, axis=0)
    tail = jnp.concatenate([rows[16:, :384], rows[16:, 384:]], axis=0)
    small = jnp.pad(jnp.concatenate(smalls, axis=1), ((0, 10), (0, 108)))
    return jnp.concatenate([rows[:16], tail, small], axis=1)


def unpack_own(packed):
    tail = jnp.concatenate([packed[:8, 768:1152], packed[8:, 768:1152]], axis=1)
    rows = jnp.concatenate([packed[:16, :768], tail], axis=0)
    small = packed[:6, 1152:]
    return [rows[i * 6 : i * 6 + 6] for i in range(4)], small


highest = lax.Precision.HIGHEST
masked_score = -1e30
epsilon = 1e-06


def rms_forward(values, gain_vec):
    scaling = lax.rsqrt(jnp.mean(values * values, axis=-1, keepdims=True) + epsilon)
    return (values * scaling * gain_vec, scaling)


def rms_backward(values, scaling, gain_vec, gradient):
    weighted = gradient * gain_vec
    inner_mean = jnp.mean(weighted * values, axis=-1, keepdims=True)
    return (
        scaling * weighted - values * scaling**3 * inner_mean,
        jnp.sum(gradient * values * scaling, axis=0),
    )


def rotary_tables(positions, head_dim):
    half_dim = head_dim // 2
    frequency = jnp.exp(
        -jnp.log(10000.0) * jnp.arange(half_dim, dtype=jnp.float32) * 2.0 / head_dim
    )
    phases = positions.astype(jnp.float32)[:, None] * frequency[None, :]
    return (jnp.cos(phases)[:, None, :], jnp.sin(phases)[:, None, :])


def rotate(values, cosine, sine_table):
    half_dim = values.shape[-1] // 2
    lower_half = values[..., :half_dim]
    upper_half = values[..., half_dim:]
    return jnp.concatenate(
        [
            lower_half * cosine - upper_half * sine_table,
            upper_half * cosine + lower_half * sine_table,
        ],
        axis=-1,
    )


def block_scores(queries, keys_blk, query_pos, key_pos, query_seg, key_seg, scaling):
    scores = (
        jnp.einsum("qhd,khd->hqk", queries, keys_blk, preferred_element_type=jnp.float32) * scaling
    )
    allowed = (key_pos[None, :] <= query_pos[:, None]) & (key_seg[None, :] == query_seg[:, None])
    return jnp.where(allowed[None], scores, masked_score)


def on_device(
    tokens,
    prev_logits,
    routes,
    segments,
    rank_order,
    norm_first,
    w_query,
    w_key,
    w_value,
    w_output,
    norm_second,
    w_router,
    w_residual,
    w_constant,
    v_constant,
    w_gate,
    w_up,
    w_down,
    cotangent,
):
    def over_ctx(array):
        return lax.all_to_all(
            jnp.broadcast_to(array[None], (8, *array.shape)), "ctx", 0, 0, tiled=True
        )

    experts = over_ctx(
        jnp.concatenate([w_gate[0], w_up[0], w_down[0].reshape(96, 1024)], axis=0)
    ).reshape(8, 3, 96, 1024)
    own = pack_own(
        [w_query, w_key, w_value, w_output],
        [w_router, w_constant, v_constant, norm_first[:, None], norm_second[:, None]],
    )
    (query_w, key_w, value_w, output_w), smalls = unpack_shards(gather_shards(own))
    router_w, constant_w, constant_v = smalls[:, :12], smalls[:, 12:16], smalls[:, 16:18]
    gain_one, gain_two = smalls[:, 18], smalls[:, 19]
    gate_w = experts[:, 0].reshape(768, 1024)
    up_w = experts[:, 1].reshape(768, 1024)
    down_w = experts[:, 2].reshape(1024, 768)
    ctx_count = lax.axis_size("ctx")
    halves = lax.axis_size("fsdp") // EXPERTS
    block_len = tokens.shape[1]
    width = HEADS * HDIM
    length = block_len * ctx_count
    scaling = HDIM ** (-0.5)
    first_position = lax.axis_index("ctx") * block_len
    positions = first_position + jnp.arange(block_len, dtype=jnp.int32)
    cosine, sine_table = rotary_tables(positions, HDIM)
    inputs_wide = tokens[0].astype(jnp.float32)
    normed_one, scale_one = rms_forward(inputs_wide, gain_one.astype(jnp.float32))
    normed_one = normed_one.astype(jnp.bfloat16)

    def project(weight):
        return jnp.dot(normed_one, weight, preferred_element_type=jnp.float32).reshape(
            block_len, HEADS, HDIM
        )

    queries = rotate(project(query_w), cosine, sine_table).astype(jnp.bfloat16)
    keys_own = rotate(project(key_w), cosine, sine_table).astype(jnp.bfloat16)
    values_own = project(value_w).astype(jnp.bfloat16)
    query_seg = segments[0]
    keys_values = over_ctx(
        jnp.concatenate([keys_own.reshape(block_len, width), values_own.reshape(block_len, width)], axis=0)
    )
    keys_all = keys_values[:, :block_len].reshape(length, width)
    values_all = keys_values[:, block_len:].reshape(length, width)
    seg_all = over_ctx(query_seg.astype(jnp.bfloat16)).reshape(length)
    key_block = min(512, length)
    block_count = length // key_block
    key_blocks = keys_all.reshape(block_count, key_block, HEADS, HDIM)
    value_blocks = values_all.reshape(block_count, key_block, HEADS, HDIM)
    seg_blocks = seg_all.astype(jnp.int32).reshape(block_count, key_block)
    key_offsets = jnp.arange(key_block, dtype=jnp.int32)
    needed = (first_position + block_len - 1) // key_block + 1

    def own_scores(index):
        return block_scores(
            queries,
            key_blocks[index],
            positions,
            index * key_block + key_offsets,
            query_seg,
            seg_blocks[index],
            scaling,
        )

    def stats_body(index, running):
        maxima, totals = running
        scores = own_scores(index)
        new_max = jnp.maximum(maxima, jnp.max(scores, axis=-1))
        totals = totals * jnp.exp(maxima - new_max) + jnp.sum(
            jnp.exp(scores - new_max[..., None]), axis=-1
        )
        return (new_max, totals)

    start_stats = (
        jnp.full((HEADS, block_len), masked_score, jnp.float32),
        jnp.zeros((HEADS, block_len), jnp.float32),
    )
    maxima, totals = lax.fori_loop(0, needed, stats_body, start_stats)
    log_total = maxima + jnp.log(totals)

    def output_body(index, running):
        weights = jnp.exp(own_scores(index) - log_total[..., None]).astype(jnp.bfloat16)
        return running + jnp.einsum(
            "hqk,khd->qhd", weights, value_blocks[index], preferred_element_type=jnp.float32
        )

    attended_sum = lax.fori_loop(
        0, needed, output_body, jnp.zeros((block_len, HEADS, HDIM), jnp.float32)
    )
    attended = attended_sum.reshape(block_len, width).astype(jnp.bfloat16)
    residual_state = inputs_wide + jnp.dot(attended, output_w, preferred_element_type=jnp.float32)
    normed_two, scale_two = rms_forward(residual_state, gain_two.astype(jnp.float32))
    normed_two = normed_two.astype(jnp.bfloat16)
    normed_wide = normed_two.astype(jnp.float32)
    prev_rows = prev_logits[0]
    logits = jnp.dot(normed_two, router_w, preferred_element_type=jnp.float32) + jnp.dot(
        prev_rows, w_residual, precision=highest
    )
    route_rows = routes[0]
    onehot = (route_rows[:, :, None] == jnp.arange(NALL, dtype=jnp.int32)[None, None, :]).astype(
        jnp.float32
    )
    chosen = jnp.sum(onehot * logits[:, None, :], axis=-1)
    chosen = jnp.exp(chosen - jnp.max(chosen, axis=1, keepdims=True))
    gate_values = chosen / jnp.sum(chosen, axis=1, keepdims=True)
    rank_rows = rank_order[0, 0]
    earlier = (rank_rows[None, :] < rank_rows[:, None]).astype(jnp.float32)
    slot_table = jnp.dot(earlier, jnp.sum(onehot, axis=1), precision=highest).astype(jnp.int32)
    pair_slot = jnp.sum(slot_table[:, None, :] * onehot.astype(jnp.int32), axis=-1)
    kept_pairs = (route_rows < EXPERTS) & (pair_slot < CAP)
    target = jnp.where(kept_pairs, route_rows * CAP + pair_slot, -1)
    tables = (jnp.arange(EXPERTS * CAP, dtype=jnp.int32)[:, None, None] == target[None]).astype(
        jnp.bfloat16
    )
    tables_split = tables.reshape(EXPERTS, CAP, block_len, 2)
    dispatched = jnp.einsum(
        "jtk,td->jd", tables, normed_two, preferred_element_type=jnp.float32
    ).astype(jnp.bfloat16)
    outgoing = jnp.repeat(dispatched.reshape(EXPERTS, CAP, width), halves, axis=0)
    received = lax.all_to_all(outgoing, "fsdp", split_axis=0, concat_axis=0, tiled=True)
    flat_rows = received.reshape(-1, received.shape[-1])
    gate_proj = jnp.dot(flat_rows, gate_w, preferred_element_type=jnp.float32)
    up_proj = jnp.dot(flat_rows, up_w, preferred_element_type=jnp.float32)
    hidden = (gate_proj * jax.nn.sigmoid(gate_proj) * up_proj).astype(jnp.bfloat16)
    piece_out = (
        jnp.dot(hidden, down_w, preferred_element_type=jnp.float32)
        .astype(jnp.bfloat16)
        .reshape(received.shape)
    )
    returned = lax.all_to_all(piece_out, "fsdp", split_axis=0, concat_axis=0, tiled=True)
    returned, arrived = (returned, received)
    ffn_pairs = jnp.einsum(
        "ectk,ehcd->tkd",
        tables_split,
        returned.reshape(EXPERTS, halves, CAP, width),
        preferred_element_type=jnp.float32,
    )
    mix_weights = jnp.dot(normed_two, constant_w, preferred_element_type=jnp.float32).reshape(
        block_len, 2, 2
    )
    mix_weights = jnp.exp(mix_weights - jnp.max(mix_weights, axis=2, keepdims=True))
    mix_weights = mix_weights / jnp.sum(mix_weights, axis=2, keepdims=True)
    constant_rows = constant_v.astype(jnp.float32).T
    constant_out = (
        mix_weights[:, :, 0:1] * normed_wide[:, None, :]
        + mix_weights[:, :, 1:2] * constant_rows[None]
    )
    is_copy = (route_rows == EXPERTS + 1).astype(jnp.float32)[:, :, None]
    is_first = (route_rows == EXPERTS + 2).astype(jnp.float32)[:, :, None]
    is_second = (route_rows == EXPERTS + 3).astype(jnp.float32)[:, :, None]
    pairs = (
        ffn_pairs
        + is_copy * normed_wide[:, None, :]
        + is_first * constant_out[:, 0:1, :]
        + is_second * constant_out[:, 1:2, :]
    )
    block_output = residual_state + jnp.sum(gate_values[:, :, None] * pairs, axis=1)
    upstream = cotangent[0].astype(jnp.float32)
    gate_grad = jnp.sum(pairs * upstream[:, None, :], axis=-1)
    pair_grad = gate_values[:, :, None] * upstream[:, None, :]
    chosen_grad = gate_values * (
        gate_grad - jnp.sum(gate_values * gate_grad, axis=1, keepdims=True)
    )
    logit_grad = jnp.sum(chosen_grad[:, :, None] * onehot, axis=1)
    normed_grad = jnp.dot(logit_grad, router_w.astype(jnp.float32).T, precision=highest)
    router_grad = jnp.dot(normed_wide.T, logit_grad, precision=highest)
    prev_grad = jnp.dot(logit_grad, w_residual.T, precision=highest)
    residual_grad = jnp.dot(prev_rows.T, logit_grad, precision=highest)
    normed_grad = normed_grad + jnp.sum(is_copy * pair_grad, axis=1)
    const_grad = jnp.stack(
        [jnp.sum(is_first * pair_grad, axis=1), jnp.sum(is_second * pair_grad, axis=1)], axis=1
    )
    mix_grad = jnp.stack(
        [
            jnp.sum(const_grad * normed_wide[:, None, :], axis=-1),
            jnp.sum(const_grad * constant_rows[None], axis=-1),
        ],
        axis=-1,
    )
    mix_grad = mix_weights * (mix_grad - jnp.sum(mix_weights * mix_grad, axis=2, keepdims=True))
    normed_grad = normed_grad + jnp.sum(mix_weights[:, :, 0:1] * const_grad, axis=1)
    vector_grad = jnp.sum(mix_weights[:, :, 1:2] * const_grad, axis=0).T
    mix_flat = mix_grad.reshape(block_len, 4)
    normed_grad = normed_grad + jnp.dot(
        mix_flat, constant_w.astype(jnp.float32).T, precision=highest
    )
    constant_grad = jnp.dot(normed_wide.T, mix_flat, precision=highest)
    slot_grad = jnp.einsum(
        "jtk,tkd->jd", tables, pair_grad.astype(jnp.bfloat16), preferred_element_type=jnp.float32
    ).astype(jnp.bfloat16)
    slot_outgoing = jnp.repeat(slot_grad.reshape(EXPERTS, CAP, width), halves, axis=0)
    arrived_grad = lax.all_to_all(slot_outgoing, "fsdp", split_axis=0, concat_axis=0, tiled=True)
    flat_rows = arrived.reshape(-1, width)
    flat_grad = arrived_grad.reshape(-1, width)
    gate_proj = jnp.dot(flat_rows, gate_w, preferred_element_type=jnp.float32)
    up_proj = jnp.dot(flat_rows, up_w, preferred_element_type=jnp.float32)
    sigmoid_gate = jax.nn.sigmoid(gate_proj)
    activated = gate_proj * sigmoid_gate
    hidden = (activated * up_proj).astype(jnp.bfloat16)
    hidden_grad = jnp.dot(flat_grad, down_w.T, preferred_element_type=jnp.float32)
    down_grad = jnp.dot(hidden.T, flat_grad, preferred_element_type=jnp.float32)
    gate_proj_grad = (
        hidden_grad * up_proj * sigmoid_gate * (1.0 + gate_proj * (1.0 - sigmoid_gate))
    ).astype(jnp.bfloat16)
    up_proj_grad = (hidden_grad * activated).astype(jnp.bfloat16)
    gate_grad_w = jnp.dot(flat_rows.T, gate_proj_grad, preferred_element_type=jnp.float32)
    up_grad_w = jnp.dot(flat_rows.T, up_proj_grad, preferred_element_type=jnp.float32)
    piece_input_grad = (
        (
            jnp.dot(gate_proj_grad, gate_w.T, preferred_element_type=jnp.float32)
            + jnp.dot(up_proj_grad, up_w.T, preferred_element_type=jnp.float32)
        )
        .astype(jnp.bfloat16)
        .reshape(arrived.shape)
    )
    returned_grad = lax.all_to_all(
        piece_input_grad, "fsdp", split_axis=0, concat_axis=0, tiled=True
    )
    normed_grad = normed_grad + jnp.einsum(
        "ectk,ehcd->td",
        tables_split,
        returned_grad.reshape(EXPERTS, halves, CAP, width),
        preferred_element_type=jnp.float32,
    )
    expert_grads = jnp.concatenate(
        [
            gate_grad_w.astype(jnp.bfloat16).reshape(8, 96, 1024),
            up_grad_w.astype(jnp.bfloat16).reshape(8, 96, 1024),
            down_grad.astype(jnp.bfloat16).reshape(8, 96, 1024),
        ],
        axis=1,
    )
    expert_sum = jnp.sum(
        lax.all_to_all(expert_grads, "ctx", 0, 0, tiled=True).astype(jnp.float32), axis=0
    )
    expert_gate_grad = expert_sum[None, :96]
    expert_up_grad = expert_sum[None, 96:192]
    expert_down_grad = expert_sum[192:].reshape(1, 128, 768)
    state_grad, gain_two_grad = rms_backward(
        residual_state, scale_two, gain_two.astype(jnp.float32), normed_grad
    )
    state_grad = state_grad + upstream
    state_low = state_grad.astype(jnp.bfloat16)
    output_grad_w = jnp.dot(attended.T, state_low, preferred_element_type=jnp.float32)
    attended_grad = (
        jnp.dot(state_low, output_w.T, preferred_element_type=jnp.float32)
        .reshape(block_len, HEADS, HDIM)
        .astype(jnp.bfloat16)
    )
    row_inner = jnp.sum(attended_sum * attended_grad.astype(jnp.float32), axis=-1).T

    def grad_body(index, running):
        query_acc, key_store, value_store = running
        key_rows = key_blocks[index]
        weights = jnp.exp(own_scores(index) - log_total[..., None])
        weight_grad = jnp.einsum(
            "qhd,khd->hqk", attended_grad, value_blocks[index], preferred_element_type=jnp.float32
        )
        score_grad = (weights * (weight_grad - row_inner[..., None])).astype(jnp.bfloat16)
        query_acc = (
            query_acc
            + jnp.einsum("hqk,khd->qhd", score_grad, key_rows, preferred_element_type=jnp.float32)
            * scaling
        )
        key_part = (
            jnp.einsum("hqk,qhd->khd", score_grad, queries, preferred_element_type=jnp.float32)
            * scaling
        )
        value_part = jnp.einsum(
            "hqk,qhd->khd",
            weights.astype(jnp.bfloat16),
            attended_grad,
            preferred_element_type=jnp.float32,
        )
        key_store = lax.dynamic_update_slice_in_dim(
            key_store, key_part.reshape(key_block, width), index * key_block, 0
        )
        value_store = lax.dynamic_update_slice_in_dim(
            value_store, value_part.reshape(key_block, width), index * key_block, 0
        )
        return (query_acc, key_store, value_store)

    start_grads = (
        jnp.zeros((block_len, HEADS, HDIM), jnp.float32),
        jnp.zeros((length, width), jnp.float32),
        jnp.zeros((length, width), jnp.float32),
    )
    query_grad, key_parts, value_parts = lax.fori_loop(0, needed, grad_body, start_grads)
    both_parts = jnp.concatenate(
        [key_parts.astype(jnp.bfloat16).reshape(8, block_len, width), value_parts.astype(jnp.bfloat16).reshape(8, block_len, width)],
        axis=1,
    )
    both_sum = jnp.sum(
        lax.all_to_all(both_parts, "ctx", 0, 0, tiled=True).astype(jnp.float32), axis=0
    )
    key_grad, value_grad = both_sum[:block_len], both_sum[block_len:]
    query_low = (
        rotate(query_grad, cosine, -sine_table).reshape(block_len, width).astype(jnp.bfloat16)
    )
    key_low = (
        rotate(key_grad.reshape(block_len, HEADS, HDIM), cosine, -sine_table)
        .reshape(block_len, width)
        .astype(jnp.bfloat16)
    )
    value_low = value_grad.astype(jnp.bfloat16)
    query_grad_w = jnp.dot(normed_one.T, query_low, preferred_element_type=jnp.float32)
    key_grad_w = jnp.dot(normed_one.T, key_low, preferred_element_type=jnp.float32)
    value_grad_w = jnp.dot(normed_one.T, value_low, preferred_element_type=jnp.float32)
    first_grad = (
        jnp.dot(query_low, query_w.T, preferred_element_type=jnp.float32)
        + jnp.dot(key_low, key_w.T, preferred_element_type=jnp.float32)
        + jnp.dot(value_low, value_w.T, preferred_element_type=jnp.float32)
    )
    tokens_grad, gain_one_grad = rms_backward(
        inputs_wide, scale_one, gain_one.astype(jnp.float32), first_grad
    )
    tokens_grad = tokens_grad + state_grad
    small_grads = jnp.pad(
        jnp.concatenate(
            [router_grad, constant_grad, vector_grad, gain_one_grad[:, None], gain_two_grad[:, None]], axis=1
        ),
        ((0, 0), (0, 108)),
    )
    packed = pack_shards(
        jnp.stack([query_grad_w, key_grad_w, value_grad_w, output_grad_w]), small_grads
    )
    summed, residual_total = scatter_shards(packed, jnp.pad(residual_grad, ((0, 4), (0, 116))))
    (sum_query, sum_key, sum_value, sum_output), small_sum = unpack_own(summed)
    sum_router, sum_constant, sum_vectors = small_sum[:, :12], small_sum[:, 12:16], small_sum[:, 16:18]
    sum_gain_one, sum_gain_two = small_sum[:, 18], small_sum[:, 19]
    residual_total = residual_total[:12, :12]
    return (
        block_output.astype(jnp.bfloat16)[None],
        tokens_grad[None],
        prev_grad[None],
        sum_gain_one,
        sum_query,
        sum_key,
        sum_value,
        sum_output,
        sum_gain_two,
        sum_router,
        residual_total,
        sum_constant,
        sum_vectors,
        expert_gate_grad,
        expert_up_grad,
        expert_down_grad,
    )


def solution(mesh):
    in_specs = (
        P("fsdp", "ctx", None),
        P("fsdp", "ctx", None),
        P("fsdp", "ctx", None),
        P("fsdp", "ctx"),
        P("fsdp", "ctx", None),
        P(("ctx", "fsdp")),
        P(("ctx", "fsdp"), None),
        P(("ctx", "fsdp"), None),
        P(("ctx", "fsdp"), None),
        P(("ctx", "fsdp"), None),
        P(("ctx", "fsdp")),
        P(("ctx", "fsdp"), None),
        P(),
        P(("ctx", "fsdp"), None),
        P(("ctx", "fsdp"), None),
        P("fsdp", "ctx", None),
        P("fsdp", "ctx", None),
        P("fsdp", "ctx", None),
        P("fsdp", "ctx", None),
    )
    out_specs = (
        P("fsdp", "ctx", None),
        P("fsdp", "ctx", None),
        P("fsdp", "ctx", None),
        P(("ctx", "fsdp")),
        P(("ctx", "fsdp"), None),
        P(("ctx", "fsdp"), None),
        P(("ctx", "fsdp"), None),
        P(("ctx", "fsdp"), None),
        P(("ctx", "fsdp")),
        P(("ctx", "fsdp"), None),
        P(),
        P(("ctx", "fsdp"), None),
        P(("ctx", "fsdp"), None),
        P("fsdp", "ctx", None),
        P("fsdp", "ctx", None),
        P("fsdp", "ctx", None),
    )
    return jax.shard_map(
        on_device, mesh=mesh, in_specs=in_specs, out_specs=out_specs, check_vma=False
    )
```

```python
import functools

import jax
import jax.numpy as jnp
import numpy as np
from jax import lax
from jax.experimental import pallas as pl
from jax.experimental.pallas import tpu as pltpu
from jax.sharding import PartitionSpec as P

HEADS = 12
HDIM = 64
EXPERTS = 8
NALL = 12
CAP = 54
WIDTH = HEADS * HDIM
PAIRS = HEADS // 2
BLK = 256
SLOTS = 64

highest = lax.Precision.HIGHEST
masked_score = -1e30
epsilon = 1e-06

MESH = pl.DeviceIdType.MESH
PART_LANES = (512, 384, 384)
PART_START = (0, 512, 896)
PART_ORDER = ((0, 1, 2), (1, 2, 0), (2, 0, 1))


def place():
    ctx = lax.axis_index("ctx")
    fsdp = lax.axis_index("fsdp")
    return ctx // 2, (ctx % 2) * 2 + fsdp // 8, (fsdp // 2) % 4, fsdp % 2


def device_at(x, z, y, core):
    return {"ctx": x * 2 + z // 2, "fsdp": (z % 2) * 8 + y * 2 + core}


def shifted(spot, axis, by):
    moved = list(spot)
    moved[axis] = (moved[axis] + by) % 4
    return tuple(moved)


def greet(devices):
    barrier = pltpu.get_barrier_semaphore()
    for device in devices:
        pl.semaphore_signal(barrier, inc=1, device_id=device, device_id_type=MESH)
    pl.semaphore_wait(barrier, len(devices))


def torus_peers(spot, core):
    peers = [device_at(*shifted(spot, axis, by), core) for axis in range(3) for by in (1, 2, 3)]
    return peers + [device_at(*spot, 1 - core)]


def sequence_peers(spot, core):
    x, z, y = spot
    return [device_at((x + by) % 4, (z + 2) % 4, y, core) for by in (1, 2, 3)]


def region(ref, spot, core, whole):
    return ref.at[
        tuple(slice(None) if axis in whole else spot[axis] for axis in range(3)) + (core,)
    ]


def gather_kernel(own_ref, tokens_ref, *refs):
    parts, blocks_ref = refs[:3], refs[3]
    net_send, net_recv, twin_send, twin_recv, own_sem, block_send, block_recv = refs[4:]
    ctx = lax.axis_index("ctx")
    *spot, core = place()
    spot = tuple(spot)
    twin = device_at(*spot, 1 - core)
    greet(torus_peers(spot, core) + sequence_peers(spot, core))

    def net(part, step, by, source, target):
        axis = PART_ORDER[part][step]
        return pltpu.make_async_remote_copy(
            src_ref=source,
            dst_ref=target,
            send_sem=net_send.at[part, step, by - 1],
            recv_sem=net_recv.at[part, step, by - 1],
            device_id=device_at(*shifted(spot, axis, by), core),
            device_id_type=MESH,
        )

    def share(part, slot, source, target):
        return pltpu.make_async_remote_copy(
            src_ref=source,
            dst_ref=target,
            send_sem=twin_send.at[part, slot],
            recv_sem=twin_recv.at[part, slot],
            device_id=twin,
            device_id_type=MESH,
        )

    def block(by, owner, target):
        return pltpu.make_async_remote_copy(
            src_ref=tokens_ref,
            dst_ref=blocks_ref.at[owner],
            send_sem=block_send.at[by - 1],
            recv_sem=block_recv.at[by - 1],
            device_id={"ctx": target, "fsdp": lax.axis_index("fsdp")},
            device_id_type=MESH,
        )

    started = []
    kept = []
    for part in range(3):
        own = own_ref.at[:, pl.ds(PART_START[part], PART_LANES[part])]
        mine = region(parts[part], spot, core, ())
        for by in (1, 2, 3):
            copy = net(part, 0, by, own, mine)
            copy.start()
            started.append(copy)
    for part in range(3):
        own = own_ref.at[:, pl.ds(PART_START[part], PART_LANES[part])]
        mine = region(parts[part], spot, core, ())
        copy = pltpu.make_async_copy(own, mine, own_sem.at[part])
        copy.start()
        kept.append(copy)
        copy = share(part, 0, own, mine)
        copy.start()
        started.append(copy)
    copy = pltpu.make_async_copy(tokens_ref, blocks_ref.at[ctx], own_sem.at[3])
    copy.start()
    kept.append(copy)
    for by in range(1, 8):

        @pl.when(ctx + by < 8)
        def _(by=by):
            block(by, ctx, ctx + by).start()

    for copy in kept:
        copy.wait()
    for step in range(3):
        for part in range(3):
            order = PART_ORDER[part]
            axis = order[step]
            whole = order[:step]
            for by in (1, 2, 3):
                came = region(parts[part], shifted(spot, axis, -by), core, whole)
                net(part, step, by, came, came).wait_recv()
                copy = share(part, 1 + step * 3 + by - 1, came, came)
                copy.start()
                started.append(copy)
            if step < 2:
                held = region(parts[part], spot, core, order[: step + 1])
                for by in (1, 2, 3):
                    copy = net(part, step + 1, by, held, held)
                    copy.start()
                    started.append(copy)
    for part in range(3):
        order = PART_ORDER[part]
        first = region(parts[part], spot, 1 - core, ())
        share(part, 0, first, first).wait_recv()
        for step in range(3):
            for by in (1, 2, 3):
                came = region(
                    parts[part], shifted(spot, order[step], -by), 1 - core, order[:step]
                )
                share(part, 1 + step * 3 + by - 1, came, came).wait_recv()
    for by in range(1, 8):

        @pl.when(ctx - by >= 0)
        def _(by=by):
            block(by, ctx - by, ctx).wait_recv()

        @pl.when(ctx + by < 8)
        def _(by=by):
            block(by, ctx, ctx + by).wait_send()

    for copy in started:
        copy.wait_send()


def gather_shards(own, tokens):
    return pl.pallas_call(
        gather_kernel,
        out_shape=[
            jax.ShapeDtypeStruct((4, 4, 4, 2, 16, lanes), jnp.bfloat16) for lanes in PART_LANES
        ]
        + [jax.ShapeDtypeStruct((8, BLK + 16, WIDTH), jnp.bfloat16)],
        in_specs=[pl.BlockSpec(memory_space=pltpu.VMEM)] * 2,
        out_specs=[pl.BlockSpec(memory_space=pl.ANY)] * 4,
        scratch_shapes=[
            pltpu.SemaphoreType.DMA((3, 3, 3)),
            pltpu.SemaphoreType.DMA((3, 3, 3)),
            pltpu.SemaphoreType.DMA((3, 10)),
            pltpu.SemaphoreType.DMA((3, 10)),
            pltpu.SemaphoreType.DMA((4,)),
            pltpu.SemaphoreType.DMA((7,)),
            pltpu.SemaphoreType.DMA((7,)),
        ],
        name="gather_shards",
        compiler_params=pltpu.CompilerParams(collective_id=1, has_side_effects=True),
    )(own, tokens)


def scatter_kernel(
    grads_ref, small_ref, others_ref, first_ref, state_grad_ref, tokens_ref, gain_ref,
    out_ref, total_ref, tokens_grad_ref, *refs
):
    *refs, total_first, block_in, block_send, block_recv = refs
    ctx = lax.axis_index("ctx")
    twin_in, held = refs[0:3], refs[3:6]
    in_one, in_two, in_three = refs[6:9], refs[9:12], refs[12:15]
    sum_one, sum_two = refs[15:18], refs[18:21]
    small_in, small_sum, net_send, net_recv, twin_send, twin_recv, small_send, small_recv = refs[21:]
    *spot, core = place()
    spot = tuple(spot)
    twin = device_at(*spot, 1 - core)
    greet(torus_peers(spot, core) + sequence_peers(spot, core))
    started = []

    def block(by, target):
        return pltpu.make_async_remote_copy(
            src_ref=others_ref.at[target],
            dst_ref=block_in.at[by - 1],
            send_sem=block_send.at[by - 1],
            recv_sem=block_recv.at[by - 1],
            device_id={"ctx": target, "fsdp": lax.axis_index("fsdp")},
            device_id_type=MESH,
        )

    for by in range(1, 8):

        @pl.when(ctx - by >= 0)
        def _(by=by):
            block(by, ctx - by).start()

    def net(part, step, by, source, target):
        axis = PART_ORDER[part][2 - step]
        return pltpu.make_async_remote_copy(
            src_ref=source,
            dst_ref=target,
            send_sem=net_send.at[part, step, by - 1],
            recv_sem=net_recv.at[part, step, by - 1],
            device_id=device_at(*shifted(spot, axis, by), core),
            device_id_type=MESH,
        )

    def share(part):
        lanes = pl.ds(PART_START[part], PART_LANES[part])
        return pltpu.make_async_remote_copy(
            src_ref=grads_ref.at[:, :, :, 1 - core, :, lanes],
            dst_ref=twin_in[part],
            send_sem=twin_send.at[part],
            recv_sem=twin_recv.at[part],
            device_id=twin,
            device_id_type=MESH,
        )

    def small(axis, by, source, slot):
        device = twin if axis == 3 else device_at(*shifted(spot, axis, by), core)
        return pltpu.make_async_remote_copy(
            src_ref=source,
            dst_ref=small_in.at[axis, slot],
            send_sem=small_send.at[axis, by - 1],
            recv_sem=small_recv.at[axis, by - 1],
            device_id=device,
            device_id_type=MESH,
        )

    for part in range(3):
        copy = share(part)
        copy.start()
        started.append(copy)
    copy = small(3, 1, small_ref, core)
    copy.start()
    started.append(copy)

    def add_pairs(part):
        start, lanes = PART_START[part], PART_LANES[part]

        def step(index, carry):
            x, z, y = index // 16, (index // 4) % 4, index % 4
            held[part][x, z, y] = (
                grads_ref[x, z, y, core, :, start : start + lanes].astype(jnp.float32)
                + twin_in[part][x, z, y].astype(jnp.float32)
            ).astype(jnp.bfloat16)
            return carry

        lax.fori_loop(0, 64, step, 0, unroll=2)

    def cut(spots, axis, at):
        return tuple(at if a == axis else slice(None) for a in spots)

    for part in range(3):
        share(part).wait_recv()
        add_pairs(part)
        axis = PART_ORDER[part][2]
        for by in (1, 2, 3):
            index = cut((0, 1, 2), axis, shifted(spot, axis, by)[axis])
            copy = net(part, 0, by, held[part].at[index], in_one[part].at[by - 1])
            copy.start()
            started.append(copy)

    small(3, 1, small_ref, 1 - core).wait_recv()
    small_in[3, core] = small_ref[...]
    small_sum[0] = small_in[3, 0] + small_in[3, 1]
    for by in (1, 2, 3):
        copy = small(0, by, small_sum.at[0], spot[0])
        copy.start()
        started.append(copy)

    def small_step(axis):
        for by in (1, 2, 3):
            small(axis, by, small_sum.at[axis], shifted(spot, axis, -by)[axis]).wait_recv()
        small_in[axis, spot[axis]] = small_sum[axis]
        total = small_in[axis, 0] + small_in[axis, 1] + small_in[axis, 2] + small_in[axis, 3]
        if axis == 2:
            total_ref[...] = total
            return
        small_sum[axis + 1] = total
        for by in (1, 2, 3):
            copy = small(axis + 1, by, small_sum.at[axis + 1], spot[axis + 1])
            copy.start()
            started.append(copy)

    for part in range(3):
        first, second, third = PART_ORDER[part]
        for by in (1, 2, 3):
            net(part, 0, by, in_one[part].at[by - 1], in_one[part].at[by - 1]).wait_recv()
        rest = tuple(a for a in (0, 1, 2) if a != third)

        def add_four(index, carry, part=part, third=third, rest=rest):
            at = {rest[0]: index // 4, rest[1]: index % 4, third: spot[third]}
            total = held[part][at[0], at[1], at[2]].astype(jnp.float32)
            for by in range(3):
                total = total + in_one[part][by, index // 4, index % 4].astype(jnp.float32)
            sum_one[part][index // 4, index % 4] = total.astype(jnp.bfloat16)
            return carry

        lax.fori_loop(0, 16, add_four, 0, unroll=2)
        for by in (1, 2, 3):
            at = shifted(spot, second, by)[second]
            source = sum_one[part].at[at] if second == rest[0] else sum_one[part].at[:, at]
            copy = net(part, 1, by, source, in_two[part].at[by - 1])
            copy.start()
            started.append(copy)
    small_step(0)
    for part in range(3):
        first, second, third = PART_ORDER[part]
        for by in (1, 2, 3):
            net(part, 1, by, in_two[part].at[by - 1], in_two[part].at[by - 1]).wait_recv()
        rest = tuple(a for a in (0, 1, 2) if a != third)
        for index in range(4):
            if second == rest[0]:
                total = sum_one[part][spot[second], index].astype(jnp.float32)
            else:
                total = sum_one[part][index, spot[second]].astype(jnp.float32)
            for by in range(3):
                total = total + in_two[part][by, index].astype(jnp.float32)
            sum_two[part][index] = total.astype(jnp.bfloat16)
        for by in (1, 2, 3):
            at = shifted(spot, first, by)[first]
            copy = net(part, 2, by, sum_two[part].at[at], in_three[part].at[by - 1])
            copy.start()
            started.append(copy)
    small_step(1)
    for part in range(3):
        first = PART_ORDER[part][0]
        for by in (1, 2, 3):
            net(part, 2, by, in_three[part].at[by - 1], in_three[part].at[by - 1]).wait_recv()
        total = sum_two[part][spot[first]].astype(jnp.float32)
        for by in range(3):
            total = total + in_three[part][by].astype(jnp.float32)
        out_ref[:, PART_START[part] : PART_START[part] + PART_LANES[part]] = total
    small_step(2)
    total_first[...] = first_ref[...]
    for by in range(1, 8):

        @pl.when(ctx + by < 8)
        def _(by=by):
            block(by, ctx).wait_recv()
            total_first[...] += block_in[by - 1].astype(jnp.float32)

        @pl.when(ctx - by >= 0)
        def _(by=by):
            block(by, ctx - by).wait_send()

    wide = tokens_ref[...].astype(jnp.float32)
    scale = rms_rows(wide)
    weighted = total_first[...] * gain_ref[...]
    tokens_grad_ref[...] = (
        state_grad_ref[...]
        + scale * weighted
        - wide * (scale**3 * jnp.mean(weighted * wide, axis=-1, keepdims=True))
    )
    for copy in started:
        copy.wait_send()


def scatter_shards(grads, small, others, first, state_grad, tokens, gain):
    by_part = lambda *lead: [pltpu.VMEM((*lead, 16, lanes), jnp.bfloat16) for lanes in PART_LANES]
    return pl.pallas_call(
        scatter_kernel,
        out_shape=[
            jax.ShapeDtypeStruct((16, 1280), jnp.float32),
            jax.ShapeDtypeStruct((16, 128), jnp.float32),
            jax.ShapeDtypeStruct((BLK, WIDTH), jnp.float32),
        ],
        in_specs=[pl.BlockSpec(memory_space=pltpu.VMEM)] * 2
        + [pl.BlockSpec(memory_space=pl.ANY)]
        + [pl.BlockSpec(memory_space=pltpu.VMEM)] * 4,
        out_specs=[pl.BlockSpec(memory_space=pltpu.VMEM)] * 3,
        scratch_shapes=[
            *by_part(4, 4, 4),
            *by_part(4, 4, 4),
            *by_part(3, 4, 4),
            *by_part(3, 4),
            *by_part(3),
            *by_part(4, 4),
            *by_part(4),
            pltpu.VMEM((4, 4, 16, 128), jnp.float32),
            pltpu.VMEM((3, 16, 128), jnp.float32),
            pltpu.SemaphoreType.DMA((3, 3, 3)),
            pltpu.SemaphoreType.DMA((3, 3, 3)),
            pltpu.SemaphoreType.DMA((3,)),
            pltpu.SemaphoreType.DMA((3,)),
            pltpu.SemaphoreType.DMA((4, 3)),
            pltpu.SemaphoreType.DMA((4, 3)),
            pltpu.VMEM((BLK, WIDTH), jnp.float32),
            pltpu.VMEM((7, BLK, WIDTH), jnp.bfloat16),
            pltpu.SemaphoreType.DMA((7,)),
            pltpu.SemaphoreType.DMA((7,)),
        ],
        name="scatter_shards",
        compiler_params=pltpu.CompilerParams(
            collective_id=2, has_side_effects=True, vmem_limit_bytes=40 * 2**20
        ),
    )(grads, small, others, first, state_grad, tokens, gain)


def placing_tables():
    left = np.zeros((192, 256), np.float32)
    right = np.zeros((192, 256), np.float32)
    small = np.zeros((48, 128), np.float32)
    for device in range(8):
        for weight in range(4):
            for row in range(6):
                at, line = weight * 48 + device * 6 + row, weight * 6 + row
                if line < 16:
                    left[at, device * 16 + line] = right[at, device * 16 + line] = 1
                else:
                    left[at, 128 + device * 16 + line - 16] = 1
                    right[at, 128 + device * 16 + line - 8] = 1
        for row in range(6):
            small[device * 6 + row, device * 16 + row] = 1
    return left, right, small


def unpack_kernel(a_ref, b_ref, c_ref, left_ref, right_ref, small_ref, weights_ref, smalls_ref):
    a, b, c = a_ref[0], b_ref[0], c_ref[0]
    tail = jnp.concatenate([b[:, 256:], c[:, :256]], axis=1)
    left = jnp.dot(
        left_ref[...],
        jnp.concatenate([a[:, :384], tail], axis=0),
        preferred_element_type=jnp.float32,
    )
    right = jnp.dot(
        right_ref[...],
        jnp.concatenate([jnp.concatenate([a[:, 384:], b[:, :256]], axis=1), tail], axis=0),
        preferred_element_type=jnp.float32,
    )
    for weight in range(4):
        rows = slice(weight * 48, weight * 48 + 48)
        weights_ref[weight, :, :384] = left[rows].astype(jnp.bfloat16)
        weights_ref[weight, :, 384:] = right[rows].astype(jnp.bfloat16)
    smalls_ref[...] = jnp.dot(
        small_ref[...], c[:, 256:], preferred_element_type=jnp.float32
    ).astype(jnp.bfloat16)


def unpack_shards(parts):
    left, right, small = (jnp.asarray(t, jnp.bfloat16) for t in placing_tables())
    whole = lambda t: pl.BlockSpec(t.shape, lambda g: (0, 0))
    return pl.pallas_call(
        unpack_kernel,
        grid=(16,),
        out_shape=[
            jax.ShapeDtypeStruct((4, WIDTH, WIDTH), jnp.bfloat16),
            jax.ShapeDtypeStruct((WIDTH, 128), jnp.bfloat16),
        ],
        in_specs=[
            *(pl.BlockSpec((1, 128, lanes), lambda g: (g, 0, 0)) for lanes in PART_LANES),
            whole(left),
            whole(right),
            whole(small),
        ],
        out_specs=[
            pl.BlockSpec((4, 48, WIDTH), lambda g: (0, g, 0)),
            pl.BlockSpec((48, 128), lambda g: (g, 0)),
        ],
        name="unpack_shards",
        compiler_params=pltpu.CompilerParams(vmem_limit_bytes=24 * 2**20),
    )(*(part.reshape(16, 128, -1) for part in parts), left, right, small)


def pack_kernel(weights_ref, smalls_ref, left_ref, right_ref, small_ref, out_ref):
    left = jnp.concatenate([weights_ref[w, :, :384] for w in range(4)], axis=0).astype(jnp.bfloat16)
    right = jnp.concatenate([weights_ref[w, :, 384:] for w in range(4)], axis=0).astype(jnp.bfloat16)
    from_left = jnp.dot(left_ref[...], left, preferred_element_type=jnp.float32)
    from_right = jnp.dot(right_ref[...], right, preferred_element_type=jnp.float32)
    out_ref[0, :, :384] = from_left[:128].astype(jnp.bfloat16)
    out_ref[0, :, 384:768] = from_right[:128].astype(jnp.bfloat16)
    out_ref[0, :, 768:1152] = (from_left[128:] + from_right[128:]).astype(jnp.bfloat16)
    out_ref[0, :, 1152:] = jnp.dot(
        small_ref[...], smalls_ref[...].astype(jnp.bfloat16), preferred_element_type=jnp.float32
    ).astype(jnp.bfloat16)


def pack_shards(weights, smalls):
    left, right, small = (jnp.asarray(t.T, jnp.bfloat16) for t in placing_tables())
    whole = lambda t: pl.BlockSpec(t.shape, lambda g: (0, 0))
    return pl.pallas_call(
        pack_kernel,
        grid=(16,),
        out_shape=jax.ShapeDtypeStruct((16, 128, 1280), jnp.bfloat16),
        in_specs=[
            pl.BlockSpec((4, 48, WIDTH), lambda g: (0, g, 0)),
            pl.BlockSpec((48, 128), lambda g: (g, 0)),
            whole(left),
            whole(right),
            whole(small),
        ],
        out_specs=pl.BlockSpec((1, 128, 1280), lambda g: (g, 0, 0)),
        name="pack_shards",
        compiler_params=pltpu.CompilerParams(vmem_limit_bytes=24 * 2**20),
    )(weights, smalls, left, right, small).reshape(4, 4, 4, 2, 16, 1280)


def pack_own(weights, smalls):
    rows = jnp.concatenate(weights, axis=0)
    tail = jnp.concatenate([rows[16:, :384], rows[16:, 384:]], axis=0)
    small = jnp.pad(jnp.concatenate(smalls, axis=1), ((0, 10), (0, 108)))
    return jnp.concatenate([rows[:16], tail, small], axis=1)


def unpack_own(packed):
    tail = jnp.concatenate([packed[:8, 768:1152], packed[8:, 768:1152]], axis=1)
    rows = jnp.concatenate([packed[:16, :768], tail], axis=0)
    small = packed[:6, 1152:]
    return [rows[i * 6 : i * 6 + 6] for i in range(4)], small


def rope_tables():
    frequency = 10000.0 ** (-2.0 * (np.arange(128) % 32) / HDIM)
    inner = np.arange(BLK)[:, None] * frequency
    outer = (np.arange(8) * BLK)[:, None] * frequency
    return [jnp.asarray(t, jnp.float32) for t in (np.cos(inner), np.sin(inner), np.cos(outer), np.sin(outer))]


def turning(index, tables):
    cos_in, sin_in, cos_out, sin_out = tables
    ca, sa = cos_out[pl.ds(index, 1), :], sin_out[pl.ds(index, 1), :]
    cb, sb = cos_in[...], sin_in[...]
    lower = lax.broadcasted_iota(jnp.int32, (BLK, 128), 1) % HDIM < HDIM // 2
    sine = sa * cb + ca * sb
    return ca * cb - sa * sb, jnp.where(lower, -sine, sine)


def swapped(values):
    lower = lax.broadcasted_iota(jnp.int32, values.shape, 1) % HDIM < HDIM // 2
    return jnp.where(lower, pltpu.roll(values, 96, 1), pltpu.roll(values, 32, 1))


def dot(left, right):
    return jnp.dot(left, right, preferred_element_type=jnp.float32)


def dot_nt(left, right):
    return lax.dot_general(left, right, (((1,), (1,)), ((), ())), preferred_element_type=jnp.float32)


def column(row):
    return jnp.broadcast_to(row, (128, row.shape[1])).T[:, 0:1]


def blocks_back(segs_ref, ctx):
    first = segs_ref[ctx, 0]
    count = jnp.int32(0)
    for index in range(8):
        count = count + jnp.where((index < ctx) & (segs_ref[index, BLK - 1] == first), 1, 0)
    return count


def mask_bias(segments_ref, bias_ref, ctx, index):
    key_seg = column(segments_ref[pl.ds(index, 1), :])
    query_seg = segments_ref[pl.ds(ctx, 1), :]
    key_pos = lax.broadcasted_iota(jnp.int32, (BLK, BLK), 0)
    query_pos = lax.broadcasted_iota(jnp.int32, (BLK, BLK), 1)
    reach = jnp.where(index == ctx, 0, BLK)
    allowed = (key_seg == query_seg) & (key_pos <= query_pos + reach)
    bias_ref[...] = jnp.where(allowed, 0.0, masked_score)


def rms_rows(values):
    return lax.rsqrt(jnp.mean(values * values, axis=-1, keepdims=True) + epsilon)


def pick(onehot, values):
    return jnp.sum(jnp.where(onehot, values, 0.0), axis=1, keepdims=True)


def lane_is(lanes):
    return lax.broadcasted_iota(jnp.int32, (BLK, 128), 1) == lanes


def forward_kernel(
    segs_ref, segments_ref, tok_ref, w_ref, small_ref, cos_in, sin_in, cos_out, sin_out,
    prev_ref, wres_ref, routes_ref, rank_ref, cot_ref,
    state_ref, normed_ref, att_ref, lse_ref, q_ref, keys_ref, values_ref, rows_ref, grads_ref,
    info_ref, proj_ref,
    qt_ref, vt_ref, bias_ref, max_ref, sum_ref, acc_ref,
):
    tables = (cos_in, sin_in, cos_out, sin_out)
    ctx = lax.axis_index("ctx")
    back = blocks_back(segs_ref, ctx)
    across = small_ref[...].astype(jnp.float32).T
    gain_one, gain_two = across[18:19], across[19:20]

    def normed_block(index):
        wide = tok_ref[index, :BLK].astype(jnp.float32)
        return (wide * rms_rows(wide) * gain_one).astype(jnp.bfloat16)

    query = dot(normed_block(ctx), w_ref[0])
    cosine, sine = turning(ctx, tables)
    for pair in range(PAIRS):
        part = query[:, pair * 128 : pair * 128 + 128]
        turned = (part * cosine + swapped(part) * sine) * (HDIM**-0.5)
        q_ref[pair] = turned.astype(jnp.bfloat16)
        across_q = turned.T.astype(jnp.bfloat16)
        blank = jnp.zeros((HDIM, BLK), jnp.bfloat16)
        qt_ref[2 * pair] = jnp.concatenate([across_q[:HDIM], blank], axis=0)
        qt_ref[2 * pair + 1] = jnp.concatenate([blank, across_q[HDIM:]], axis=0)
    max_ref[...] = jnp.full(max_ref.shape, masked_score, jnp.float32)
    sum_ref[...] = jnp.zeros_like(sum_ref)
    acc_ref[...] = jnp.zeros_like(acc_ref)

    def block(step, carry):
        index = ctx - step
        normed = normed_block(index)
        key = dot(normed, w_ref[1])
        value = dot(normed, w_ref[2])
        cosine, sine = turning(index, tables)
        for pair in range(PAIRS):
            lanes = slice(pair * 128, pair * 128 + 128)
            part = key[:, lanes]
            keys_ref[index, pair] = (part * cosine + swapped(part) * sine).astype(jnp.bfloat16)
            values_ref[index, pair] = value[:, lanes].astype(jnp.bfloat16)
            vt_ref[lanes, :] = value[:, lanes].T.astype(jnp.bfloat16)
        mask_bias(segments_ref, bias_ref, ctx, index)
        for head in range(HEADS):
            rows = slice(head * HDIM, head * HDIM + HDIM)
            scores = dot(keys_ref[index, head // 2], qt_ref[head]) + bias_ref[...]
            before = max_ref[head : head + 1]
            top = jnp.maximum(before, jnp.max(scores, axis=0, keepdims=True))
            weights = jnp.exp(scores - top)
            shrink = jnp.exp(before - top)
            sum_ref[head : head + 1] = sum_ref[head : head + 1] * shrink + jnp.sum(
                weights, axis=0, keepdims=True
            )
            max_ref[head : head + 1] = top
            acc_ref[rows] = acc_ref[rows] * shrink + dot(vt_ref[rows, :], weights.astype(jnp.bfloat16))
        return carry

    lax.fori_loop(0, back + 1, block, 0)
    for head in range(HEADS):
        rows = slice(head * HDIM, head * HDIM + HDIM)
        att_ref[rows] = acc_ref[rows] / sum_ref[head : head + 1]
    lse_ref[...] = max_ref[...] + jnp.log(jnp.maximum(sum_ref[...], 1e-30))
    attended = att_ref[...].T.astype(jnp.bfloat16)
    state = tok_ref[ctx, :BLK].astype(jnp.float32) + dot(attended, w_ref[3])
    state_ref[...] = state
    normed_two = (state * rms_rows(state) * gain_two).astype(jnp.bfloat16)
    normed_ref[...] = normed_two

    proj = dot(normed_two, small_ref[...])
    proj_ref[...] = proj
    logits = proj + jnp.dot(
        prev_ref[...], wres_ref[...], precision=highest, preferred_element_type=jnp.float32
    )
    lanes = lax.broadcasted_iota(jnp.int32, (BLK, 128), 1)
    route_0, route_1 = routes_ref[:, 0:1], routes_ref[:, 1:2]
    hot_0, hot_1 = lanes == route_0, lanes == route_1
    chosen_0, chosen_1 = pick(hot_0, logits), pick(hot_1, logits)
    top = jnp.maximum(chosen_0, chosen_1)
    chosen_0, chosen_1 = jnp.exp(chosen_0 - top), jnp.exp(chosen_1 - top)
    gate_0, gate_1 = chosen_0 / (chosen_0 + chosen_1), chosen_1 / (chosen_0 + chosen_1)
    rank = rank_ref[...]
    earlier = (rank < column(rank)).astype(jnp.float32).astype(jnp.bfloat16)
    slots = dot(earlier, (hot_0 | hot_1).astype(jnp.float32).astype(jnp.bfloat16))

    def target(route, hot):
        slot = pick(hot, slots)
        return jnp.where(
            (route < EXPERTS) & (slot < CAP), route.astype(jnp.float32) * SLOTS + slot, -1.0
        )

    target_0, target_1 = target(route_0, hot_0), target(route_1, hot_1)
    info = jnp.where(lanes == 0, gate_0, 0.0) + jnp.where(lanes == 1, gate_1, 0.0)
    info = info + jnp.where(lanes == 2, target_0, 0.0) + jnp.where(lanes == 3, target_1, 0.0)
    info_ref[...] = info
    targets = info.T
    rows = lax.broadcasted_iota(jnp.int32, (EXPERTS * SLOTS, BLK), 0).astype(jnp.float32)
    table_0 = (rows == targets[2:3]).astype(jnp.float32).astype(jnp.bfloat16)
    table_1 = (rows == targets[3:4]).astype(jnp.float32).astype(jnp.bfloat16)
    rows_ref[...] = dot(table_0 + table_1, normed_two).astype(jnp.bfloat16)
    upstream = cot_ref[...].astype(jnp.float32)
    grads_ref[...] = dot(
        jnp.concatenate([table_0, table_1], axis=1),
        jnp.concatenate([gate_0 * upstream, gate_1 * upstream], axis=0).astype(jnp.bfloat16),
    ).astype(jnp.bfloat16)


def attend(segs, segments, tok, weights, smalls, prev, wres, routes, rank, cot):
    vmem = pl.BlockSpec(memory_space=pltpu.VMEM)
    shape = jax.ShapeDtypeStruct
    low, wide = jnp.bfloat16, jnp.float32
    return pl.pallas_call(
        forward_kernel,
        out_shape=[
            shape((BLK, WIDTH), wide),
            shape((BLK, WIDTH), low),
            shape((WIDTH, BLK), wide),
            shape((16, BLK), wide),
            shape((PAIRS, BLK, 128), low),
            shape((8, PAIRS, BLK, 128), low),
            shape((8, PAIRS, BLK, 128), low),
            shape((EXPERTS * SLOTS, WIDTH), low),
            shape((EXPERTS * SLOTS, WIDTH), low),
            shape((BLK, 128), wide),
            shape((BLK, 128), wide),
        ],
        in_specs=[pl.BlockSpec(memory_space=pltpu.SMEM)] + [vmem] * 13,
        out_specs=[vmem] * 11,
        scratch_shapes=[
            pltpu.VMEM((HEADS, 128, BLK), low),
            pltpu.VMEM((WIDTH, BLK), low),
            pltpu.VMEM((BLK, BLK), wide),
            pltpu.VMEM((16, BLK), wide),
            pltpu.VMEM((16, BLK), wide),
            pltpu.VMEM((WIDTH, BLK), wide),
        ],
        name="attend",
        compiler_params=pltpu.CompilerParams(vmem_limit_bytes=48 * 2**20),
        cost_estimate=pl.CostEstimate(flops=3 * 10**10, bytes_accessed=10**7, transcendentals=10**6),
    )(segs, segments, tok, weights, smalls, *rope_tables(), prev, wres, routes, rank, cot)


def split(values):
    high = values.astype(jnp.bfloat16)
    low = (values - high.astype(jnp.float32)).astype(jnp.bfloat16)
    return jnp.concatenate([high, low], axis=1)


def backward_kernel(
    segs_ref, segments_ref, tok_ref, w_ref, small_ref, cos_in, sin_in, cos_out, sin_out,
    prev_ref, wres_ref, routes_ref, cot_ref,
    state_ref, normed_ref, att_ref, lse_ref, q_ref, keys_ref, values_ref, info_ref, proj_ref,
    back_rows_ref, back_grads_ref,
    out_ref, prev_grad_ref, res_grad_ref, dw_ref, dsmall_ref, others_ref, own_ref, state_grad_ref,
    qt_ref, ot_ref, o_ref, qm_ref, bias_ref, inner_ref, dqt_ref, gain_ref, dk_ref, dv_ref,
):
    tables = (cos_in, sin_in, cos_out, sin_out)
    ctx = lax.axis_index("ctx")
    back = blocks_back(segs_ref, ctx)
    across = small_ref[...].astype(jnp.float32).T
    gain_one, gain_two = across[18:19], across[19:20]
    value_rows = across[16:18]

    lanes = lax.broadcasted_iota(jnp.int32, (BLK, 128), 1)
    info = info_ref[...]
    gates = (info[:, 0:1], info[:, 1:2])
    slots = lax.broadcasted_iota(jnp.int32, (BLK, EXPERTS * SLOTS), 1).astype(jnp.float32)
    tables_of = [
        (slots == info[:, 2 + k : 3 + k]).astype(jnp.float32).astype(jnp.bfloat16) for k in (0, 1)
    ]
    routes = (routes_ref[:, 0:1], routes_ref[:, 1:2])
    hots = [lanes == routes[k] for k in (0, 1)]
    named = [
        [(routes[k] == EXPERTS + 1 + kind).astype(jnp.float32) for kind in range(3)] for k in (0, 1)
    ]
    proj = proj_ref[...]
    mixes = []
    for c in (0, 1):
        first, second = proj[:, 12 + 2 * c : 13 + 2 * c], proj[:, 13 + 2 * c : 14 + 2 * c]
        top = jnp.maximum(first, second)
        first, second = jnp.exp(first - top), jnp.exp(second - top)
        mixes.append((first / (first + second), second / (first + second)))
    normed_low = normed_ref[...]
    normed_two = normed_low.astype(jnp.float32)
    upstream_low = cot_ref[...]
    upstream = upstream_low.astype(jnp.float32)
    state = state_ref[...]
    back_rows = back_rows_ref[...]
    result = state
    gate_grads = []
    for k in (0, 1):
        copy, one, two = named[k]
        pair = dot(tables_of[k], back_rows)
        pair = pair + (copy + one * mixes[0][0] + two * mixes[1][0]) * normed_two
        pair = pair + (one * mixes[0][1]) * value_rows[0:1] + (two * mixes[1][1]) * value_rows[1:2]
        result = result + gates[k] * pair
        gate_grads.append(jnp.sum(pair * upstream, axis=1, keepdims=True))
    out_ref[...] = result.astype(jnp.bfloat16)
    inner = gates[0] * gate_grads[0] + gates[1] * gate_grads[1]
    logit_grad = jnp.zeros((BLK, 128), jnp.float32)
    for k in (0, 1):
        logit_grad = logit_grad + jnp.where(hots[k], gates[k] * (gate_grads[k] - inner), 0.0)
    prev_grad_ref[...] = lax.dot_general(
        logit_grad, wres_ref[...], (((1,), (1,)), ((), ())),
        precision=highest, preferred_element_type=jnp.float32,
    )
    res_grad_ref[...] = jnp.dot(
        prev_ref[...].T, logit_grad, precision=highest, preferred_element_type=jnp.float32
    )[:16]
    on_normed = jnp.sum(normed_two * upstream, axis=1, keepdims=True)
    on_vectors = dot(upstream_low, small_ref[...])
    flat = logit_grad
    weight_up = gates[0] * named[0][0] + gates[1] * named[1][0]
    vector_weights = jnp.zeros((BLK, 128), jnp.float32)
    for c in (0, 1):
        scale = gates[0] * named[0][1 + c] + gates[1] * named[1][1 + c]
        mix_0, mix_1 = mixes[c]
        m_0, m_1 = scale * on_normed, scale * on_vectors[:, 16 + c : 17 + c]
        mean = mix_0 * m_0 + mix_1 * m_1
        flat = flat + jnp.where(lanes == 12 + 2 * c, mix_0 * (m_0 - mean), 0.0)
        flat = flat + jnp.where(lanes == 13 + 2 * c, mix_1 * (m_1 - mean), 0.0)
        weight_up = weight_up + mix_0 * scale
        vector_weights = vector_weights + jnp.where(lanes == 16 + c, mix_1 * scale, 0.0)
    flat_split = split(flat)
    normed_grad = dot_nt(flat_split, jnp.concatenate([small_ref[...]] * 2, axis=1))
    normed_grad = normed_grad + weight_up * upstream
    normed_grad = normed_grad + dot(tables_of[0] + tables_of[1], back_grads_ref[...])
    normed_across = normed_two.T.astype(jnp.bfloat16)
    upstream_across = upstream.T.astype(jnp.bfloat16)
    small_grad = dot(normed_across, flat_split)
    small_vector = dot(upstream_across, split(vector_weights))
    small_grad = small_grad[:, :128] + small_grad[:, 128:] + small_vector[:, :128] + small_vector[:, 128:]
    scale_two = rms_rows(state)
    weighted = normed_grad * gain_two
    state_grad = (
        upstream
        + scale_two * weighted
        - state * (scale_two**3 * jnp.mean(weighted * state, axis=-1, keepdims=True))
    )
    state_grad_ref[...] = state_grad
    gain_two_row = jnp.sum(normed_grad * state * scale_two, axis=0, keepdims=True)
    state_low = state_grad.astype(jnp.bfloat16)
    attended = att_ref[...]
    dw_ref[3] = dot(attended.astype(jnp.bfloat16), state_low)
    att_grad = dot_nt(state_low, w_ref[3])
    blank = jnp.zeros((HDIM, BLK), jnp.bfloat16)
    low_half = lax.broadcasted_iota(jnp.int32, (BLK, 128), 1) < HDIM
    none = jnp.zeros((BLK, 128), jnp.bfloat16)
    inner_ref[...] = jnp.zeros_like(inner_ref)
    for pair in range(PAIRS):
        part = att_grad[:, pair * 128 : pair * 128 + 128].astype(jnp.bfloat16)
        across_o = part.astype(jnp.float32).T
        products = across_o * attended[pair * 128 : pair * 128 + 128]
        across_o = across_o.astype(jnp.bfloat16)
        across_q = q_ref[pair].astype(jnp.float32).T.astype(jnp.bfloat16)
        for half in (0, 1):
            head = 2 * pair + half
            rows = slice(half * HDIM, half * HDIM + HDIM)
            inner_ref[head : head + 1] = jnp.sum(products[rows], axis=0, keepdims=True)
            order = (lambda a, b: [a, b]) if half == 0 else (lambda a, b: [b, a])
            ot_ref[head] = jnp.concatenate(order(across_o[rows], blank), axis=0)
            qt_ref[head] = jnp.concatenate(order(across_q[rows], blank), axis=0)
        o_ref[pair, :BLK] = jnp.where(low_half, part, none)
        o_ref[pair, BLK:] = jnp.where(low_half, none, part)
        qm_ref[pair, :BLK] = jnp.where(low_half, q_ref[pair], none)
        qm_ref[pair, BLK:] = jnp.where(low_half, none, q_ref[pair])
    dqt_ref[...] = jnp.zeros_like(dqt_ref)
    dw_ref[1] = jnp.zeros((WIDTH, WIDTH), jnp.float32)
    dw_ref[2] = jnp.zeros((WIDTH, WIDTH), jnp.float32)
    gain_ref[...] = jnp.zeros_like(gain_ref)

    def normed_block(index):
        wide = tok_ref[index, :BLK].astype(jnp.float32)
        scaled = wide * rms_rows(wide)
        return scaled, (scaled * gain_one).T.astype(jnp.bfloat16)

    def block(step, carry):
        index = ctx - step
        mask_bias(segments_ref, bias_ref, ctx, index)
        cosine, sine = turning(index, tables)
        for pair in range(PAIRS):
            key, value = keys_ref[index, pair], values_ref[index, pair]
            key_across = key.astype(jnp.float32).T.astype(jnp.bfloat16)
            weights, score_grads = [], []
            for half in (0, 1):
                head = 2 * pair + half
                scores = dot(key, qt_ref[head]) + bias_ref[...]
                weight = jnp.exp(scores - lse_ref[head : head + 1])
                weight_grad = dot(value, ot_ref[head])
                score_grad = (weight * (weight_grad - inner_ref[head : head + 1])).astype(jnp.bfloat16)
                weights.append(weight.astype(jnp.bfloat16))
                score_grads.append(score_grad)
                rows = slice(head * HDIM, head * HDIM + HDIM)
                dqt_ref[rows] += dot(key_across[half * HDIM : half * HDIM + HDIM], score_grad)
            lanes = slice(pair * 128, pair * 128 + 128)
            dv_ref[:, lanes] = dot(jnp.concatenate(weights, axis=1), o_ref[pair]).astype(jnp.bfloat16)
            dk = dot(jnp.concatenate(score_grads, axis=1), qm_ref[pair])
            dk_ref[:, lanes] = (dk * cosine - swapped(dk) * sine).astype(jnp.bfloat16)
        scaled, normed_across = normed_block(index)
        dw_ref[1] += dot(normed_across, dk_ref[...])
        dw_ref[2] += dot(normed_across, dv_ref[...])
        first = dot_nt(dk_ref[...], w_ref[1]) + dot_nt(dv_ref[...], w_ref[2])
        gain_ref[...] += jnp.sum(first * scaled, axis=0, keepdims=True)
        others_ref[index] = first.astype(jnp.bfloat16)

        @pl.when(step == 0)
        def _():
            own_ref[...] = first

        return carry

    lax.fori_loop(0, back + 1, block, 0)

    def clear(index, carry):
        others_ref[index] = jnp.zeros((BLK, WIDTH), jnp.bfloat16)
        return carry

    lax.fori_loop(0, ctx - back, clear, 0)
    cosine, sine = turning(ctx, tables)
    for pair in range(PAIRS):
        lanes = slice(pair * 128, pair * 128 + 128)
        dq = dqt_ref[lanes, :].T * (HDIM**-0.5)
        dk_ref[:, lanes] = (dq * cosine - swapped(dq) * sine).astype(jnp.bfloat16)
    scaled, normed_across = normed_block(ctx)
    dw_ref[0] = dot(normed_across, dk_ref[...])
    first = dot_nt(dk_ref[...], w_ref[0])
    own_ref[...] += first
    gain_one_row = gain_ref[...] + jnp.sum(first * scaled, axis=0, keepdims=True)
    lanes = lax.broadcasted_iota(jnp.int32, (WIDTH, 128), 1)
    ones = jnp.broadcast_to(gain_one_row, (128, WIDTH)).T
    twos = jnp.broadcast_to(gain_two_row, (128, WIDTH)).T
    dsmall_ref[...] = jnp.where(lanes == 18, ones, jnp.where(lanes == 19, twos, small_grad))


def unattend(segs, segments, tok, weights, smalls, prev, wres, routes, cot, kept, back_rows, back_grads):
    vmem = pl.BlockSpec(memory_space=pltpu.VMEM)
    shape = jax.ShapeDtypeStruct
    low, wide = jnp.bfloat16, jnp.float32
    state, normed, att, lse, q, keys, values, info, proj = kept
    return pl.pallas_call(
        backward_kernel,
        out_shape=[
            shape((BLK, WIDTH), low),
            shape((BLK, 128), wide),
            shape((16, 128), wide),
            shape((4, WIDTH, WIDTH), wide),
            shape((WIDTH, 128), wide),
            shape((8, BLK, WIDTH), low),
            shape((BLK, WIDTH), wide),
            shape((BLK, WIDTH), wide),
        ],
        in_specs=[pl.BlockSpec(memory_space=pltpu.SMEM)] + [vmem] * 23,
        out_specs=[vmem] * 8,
        scratch_shapes=[
            pltpu.VMEM((HEADS, 128, BLK), low),
            pltpu.VMEM((HEADS, 128, BLK), low),
            pltpu.VMEM((PAIRS, 2 * BLK, 128), low),
            pltpu.VMEM((PAIRS, 2 * BLK, 128), low),
            pltpu.VMEM((BLK, BLK), wide),
            pltpu.VMEM((16, BLK), wide),
            pltpu.VMEM((WIDTH, BLK), wide),
            pltpu.VMEM((1, WIDTH), wide),
            pltpu.VMEM((BLK, WIDTH), low),
            pltpu.VMEM((BLK, WIDTH), low),
        ],
        name="unattend",
        compiler_params=pltpu.CompilerParams(vmem_limit_bytes=56 * 2**20),
        cost_estimate=pl.CostEstimate(flops=4 * 10**10, bytes_accessed=10**7, transcendentals=10**6),
    )(
        segs, segments, tok, weights, smalls, *rope_tables(), prev, wres, routes, cot,
        state, normed, att, lse, q, keys, values, info, proj, back_rows, back_grads,
    )


def dot_tn(left, right):
    return lax.dot_general(left, right, (((0,), (0,)), ((), ())), preferred_element_type=jnp.float32)


def experts_kernel(
    rows_ref, grads_ref, gate_up_ref, down_ref,
    back_rows_ref, back_grads_ref, d_gate_up_ref, d_down_ref,
    gate_w, up_w, down_w, x_ref, g_ref, gate_ref, up_ref, hidden_ref, d_gate, d_up,
    mine_ref, twin_out, twin_in, sums_ref,
    load_sem, send_sem, recv_sem, share_send, share_recv, half_send, half_recv, ret_send, ret_recv,
    own_sem,
):
    ctx, fsdp = lax.axis_index("ctx"), lax.axis_index("fsdp")
    chip, core = fsdp // 2, fsdp % 2
    other = 1 - core
    half = EXPERTS * SLOTS

    def at(where, on):
        return {"ctx": ctx, "fsdp": where * 2 + on}

    greet([at((chip + by) % EXPERTS, core) for by in range(1, EXPERTS)] + [at(chip, other)])
    loads = []
    for index in range(8):
        for source, target, size in (
            (gate_up_ref.at[index, :96], gate_w, 96),
            (gate_up_ref.at[index, 96:], up_w, 96),
            (down_ref.at[index], down_w, 128),
        ):
            copy = pltpu.make_async_copy(
                source, target.at[pl.ds(index * size, size)], load_sem.at[len(loads)]
            )
            loads.append(copy)

    def slots(index, on):
        return pl.ds(pl.multiple_of((on * EXPERTS + index) * SLOTS, SLOTS), SLOTS)

    def chunk(index):
        return pl.ds(pl.multiple_of(index * SLOTS, SLOTS), SLOTS)

    buffers = ((rows_ref, x_ref), (grads_ref, g_ref))

    def dispatch(kind, by):
        source, target = buffers[kind]
        where = (chip + by) % EXPERTS
        return pltpu.make_async_remote_copy(
            src_ref=source.at[chunk(where)],
            dst_ref=target.at[slots(chip, core)],
            send_sem=send_sem.at[kind, by - 1],
            recv_sem=recv_sem.at[kind, by - 1],
            device_id=at(where, core),
            device_id_type=MESH,
        )

    def share(kind, by, on):
        source, target = buffers[kind]
        spot = slots((chip - by) % EXPERTS, on)
        return pltpu.make_async_remote_copy(
            src_ref=target.at[spot],
            dst_ref=target.at[spot],
            send_sem=share_send.at[kind, by],
            recv_sem=share_recv.at[kind, by],
            device_id=at(chip, other),
            device_id_type=MESH,
        )

    def exchange(kind):
        return pltpu.make_async_remote_copy(
            src_ref=twin_out.at[kind],
            dst_ref=twin_in.at[kind],
            send_sem=half_send.at[kind],
            recv_sem=half_recv.at[kind],
            device_id=at(chip, other),
            device_id_type=MESH,
        )

    returned = (back_rows_ref, back_grads_ref)

    def give_back(kind, by):
        where = (chip + by) % EXPERTS
        return pltpu.make_async_remote_copy(
            src_ref=sums_ref.at[kind, chunk(where)],
            dst_ref=returned[kind].at[chunk(chip)],
            send_sem=ret_send.at[kind, by - 1],
            recv_sem=ret_recv.at[kind, by - 1],
            device_id=at(where, core),
            device_id_type=MESH,
        )

    started = []
    for kind in (0, 1):
        for by in range(1, EXPERTS):
            copy = dispatch(kind, by)
            copy.start()
            started.append(copy)
    for copy in loads:
        copy.start()
    for kind in (0, 1):
        source, target = buffers[kind]
        copy = pltpu.make_async_copy(
            source.at[chunk(chip)], target.at[slots(chip, core)], own_sem.at[kind]
        )
        copy.start()
        copy.wait()
        copy = share(kind, 0, core)
        copy.start()
        started.append(copy)

    def arrive(kind):
        for by in range(1, EXPERTS):
            dispatch(kind, by).wait_recv()
            copy = share(kind, by, core)
            copy.start()
            started.append(copy)

    def arrive_shared(kind):
        for by in range(EXPERTS):
            share(kind, by, other).wait_recv()

    def tiles(on, body):
        def step(index, carry):
            start = pl.multiple_of(on * half + index * 256, 256)
            body(pl.ds(start, 256), pl.ds(pl.multiple_of(index * 256, 256), 256))
            return carry

        lax.fori_loop(0, half // 256, step, 0)

    def forward(on, keep):
        def tile(rows, inner):
            x = x_ref[rows]
            gate, up = dot(x, gate_w[...]), dot(x, up_w[...])
            gate_ref[rows], up_ref[rows] = gate, up
            hidden = (gate * jax.nn.sigmoid(gate) * up).astype(jnp.bfloat16)
            hidden_ref[rows] = hidden
            keep(inner, dot(hidden, down_w[...]))

        tiles(on, tile)

    def backward(on, keep):
        def tile(rows, inner):
            hidden_grad = dot_nt(g_ref[rows], down_w[...])
            gate, up = gate_ref[rows], up_ref[rows]
            sigmoid = jax.nn.sigmoid(gate)
            d_gate[rows] = (
                hidden_grad * up * sigmoid * (1.0 + gate * (1.0 - sigmoid))
            ).astype(jnp.bfloat16)
            d_up[rows] = (hidden_grad * gate * sigmoid).astype(jnp.bfloat16)
            keep(inner, dot_nt(d_gate[rows], gate_w[...]) + dot_nt(d_up[rows], up_w[...]))

        tiles(on, tile)

    def keep_mine(kind):
        def keep(rows, values):
            mine_ref[kind, rows] = values

        return keep

    def keep_twin(kind):
        def keep(rows, values):
            twin_out[kind, rows] = values.astype(jnp.bfloat16)

        return keep

    def finish(kind):
        exchange(kind).wait_recv()

        def step(index, carry):
            rows = pl.ds(pl.multiple_of(index * 128, 128), 128)
            sums_ref[kind, rows] = (
                mine_ref[kind, rows] + twin_in[kind, rows].astype(jnp.float32)
            ).astype(jnp.bfloat16)
            return carry

        lax.fori_loop(0, half // 128, step, 0)
        for by in range(1, EXPERTS):
            copy = give_back(kind, by)
            copy.start()
            started.append(copy)
        copy = pltpu.make_async_copy(
            sums_ref.at[kind, chunk(chip)], returned[kind].at[chunk(chip)], own_sem.at[kind]
        )
        copy.start()
        copy.wait()

    arrive(0)
    for copy in loads:
        copy.wait()
    forward(core, keep_mine(0))
    arrive(1)
    arrive_shared(0)
    forward(other, keep_twin(0))
    copy = exchange(0)
    copy.start()
    started.append(copy)
    backward(core, keep_mine(1))
    finish(0)
    arrive_shared(1)
    backward(other, keep_twin(1))
    copy = exchange(1)
    copy.start()
    started.append(copy)

    def down_tile(index, carry):
        lanes = pl.ds(pl.multiple_of(index * 256, 256), 256)
        part = dot_tn(hidden_ref[:, lanes], g_ref[...]).astype(jnp.bfloat16)
        d_down_ref[2 * index] = part[:128]
        d_down_ref[2 * index + 1] = part[128:]
        return carry

    lax.fori_loop(0, 4, down_tile, 0)
    finish(1)

    def gate_tile(index, carry):
        lanes = pl.ds(pl.multiple_of(index * 256, 256), 256)
        for start, grad in ((0, d_gate), (96, d_up)):
            part = dot_tn(x_ref[...], grad[:, lanes]).astype(jnp.bfloat16)
            for piece in range(8):
                d_gate_up_ref[piece, start : start + 96, lanes] = part[piece * 96 : piece * 96 + 96]
        return carry

    lax.fori_loop(0, 4, gate_tile, 0)
    for kind in (0, 1):
        for by in range(1, EXPERTS):
            give_back(kind, by).wait_recv()
    for copy in started:
        copy.wait_send()


def run_experts(rows, grads, gate_up, down):
    vmem, anywhere = pl.BlockSpec(memory_space=pltpu.VMEM), pl.BlockSpec(memory_space=pl.ANY)
    low, wide = jnp.bfloat16, jnp.float32
    half, whole = EXPERTS * SLOTS, 2 * EXPERTS * SLOTS
    dma = pltpu.SemaphoreType.DMA
    return pl.pallas_call(
        experts_kernel,
        out_shape=[
            jax.ShapeDtypeStruct((half, WIDTH), low),
            jax.ShapeDtypeStruct((half, WIDTH), low),
            jax.ShapeDtypeStruct((8, 192, 1024), low),
            jax.ShapeDtypeStruct((8, 128, WIDTH), low),
        ],
        in_specs=[vmem, vmem, anywhere, anywhere],
        out_specs=[vmem] * 4,
        scratch_shapes=[
            pltpu.VMEM((WIDTH, 1024), low),
            pltpu.VMEM((WIDTH, 1024), low),
            pltpu.VMEM((1024, WIDTH), low),
            pltpu.VMEM((whole, WIDTH), low),
            pltpu.VMEM((whole, WIDTH), low),
            pltpu.VMEM((whole, 1024), wide),
            pltpu.VMEM((whole, 1024), wide),
            pltpu.VMEM((whole, 1024), low),
            pltpu.VMEM((whole, 1024), low),
            pltpu.VMEM((whole, 1024), low),
            pltpu.VMEM((2, half, WIDTH), wide),
            pltpu.VMEM((2, half, WIDTH), low),
            pltpu.VMEM((2, half, WIDTH), low),
            pltpu.VMEM((2, half, WIDTH), low),
            dma((24,)),
            dma((2, 7)),
            dma((2, 7)),
            dma((2, 8)),
            dma((2, 8)),
            dma((2,)),
            dma((2,)),
            dma((2, 7)),
            dma((2, 7)),
            dma((2,)),
        ],
        name="run_experts",
        compiler_params=pltpu.CompilerParams(
            collective_id=3, has_side_effects=True, vmem_limit_bytes=56 * 2**20
        ),
    )(rows, grads, gate_up, down)


def over_ctx(array):
    return lax.all_to_all(jnp.broadcast_to(array[None], (8, *array.shape)), "ctx", 0, 0, tiled=True)


def on_device(
    tokens, prev_logits, routes, segments, rank_order, norm_first, w_query, w_key, w_value, w_output,
    norm_second, w_router, w_residual, w_constant, v_constant, w_gate, w_up, w_down, cotangent,
):
    own = pack_own(
        [w_query, w_key, w_value, w_output],
        [w_router, w_constant, v_constant, norm_first[:, None], norm_second[:, None]],
    )
    marks = jnp.pad(segments.astype(jnp.bfloat16), ((0, 15), (0, WIDTH - BLK)))
    *parts, blocks = gather_shards(own, jnp.concatenate([tokens[0], marks], axis=0))
    gate_up, down = jnp.concatenate([w_gate[0], w_up[0]], axis=0), w_down[0]
    gate_up, down, parts = lax.optimization_barrier((gate_up, down, parts))
    gate_up, down = over_ctx(gate_up), over_ctx(down)
    weights, smalls = unpack_shards(parts)
    seg_wide = blocks[:, BLK, :BLK].astype(jnp.float32)
    seg_int = seg_wide.astype(jnp.int32)
    prev = jnp.pad(prev_logits[0], ((0, 0), (0, 116)))
    wres = jnp.pad(w_residual, ((0, 116), (0, 116)))
    state, normed, att, lse, q, keys, values, rows, grads, info, proj = attend(
        seg_int, seg_wide, blocks, weights, smalls, prev, wres, routes[0],
        rank_order[0].astype(jnp.float32), cotangent[0],
    )
    returned, returned_grad, d_gate_up, d_down = run_experts(rows, grads, gate_up, down)

    def sum_over_ctx(array):
        return jnp.sum(lax.all_to_all(array, "ctx", 0, 0, tiled=True).astype(jnp.float32), axis=0)

    gate_up_sum, down_sum = sum_over_ctx(d_gate_up), sum_over_ctx(d_down)
    out, prev_grad, res_grad, dw, dsmall, others, first, state_grad = unattend(
        seg_int, seg_wide, blocks, weights, smalls, prev, wres, routes[0], cotangent[0],
        (state, normed, att, lse, q, keys, values, info, proj), returned, returned_grad,
    )
    summed, residual_total, tokens_grad = scatter_shards(
        pack_shards(dw, dsmall), res_grad, others, first, state_grad, tokens[0],
        smalls[:, 18].astype(jnp.float32)[None],
    )
    (sum_query, sum_key, sum_value, sum_output), small_sum = unpack_own(summed)
    return (
        out[None],
        tokens_grad[None],
        prev_grad[None, :, :12],
        small_sum[:, 18],
        sum_query,
        sum_key,
        sum_value,
        sum_output,
        small_sum[:, 19],
        small_sum[:, :12],
        residual_total[:12, :12],
        small_sum[:, 12:16],
        small_sum[:, 16:18],
        gate_up_sum[None, :96],
        gate_up_sum[None, 96:],
        down_sum[None],
    )


def solution(mesh):
    in_specs = (
        P("fsdp", "ctx", None),
        P("fsdp", "ctx", None),
        P("fsdp", "ctx", None),
        P("fsdp", "ctx"),
        P("fsdp", "ctx", None),
        P(("ctx", "fsdp")),
        P(("ctx", "fsdp"), None),
        P(("ctx", "fsdp"), None),
        P(("ctx", "fsdp"), None),
        P(("ctx", "fsdp"), None),
        P(("ctx", "fsdp")),
        P(("ctx", "fsdp"), None),
        P(),
        P(("ctx", "fsdp"), None),
        P(("ctx", "fsdp"), None),
        P("fsdp", "ctx", None),
        P("fsdp", "ctx", None),
        P("fsdp", "ctx", None),
        P("fsdp", "ctx", None),
    )
    out_specs = (
        P("fsdp", "ctx", None),
        P("fsdp", "ctx", None),
        P("fsdp", "ctx", None),
        P(("ctx", "fsdp")),
        P(("ctx", "fsdp"), None),
        P(("ctx", "fsdp"), None),
        P(("ctx", "fsdp"), None),
        P(("ctx", "fsdp"), None),
        P(("ctx", "fsdp")),
        P(("ctx", "fsdp"), None),
        P(),
        P(("ctx", "fsdp"), None),
        P(("ctx", "fsdp"), None),
        P("fsdp", "ctx", None),
        P("fsdp", "ctx", None),
        P("fsdp", "ctx", None),
    )
    return jax.shard_map(
        on_device, mesh=mesh, in_specs=in_specs, out_specs=out_specs, check_vma=False
    )
```

```python
import functools

import jax
import jax.numpy as jnp
import numpy as np
from jax import lax
from jax.experimental import pallas as pl
from jax.experimental.pallas import tpu as pltpu
from jax.sharding import PartitionSpec as P

HEADS = 12
HDIM = 64
EXPERTS = 8
NALL = 12
CAP = 54
WIDTH = HEADS * HDIM
PAIRS = HEADS // 2
BLK = 256
SLOTS = 64

highest = lax.Precision.HIGHEST
masked_score = -1e30
epsilon = 1e-06

MESH = pl.DeviceIdType.MESH
PART_LANES = (512, 384, 384)
PART_START = (0, 512, 896)
PART_ORDER = ((0, 1, 2), (1, 2, 0), (2, 0, 1))


def place():
    ctx = lax.axis_index("ctx")
    fsdp = lax.axis_index("fsdp")
    return ctx // 2, (ctx % 2) * 2 + fsdp // 8, (fsdp // 2) % 4, fsdp % 2


def device_at(x, z, y, core):
    return {"ctx": x * 2 + z // 2, "fsdp": (z % 2) * 8 + y * 2 + core}


def shifted(spot, axis, by):
    moved = list(spot)
    moved[axis] = (moved[axis] + by) % 4
    return tuple(moved)


def greet(devices):
    barrier = pltpu.get_barrier_semaphore()
    for device in devices:
        pl.semaphore_signal(barrier, inc=1, device_id=device, device_id_type=MESH)
    pl.semaphore_wait(barrier, len(devices))


def torus_peers(spot, core):
    peers = [device_at(*shifted(spot, axis, by), core) for axis in range(3) for by in (1, 2, 3)]
    return peers + [device_at(*spot, 1 - core)]


def sequence_peers(spot, core):
    x, z, y = spot
    return [device_at((x + by) % 4, (z + 2) % 4, y, core) for by in (1, 2, 3)]


def region(ref, spot, core, whole):
    return ref.at[
        tuple(slice(None) if axis in whole else spot[axis] for axis in range(3)) + (core,)
    ]


def placing_tables():
    left = np.zeros((192, 256), np.float32)
    right = np.zeros((192, 256), np.float32)
    small = np.zeros((48, 128), np.float32)
    for device in range(8):
        for weight in range(4):
            for row in range(6):
                at, line = weight * 48 + device * 6 + row, weight * 6 + row
                if line < 16:
                    left[at, device * 16 + line] = right[at, device * 16 + line] = 1
                else:
                    left[at, 128 + device * 16 + line - 16] = 1
                    right[at, 128 + device * 16 + line - 8] = 1
        for row in range(6):
            small[device * 6 + row, device * 16 + row] = 1
    return left, right, small


def rope_tables():
    frequency = 10000.0 ** (-2.0 * (np.arange(128) % 32) / HDIM)
    inner = np.arange(BLK)[:, None] * frequency
    outer = (np.arange(8) * BLK)[:, None] * frequency
    return [jnp.asarray(t, jnp.float32) for t in (np.cos(inner), np.sin(inner), np.cos(outer), np.sin(outer))]


def turning(index, tables):
    cos_in, sin_in, cos_out, sin_out = tables
    ca, sa = cos_out[pl.ds(index, 1), :], sin_out[pl.ds(index, 1), :]
    cb, sb = cos_in[...], sin_in[...]
    lower = lax.broadcasted_iota(jnp.int32, (BLK, 128), 1) % HDIM < HDIM // 2
    sine = sa * cb + ca * sb
    return ca * cb - sa * sb, jnp.where(lower, -sine, sine)


def swapped(values):
    lower = lax.broadcasted_iota(jnp.int32, values.shape, 1) % HDIM < HDIM // 2
    return jnp.where(lower, pltpu.roll(values, 96, 1), pltpu.roll(values, 32, 1))


def dot(left, right):
    return jnp.dot(left, right, preferred_element_type=jnp.float32)


def dot_nt(left, right):
    return lax.dot_general(left, right, (((1,), (1,)), ((), ())), preferred_element_type=jnp.float32)


def column(row):
    return jnp.broadcast_to(row, (128, row.shape[1])).T[:, 0:1]


def mask_bias(key_block, query_block, bias_ref, ctx, index):
    key_seg = column(key_block[BLK:, :BLK].astype(jnp.float32)[:1])
    query_seg = query_block[BLK:, :BLK].astype(jnp.float32)[:1]
    key_pos = lax.broadcasted_iota(jnp.int32, (BLK, BLK), 0)
    query_pos = lax.broadcasted_iota(jnp.int32, (BLK, BLK), 1)
    reach = jnp.where(index == ctx, 0, BLK)
    allowed = (key_seg == query_seg) & (key_pos <= query_pos + reach)
    bias_ref[...] = jnp.where(allowed, 0.0, masked_score)


def rms_rows(values):
    return lax.rsqrt(jnp.mean(values * values, axis=-1, keepdims=True) + epsilon)


def pick(onehot, values):
    return jnp.sum(jnp.where(onehot, values, 0.0), axis=1, keepdims=True)


def lane_is(lanes):
    return lax.broadcasted_iota(jnp.int32, (BLK, 128), 1) == lanes


def dot_tn(left, right):
    return lax.dot_general(left, right, (((0,), (0,)), ((), ())), preferred_element_type=jnp.float32)


def row_tile(values):
    *weights, small = values
    rows = jnp.concatenate([w.astype(jnp.float32) for w in weights], axis=0)
    tail = jnp.concatenate([rows[16:, :384], rows[16:, 384:]], axis=0)
    return jnp.concatenate([rows[:16], tail, small], axis=1).astype(jnp.bfloat16)


def front_kernel(
    wq_ref, wk_ref, wv_ref, wo_ref, router_ref, constant_ref, vector_ref, gain_one_ref, gain_two_ref,
    tokens_ref, segments_in, gate_in, up_in,
    left_ref, right_ref, place_ref, cos_in, sin_in, cos_out, sin_out,
    prev_ref, wres_ref, routes_ref, rank_ref, cot_ref,
    state_ref, normed_ref, att_ref, lse_ref, q_ref, keys_ref, values_ref, rows_ref, grads_ref,
    info_ref, proj_ref, blocks_ref, w_ref, small_ref, gate_up_ref,
    part_a, part_b, part_c, own_ref, qt_ref, vt_ref, bias_ref, max_ref, sum_ref, acc_ref,
    prev_pad, wres_pad, few_wide, few_tall,
    net_send, net_recv, twin_send, twin_recv, own_sem, seq_send, seq_recv, fwd_send, fwd_recv,
):
    parts = (part_a, part_b, part_c)
    tables = (cos_in, sin_in, cos_out, sin_out)
    ctx, fsdp = lax.axis_index("ctx"), lax.axis_index("fsdp")
    along, side = ctx // 2, ctx % 2
    *spot, core = place()
    spot = tuple(spot)
    twin = device_at(*spot, 1 - core)
    few_wide[...] = jnp.zeros_like(few_wide)
    few_wide[12:16, :6] = constant_ref[...].astype(jnp.float32)
    few_wide[16:18, :6] = vector_ref[...].astype(jnp.float32)
    few_wide[18:19, :6] = gain_one_ref[...].astype(jnp.float32)
    few_wide[19:20, :6] = gain_two_ref[...].astype(jnp.float32)
    few_tall[...] = few_wide[...].T[:16]
    few_tall[:6, :NALL] = router_ref[...].astype(jnp.float32)
    own_ref[...] = row_tile([wq_ref[...], wk_ref[...], wv_ref[...], wo_ref[...], few_tall[...]])
    marks = jnp.concatenate(
        [segments_in[...].astype(jnp.float32), jnp.zeros((1, WIDTH - BLK), jnp.float32)], axis=1
    )
    blocks_ref[ctx, :BLK] = tokens_ref[...]
    blocks_ref[ctx, BLK:] = jnp.broadcast_to(marks, (16, WIDTH)).astype(jnp.bfloat16)
    greet(torus_peers(spot, core) + sequence_peers(spot, core))

    def net(part, step, by, source, target):
        axis = PART_ORDER[part][step]
        return pltpu.make_async_remote_copy(
            src_ref=source,
            dst_ref=target,
            send_sem=net_send.at[part, step, by - 1],
            recv_sem=net_recv.at[part, step, by - 1],
            device_id=device_at(*shifted(spot, axis, by), core),
            device_id_type=MESH,
        )

    def share(part, slot, source, target):
        return pltpu.make_async_remote_copy(
            src_ref=source,
            dst_ref=target,
            send_sem=twin_send.at[part, slot],
            recv_sem=twin_recv.at[part, slot],
            device_id=twin,
            device_id_type=MESH,
        )

    payloads = ((blocks_ref, 128, BLK + 16), (gate_up_ref, 96, 192))

    def seq(kind, route, by, source, rows):
        array = payloads[kind][0]
        to_side = side if route in (1, 3) else 1 - side
        target = ((along + by) % 4) * 2 + to_side
        semaphores = (fwd_send, fwd_recv) if route == 3 else (seq_send, seq_recv)
        slot = {0: 0, 1: by, 2: 3 + by, 3: by - 1}[route]
        view = array.at[source, rows]
        return pltpu.make_async_remote_copy(
            src_ref=view,
            dst_ref=view,
            send_sem=semaphores[0].at[kind, slot],
            recv_sem=semaphores[1].at[kind, slot],
            device_id={"ctx": target, "fsdp": fsdp},
            device_id_type=MESH,
        )

    def rows_of(kind, route):
        array, cut, end = payloads[kind]
        return (pl.ds(0, end), pl.ds(0, end), pl.ds(0, cut), pl.ds(cut, end - cut))[route]

    def needed(kind, by):
        return along + by < 4 if kind == 0 else along >= 0

    def send_own(kind):
        seq(kind, 0, 0, ctx, rows_of(kind, 0)).start()
        for by in (1, 2, 3):

            @pl.when(needed(kind, by))
            def _(by=by):
                seq(kind, 1, by, ctx, rows_of(kind, 1)).start()
                seq(kind, 2, by, ctx, rows_of(kind, 2)).start()

    def beside():
        return along * 2 + 1 - side

    def send_on(kind):
        seq(kind, 0, 0, beside(), rows_of(kind, 0)).wait_recv()
        for by in (1, 2, 3):

            @pl.when(needed(kind, by))
            def _(by=by):
                seq(kind, 3, by, beside(), rows_of(kind, 3)).start()

    def behind(by, on_side):
        return ((along - by + 4) % 4) * 2 + on_side

    def wait_along(kind, by):
        seq(kind, 1, by, behind(by, side), rows_of(kind, 1)).wait_recv()

    def wait_across(kind, by):
        seq(kind, 2, by, behind(by, 1 - side), rows_of(kind, 2)).wait_recv()
        seq(kind, 3, by, behind(by, 1 - side), rows_of(kind, 3)).wait_recv()

    def wait_sent(kind):
        seq(kind, 0, 0, ctx, rows_of(kind, 0)).wait_send()
        for by in (1, 2, 3):

            @pl.when(needed(kind, by))
            def _(by=by):
                seq(kind, 1, by, ctx, rows_of(kind, 1)).wait_send()
                seq(kind, 2, by, ctx, rows_of(kind, 2)).wait_send()
                seq(kind, 3, by, beside(), rows_of(kind, 3)).wait_send()

    started = []
    kept = []
    for part in range(3):
        own = own_ref.at[:, pl.ds(PART_START[part], PART_LANES[part])]
        mine = region(parts[part], spot, core, ())
        for by in (1, 2, 3):
            copy = net(part, 0, by, own, mine)
            copy.start()
            started.append(copy)
    for part in range(3):
        own = own_ref.at[:, pl.ds(PART_START[part], PART_LANES[part])]
        mine = region(parts[part], spot, core, ())
        copy = pltpu.make_async_copy(own, mine, own_sem.at[part])
        copy.start()
        kept.append(copy)
        copy = share(part, 0, own, mine)
        copy.start()
        started.append(copy)
    own_experts = [
        pltpu.make_async_copy(gate_in, gate_up_ref.at[ctx, :96], own_sem.at[3]),
        pltpu.make_async_copy(up_in, gate_up_ref.at[ctx, 96:], own_sem.at[4]),
    ]
    for copy in own_experts:
        copy.start()
    for copy in kept + own_experts:
        copy.wait()
    for step in range(3):
        for part in range(3):
            order = PART_ORDER[part]
            axis = order[step]
            whole = order[:step]
            for by in (1, 2, 3):
                here = region(parts[part], shifted(spot, axis, -by), core, whole)
                net(part, step, by, here, here).wait_recv()
                copy = share(part, 1 + step * 3 + by - 1, here, here)
                copy.start()
                started.append(copy)
            if step < 2:
                held = region(parts[part], spot, core, order[: step + 1])
                for by in (1, 2, 3):
                    copy = net(part, step + 1, by, held, held)
                    copy.start()
                    started.append(copy)
        if step == 1:
            send_own(0)
    for part in range(3):
        order = PART_ORDER[part]
        first = region(parts[part], spot, 1 - core, ())
        share(part, 0, first, first).wait_recv()
        for step in range(3):
            for by in (1, 2, 3):
                here = region(
                    parts[part], shifted(spot, order[step], -by), 1 - core, order[:step]
                )
                share(part, 1 + step * 3 + by - 1, here, here).wait_recv()

    def unpack(group, carry):
        a, b, c = (
            part[group // 4, group % 4].reshape(128, lanes)
            for part, lanes in zip(parts, PART_LANES, strict=True)
        )
        tail = jnp.concatenate([b[:, 256:], c[:, :256]], axis=1)
        left = dot(left_ref[...], jnp.concatenate([a[:, :384], tail], axis=0))
        right_rows = jnp.concatenate([a[:, 384:], b[:, :256]], axis=1)
        right = dot(right_ref[...], jnp.concatenate([right_rows, tail], axis=0))
        rows = pl.ds(pl.multiple_of(group * 48, 16), 48)
        for weight in range(4):
            w_ref[weight, rows, :384] = left[weight * 48 : weight * 48 + 48].astype(jnp.bfloat16)
            w_ref[weight, rows, 384:] = right[weight * 48 : weight * 48 + 48].astype(jnp.bfloat16)
        small_ref[rows] = dot(place_ref[...], c[:, 256:]).astype(jnp.bfloat16)
        return carry

    lax.fori_loop(0, 16, unpack, 0)
    across = small_ref[...].astype(jnp.float32).T
    gain_one, gain_two = across[18:19], across[19:20]

    def normed_block(index):
        wide = blocks_ref[index, :BLK].astype(jnp.float32)
        return (wide * rms_rows(wide) * gain_one).astype(jnp.bfloat16)

    query = dot(normed_block(ctx), w_ref[0])
    cosine, sine = turning(ctx, tables)
    for pair in range(PAIRS):
        part = query[:, pair * 128 : pair * 128 + 128]
        turned = (part * cosine + swapped(part) * sine) * (HDIM**-0.5)
        q_ref[pair] = turned.astype(jnp.bfloat16)
        across_q = turned.T.astype(jnp.bfloat16)
        blank = jnp.zeros((HDIM, BLK), jnp.bfloat16)
        qt_ref[2 * pair] = jnp.concatenate([across_q[:HDIM], blank], axis=0)
        qt_ref[2 * pair + 1] = jnp.concatenate([blank, across_q[HDIM:]], axis=0)
    max_ref[...] = jnp.full(max_ref.shape, masked_score, jnp.float32)
    sum_ref[...] = jnp.zeros_like(sum_ref)
    acc_ref[...] = jnp.zeros_like(acc_ref)

    def block(step, carry):
        index = ctx - step

        @pl.when((step > 0) & (step % 2 == 0))
        def _():
            wait_along_at(step // 2)

        @pl.when((step % 2 == 1) & ((step + 1) // 2 - side > 0))
        def _():
            wait_across_at((step + 1) // 2 - side)

        normed = normed_block(index)
        key = dot(normed, w_ref[1])
        value = dot(normed, w_ref[2])
        cosine, sine = turning(index, tables)
        for pair in range(PAIRS):
            lanes = slice(pair * 128, pair * 128 + 128)
            part = key[:, lanes]
            keys_ref[index, pair] = (part * cosine + swapped(part) * sine).astype(jnp.bfloat16)
            values_ref[index, pair] = value[:, lanes].astype(jnp.bfloat16)
            vt_ref[lanes, :] = value[:, lanes].T.astype(jnp.bfloat16)
        mask_bias(blocks_ref.at[index], blocks_ref.at[ctx], bias_ref, ctx, index)
        for head in range(HEADS):
            rows = slice(head * HDIM, head * HDIM + HDIM)
            scores = dot(keys_ref[index, head // 2], qt_ref[head]) + bias_ref[...]
            before = max_ref[head : head + 1]
            top = jnp.maximum(before, jnp.max(scores, axis=0, keepdims=True))
            weights = jnp.exp(scores - top)
            shrink = jnp.exp(before - top)
            sum_ref[head : head + 1] = sum_ref[head : head + 1] * shrink + jnp.sum(
                weights, axis=0, keepdims=True
            )
            max_ref[head : head + 1] = top
            acc_ref[rows] = acc_ref[rows] * shrink + dot(vt_ref[rows, :], weights.astype(jnp.bfloat16))

        @pl.when(step == 0)
        def _():
            send_on(0)
            send_own(1)

        @pl.when(step == jnp.minimum(ctx, 3))
        def _():
            send_on(1)

        return carry

    def wait_along_at(by):
        source = (along - by) * 2 + side
        seq_at(1, by, source).wait_recv()

    def wait_across_at(by):
        source = (along - by) * 2 + 1 - side
        seq_at(2, by, source).wait_recv()
        seq_at(3, by, source).wait_recv()

    def seq_at(route, by, source):
        view = blocks_ref.at[source, rows_of(0, route)]
        semaphores = (fwd_send, fwd_recv) if route == 3 else (seq_send, seq_recv)
        slot = {1: by, 2: 3 + by, 3: by - 1}[route]
        return pltpu.make_async_remote_copy(
            src_ref=view,
            dst_ref=view,
            send_sem=semaphores[0].at[0, slot],
            recv_sem=semaphores[1].at[0, slot],
            device_id=twin,
            device_id_type=MESH,
        )

    lax.fori_loop(0, ctx + 1, block, 0)
    for head in range(HEADS):
        rows = slice(head * HDIM, head * HDIM + HDIM)
        att_ref[rows] = acc_ref[rows] / sum_ref[head : head + 1]
    lse_ref[...] = max_ref[...] + jnp.log(jnp.maximum(sum_ref[...], 1e-30))
    attended = att_ref[...].T.astype(jnp.bfloat16)
    state = blocks_ref[ctx, :BLK].astype(jnp.float32) + dot(attended, w_ref[3])
    state_ref[...] = state
    normed_two = (state * rms_rows(state) * gain_two).astype(jnp.bfloat16)
    normed_ref[...] = normed_two

    proj = dot(normed_two, small_ref[...])
    proj_ref[...] = proj
    pad_routing(prev_ref, wres_ref, prev_pad, wres_pad)
    logits = proj + jnp.dot(
        prev_pad[...].T, wres_pad[...], precision=highest, preferred_element_type=jnp.float32
    )
    lanes = lax.broadcasted_iota(jnp.int32, (BLK, 128), 1).astype(jnp.float32)
    routes = routes_ref[...].astype(jnp.float32)
    route_0, route_1 = column(routes[0:1]), column(routes[1:2])
    hot_0, hot_1 = lanes == route_0, lanes == route_1
    chosen_0, chosen_1 = pick(hot_0, logits), pick(hot_1, logits)
    top = jnp.maximum(chosen_0, chosen_1)
    chosen_0, chosen_1 = jnp.exp(chosen_0 - top), jnp.exp(chosen_1 - top)
    gate_0, gate_1 = chosen_0 / (chosen_0 + chosen_1), chosen_1 / (chosen_0 + chosen_1)
    rank = rank_ref[...].astype(jnp.float32)
    earlier = (rank < column(rank)).astype(jnp.float32).astype(jnp.bfloat16)
    slots = dot(earlier, (hot_0 | hot_1).astype(jnp.float32).astype(jnp.bfloat16))

    def target(route, hot):
        slot = pick(hot, slots)
        return jnp.where(
            (route < EXPERTS) & (slot < CAP), route * SLOTS + slot, -1.0
        )

    target_0, target_1 = target(route_0, hot_0), target(route_1, hot_1)
    info = jnp.where(lanes == 0, gate_0, 0.0) + jnp.where(lanes == 1, gate_1, 0.0)
    info = info + jnp.where(lanes == 2, target_0, 0.0) + jnp.where(lanes == 3, target_1, 0.0)
    info_ref[...] = info
    targets = info.T
    rows = lax.broadcasted_iota(jnp.int32, (EXPERTS * SLOTS, BLK), 0).astype(jnp.float32)
    table_0 = (rows == targets[2:3]).astype(jnp.float32).astype(jnp.bfloat16)
    table_1 = (rows == targets[3:4]).astype(jnp.float32).astype(jnp.bfloat16)
    rows_ref[...] = dot(table_0 + table_1, normed_two).astype(jnp.bfloat16)
    upstream = cot_ref[...].astype(jnp.float32)
    grads_ref[...] = dot(
        jnp.concatenate([table_0, table_1], axis=1),
        jnp.concatenate([gate_0 * upstream, gate_1 * upstream], axis=0).astype(jnp.bfloat16),
    ).astype(jnp.bfloat16)
    for by in (1, 2, 3):
        wait_along(1, by)
        wait_across(1, by)
    for kind in (0, 1):
        wait_sent(kind)
    for copy in started:
        copy.wait_send()


def pad_routing(prev_ref, wres_ref, prev_pad, wres_pad):
    prev_pad[...] = jnp.zeros_like(prev_pad)
    prev_pad[:NALL] = prev_ref[:, 0, :]
    wres_pad[...] = jnp.zeros_like(wres_pad)
    wres_pad[:NALL, :NALL] = wres_ref[...]


def run_front(weights, few, tokens, segments, gate, up, prev, wres, routes, rank, cot):
    vmem, anywhere = pl.BlockSpec(memory_space=pltpu.VMEM), pl.BlockSpec(memory_space=pl.ANY)
    shape = jax.ShapeDtypeStruct
    low, wide = jnp.bfloat16, jnp.float32
    dma = pltpu.SemaphoreType.DMA
    left, right, small = (jnp.asarray(t, low) for t in placing_tables())
    return pl.pallas_call(
        front_kernel,
        out_shape=[
            shape((BLK, WIDTH), wide),
            shape((BLK, WIDTH), low),
            shape((WIDTH, BLK), wide),
            shape((16, BLK), wide),
            shape((PAIRS, BLK, 128), low),
            shape((8, PAIRS, BLK, 128), low),
            shape((8, PAIRS, BLK, 128), low),
            shape((EXPERTS * SLOTS, WIDTH), low),
            shape((EXPERTS * SLOTS, WIDTH), low),
            shape((BLK, 128), wide),
            shape((BLK, 128), wide),
            shape((8, BLK + 16, WIDTH), low),
            shape((4, WIDTH, WIDTH), low),
            shape((WIDTH, 128), low),
            shape((8, 192, 1024), low),
        ],
        in_specs=[vmem] * 25,
        out_specs=[vmem] * 14 + [anywhere],
        scratch_shapes=[
            *(pltpu.VMEM((4, 4, 4, 2, 16, lanes), low) for lanes in PART_LANES),
            pltpu.VMEM((16, 1280), low),
            pltpu.VMEM((HEADS, 128, BLK), low),
            pltpu.VMEM((WIDTH, BLK), low),
            pltpu.VMEM((BLK, BLK), wide),
            pltpu.VMEM((16, BLK), wide),
            pltpu.VMEM((16, BLK), wide),
            pltpu.VMEM((WIDTH, BLK), wide),
            pltpu.VMEM((128, BLK), wide),
            pltpu.VMEM((128, 128), wide),
            pltpu.VMEM((128, 128), wide),
            pltpu.VMEM((16, 128), wide),
            dma((3, 3, 3)),
            dma((3, 3, 3)),
            dma((3, 10)),
            dma((3, 10)),
            dma((5,)),
            dma((2, 7)),
            dma((2, 7)),
            dma((2, 3)),
            dma((2, 3)),
        ],
        name="front",
        compiler_params=pltpu.CompilerParams(
            collective_id=1, has_side_effects=True, vmem_limit_bytes=56 * 2**20
        ),
    )(
        *weights, *few, tokens, segments, gate, up, left, right, small, *rope_tables(),
        prev, wres, routes, rank, cot,
    )


def experts_kernel(
    rows_ref, grads_ref, gate_up_ref, down_ref,
    back_rows_ref, back_grads_ref, d_gate_up_ref, d_down_ref,
    gate_w, up_w, down_w, x_ref, g_ref, gate_ref, up_ref, hidden_ref, d_gate, d_up,
    mine_ref, twin_out, twin_in, sums_ref,
    down_send, down_recv, load_sem, send_sem, recv_sem, share_send, share_recv, half_send, half_recv, ret_send, ret_recv,
    own_sem,
):
    ctx, fsdp = lax.axis_index("ctx"), lax.axis_index("fsdp")
    chip, core = fsdp // 2, fsdp % 2
    other = 1 - core
    half = EXPERTS * SLOTS

    def at(where, on):
        return {"ctx": ctx, "fsdp": where * 2 + on}

    greet(
        [at((chip + by) % EXPERTS, core) for by in range(1, EXPERTS)]
        + [at(chip, other)]
        + [{"ctx": (ctx + by) % 8, "fsdp": fsdp} for by in range(1, 8)]
    )

    def down(by, owner):
        spot = down_w.at[pl.ds(pl.multiple_of(owner * 128, 128), 128)]
        return pltpu.make_async_remote_copy(
            src_ref=down_ref,
            dst_ref=spot,
            send_sem=down_send.at[by - 1],
            recv_sem=down_recv.at[by - 1],
            device_id={"ctx": (ctx + by) % 8, "fsdp": fsdp},
            device_id_type=MESH,
        )

    loads = []
    for index in range(8):
        for source, target, size in (
            (gate_up_ref.at[index, :96], gate_w, 96),
            (gate_up_ref.at[index, 96:], up_w, 96),
        ):
            copy = pltpu.make_async_copy(
                source, target.at[pl.ds(index * size, size)], load_sem.at[len(loads)]
            )
            loads.append(copy)
    loads.append(
        pltpu.make_async_copy(
            down_ref, down_w.at[pl.ds(pl.multiple_of(ctx * 128, 128), 128)], load_sem.at[16]
        )
    )

    def slots(index, on):
        return pl.ds(pl.multiple_of((on * EXPERTS + index) * SLOTS, SLOTS), SLOTS)

    def chunk(index):
        return pl.ds(pl.multiple_of(index * SLOTS, SLOTS), SLOTS)

    buffers = ((rows_ref, x_ref), (grads_ref, g_ref))

    def dispatch(kind, by):
        source, target = buffers[kind]
        where = (chip + by) % EXPERTS
        return pltpu.make_async_remote_copy(
            src_ref=source.at[chunk(where)],
            dst_ref=target.at[slots(chip, core)],
            send_sem=send_sem.at[kind, by - 1],
            recv_sem=recv_sem.at[kind, by - 1],
            device_id=at(where, core),
            device_id_type=MESH,
        )

    def share(kind, by, on):
        source, target = buffers[kind]
        spot = slots((chip - by) % EXPERTS, on)
        return pltpu.make_async_remote_copy(
            src_ref=target.at[spot],
            dst_ref=target.at[spot],
            send_sem=share_send.at[kind, by],
            recv_sem=share_recv.at[kind, by],
            device_id=at(chip, other),
            device_id_type=MESH,
        )

    def exchange(kind):
        return pltpu.make_async_remote_copy(
            src_ref=twin_out.at[kind],
            dst_ref=twin_in.at[kind],
            send_sem=half_send.at[kind],
            recv_sem=half_recv.at[kind],
            device_id=at(chip, other),
            device_id_type=MESH,
        )

    returned = (back_rows_ref, back_grads_ref)

    def give_back(kind, by):
        where = (chip + by) % EXPERTS
        return pltpu.make_async_remote_copy(
            src_ref=sums_ref.at[kind, chunk(where)],
            dst_ref=returned[kind].at[chunk(chip)],
            send_sem=ret_send.at[kind, by - 1],
            recv_sem=ret_recv.at[kind, by - 1],
            device_id=at(where, core),
            device_id_type=MESH,
        )

    started = []
    for kind in (0, 1):
        for by in range(1, EXPERTS):
            copy = dispatch(kind, by)
            copy.start()
            started.append(copy)
    for by in range(1, 8):
        copy = down(by, ctx)
        copy.start()
        started.append(copy)
    for copy in loads:
        copy.start()
    for kind in (0, 1):
        source, target = buffers[kind]
        copy = pltpu.make_async_copy(
            source.at[chunk(chip)], target.at[slots(chip, core)], own_sem.at[kind]
        )
        copy.start()
        copy.wait()
        copy = share(kind, 0, core)
        copy.start()
        started.append(copy)

    def arrive(kind):
        for by in range(1, EXPERTS):
            dispatch(kind, by).wait_recv()
            copy = share(kind, by, core)
            copy.start()
            started.append(copy)

    def arrive_shared(kind):
        for by in range(EXPERTS):
            share(kind, by, other).wait_recv()

    def tiles(on, body):
        def step(index, carry):
            start = pl.multiple_of(on * half + index * 256, 256)
            body(pl.ds(start, 256), pl.ds(pl.multiple_of(index * 256, 256), 256))
            return carry

        lax.fori_loop(0, half // 256, step, 0)

    def forward(on, keep):
        def tile(rows, inner):
            x = x_ref[rows]
            gate, up = dot(x, gate_w[...]), dot(x, up_w[...])
            gate_ref[rows], up_ref[rows] = gate, up
            hidden_ref[rows] = (gate * jax.nn.sigmoid(gate) * up).astype(jnp.bfloat16)

        def result(rows, inner):
            keep(inner, dot(hidden_ref[rows], down_w[...]))

        tiles(on, tile)
        if on is core:
            for by in range(1, 8):
                down(by, (ctx - by + 8) % 8).wait_recv()
        tiles(on, result)

    def backward(on, keep):
        def tile(rows, inner):
            hidden_grad = dot_nt(g_ref[rows], down_w[...])
            gate, up = gate_ref[rows], up_ref[rows]
            sigmoid = jax.nn.sigmoid(gate)
            d_gate[rows] = (
                hidden_grad * up * sigmoid * (1.0 + gate * (1.0 - sigmoid))
            ).astype(jnp.bfloat16)
            d_up[rows] = (hidden_grad * gate * sigmoid).astype(jnp.bfloat16)
            keep(inner, dot_nt(d_gate[rows], gate_w[...]) + dot_nt(d_up[rows], up_w[...]))

        tiles(on, tile)

    def keep_mine(kind):
        def keep(rows, values):
            mine_ref[kind, rows] = values

        return keep

    def keep_twin(kind):
        def keep(rows, values):
            twin_out[kind, rows] = values.astype(jnp.bfloat16)

        return keep

    def finish(kind):
        exchange(kind).wait_recv()

        def step(index, carry):
            rows = pl.ds(pl.multiple_of(index * 128, 128), 128)
            sums_ref[kind, rows] = (
                mine_ref[kind, rows] + twin_in[kind, rows].astype(jnp.float32)
            ).astype(jnp.bfloat16)
            return carry

        lax.fori_loop(0, half // 128, step, 0)
        for by in range(1, EXPERTS):
            copy = give_back(kind, by)
            copy.start()
            started.append(copy)
        copy = pltpu.make_async_copy(
            sums_ref.at[kind, chunk(chip)], returned[kind].at[chunk(chip)], own_sem.at[kind]
        )
        copy.start()
        copy.wait()

    arrive(0)
    for copy in loads:
        copy.wait()
    forward(core, keep_mine(0))
    arrive(1)
    arrive_shared(0)
    forward(other, keep_twin(0))
    copy = exchange(0)
    copy.start()
    started.append(copy)
    backward(core, keep_mine(1))
    finish(0)
    arrive_shared(1)
    backward(other, keep_twin(1))
    copy = exchange(1)
    copy.start()
    started.append(copy)

    def down_tile(index, carry):
        lanes = pl.ds(pl.multiple_of(index * 256, 256), 256)
        part = dot_tn(hidden_ref[:, lanes], g_ref[...]).astype(jnp.bfloat16)
        d_down_ref[2 * index] = part[:128]
        d_down_ref[2 * index + 1] = part[128:]
        return carry

    lax.fori_loop(0, 4, down_tile, 0)
    finish(1)

    def gate_tile(index, carry):
        lanes = pl.ds(pl.multiple_of(index * 256, 256), 256)
        for start, grad in ((0, d_gate), (96, d_up)):
            part = dot_tn(x_ref[...], grad[:, lanes]).astype(jnp.bfloat16)
            for piece in range(8):
                d_gate_up_ref[piece, start : start + 96, lanes] = part[piece * 96 : piece * 96 + 96]
        return carry

    lax.fori_loop(0, 4, gate_tile, 0)
    for kind in (0, 1):
        for by in range(1, EXPERTS):
            give_back(kind, by).wait_recv()
    for copy in started:
        copy.wait_send()


def run_experts(rows, grads, gate_up, down):
    vmem, anywhere = pl.BlockSpec(memory_space=pltpu.VMEM), pl.BlockSpec(memory_space=pl.ANY)
    low, wide = jnp.bfloat16, jnp.float32
    half, whole = EXPERTS * SLOTS, 2 * EXPERTS * SLOTS
    dma = pltpu.SemaphoreType.DMA
    return pl.pallas_call(
        experts_kernel,
        out_shape=[
            jax.ShapeDtypeStruct((half, WIDTH), low),
            jax.ShapeDtypeStruct((half, WIDTH), low),
            jax.ShapeDtypeStruct((8, 192, 1024), low),
            jax.ShapeDtypeStruct((8, 128, WIDTH), low),
        ],
        in_specs=[vmem, vmem, anywhere, anywhere],
        out_specs=[vmem] * 4,
        scratch_shapes=[
            pltpu.VMEM((WIDTH, 1024), low),
            pltpu.VMEM((WIDTH, 1024), low),
            pltpu.VMEM((1024, WIDTH), low),
            pltpu.VMEM((whole, WIDTH), low),
            pltpu.VMEM((whole, WIDTH), low),
            pltpu.VMEM((whole, 1024), wide),
            pltpu.VMEM((whole, 1024), wide),
            pltpu.VMEM((whole, 1024), low),
            pltpu.VMEM((whole, 1024), low),
            pltpu.VMEM((whole, 1024), low),
            pltpu.VMEM((2, half, WIDTH), wide),
            pltpu.VMEM((2, half, WIDTH), low),
            pltpu.VMEM((2, half, WIDTH), low),
            pltpu.VMEM((2, half, WIDTH), low),
            dma((7,)),
            dma((7,)),
            dma((17,)),
            dma((2, 7)),
            dma((2, 7)),
            dma((2, 8)),
            dma((2, 8)),
            dma((2,)),
            dma((2,)),
            dma((2, 7)),
            dma((2, 7)),
            dma((2,)),
        ],
        name="run_experts",
        compiler_params=pltpu.CompilerParams(
            collective_id=3, has_side_effects=True, vmem_limit_bytes=56 * 2**20
        ),
    )(rows, grads, gate_up, down)


def split(values):
    high = values.astype(jnp.bfloat16)
    low = (values - high.astype(jnp.float32)).astype(jnp.bfloat16)
    return jnp.concatenate([high, low], axis=1)


def back_kernel(
    blocks_ref, w_ref, small_ref, cos_in, sin_in, cos_out, sin_out, left_ref, right_ref, place_ref,
    prev_ref, wres_ref, routes_ref, cot_ref,
    state_ref, normed_ref, att_ref, lse_ref, q_ref, keys_ref, values_ref, info_ref, proj_ref,
    back_rows_ref, back_grads_ref, d_gate_up, d_down,
    out_ref, prev_grad_ref, total_ref, tokens_grad_ref, sums_ref, few_ref,
    gate_out, up_out, down_out,
    *scratch,
):
    (
        qt_ref, ot_ref, o_ref, qm_ref, bias_ref, inner_ref, dqt_ref, gain_ref, dk_ref, dv_ref,
        prev_pad, wres_pad, dw_ref, few_sum, kv_ref, tok_ref, mine_ref, kv_sem, own_ref, state_grad_ref, others_ref, grads_ref, block_in,
        gate_up_in, down_in, small_in, small_sum,
        block_send, block_recv, exp_send, exp_recv, load_sem,
        net_send, net_recv, twin_send, twin_recv, small_send, small_recv,
        *more,
    ) = scratch
    twin_in, held, in_one, in_two, in_three, sum_one, sum_two = (
        more[0], more[1], more[2:5], more[5:8], more[8:11], more[11:14], more[14:17]
    )
    tables = (cos_in, sin_in, cos_out, sin_out)
    ctx, fsdp = lax.axis_index("ctx"), lax.axis_index("fsdp")
    *spot, core = place()
    spot = tuple(spot)
    twin = device_at(*spot, 1 - core)
    started = []
    greet(torus_peers(spot, core) + sequence_peers(spot, core))

    def expert(kind, by):
        source, target = ((d_gate_up, gate_up_in), (d_down, down_in))[kind]
        where = (ctx + by) % 8
        return pltpu.make_async_remote_copy(
            src_ref=source.at[where],
            dst_ref=target.at[by],
            send_sem=exp_send.at[kind, by - 1],
            recv_sem=exp_recv.at[kind, by - 1],
            device_id={"ctx": where, "fsdp": fsdp},
            device_id_type=MESH,
        )

    for kind in (0, 1):
        for by in range(1, 8):
            copy = expert(kind, by)
            copy.start()
            started.append(copy)
    kept = [
        pltpu.make_async_copy(d_gate_up.at[ctx], gate_up_in.at[0], load_sem.at[0]),
        pltpu.make_async_copy(d_down.at[ctx], down_in.at[0], load_sem.at[1]),
    ]
    own_block = pltpu.make_async_copy(blocks_ref.at[ctx], mine_ref, load_sem.at[2])
    own_block.start()
    for copy in kept:
        copy.start()

    def load_kv(index, slot):
        return [
            pltpu.make_async_copy(source.at[index], kv_ref.at[slot, kind], kv_sem.at[slot, kind])
            for kind, source in enumerate((keys_ref, values_ref))
        ] + [pltpu.make_async_copy(blocks_ref.at[index], tok_ref.at[slot], kv_sem.at[slot, 2])]

    for copy in load_kv(0, 0):
        copy.start()

    def block_copy(by, target):
        return pltpu.make_async_remote_copy(
            src_ref=others_ref.at[target],
            dst_ref=block_in.at[by - 1],
            send_sem=block_send.at[by - 1],
            recv_sem=block_recv.at[by - 1],
            device_id={"ctx": target, "fsdp": fsdp},
            device_id_type=MESH,
        )

    across = small_ref[...].astype(jnp.float32).T
    gain_one, gain_two = across[18:19], across[19:20]
    value_rows = across[16:18]

    lanes = lax.broadcasted_iota(jnp.int32, (BLK, 128), 1)
    info = info_ref[...]
    gates = (info[:, 0:1], info[:, 1:2])
    slots = lax.broadcasted_iota(jnp.int32, (BLK, EXPERTS * SLOTS), 1).astype(jnp.float32)
    tables_of = [
        (slots == info[:, 2 + k : 3 + k]).astype(jnp.float32).astype(jnp.bfloat16) for k in (0, 1)
    ]
    route_rows = routes_ref[...].astype(jnp.float32)
    routes = (column(route_rows[0:1]), column(route_rows[1:2]))
    hots = [lanes.astype(jnp.float32) == routes[k] for k in (0, 1)]
    named = [
        [(routes[k] == EXPERTS + 1 + kind).astype(jnp.float32) for kind in range(3)] for k in (0, 1)
    ]
    proj = proj_ref[...]
    mixes = []
    for c in (0, 1):
        first, second = proj[:, 12 + 2 * c : 13 + 2 * c], proj[:, 13 + 2 * c : 14 + 2 * c]
        top = jnp.maximum(first, second)
        first, second = jnp.exp(first - top), jnp.exp(second - top)
        mixes.append((first / (first + second), second / (first + second)))
    normed_low = normed_ref[...]
    normed_two = normed_low.astype(jnp.float32)
    upstream_low = cot_ref[...]
    upstream = upstream_low.astype(jnp.float32)
    state = state_ref[...]
    back_rows = back_rows_ref[...]
    result = state
    gate_grads = []
    for k in (0, 1):
        copy, one, two = named[k]
        pair = dot(tables_of[k], back_rows)
        pair = pair + (copy + one * mixes[0][0] + two * mixes[1][0]) * normed_two
        pair = pair + (one * mixes[0][1]) * value_rows[0:1] + (two * mixes[1][1]) * value_rows[1:2]
        result = result + gates[k] * pair
        gate_grads.append(jnp.sum(pair * upstream, axis=1, keepdims=True))
    out_ref[...] = result.astype(jnp.bfloat16)
    inner = gates[0] * gate_grads[0] + gates[1] * gate_grads[1]
    logit_grad = jnp.zeros((BLK, 128), jnp.float32)
    for k in (0, 1):
        logit_grad = logit_grad + jnp.where(hots[k], gates[k] * (gate_grads[k] - inner), 0.0)
    pad_routing(prev_ref, wres_ref, prev_pad, wres_pad)
    prev_grad_ref[...] = lax.dot_general(
        wres_pad[...], logit_grad, (((1,), (1,)), ((), ())),
        precision=highest, preferred_element_type=jnp.float32,
    )[:16]
    small_sum[3] = jnp.dot(
        prev_pad[...], logit_grad, precision=highest, preferred_element_type=jnp.float32
    )[:16]
    on_normed = jnp.sum(normed_two * upstream, axis=1, keepdims=True)
    on_vectors = dot(upstream_low, small_ref[...])
    flat = logit_grad
    weight_up = gates[0] * named[0][0] + gates[1] * named[1][0]
    vector_weights = jnp.zeros((BLK, 128), jnp.float32)
    for c in (0, 1):
        scale = gates[0] * named[0][1 + c] + gates[1] * named[1][1 + c]
        mix_0, mix_1 = mixes[c]
        m_0, m_1 = scale * on_normed, scale * on_vectors[:, 16 + c : 17 + c]
        mean = mix_0 * m_0 + mix_1 * m_1
        flat = flat + jnp.where(lanes == 12 + 2 * c, mix_0 * (m_0 - mean), 0.0)
        flat = flat + jnp.where(lanes == 13 + 2 * c, mix_1 * (m_1 - mean), 0.0)
        weight_up = weight_up + mix_0 * scale
        vector_weights = vector_weights + jnp.where(lanes == 16 + c, mix_1 * scale, 0.0)
    flat_split = split(flat)
    normed_grad = dot_nt(flat_split, jnp.concatenate([small_ref[...]] * 2, axis=1))
    normed_grad = normed_grad + weight_up * upstream
    normed_grad = normed_grad + dot(tables_of[0] + tables_of[1], back_grads_ref[...])
    normed_across = normed_two.T.astype(jnp.bfloat16)
    upstream_across = upstream.T.astype(jnp.bfloat16)
    small_grad = dot(normed_across, flat_split)
    small_vector = dot(upstream_across, split(vector_weights))
    small_grad = small_grad[:, :128] + small_grad[:, 128:] + small_vector[:, :128] + small_vector[:, 128:]
    scale_two = rms_rows(state)
    weighted = normed_grad * gain_two
    state_grad = (
        upstream
        + scale_two * weighted
        - state * (scale_two**3 * jnp.mean(weighted * state, axis=-1, keepdims=True))
    )
    state_grad_ref[...] = state_grad
    gain_two_row = jnp.sum(normed_grad * state * scale_two, axis=0, keepdims=True)
    state_low = state_grad.astype(jnp.bfloat16)
    attended = att_ref[...]
    dw_ref[3] = dot(attended.astype(jnp.bfloat16), state_low)
    att_grad = dot_nt(state_low, w_ref[3])
    blank = jnp.zeros((HDIM, BLK), jnp.bfloat16)
    low_half = lax.broadcasted_iota(jnp.int32, (BLK, 128), 1) < HDIM
    none = jnp.zeros((BLK, 128), jnp.bfloat16)
    inner_ref[...] = jnp.zeros_like(inner_ref)
    for pair in range(PAIRS):
        part = att_grad[:, pair * 128 : pair * 128 + 128].astype(jnp.bfloat16)
        across_o = part.astype(jnp.float32).T
        products = across_o * attended[pair * 128 : pair * 128 + 128]
        across_o = across_o.astype(jnp.bfloat16)
        across_q = q_ref[pair].astype(jnp.float32).T.astype(jnp.bfloat16)
        for half in (0, 1):
            head = 2 * pair + half
            rows = slice(half * HDIM, half * HDIM + HDIM)
            inner_ref[head : head + 1] = jnp.sum(products[rows], axis=0, keepdims=True)
            order = (lambda a, b: [a, b]) if half == 0 else (lambda a, b: [b, a])
            ot_ref[head] = jnp.concatenate(order(across_o[rows], blank), axis=0)
            qt_ref[head] = jnp.concatenate(order(across_q[rows], blank), axis=0)
        o_ref[pair, :BLK] = jnp.where(low_half, part, none)
        o_ref[pair, BLK:] = jnp.where(low_half, none, part)
        qm_ref[pair, :BLK] = jnp.where(low_half, q_ref[pair], none)
        qm_ref[pair, BLK:] = jnp.where(low_half, none, q_ref[pair])
    dqt_ref[...] = jnp.zeros_like(dqt_ref)
    dw_ref[1] = jnp.zeros((WIDTH, WIDTH), jnp.float32)
    dw_ref[2] = jnp.zeros((WIDTH, WIDTH), jnp.float32)
    gain_ref[...] = jnp.zeros_like(gain_ref)

    own_block.wait()

    def normed_block(array):
        wide = array[:BLK].astype(jnp.float32)
        scaled = wide * rms_rows(wide)
        return scaled, (scaled * gain_one).T.astype(jnp.bfloat16)

    def block(index, carry):
        slot = index % 2
        for copy in load_kv(index, slot):
            copy.wait()

        @pl.when(index < ctx)
        def _():
            for copy in load_kv(index + 1, 1 - slot):
                copy.start()

        mask_bias(tok_ref.at[slot], mine_ref, bias_ref, ctx, index)
        cosine, sine = turning(index, tables)
        for pair in range(PAIRS):
            key, value = kv_ref[slot, 0, pair], kv_ref[slot, 1, pair]
            key_across = key.astype(jnp.float32).T.astype(jnp.bfloat16)
            weights, score_grads = [], []
            for half in (0, 1):
                head = 2 * pair + half
                scores = dot(key, qt_ref[head]) + bias_ref[...]
                weight = jnp.exp(scores - lse_ref[head : head + 1])
                weight_grad = dot(value, ot_ref[head])
                score_grad = (weight * (weight_grad - inner_ref[head : head + 1])).astype(jnp.bfloat16)
                weights.append(weight.astype(jnp.bfloat16))
                score_grads.append(score_grad)
                rows = slice(head * HDIM, head * HDIM + HDIM)
                dqt_ref[rows] += dot(key_across[half * HDIM : half * HDIM + HDIM], score_grad)
            lanes = slice(pair * 128, pair * 128 + 128)
            dv_ref[:, lanes] = dot(jnp.concatenate(weights, axis=1), o_ref[pair]).astype(jnp.bfloat16)
            dk = dot(jnp.concatenate(score_grads, axis=1), qm_ref[pair])
            dk_ref[:, lanes] = (dk * cosine - swapped(dk) * sine).astype(jnp.bfloat16)
        scaled, normed_across = normed_block(tok_ref.at[slot])
        dw_ref[1] += dot(normed_across, dk_ref[...])
        dw_ref[2] += dot(normed_across, dv_ref[...])
        first = dot_nt(dk_ref[...], w_ref[1]) + dot_nt(dv_ref[...], w_ref[2])
        gain_ref[...] += jnp.sum(first * scaled, axis=0, keepdims=True)

        @pl.when(index < ctx)
        def _():
            others_ref[index] = first.astype(jnp.bfloat16)
            block_copy(ctx - index, index).start()

        @pl.when(index == ctx)
        def _():
            own_ref[...] = first

        return carry

    lax.fori_loop(0, ctx + 1, block, 0)
    cosine, sine = turning(ctx, tables)
    for pair in range(PAIRS):
        lanes = slice(pair * 128, pair * 128 + 128)
        dq = dqt_ref[lanes, :].T * (HDIM**-0.5)
        dk_ref[:, lanes] = (dq * cosine - swapped(dq) * sine).astype(jnp.bfloat16)
    scaled, normed_across = normed_block(mine_ref)
    dw_ref[0] = dot(normed_across, dk_ref[...])
    first = dot_nt(dk_ref[...], w_ref[0])
    own_ref[...] += first
    gain_one_row = gain_ref[...] + jnp.sum(first * scaled, axis=0, keepdims=True)
    lanes = lax.broadcasted_iota(jnp.int32, (WIDTH, 128), 1)
    ones = jnp.broadcast_to(gain_one_row, (128, WIDTH)).T
    twos = jnp.broadcast_to(gain_two_row, (128, WIDTH)).T
    few = jnp.where(lanes == 18, ones, jnp.where(lanes == 19, twos, small_grad))
    few_sum[...] = few

    def share(x):
        return pltpu.make_async_remote_copy(
            src_ref=grads_ref.at[x, :, :, 1 - core],
            dst_ref=twin_in.at[x],
            send_sem=twin_send.at[x],
            recv_sem=twin_recv.at[x],
            device_id=twin,
            device_id_type=MESH,
        )

    def pack(group, carry):
        rows = pl.ds(pl.multiple_of(group * 48, 16), 48)

        def lane_half(start):
            return jnp.concatenate(
                [dw_ref[w, rows, start : start + 384] for w in range(4)], axis=0
            ).astype(jnp.bfloat16)

        from_left = dot(left_ref[...], lane_half(0))
        from_right = dot(right_ref[...], lane_half(384))
        placed = dot(place_ref[...], few_sum[rows].astype(jnp.bfloat16))
        whole = jnp.concatenate(
            [from_left[:128], from_right[:128], from_left[128:] + from_right[128:], placed], axis=1
        )
        grads_ref[group // 4, group % 4] = whole.astype(jnp.bfloat16).reshape(4, 2, 16, 1280)
        return carry

    for x in range(4):
        lax.fori_loop(4 * x, 4 * x + 4, pack, 0)
        copy = share(x)
        copy.start()
        started.append(copy)

    def net(part, step, by, source, target):
        axis = PART_ORDER[part][2 - step]
        return pltpu.make_async_remote_copy(
            src_ref=source,
            dst_ref=target,
            send_sem=net_send.at[part, step, by - 1],
            recv_sem=net_recv.at[part, step, by - 1],
            device_id=device_at(*shifted(spot, axis, by), core),
            device_id_type=MESH,
        )

    def small(axis, by, source, slot):
        device = twin if axis == 3 else device_at(*shifted(spot, axis, by), core)
        return pltpu.make_async_remote_copy(
            src_ref=source,
            dst_ref=small_in.at[axis, slot],
            send_sem=small_send.at[axis, by - 1],
            recv_sem=small_recv.at[axis, by - 1],
            device_id=device,
            device_id_type=MESH,
        )

    copy = small(3, 1, small_sum.at[3], core)
    copy.start()
    started.append(copy)

    for x in range(4):
        share(x).wait_recv()

        def add_pair(index, carry, x=x):
            z, y = index // 4, index % 4
            held[x, z, y] = (
                grads_ref[x, z, y, core].astype(jnp.float32) + twin_in[x, z, y].astype(jnp.float32)
            ).astype(jnp.bfloat16)
            return carry

        lax.fori_loop(0, 16, add_pair, 0, unroll=2)

    def lanes_of(part):
        return pl.ds(PART_START[part], PART_LANES[part])

    for part in range(3):
        axis = PART_ORDER[part][2]
        for by in (1, 2, 3):
            at = shifted(spot, axis, by)[axis]
            index = tuple(at if a == axis else slice(None) for a in range(3))
            copy = net(
                part, 0, by, held.at[(*index, slice(None), lanes_of(part))], in_one[part].at[by - 1]
            )
            copy.start()
            started.append(copy)

    small(3, 1, small_sum.at[3], 1 - core).wait_recv()
    small_in[3, core] = small_sum[3]
    small_sum[0] = small_in[3, 0] + small_in[3, 1]
    for by in (1, 2, 3):
        copy = small(0, by, small_sum.at[0], spot[0])
        copy.start()
        started.append(copy)

    def small_step(axis):
        for by in (1, 2, 3):
            small(axis, by, small_sum.at[axis], shifted(spot, axis, -by)[axis]).wait_recv()
        small_in[axis, spot[axis]] = small_sum[axis]
        total = small_in[axis, 0] + small_in[axis, 1] + small_in[axis, 2] + small_in[axis, 3]
        if axis == 2:
            total_ref[...] = total
            return
        small_sum[axis + 1] = total
        for by in (1, 2, 3):
            copy = small(axis + 1, by, small_sum.at[axis + 1], spot[axis + 1])
            copy.start()
            started.append(copy)

    for part in range(3):
        first, second, third = PART_ORDER[part]
        for by in (1, 2, 3):
            net(part, 0, by, in_one[part].at[by - 1], in_one[part].at[by - 1]).wait_recv()
        rest = tuple(a for a in (0, 1, 2) if a != third)
        lanes = slice(PART_START[part], PART_START[part] + PART_LANES[part])

        def add_four(index, carry, part=part, third=third, rest=rest, lanes=lanes):
            at = {rest[0]: index // 4, rest[1]: index % 4, third: spot[third]}
            total = held[at[0], at[1], at[2], :, lanes].astype(jnp.float32)
            for by in range(3):
                total = total + in_one[part][by, index // 4, index % 4].astype(jnp.float32)
            sum_one[part][index // 4, index % 4] = total.astype(jnp.bfloat16)
            return carry

        lax.fori_loop(0, 16, add_four, 0, unroll=2)
        for by in (1, 2, 3):
            at = shifted(spot, second, by)[second]
            source = sum_one[part].at[at] if second == rest[0] else sum_one[part].at[:, at]
            copy = net(part, 1, by, source, in_two[part].at[by - 1])
            copy.start()
            started.append(copy)
    small_step(0)

    for copy in kept:
        copy.wait()
    for kind in (0, 1):
        for by in range(1, 8):
            expert(kind, by).wait_recv()

    def sum_eight(source, rows):
        total = source[0, rows].astype(jnp.float32)
        for by in range(1, 8):
            total = total + source[by, rows].astype(jnp.float32)
        return total

    def expert_rows(index, carry):
        rows = pl.ds(pl.multiple_of(index * 16, 16), 16)
        gate_out[rows] = sum_eight(gate_up_in, rows)
        up_out[rows] = sum_eight(gate_up_in, pl.ds(pl.multiple_of(96 + index * 16, 16), 16))
        return carry

    lax.fori_loop(0, 6, expert_rows, 0)

    def down_rows(index, carry):
        rows = pl.ds(pl.multiple_of(index * 16, 16), 16)
        down_out[rows] = sum_eight(down_in, rows)
        return carry

    lax.fori_loop(0, 8, down_rows, 0)

    for part in range(3):
        first, second, third = PART_ORDER[part]
        for by in (1, 2, 3):
            net(part, 1, by, in_two[part].at[by - 1], in_two[part].at[by - 1]).wait_recv()
        rest = tuple(a for a in (0, 1, 2) if a != third)
        for index in range(4):
            if second == rest[0]:
                total = sum_one[part][spot[second], index].astype(jnp.float32)
            else:
                total = sum_one[part][index, spot[second]].astype(jnp.float32)
            for by in range(3):
                total = total + in_two[part][by, index].astype(jnp.float32)
            sum_two[part][index] = total.astype(jnp.bfloat16)
        for by in (1, 2, 3):
            at = shifted(spot, first, by)[first]
            copy = net(part, 2, by, sum_two[part].at[at], in_three[part].at[by - 1])
            copy.start()
            started.append(copy)
    small_step(1)

    for by in range(1, 8):

        @pl.when(ctx + by < 8)
        def _(by=by):
            block_copy(by, ctx).wait_recv()
            own_ref[...] += block_in[by - 1].astype(jnp.float32)

        @pl.when(ctx - by >= 0)
        def _(by=by):
            block_copy(by, ctx - by).wait_send()

    wide = mine_ref[:BLK].astype(jnp.float32)
    scale = rms_rows(wide)
    weighted = own_ref[...] * gain_one
    tokens_grad_ref[...] = (
        state_grad_ref[...]
        + scale * weighted
        - wide * (scale**3 * jnp.mean(weighted * wide, axis=-1, keepdims=True))
    )
    finals = []
    for part in range(3):
        first = PART_ORDER[part][0]
        for by in (1, 2, 3):
            net(part, 2, by, in_three[part].at[by - 1], in_three[part].at[by - 1]).wait_recv()
        total = sum_two[part][spot[first]].astype(jnp.float32)
        for by in range(3):
            total = total + in_three[part][by].astype(jnp.float32)
        finals.append(total)
    final = jnp.concatenate(finals, axis=1)
    sums_ref[:16] = final[:, :768]
    sums_ref[16:] = jnp.concatenate([final[:8, 768:1152], final[8:, 768:1152]], axis=1)
    few_ref[...] = final[:8, 1152:]
    small_step(2)
    for copy in started:
        copy.wait_send()


def run_back(blocks, weights, smalls, prev, wres, routes, cot, kept, back_rows, back_grads, d_gate_up, d_down):
    vmem, anywhere = pl.BlockSpec(memory_space=pltpu.VMEM), pl.BlockSpec(memory_space=pl.ANY)
    shape = jax.ShapeDtypeStruct
    low, wide = jnp.bfloat16, jnp.float32
    dma = pltpu.SemaphoreType.DMA
    left, right, small = (jnp.asarray(t.T, low) for t in placing_tables())
    by_part = lambda *lead: [pltpu.VMEM((*lead, 16, lanes), low) for lanes in PART_LANES]
    return pl.pallas_call(
        back_kernel,
        out_shape=[
            shape((BLK, WIDTH), low),
            shape((16, BLK), wide),
            shape((16, 128), wide),
            shape((BLK, WIDTH), wide),
            shape((24, WIDTH), wide),
            shape((8, 128), wide),
            shape((96, 1024), wide),
            shape((96, 1024), wide),
            shape((128, WIDTH), wide),
        ],
        in_specs=[anywhere] + [vmem] * 18 + [anywhere] * 2 + [vmem] * 4 + [anywhere] * 2,
        out_specs=[vmem] * 9,
        scratch_shapes=[
            pltpu.VMEM((HEADS, 128, BLK), low),
            pltpu.VMEM((HEADS, 128, BLK), low),
            pltpu.VMEM((PAIRS, 2 * BLK, 128), low),
            pltpu.VMEM((PAIRS, 2 * BLK, 128), low),
            pltpu.VMEM((BLK, BLK), wide),
            pltpu.VMEM((16, BLK), wide),
            pltpu.VMEM((WIDTH, BLK), wide),
            pltpu.VMEM((1, WIDTH), wide),
            pltpu.VMEM((BLK, WIDTH), low),
            pltpu.VMEM((BLK, WIDTH), low),
            pltpu.VMEM((128, BLK), wide),
            pltpu.VMEM((128, 128), wide),
            pltpu.VMEM((4, WIDTH, WIDTH), wide),
            pltpu.VMEM((WIDTH, 128), wide),
            pltpu.VMEM((2, 2, PAIRS, BLK, 128), low),
            pltpu.VMEM((2, BLK + 16, WIDTH), low),
            pltpu.VMEM((BLK + 16, WIDTH), low),
            dma((2, 3)),
            pltpu.VMEM((BLK, WIDTH), wide),
            pltpu.VMEM((BLK, WIDTH), wide),
            pltpu.VMEM((8, BLK, WIDTH), low),
            pltpu.VMEM((4, 4, 4, 2, 16, 1280), low),
            pltpu.VMEM((7, BLK, WIDTH), low),
            pltpu.VMEM((8, 192, 1024), low),
            pltpu.VMEM((8, 128, WIDTH), low),
            pltpu.VMEM((4, 4, 16, 128), wide),
            pltpu.VMEM((4, 16, 128), wide),
            dma((7,)),
            dma((7,)),
            dma((2, 7)),
            dma((2, 7)),
            dma((3,)),
            dma((3, 3, 3)),
            dma((3, 3, 3)),
            dma((4,)),
            dma((4,)),
            dma((4, 3)),
            dma((4, 3)),
            pltpu.VMEM((4, 4, 4, 16, 1280), low),
            pltpu.VMEM((4, 4, 4, 16, 1280), low),
            *by_part(3, 4, 4),
            *by_part(3, 4),
            *by_part(3),
            *by_part(4, 4),
            *by_part(4),
        ],
        name="back",
        compiler_params=pltpu.CompilerParams(
            collective_id=2, has_side_effects=True, vmem_limit_bytes=62 * 2**20
        ),
    )(
        blocks, weights, smalls, *rope_tables(), left, right, small, prev, wres, routes, cot,
        *kept, back_rows, back_grads, d_gate_up, d_down,
    )


def finish_kernel(
    out_in, tokens_in, gate_in, up_in, down_in, prev_in, total_in, sums_in, few_in,
    out, tokens_grad, gate, up, down, prev, total, sum_q, sum_k, sum_v, sum_o,
    gain_one, gain_two, router, constant, vectors, prev_at, total_at, sums_at, few_at, sems,
):
    pairs = (
        (prev_in, prev_at), (total_in, total_at), (sums_in, sums_at), (few_in, few_at),
        (tokens_in, tokens_grad), (out_in, out), (gate_in, gate), (up_in, up), (down_in, down),
    )
    copies = [
        pltpu.make_async_copy(source, target, sems.at[index])
        for index, (source, target) in enumerate(pairs)
    ]
    for copy in copies:
        copy.start()
    for copy in copies[:4]:
        copy.wait()
    prev[:, 0, :] = prev_at[:NALL]
    total[...] = total_at[:NALL, :NALL]
    for weight, ref in enumerate((sum_q, sum_k, sum_v, sum_o)):
        ref[...] = sums_at[weight * 6 : weight * 6 + 6]
    few = few_at[...]
    router[...] = few[:6, :NALL]
    tall = jnp.concatenate([few, jnp.zeros((120, 128), jnp.float32)], axis=0).T
    constant[...] = tall[12:16, :6]
    vectors[...] = tall[16:18, :6]
    gain_one[...] = tall[18:19, :6]
    gain_two[...] = tall[19:20, :6]
    for copy in copies[4:]:
        copy.wait()


def finish(out, tokens_grad, gate, up, down, prev, total, sums, few):
    vmem = pl.BlockSpec(memory_space=pltpu.VMEM)
    shape = jax.ShapeDtypeStruct
    wide = jnp.float32
    like = [shape(a.shape, a.dtype) for a in (out, tokens_grad, gate, up, down)]
    few_shapes = [(1, 6), (1, 6), (6, NALL), (4, 6), (2, 6)]
    return pl.pallas_call(
        finish_kernel,
        out_shape=like
        + [shape((NALL, 1, BLK), wide), shape((NALL, NALL), wide)]
        + [shape((6, WIDTH), wide)] * 4
        + [shape(s, wide) for s in few_shapes],
        in_specs=[pl.BlockSpec(memory_space=pl.ANY)] * 9,
        out_specs=[vmem] * 16,
        scratch_shapes=[
            *(pltpu.VMEM(a.shape, a.dtype) for a in (prev, total, sums, few)),
            pltpu.SemaphoreType.DMA((9,)),
        ],
        name="finish",
        compiler_params=pltpu.CompilerParams(vmem_limit_bytes=62 * 2**20),
    )(out, tokens_grad, gate, up, down, prev, total, sums, few)


def on_device(
    tokens, prev_logits, routes, segments, rank_order, norm_first, w_query, w_key, w_value, w_output,
    norm_second, w_router, w_residual, w_constant, v_constant, w_gate, w_up, w_down, cotangent,
):
    few = [w_router, w_constant.T, v_constant.T, norm_first[None], norm_second[None]]
    prev = jnp.transpose(prev_logits, (2, 0, 1))
    (
        state, normed, att, lse, q, keys, values, rows, grads, info, proj, blocks, weights, smalls, gate_up,
    ) = run_front(
        [w_query, w_key, w_value, w_output], few, tokens[0], segments, w_gate[0], w_up[0],
        prev, w_residual, routes[0].T, rank_order[0], cotangent[0],
    )
    back_rows, back_grads, d_gate_up, d_down = run_experts(rows, grads, gate_up, w_down[0])
    (
        out, prev_grad, residual, tokens_grad, sums, small, d_gate, d_up, d_down,
    ) = run_back(
        blocks, weights, smalls, prev, w_residual, routes[0].T, cotangent[0],
        (state, normed, att, lse, q, keys, values, info, proj), back_rows, back_grads,
        d_gate_up, d_down,
    )
    (
        out, tokens_grad, d_gate, d_up, d_down, prev_grad, residual, sum_q, sum_k, sum_v, sum_o,
        gain_one, gain_two, router, constant, vectors,
    ) = finish(out, tokens_grad, d_gate, d_up, d_down, prev_grad, residual, sums, small)
    return (
        out[None],
        tokens_grad[None],
        jnp.transpose(prev_grad, (1, 2, 0)),
        gain_one[0],
        sum_q,
        sum_k,
        sum_v,
        sum_o,
        gain_two[0],
        router,
        residual,
        constant.T,
        vectors.T,
        d_gate[None],
        d_up[None],
        d_down[None],
    )


def solution(mesh):
    in_specs = (
        P("fsdp", "ctx", None),
        P("fsdp", "ctx", None),
        P("fsdp", "ctx", None),
        P("fsdp", "ctx"),
        P("fsdp", "ctx", None),
        P(("ctx", "fsdp")),
        P(("ctx", "fsdp"), None),
        P(("ctx", "fsdp"), None),
        P(("ctx", "fsdp"), None),
        P(("ctx", "fsdp"), None),
        P(("ctx", "fsdp")),
        P(("ctx", "fsdp"), None),
        P(),
        P(("ctx", "fsdp"), None),
        P(("ctx", "fsdp"), None),
        P("fsdp", "ctx", None),
        P("fsdp", "ctx", None),
        P("fsdp", "ctx", None),
        P("fsdp", "ctx", None),
    )
    out_specs = (
        P("fsdp", "ctx", None),
        P("fsdp", "ctx", None),
        P("fsdp", "ctx", None),
        P(("ctx", "fsdp")),
        P(("ctx", "fsdp"), None),
        P(("ctx", "fsdp"), None),
        P(("ctx", "fsdp"), None),
        P(("ctx", "fsdp"), None),
        P(("ctx", "fsdp")),
        P(("ctx", "fsdp"), None),
        P(),
        P(("ctx", "fsdp"), None),
        P(("ctx", "fsdp"), None),
        P("fsdp", "ctx", None),
        P("fsdp", "ctx", None),
        P("fsdp", "ctx", None),
    )
    return jax.shard_map(
        on_device, mesh=mesh, in_specs=in_specs, out_specs=out_specs, check_vma=False
    )
```

```python
import functools

import jax
import jax.numpy as jnp
import numpy as np
from jax import lax
from jax.experimental import pallas as pl
from jax.experimental.pallas import tpu as pltpu
from jax.sharding import PartitionSpec as P

HEADS = 12
HDIM = 64
EXPERTS = 8
NALL = 12
CAP = 54
WIDTH = HEADS * HDIM
PAIRS = HEADS // 2
BLK = 256
SLOTS = 64

highest = lax.Precision.HIGHEST
masked_score = -1e30
epsilon = 1e-06

MESH = pl.DeviceIdType.MESH
PART_LANES = (512, 384, 384)
PART_START = (0, 512, 896)
PART_ORDER = ((0, 1, 2), (1, 2, 0), (2, 0, 1))


def place():
    ctx = lax.axis_index("ctx")
    fsdp = lax.axis_index("fsdp")
    return ctx // 2, (ctx % 2) * 2 + fsdp // 8, (fsdp // 2) % 4, fsdp % 2


def device_at(x, z, y, core):
    return {"ctx": x * 2 + z // 2, "fsdp": (z % 2) * 8 + y * 2 + core}


def shifted(spot, axis, by):
    moved = list(spot)
    moved[axis] = (moved[axis] + by) % 4
    return tuple(moved)


def greet(devices):
    barrier = pltpu.get_barrier_semaphore()
    for device in devices:
        pl.semaphore_signal(barrier, inc=1, device_id=device, device_id_type=MESH)
    pl.semaphore_wait(barrier, len(devices))


def torus_peers(spot, core):
    peers = [device_at(*shifted(spot, axis, by), core) for axis in range(3) for by in (1, 2, 3)]
    return peers + [device_at(*spot, 1 - core)]


def sequence_peers(spot, core):
    x, z, y = spot
    return [device_at((x + by) % 4, (z + 2) % 4, y, core) for by in (1, 2, 3)]


def region(ref, spot, core, whole):
    return ref.at[
        tuple(slice(None) if axis in whole else spot[axis] for axis in range(3)) + (core,)
    ]


def placing_tables():
    left = np.zeros((192, 256), np.float32)
    right = np.zeros((192, 256), np.float32)
    small = np.zeros((48, 128), np.float32)
    for device in range(8):
        for weight in range(4):
            for row in range(6):
                at, line = weight * 48 + device * 6 + row, weight * 6 + row
                if line < 16:
                    left[at, device * 16 + line] = right[at, device * 16 + line] = 1
                else:
                    left[at, 128 + device * 16 + line - 16] = 1
                    right[at, 128 + device * 16 + line - 8] = 1
        for row in range(6):
            small[device * 6 + row, device * 16 + row] = 1
    return left, right, small


def rope_tables():
    frequency = 10000.0 ** (-2.0 * (np.arange(128) % 32) / HDIM)
    inner = np.arange(BLK)[:, None] * frequency
    outer = (np.arange(8) * BLK)[:, None] * frequency
    return [jnp.asarray(t, jnp.float32) for t in (np.cos(inner), np.sin(inner), np.cos(outer), np.sin(outer))]


def turning(index, tables):
    cos_in, sin_in, cos_out, sin_out = tables
    ca, sa = cos_out[pl.ds(index, 1), :], sin_out[pl.ds(index, 1), :]
    cb, sb = cos_in[...], sin_in[...]
    lower = lax.broadcasted_iota(jnp.int32, (BLK, 128), 1) % HDIM < HDIM // 2
    sine = sa * cb + ca * sb
    return ca * cb - sa * sb, jnp.where(lower, -sine, sine)


def swapped(values):
    lower = lax.broadcasted_iota(jnp.int32, values.shape, 1) % HDIM < HDIM // 2
    return jnp.where(lower, pltpu.roll(values, 96, 1), pltpu.roll(values, 32, 1))


def dot(left, right):
    return jnp.dot(left, right, preferred_element_type=jnp.float32)


def dot_nt(left, right):
    return lax.dot_general(left, right, (((1,), (1,)), ((), ())), preferred_element_type=jnp.float32)


def column(row):
    return jnp.broadcast_to(row, (128, row.shape[1])).T[:, 0:1]


def mask_bias(key_block, query_block, bias_ref, ctx, index):
    key_seg = column(key_block[BLK:, :BLK].astype(jnp.float32)[:1])
    query_seg = query_block[BLK:, :BLK].astype(jnp.float32)[:1]
    key_pos = lax.broadcasted_iota(jnp.int32, (BLK, BLK), 0)
    query_pos = lax.broadcasted_iota(jnp.int32, (BLK, BLK), 1)
    reach = jnp.where(index == ctx, 0, BLK)
    allowed = (key_seg == query_seg) & (key_pos <= query_pos + reach)
    bias_ref[...] = jnp.where(allowed, 0.0, masked_score)


def rms_rows(values):
    return lax.rsqrt(jnp.mean(values * values, axis=-1, keepdims=True) + epsilon)


def pick(onehot, values):
    return jnp.sum(jnp.where(onehot, values, 0.0), axis=1, keepdims=True)


def lane_is(lanes):
    return lax.broadcasted_iota(jnp.int32, (BLK, 128), 1) == lanes


def dot_tn(left, right):
    return lax.dot_general(left, right, (((0,), (0,)), ((), ())), preferred_element_type=jnp.float32)


def row_tile(values):
    *weights, small = values
    rows = jnp.concatenate([w.astype(jnp.float32) for w in weights], axis=0)
    tail = jnp.concatenate([rows[16:, :384], rows[16:, 384:]], axis=0)
    return jnp.concatenate([rows[:16], tail, small], axis=1).astype(jnp.bfloat16)


def forward_kernel(
    wq_ref, wk_ref, wv_ref, wo_ref, router_ref, constant_ref, vector_ref, gain_one_ref, gain_two_ref,
    tokens_ref, segments_in, gate_in, up_in, down_in,
    left_ref, right_ref, place_ref, cos_in, sin_in, cos_out, sin_out,
    prev_ref, wres_ref, routes_ref, rank_ref, cot_ref,
    state_ref, normed_ref, att_ref, lse_ref, q_ref, keys_ref, values_ref,
    info_ref, proj_ref, blocks_ref, w_ref, small_ref, pay_ref,
    back_rows_ref, back_grads_ref, d_gate_up_ref, d_down_ref,
    part_a, part_b, part_c, own_ref, qt_ref, vt_ref, bias_ref, max_ref, sum_ref, acc_ref,
    prev_pad, wres_pad, few_wide, few_tall, kv_ref, rows_ref, grads_ref,
    gate_w, up_w, down_w, x_ref, g_ref, gate_ref, up_ref, hidden_ref, d_gate, d_up,
    mine_ref, twin_out, twin_in,
    net_send, net_recv, twin_send, twin_recv, own_sem, ring_send, ring_recv, kv_sem,
    load_sem, send_sem, recv_sem, share_send, share_recv, half_send, half_recv, ret_send, ret_recv,
    keep_sem,
):
    parts = (part_a, part_b, part_c)
    tables = (cos_in, sin_in, cos_out, sin_out)
    ctx, fsdp = lax.axis_index("ctx"), lax.axis_index("fsdp")
    along, side = ctx // 2, ctx % 2
    *spot, core = place()
    spot = tuple(spot)
    twin = device_at(*spot, 1 - core)
    few_wide[...] = jnp.zeros_like(few_wide)
    few_wide[12:16, :6] = constant_ref[...].astype(jnp.float32)
    few_wide[16:18, :6] = vector_ref[...].astype(jnp.float32)
    few_wide[18:19, :6] = gain_one_ref[...].astype(jnp.float32)
    few_wide[19:20, :6] = gain_two_ref[...].astype(jnp.float32)
    few_tall[...] = few_wide[...].T[:16]
    few_tall[:6, :NALL] = router_ref[...].astype(jnp.float32)
    own_ref[...] = row_tile([wq_ref[...], wk_ref[...], wv_ref[...], wo_ref[...], few_tall[...]])
    marks = jnp.concatenate(
        [segments_in[...].astype(jnp.float32), jnp.zeros((1, WIDTH - BLK), jnp.float32)], axis=1
    )
    blocks_ref[ctx, :BLK] = tokens_ref[...]
    blocks_ref[ctx, BLK:] = jnp.broadcast_to(marks, (16, WIDTH)).astype(jnp.bfloat16)
    chip = fsdp // 2

    def at_expert(where, on):
        return {"ctx": ctx, "fsdp": where * 2 + on}

    greet(
        torus_peers(spot, core)
        + [at_expert((chip + by) % EXPERTS, core) for by in range(1, EXPERTS)]
    )

    def net(part, step, by, source, target):
        axis = PART_ORDER[part][step]
        return pltpu.make_async_remote_copy(
            src_ref=source,
            dst_ref=target,
            send_sem=net_send.at[part, step, by - 1],
            recv_sem=net_recv.at[part, step, by - 1],
            device_id=device_at(*shifted(spot, axis, by), core),
            device_id_type=MESH,
        )

    def share(part, slot, source, target):
        return pltpu.make_async_remote_copy(
            src_ref=source,
            dst_ref=target,
            send_sem=twin_send.at[part, slot],
            recv_sem=twin_recv.at[part, slot],
            device_id=twin,
            device_id_type=MESH,
        )

    payloads = ((blocks_ref, (0, 64, 144, 224, BLK + 16)), (pay_ref, (0, 64, 144, 224, 288)))
    spans = {"all": (0, 4), "p": (1, 3), "h1": (0, 2), "h2": (2, 4), "q1": (0, 1), "p1": (1, 2), "p2": (2, 3), "q2": (3, 4)}
    messages = (
        (1, (0, 0), "all"), (-1, (0, 0), "all"), (0, (0, 0), "all"),
        (1, (0, 1), "p"), (-1, (0, 1), "p"),
        (1, (-1, 0), "h1"), (-1, (1, 0), "h2"),
        (0, (-1, 0), "q1"), (0, (-1, 0), "q2"), (0, (1, 0), "q1"), (0, (1, 0), "q2"),
        (1, (-1, 1), "p1"), (-1, (1, 1), "p2"),
        (0, (2, 0), "q1"), (0, (2, 0), "q2"),
    )

    def ring(kind, number, arriving=False):
        to, (steps, across_it), rows = messages[number]
        if arriving:
            steps = steps - to
            across_it = across_it if to else 1 - across_it
        array, cuts = payloads[kind]
        first, last = (cuts[i] for i in spans[rows])
        on = side if across_it == 0 else 1 - side
        view = array.at[((along + steps + 4) % 4) * 2 + on, pl.ds(first, last - first)]
        target = ((along + to + 4) % 4) * 2 + (side if to else 1 - side)
        return pltpu.make_async_remote_copy(
            src_ref=view,
            dst_ref=view,
            send_sem=ring_send.at[kind, number],
            recv_sem=ring_recv.at[kind, number],
            device_id={"ctx": target, "fsdp": fsdp},
            device_id_type=MESH,
        )

    def pass_on(kind, stage):
        plan = (
            ((None, (0, 1, 2)),),
            ((2, (3, 4)),),
            ((0, (5, 7, 8)), (1, (6, 9, 10))),
            ((3, (11,)), (4, (12,)), (5, (13,)), (6, (14,))),
            tuple((number, ()) for number in range(7, 15)),
        )[stage]
        for number, then in plan:
            if number is not None:
                ring(kind, number, arriving=True).wait_recv()
            for follow in then:
                ring(kind, follow).start()

    started = []
    kept = []
    for part in range(3):
        own = own_ref.at[:, pl.ds(PART_START[part], PART_LANES[part])]
        mine = region(parts[part], spot, core, ())
        for by in (1, 2, 3):
            copy = net(part, 0, by, own, mine)
            copy.start()
            started.append(copy)
    for part in range(3):
        own = own_ref.at[:, pl.ds(PART_START[part], PART_LANES[part])]
        mine = region(parts[part], spot, core, ())
        copy = pltpu.make_async_copy(own, mine, own_sem.at[part])
        copy.start()
        kept.append(copy)
        copy = share(part, 0, own, mine)
        copy.start()
        started.append(copy)
    tail = [(down_in.at[:96], pay_ref.at[ctx, 192:, pl.ds(0, WIDTH)])] + [
        (down_in.at[96:, pl.ds(256 * m, 256)], pay_ref.at[ctx, pl.ds(192 + 32 * m, 32), pl.ds(WIDTH, 256)])
        for m in range(3)
    ]
    pieces = [(gate_in, pay_ref.at[ctx, :96]), (up_in, pay_ref.at[ctx, 96:192]), *tail]
    own_experts = [
        pltpu.make_async_copy(source, target, own_sem.at[3 + number])
        for number, (source, target) in enumerate(pieces)
    ]
    for copy in own_experts:
        copy.start()
    for copy in kept + own_experts:
        copy.wait()
    for step in range(3):
        for part in range(3):
            order = PART_ORDER[part]
            axis = order[step]
            whole = order[:step]
            for by in (1, 2, 3):
                here = region(parts[part], shifted(spot, axis, -by), core, whole)
                net(part, step, by, here, here).wait_recv()
                copy = share(part, 1 + step * 3 + by - 1, here, here)
                copy.start()
                started.append(copy)
            if step < 2:
                held = region(parts[part], spot, core, order[: step + 1])
                for by in (1, 2, 3):
                    copy = net(part, step + 1, by, held, held)
                    copy.start()
                    started.append(copy)
        if step == 1:
            pass_on(0, 0)
    for part in range(3):
        order = PART_ORDER[part]
        first = region(parts[part], spot, 1 - core, ())
        share(part, 0, first, first).wait_recv()
        for step in range(3):
            for by in (1, 2, 3):
                here = region(
                    parts[part], shifted(spot, order[step], -by), 1 - core, order[:step]
                )
                share(part, 1 + step * 3 + by - 1, here, here).wait_recv()

    def unpack(group, carry):
        a, b, c = (
            part[group // 4, group % 4].reshape(128, lanes)
            for part, lanes in zip(parts, PART_LANES, strict=True)
        )
        tail = jnp.concatenate([b[:, 256:], c[:, :256]], axis=1)
        left = dot(left_ref[...], jnp.concatenate([a[:, :384], tail], axis=0))
        right_rows = jnp.concatenate([a[:, 384:], b[:, :256]], axis=1)
        right = dot(right_ref[...], jnp.concatenate([right_rows, tail], axis=0))
        rows = pl.ds(pl.multiple_of(group * 48, 16), 48)
        for weight in range(4):
            w_ref[weight, rows, :384] = left[weight * 48 : weight * 48 + 48].astype(jnp.bfloat16)
            w_ref[weight, rows, 384:] = right[weight * 48 : weight * 48 + 48].astype(jnp.bfloat16)
        small_ref[rows] = dot(place_ref[...], c[:, 256:]).astype(jnp.bfloat16)
        return carry

    pass_on(0, 1)
    lax.fori_loop(0, 16, unpack, 0)
    across = small_ref[...].astype(jnp.float32).T
    gain_one, gain_two = across[18:19], across[19:20]

    def normed_block(index):
        wide = blocks_ref[index, :BLK].astype(jnp.float32)
        return (wide * rms_rows(wide) * gain_one).astype(jnp.bfloat16)

    query = dot(normed_block(ctx), w_ref[0])
    cosine, sine = turning(ctx, tables)
    for pair in range(PAIRS):
        part = query[:, pair * 128 : pair * 128 + 128]
        turned = (part * cosine + swapped(part) * sine) * (HDIM**-0.5)
        q_ref[pair] = turned.astype(jnp.bfloat16)
        across_q = turned.T.astype(jnp.bfloat16)
        blank = jnp.zeros((HDIM, BLK), jnp.bfloat16)
        qt_ref[2 * pair] = jnp.concatenate([across_q[:HDIM], blank], axis=0)
        qt_ref[2 * pair + 1] = jnp.concatenate([blank, across_q[HDIM:]], axis=0)
    max_ref[...] = jnp.full(max_ref.shape, masked_score, jnp.float32)
    sum_ref[...] = jnp.zeros_like(sum_ref)
    acc_ref[...] = jnp.zeros_like(acc_ref)

    def keep_block(index, slot):
        return [
            pltpu.make_async_copy(kv_ref.at[slot, kind], target.at[index], kv_sem.at[slot, kind])
            for kind, target in enumerate((keys_ref, values_ref))
        ]

    def block_at(step):
        odd = step % 2
        x = along - (step + odd) // 2 + odd * side
        return jnp.where(step == 0, ctx, x * 2 + 1 - odd)

    def block(step, carry):
        index = block_at(step)
        slot = step % 2

        @pl.when(step >= 2)
        def _():
            for copy in keep_block(block_at(step - 2), slot):
                copy.wait()

        normed = normed_block(index)
        key = dot(normed, w_ref[1])
        value = dot(normed, w_ref[2])
        cosine, sine = turning(index, tables)
        for pair in range(PAIRS):
            lanes = slice(pair * 128, pair * 128 + 128)
            part = key[:, lanes]
            kv_ref[slot, 0, pair] = (part * cosine + swapped(part) * sine).astype(jnp.bfloat16)
            kv_ref[slot, 1, pair] = value[:, lanes].astype(jnp.bfloat16)
            vt_ref[lanes, :] = value[:, lanes].T.astype(jnp.bfloat16)
        mask_bias(blocks_ref.at[index], blocks_ref.at[ctx], bias_ref, ctx, index)
        for head in range(HEADS):
            rows = slice(head * HDIM, head * HDIM + HDIM)
            scores = dot(kv_ref[slot, 0, head // 2], qt_ref[head]) + bias_ref[...]
            before = max_ref[head : head + 1]
            top = jnp.maximum(before, jnp.max(scores, axis=0, keepdims=True))
            weights = jnp.exp(scores - top)
            shrink = jnp.exp(before - top)
            sum_ref[head : head + 1] = sum_ref[head : head + 1] * shrink + jnp.sum(
                weights, axis=0, keepdims=True
            )
            max_ref[head : head + 1] = top
            acc_ref[rows] = acc_ref[rows] * shrink + dot(vt_ref[rows, :], weights.astype(jnp.bfloat16))

        for copy in keep_block(index, slot):
            copy.start()
        for when, todo in (
            (0, ((0, 2),)),
            (1, ((0, 3), (0, 4), (1, 0))),
            (4, ((1, 1), (1, 2))),
            (6, ((1, 3),)),
        ):

            @pl.when(step == jnp.minimum(ctx, when))
            def _(todo=todo):
                for kind, stage in todo:
                    pass_on(kind, stage)

        return carry

    lax.fori_loop(0, ctx + 1, block, 0)
    for head in range(HEADS):
        rows = slice(head * HDIM, head * HDIM + HDIM)
        att_ref[rows] = acc_ref[rows] / sum_ref[head : head + 1]
    lse_ref[...] = max_ref[...] + jnp.log(jnp.maximum(sum_ref[...], 1e-30))
    attended = att_ref[...].T.astype(jnp.bfloat16)
    state = blocks_ref[ctx, :BLK].astype(jnp.float32) + dot(attended, w_ref[3])
    state_ref[...] = state
    normed_two = (state * rms_rows(state) * gain_two).astype(jnp.bfloat16)
    normed_ref[...] = normed_two

    proj = dot(normed_two, small_ref[...])
    proj_ref[...] = proj
    pad_routing(prev_ref, wres_ref, prev_pad, wres_pad)
    logits = proj + jnp.dot(
        prev_pad[...].T, wres_pad[...], precision=highest, preferred_element_type=jnp.float32
    )
    lanes = lax.broadcasted_iota(jnp.int32, (BLK, 128), 1).astype(jnp.float32)
    routes = routes_ref[...].astype(jnp.float32)
    route_0, route_1 = column(routes[0:1]), column(routes[1:2])
    hot_0, hot_1 = lanes == route_0, lanes == route_1
    chosen_0, chosen_1 = pick(hot_0, logits), pick(hot_1, logits)
    top = jnp.maximum(chosen_0, chosen_1)
    chosen_0, chosen_1 = jnp.exp(chosen_0 - top), jnp.exp(chosen_1 - top)
    gate_0, gate_1 = chosen_0 / (chosen_0 + chosen_1), chosen_1 / (chosen_0 + chosen_1)
    rank = rank_ref[...].astype(jnp.float32)
    earlier = (rank < column(rank)).astype(jnp.float32).astype(jnp.bfloat16)
    slots = dot(earlier, (hot_0 | hot_1).astype(jnp.float32).astype(jnp.bfloat16))

    def target(route, hot):
        slot = pick(hot, slots)
        return jnp.where(
            (route < EXPERTS) & (slot < CAP), route * SLOTS + slot, -1.0
        )

    target_0, target_1 = target(route_0, hot_0), target(route_1, hot_1)
    info = jnp.where(lanes == 0, gate_0, 0.0) + jnp.where(lanes == 1, gate_1, 0.0)
    info = info + jnp.where(lanes == 2, target_0, 0.0) + jnp.where(lanes == 3, target_1, 0.0)
    info_ref[...] = info
    targets = info.T
    rows = lax.broadcasted_iota(jnp.int32, (EXPERTS * SLOTS, BLK), 0).astype(jnp.float32)
    table_0 = (rows == targets[2:3]).astype(jnp.float32).astype(jnp.bfloat16)
    table_1 = (rows == targets[3:4]).astype(jnp.float32).astype(jnp.bfloat16)
    rows_ref[...] = dot(table_0 + table_1, normed_two).astype(jnp.bfloat16)
    upstream = cot_ref[...].astype(jnp.float32)
    grads_ref[...] = dot(
        jnp.concatenate([table_0, table_1], axis=1),
        jnp.concatenate([gate_0 * upstream, gate_1 * upstream], axis=0).astype(jnp.bfloat16),
    ).astype(jnp.bfloat16)
    for back in (0, 1):

        @pl.when(ctx - back >= 0)
        def _(back=back):
            for copy in keep_block(block_at(ctx - back), (ctx - back) % 2):
                copy.wait()

    other = 1 - core
    half = EXPERTS * SLOTS

    def slots(index, on):
        return pl.ds(pl.multiple_of((on * EXPERTS + index) * SLOTS, SLOTS), SLOTS)

    def chunk(index):
        return pl.ds(pl.multiple_of(index * SLOTS, SLOTS), SLOTS)

    buffers = ((rows_ref, x_ref), (grads_ref, g_ref))

    def dispatch(kind, by):
        source, target = buffers[kind]
        where = (chip + by) % EXPERTS
        return pltpu.make_async_remote_copy(
            src_ref=source.at[chunk(where)],
            dst_ref=target.at[slots(chip, core)],
            send_sem=send_sem.at[kind, by - 1],
            recv_sem=recv_sem.at[kind, by - 1],
            device_id=at_expert(where, core),
            device_id_type=MESH,
        )

    def share(kind, by, on):
        source, target = buffers[kind]
        spot = slots((chip - by) % EXPERTS, on)
        return pltpu.make_async_remote_copy(
            src_ref=target.at[spot],
            dst_ref=target.at[spot],
            send_sem=share_send.at[kind, by],
            recv_sem=share_recv.at[kind, by],
            device_id=at_expert(chip, other),
            device_id_type=MESH,
        )

    def exchange(kind):
        return pltpu.make_async_remote_copy(
            src_ref=twin_out.at[kind],
            dst_ref=twin_in.at[kind],
            send_sem=half_send.at[kind],
            recv_sem=half_recv.at[kind],
            device_id=at_expert(chip, other),
            device_id_type=MESH,
        )

    returned = (back_rows_ref, back_grads_ref)

    def give_back(kind, by):
        where = (chip + by) % EXPERTS
        return pltpu.make_async_remote_copy(
            src_ref=mine_ref.at[kind, chunk(where)],
            dst_ref=returned[kind].at[chunk(chip)],
            send_sem=ret_send.at[kind, by - 1],
            recv_sem=ret_recv.at[kind, by - 1],
            device_id=at_expert(where, core),
            device_id_type=MESH,
        )

    for kind in (0, 1):
        for by in range(1, EXPERTS):
            copy = dispatch(kind, by)
            copy.start()
            started.append(copy)
    for kind in (0, 1):
        source, target = buffers[kind]
        copy = pltpu.make_async_copy(
            source.at[chunk(chip)], target.at[slots(chip, core)], keep_sem.at[kind]
        )
        copy.start()
        copy.wait()
        copy = share(kind, 0, core)
        copy.start()
        started.append(copy)

    def arrive(kind):
        for by in range(1, EXPERTS):
            dispatch(kind, by).wait_recv()
            copy = share(kind, by, core)
            copy.start()
            started.append(copy)

    def arrive_shared(kind):
        for by in range(EXPERTS):
            share(kind, by, other).wait_recv()

    def tiles(on, body):
        def step(index, carry):
            start = pl.multiple_of(on * half + index * 256, 256)
            body(pl.ds(start, 256), pl.ds(pl.multiple_of(index * 256, 256), 256))
            return carry

        lax.fori_loop(0, half // 256, step, 0)

    def forward(on, keep):
        def tile(rows, inner):
            x = x_ref[rows]
            gate, up = dot(x, gate_w[...]), dot(x, up_w[...])
            gate_ref[rows], up_ref[rows] = gate, up
            hidden_ref[rows] = (gate * jax.nn.sigmoid(gate) * up).astype(jnp.bfloat16)

        def result(rows, inner):
            keep(inner, dot(hidden_ref[rows], down_w[...]))

        tiles(on, tile)
        tiles(on, result)

    def backward(on, keep):
        def tile(rows, inner):
            hidden_grad = dot_nt(g_ref[rows], down_w[...])
            gate, up = gate_ref[rows], up_ref[rows]
            sigmoid = jax.nn.sigmoid(gate)
            d_gate[rows] = (
                hidden_grad * up * sigmoid * (1.0 + gate * (1.0 - sigmoid))
            ).astype(jnp.bfloat16)
            d_up[rows] = (hidden_grad * gate * sigmoid).astype(jnp.bfloat16)
            keep(inner, dot_nt(d_gate[rows], gate_w[...]) + dot_nt(d_up[rows], up_w[...]))

        tiles(on, tile)

    def keep_mine(kind):
        def keep(rows, values):
            mine_ref[kind, rows] = values.astype(jnp.bfloat16)

        return keep

    def keep_twin(kind):
        def keep(rows, values):
            twin_out[kind, rows] = values.astype(jnp.bfloat16)

        return keep

    def finish(kind):
        exchange(kind).wait_recv()

        def step(index, carry):
            rows = pl.ds(pl.multiple_of(index * 128, 128), 128)
            mine_ref[kind, rows] = (
                mine_ref[kind, rows].astype(jnp.float32) + twin_in[kind, rows].astype(jnp.float32)
            ).astype(jnp.bfloat16)
            return carry

        lax.fori_loop(0, half // 128, step, 0)
        for by in range(1, EXPERTS):
            copy = give_back(kind, by)
            copy.start()
            started.append(copy)
        copy = pltpu.make_async_copy(
            mine_ref.at[kind, chunk(chip)], returned[kind].at[chunk(chip)], keep_sem.at[kind]
        )
        copy.start()
        copy.wait()

    def load(owner):
        parts = [
            (pay_ref.at[owner, :96], gate_w.at[pl.ds(pl.multiple_of(owner * 96, 16), 96)]),
            (pay_ref.at[owner, 96:192], up_w.at[pl.ds(pl.multiple_of(owner * 96, 16), 96)]),
            (
                pay_ref.at[owner, 192:, pl.ds(0, WIDTH)],
                down_w.at[pl.ds(pl.multiple_of(owner * 128, 16), 96)],
            ),
        ] + [
            (
                pay_ref.at[owner, pl.ds(192 + 32 * m, 32), pl.ds(WIDTH, 256)],
                down_w.at[pl.ds(pl.multiple_of(owner * 128 + 96, 16), 32), pl.ds(256 * m, 256)],
            )
            for m in range(3)
        ]
        return [
            pltpu.make_async_copy(source, target, load_sem.at[owner, number])
            for number, (source, target) in enumerate(parts)
        ]

    pass_on(1, 4)
    for owner in range(8):
        for copy in load(owner):
            copy.start()
    arrive(0)
    for owner in range(8):
        for copy in load(owner):
            copy.wait()
    forward(core, keep_mine(0))
    arrive(1)
    arrive_shared(0)
    forward(other, keep_twin(0))
    copy = exchange(0)
    copy.start()
    started.append(copy)
    backward(core, keep_mine(1))
    finish(0)
    arrive_shared(1)
    backward(other, keep_twin(1))
    copy = exchange(1)
    copy.start()
    started.append(copy)

    def down_tile(index, carry):
        lanes = pl.ds(pl.multiple_of(index * 256, 256), 256)
        part = dot_tn(hidden_ref[:, lanes], g_ref[...]).astype(jnp.bfloat16)
        d_down_ref[2 * index] = part[:128]
        d_down_ref[2 * index + 1] = part[128:]
        return carry

    lax.fori_loop(0, 4, down_tile, 0)
    finish(1)

    def gate_tile(index, carry):
        lanes = pl.ds(pl.multiple_of(index * 256, 256), 256)
        for start, grad in ((0, d_gate), (96, d_up)):
            part = dot_tn(x_ref[...], grad[:, lanes]).astype(jnp.bfloat16)
            for piece in range(8):
                d_gate_up_ref[piece, start : start + 96, lanes] = part[piece * 96 : piece * 96 + 96]
        return carry

    lax.fori_loop(0, 4, gate_tile, 0)
    for kind in (0, 1):
        for by in range(1, EXPERTS):
            give_back(kind, by).wait_recv()
    for kind in (0, 1):
        for number in range(len(messages)):
            ring(kind, number).wait_send()
    for copy in started:
        copy.wait_send()


def pad_routing(prev_ref, wres_ref, prev_pad, wres_pad):
    prev_pad[...] = jnp.zeros_like(prev_pad)
    prev_pad[:NALL] = prev_ref[:, 0, :]
    wres_pad[...] = jnp.zeros_like(wres_pad)
    wres_pad[:NALL, :NALL] = wres_ref[...]


def run_forward(weights, few, tokens, segments, experts, prev, wres, routes, rank, cot):
    vmem, anywhere = pl.BlockSpec(memory_space=pltpu.VMEM), pl.BlockSpec(memory_space=pl.ANY)
    shape = jax.ShapeDtypeStruct
    low, wide = jnp.bfloat16, jnp.float32
    dma = pltpu.SemaphoreType.DMA
    half, whole = EXPERTS * SLOTS, 2 * EXPERTS * SLOTS
    left, right, small = (jnp.asarray(t, low) for t in placing_tables())
    return pl.pallas_call(
        forward_kernel,
        out_shape=[
            shape((BLK, WIDTH), wide),
            shape((BLK, WIDTH), low),
            shape((WIDTH, BLK), wide),
            shape((16, BLK), wide),
            shape((PAIRS, BLK, 128), low),
            shape((8, PAIRS, BLK, 128), low),
            shape((8, PAIRS, BLK, 128), low),
            shape((BLK, 128), wide),
            shape((BLK, 128), wide),
            shape((8, BLK + 16, WIDTH), low),
            shape((4, WIDTH, WIDTH), low),
            shape((WIDTH, 128), low),
            shape((8, 288, 1024), low),
            shape((half, WIDTH), low),
            shape((half, WIDTH), low),
            shape((8, 192, 1024), low),
            shape((8, 128, WIDTH), low),
        ],
        in_specs=[vmem] * 26,
        out_specs=[vmem] * 5 + [anywhere] * 2 + [vmem] * 5 + [anywhere] + [vmem] * 4,
        scratch_shapes=[
            *(pltpu.VMEM((4, 4, 4, 2, 16, lanes), low) for lanes in PART_LANES),
            pltpu.VMEM((16, 1280), low),
            pltpu.VMEM((HEADS, 128, BLK), low),
            pltpu.VMEM((WIDTH, BLK), low),
            pltpu.VMEM((BLK, BLK), wide),
            pltpu.VMEM((16, BLK), wide),
            pltpu.VMEM((16, BLK), wide),
            pltpu.VMEM((WIDTH, BLK), wide),
            pltpu.VMEM((128, BLK), wide),
            pltpu.VMEM((128, 128), wide),
            pltpu.VMEM((128, 128), wide),
            pltpu.VMEM((16, 128), wide),
            pltpu.VMEM((2, 2, PAIRS, BLK, 128), low),
            pltpu.VMEM((half, WIDTH), low),
            pltpu.VMEM((half, WIDTH), low),
            pltpu.VMEM((WIDTH, 1024), low),
            pltpu.VMEM((WIDTH, 1024), low),
            pltpu.VMEM((1024, WIDTH), low),
            pltpu.VMEM((whole, WIDTH), low),
            pltpu.VMEM((whole, WIDTH), low),
            pltpu.VMEM((whole, 1024), wide),
            pltpu.VMEM((whole, 1024), wide),
            pltpu.VMEM((whole, 1024), low),
            pltpu.VMEM((whole, 1024), low),
            pltpu.VMEM((whole, 1024), low),
            pltpu.VMEM((2, half, WIDTH), low),
            pltpu.VMEM((2, half, WIDTH), low),
            pltpu.VMEM((2, half, WIDTH), low),
            dma((3, 3, 3)),
            dma((3, 3, 3)),
            dma((3, 10)),
            dma((3, 10)),
            dma((9,)),
            dma((2, 15)),
            dma((2, 15)),
            dma((2, 2)),
            dma((8, 6)),
            dma((2, 7)),
            dma((2, 7)),
            dma((2, 8)),
            dma((2, 8)),
            dma((2,)),
            dma((2,)),
            dma((2, 7)),
            dma((2, 7)),
            dma((2,)),
        ],
        name="forward",
        compiler_params=pltpu.CompilerParams(
            collective_id=1, has_side_effects=True, vmem_limit_bytes=63 * 2**20
        ),
    )(
        *weights, *few, tokens, segments, *experts, left, right, small, *rope_tables(),
        prev, wres, routes, rank, cot,
    )


def split(values):
    high = values.astype(jnp.bfloat16)
    low = (values - high.astype(jnp.float32)).astype(jnp.bfloat16)
    return jnp.concatenate([high, low], axis=1)


def back_kernel(
    blocks_ref, w_ref, small_ref, cos_in, sin_in, cos_out, sin_out, left_ref, right_ref, place_ref,
    prev_ref, wres_ref, routes_ref, cot_ref,
    state_ref, normed_ref, att_ref, lse_ref, q_ref, keys_ref, values_ref, info_ref, proj_ref,
    back_rows_ref, back_grads_ref, d_gate_up, d_down,
    out_ref, prev_grad_ref, total_ref, tokens_grad_ref, sums_ref, few_ref,
    gate_out, up_out, down_out,
    *scratch,
):
    (
        qt_ref, ot_ref, o_ref, qm_ref, bias_ref, inner_ref, dqt_ref, gain_ref, dk_ref, dv_ref,
        prev_pad, wres_pad, dw_ref, few_sum, kv_ref, tok_ref, mine_ref, kv_sem, own_ref, state_grad_ref, others_ref, grads_ref, block_in,
        gate_up_in, down_in, small_in, small_sum,
        block_send, block_recv, exp_send, exp_recv, load_sem,
        net_send, net_recv, twin_send, twin_recv, small_send, small_recv,
        *more,
    ) = scratch
    twin_in, held, in_one, in_two, in_three, sum_one, sum_two = (
        more[0], more[1], more[2:5], more[5:8], more[8:11], more[11:14], more[14:17]
    )
    tables = (cos_in, sin_in, cos_out, sin_out)
    ctx, fsdp = lax.axis_index("ctx"), lax.axis_index("fsdp")
    *spot, core = place()
    spot = tuple(spot)
    twin = device_at(*spot, 1 - core)
    started = []
    greet(torus_peers(spot, core) + sequence_peers(spot, core))

    def expert(kind, by):
        source, target = ((d_gate_up, gate_up_in), (d_down, down_in))[kind]
        where = (ctx + by) % 8
        return pltpu.make_async_remote_copy(
            src_ref=source.at[where],
            dst_ref=target.at[by],
            send_sem=exp_send.at[kind, by - 1],
            recv_sem=exp_recv.at[kind, by - 1],
            device_id={"ctx": where, "fsdp": fsdp},
            device_id_type=MESH,
        )

    for kind in (0, 1):
        for by in range(1, 8):
            copy = expert(kind, by)
            copy.start()
            started.append(copy)
    kept = [
        pltpu.make_async_copy(d_gate_up.at[ctx], gate_up_in.at[0], load_sem.at[0]),
        pltpu.make_async_copy(d_down.at[ctx], down_in.at[0], load_sem.at[1]),
    ]
    own_block = pltpu.make_async_copy(blocks_ref.at[ctx], mine_ref, load_sem.at[2])
    own_block.start()
    for copy in kept:
        copy.start()

    def load_kv(index, slot):
        return [
            pltpu.make_async_copy(source.at[index], kv_ref.at[slot, kind], kv_sem.at[slot, kind])
            for kind, source in enumerate((keys_ref, values_ref))
        ] + [pltpu.make_async_copy(blocks_ref.at[index], tok_ref.at[slot], kv_sem.at[slot, 2])]

    for copy in load_kv(0, 0):
        copy.start()

    def block_copy(by, target):
        return pltpu.make_async_remote_copy(
            src_ref=others_ref.at[target],
            dst_ref=block_in.at[by - 1],
            send_sem=block_send.at[by - 1],
            recv_sem=block_recv.at[by - 1],
            device_id={"ctx": target, "fsdp": fsdp},
            device_id_type=MESH,
        )

    across = small_ref[...].astype(jnp.float32).T
    gain_one, gain_two = across[18:19], across[19:20]
    value_rows = across[16:18]

    lanes = lax.broadcasted_iota(jnp.int32, (BLK, 128), 1)
    info = info_ref[...]
    gates = (info[:, 0:1], info[:, 1:2])
    slots = lax.broadcasted_iota(jnp.int32, (BLK, EXPERTS * SLOTS), 1).astype(jnp.float32)
    tables_of = [
        (slots == info[:, 2 + k : 3 + k]).astype(jnp.float32).astype(jnp.bfloat16) for k in (0, 1)
    ]
    route_rows = routes_ref[...].astype(jnp.float32)
    routes = (column(route_rows[0:1]), column(route_rows[1:2]))
    hots = [lanes.astype(jnp.float32) == routes[k] for k in (0, 1)]
    named = [
        [(routes[k] == EXPERTS + 1 + kind).astype(jnp.float32) for kind in range(3)] for k in (0, 1)
    ]
    proj = proj_ref[...]
    mixes = []
    for c in (0, 1):
        first, second = proj[:, 12 + 2 * c : 13 + 2 * c], proj[:, 13 + 2 * c : 14 + 2 * c]
        top = jnp.maximum(first, second)
        first, second = jnp.exp(first - top), jnp.exp(second - top)
        mixes.append((first / (first + second), second / (first + second)))
    normed_low = normed_ref[...]
    normed_two = normed_low.astype(jnp.float32)
    upstream_low = cot_ref[...]
    upstream = upstream_low.astype(jnp.float32)
    state = state_ref[...]
    back_rows = back_rows_ref[...]
    result = state
    gate_grads = []
    for k in (0, 1):
        copy, one, two = named[k]
        pair = dot(tables_of[k], back_rows)
        pair = pair + (copy + one * mixes[0][0] + two * mixes[1][0]) * normed_two
        pair = pair + (one * mixes[0][1]) * value_rows[0:1] + (two * mixes[1][1]) * value_rows[1:2]
        result = result + gates[k] * pair
        gate_grads.append(jnp.sum(pair * upstream, axis=1, keepdims=True))
    out_ref[...] = result.astype(jnp.bfloat16)
    inner = gates[0] * gate_grads[0] + gates[1] * gate_grads[1]
    logit_grad = jnp.zeros((BLK, 128), jnp.float32)
    for k in (0, 1):
        logit_grad = logit_grad + jnp.where(hots[k], gates[k] * (gate_grads[k] - inner), 0.0)
    pad_routing(prev_ref, wres_ref, prev_pad, wres_pad)
    prev_grad_ref[...] = lax.dot_general(
        wres_pad[...], logit_grad, (((1,), (1,)), ((), ())),
        precision=highest, preferred_element_type=jnp.float32,
    )[:16]
    small_sum[3] = jnp.dot(
        prev_pad[...], logit_grad, precision=highest, preferred_element_type=jnp.float32
    )[:16]
    on_normed = jnp.sum(normed_two * upstream, axis=1, keepdims=True)
    on_vectors = dot(upstream_low, small_ref[...])
    flat = logit_grad
    weight_up = gates[0] * named[0][0] + gates[1] * named[1][0]
    vector_weights = jnp.zeros((BLK, 128), jnp.float32)
    for c in (0, 1):
        scale = gates[0] * named[0][1 + c] + gates[1] * named[1][1 + c]
        mix_0, mix_1 = mixes[c]
        m_0, m_1 = scale * on_normed, scale * on_vectors[:, 16 + c : 17 + c]
        mean = mix_0 * m_0 + mix_1 * m_1
        flat = flat + jnp.where(lanes == 12 + 2 * c, mix_0 * (m_0 - mean), 0.0)
        flat = flat + jnp.where(lanes == 13 + 2 * c, mix_1 * (m_1 - mean), 0.0)
        weight_up = weight_up + mix_0 * scale
        vector_weights = vector_weights + jnp.where(lanes == 16 + c, mix_1 * scale, 0.0)
    flat_split = split(flat)
    normed_grad = dot_nt(flat_split, jnp.concatenate([small_ref[...]] * 2, axis=1))
    normed_grad = normed_grad + weight_up * upstream
    normed_grad = normed_grad + dot(tables_of[0] + tables_of[1], back_grads_ref[...])
    normed_across = normed_two.T.astype(jnp.bfloat16)
    upstream_across = upstream.T.astype(jnp.bfloat16)
    small_grad = dot(normed_across, flat_split)
    small_vector = dot(upstream_across, split(vector_weights))
    small_grad = small_grad[:, :128] + small_grad[:, 128:] + small_vector[:, :128] + small_vector[:, 128:]
    scale_two = rms_rows(state)
    weighted = normed_grad * gain_two
    state_grad = (
        upstream
        + scale_two * weighted
        - state * (scale_two**3 * jnp.mean(weighted * state, axis=-1, keepdims=True))
    )
    state_grad_ref[...] = state_grad
    gain_two_row = jnp.sum(normed_grad * state * scale_two, axis=0, keepdims=True)
    state_low = state_grad.astype(jnp.bfloat16)
    attended = att_ref[...]
    dw_ref[3] = dot(attended.astype(jnp.bfloat16), state_low)
    att_grad = dot_nt(state_low, w_ref[3])
    blank = jnp.zeros((HDIM, BLK), jnp.bfloat16)
    low_half = lax.broadcasted_iota(jnp.int32, (BLK, 128), 1) < HDIM
    none = jnp.zeros((BLK, 128), jnp.bfloat16)
    inner_ref[...] = jnp.zeros_like(inner_ref)
    for pair in range(PAIRS):
        part = att_grad[:, pair * 128 : pair * 128 + 128].astype(jnp.bfloat16)
        across_o = part.astype(jnp.float32).T
        products = across_o * attended[pair * 128 : pair * 128 + 128]
        across_o = across_o.astype(jnp.bfloat16)
        across_q = q_ref[pair].astype(jnp.float32).T.astype(jnp.bfloat16)
        for half in (0, 1):
            head = 2 * pair + half
            rows = slice(half * HDIM, half * HDIM + HDIM)
            inner_ref[head : head + 1] = jnp.sum(products[rows], axis=0, keepdims=True)
            order = (lambda a, b: [a, b]) if half == 0 else (lambda a, b: [b, a])
            ot_ref[head] = jnp.concatenate(order(across_o[rows], blank), axis=0)
            qt_ref[head] = jnp.concatenate(order(across_q[rows], blank), axis=0)
        o_ref[pair, :BLK] = jnp.where(low_half, part, none)
        o_ref[pair, BLK:] = jnp.where(low_half, none, part)
        qm_ref[pair, :BLK] = jnp.where(low_half, q_ref[pair], none)
        qm_ref[pair, BLK:] = jnp.where(low_half, none, q_ref[pair])
    dqt_ref[...] = jnp.zeros_like(dqt_ref)
    dw_ref[1] = jnp.zeros((WIDTH, WIDTH), jnp.float32)
    dw_ref[2] = jnp.zeros((WIDTH, WIDTH), jnp.float32)
    gain_ref[...] = jnp.zeros_like(gain_ref)

    own_block.wait()

    def normed_block(array):
        wide = array[:BLK].astype(jnp.float32)
        scaled = wide * rms_rows(wide)
        return scaled, (scaled * gain_one).T.astype(jnp.bfloat16)

    def block(index, carry):
        slot = index % 2
        for copy in load_kv(index, slot):
            copy.wait()

        @pl.when(index < ctx)
        def _():
            for copy in load_kv(index + 1, 1 - slot):
                copy.start()

        mask_bias(tok_ref.at[slot], mine_ref, bias_ref, ctx, index)
        cosine, sine = turning(index, tables)
        for pair in range(PAIRS):
            key, value = kv_ref[slot, 0, pair], kv_ref[slot, 1, pair]
            key_across = key.astype(jnp.float32).T.astype(jnp.bfloat16)
            weights, score_grads = [], []
            for half in (0, 1):
                head = 2 * pair + half
                scores = dot(key, qt_ref[head]) + bias_ref[...]
                weight = jnp.exp(scores - lse_ref[head : head + 1])
                weight_grad = dot(value, ot_ref[head])
                score_grad = (weight * (weight_grad - inner_ref[head : head + 1])).astype(jnp.bfloat16)
                weights.append(weight.astype(jnp.bfloat16))
                score_grads.append(score_grad)
                rows = slice(head * HDIM, head * HDIM + HDIM)
                dqt_ref[rows] += dot(key_across[half * HDIM : half * HDIM + HDIM], score_grad)
            lanes = slice(pair * 128, pair * 128 + 128)
            dv_ref[:, lanes] = dot(jnp.concatenate(weights, axis=1), o_ref[pair]).astype(jnp.bfloat16)
            dk = dot(jnp.concatenate(score_grads, axis=1), qm_ref[pair])
            dk_ref[:, lanes] = (dk * cosine - swapped(dk) * sine).astype(jnp.bfloat16)
        scaled, normed_across = normed_block(tok_ref.at[slot])
        dw_ref[1] += dot(normed_across, dk_ref[...])
        dw_ref[2] += dot(normed_across, dv_ref[...])
        first = dot_nt(dk_ref[...], w_ref[1]) + dot_nt(dv_ref[...], w_ref[2])
        gain_ref[...] += jnp.sum(first * scaled, axis=0, keepdims=True)

        @pl.when(index < ctx)
        def _():
            others_ref[index] = first.astype(jnp.bfloat16)
            block_copy(ctx - index, index).start()

        @pl.when(index == ctx)
        def _():
            own_ref[...] = first

        return carry

    lax.fori_loop(0, ctx + 1, block, 0)
    cosine, sine = turning(ctx, tables)
    for pair in range(PAIRS):
        lanes = slice(pair * 128, pair * 128 + 128)
        dq = dqt_ref[lanes, :].T * (HDIM**-0.5)
        dk_ref[:, lanes] = (dq * cosine - swapped(dq) * sine).astype(jnp.bfloat16)
    scaled, normed_across = normed_block(mine_ref)
    dw_ref[0] = dot(normed_across, dk_ref[...])
    first = dot_nt(dk_ref[...], w_ref[0])
    own_ref[...] += first
    gain_one_row = gain_ref[...] + jnp.sum(first * scaled, axis=0, keepdims=True)
    lanes = lax.broadcasted_iota(jnp.int32, (WIDTH, 128), 1)
    ones = jnp.broadcast_to(gain_one_row, (128, WIDTH)).T
    twos = jnp.broadcast_to(gain_two_row, (128, WIDTH)).T
    few = jnp.where(lanes == 18, ones, jnp.where(lanes == 19, twos, small_grad))
    few_sum[...] = few

    def share(x):
        return pltpu.make_async_remote_copy(
            src_ref=grads_ref.at[x, :, :, 1 - core],
            dst_ref=twin_in.at[x],
            send_sem=twin_send.at[x],
            recv_sem=twin_recv.at[x],
            device_id=twin,
            device_id_type=MESH,
        )

    def pack(group, carry):
        rows = pl.ds(pl.multiple_of(group * 48, 16), 48)

        def lane_half(start):
            return jnp.concatenate(
                [dw_ref[w, rows, start : start + 384] for w in range(4)], axis=0
            ).astype(jnp.bfloat16)

        from_left = dot(left_ref[...], lane_half(0))
        from_right = dot(right_ref[...], lane_half(384))
        placed = dot(place_ref[...], few_sum[rows].astype(jnp.bfloat16))
        whole = jnp.concatenate(
            [from_left[:128], from_right[:128], from_left[128:] + from_right[128:], placed], axis=1
        )
        grads_ref[group // 4, group % 4] = whole.astype(jnp.bfloat16).reshape(4, 2, 16, 1280)
        return carry

    for x in range(4):
        lax.fori_loop(4 * x, 4 * x + 4, pack, 0)
        copy = share(x)
        copy.start()
        started.append(copy)

    def net(part, step, by, source, target):
        axis = PART_ORDER[part][2 - step]
        return pltpu.make_async_remote_copy(
            src_ref=source,
            dst_ref=target,
            send_sem=net_send.at[part, step, by - 1],
            recv_sem=net_recv.at[part, step, by - 1],
            device_id=device_at(*shifted(spot, axis, by), core),
            device_id_type=MESH,
        )

    def small(axis, by, source, slot):
        device = twin if axis == 3 else device_at(*shifted(spot, axis, by), core)
        return pltpu.make_async_remote_copy(
            src_ref=source,
            dst_ref=small_in.at[axis, slot],
            send_sem=small_send.at[axis, by - 1],
            recv_sem=small_recv.at[axis, by - 1],
            device_id=device,
            device_id_type=MESH,
        )

    copy = small(3, 1, small_sum.at[3], core)
    copy.start()
    started.append(copy)

    for x in range(4):
        share(x).wait_recv()

        def add_pair(index, carry, x=x):
            z, y = index // 4, index % 4
            held[x, z, y] = (
                grads_ref[x, z, y, core].astype(jnp.float32) + twin_in[x, z, y].astype(jnp.float32)
            ).astype(jnp.bfloat16)
            return carry

        lax.fori_loop(0, 16, add_pair, 0, unroll=2)

    def lanes_of(part):
        return pl.ds(PART_START[part], PART_LANES[part])

    for part in range(3):
        axis = PART_ORDER[part][2]
        for by in (1, 2, 3):
            at = shifted(spot, axis, by)[axis]
            index = tuple(at if a == axis else slice(None) for a in range(3))
            copy = net(
                part, 0, by, held.at[(*index, slice(None), lanes_of(part))], in_one[part].at[by - 1]
            )
            copy.start()
            started.append(copy)

    small(3, 1, small_sum.at[3], 1 - core).wait_recv()
    small_in[3, core] = small_sum[3]
    small_sum[0] = small_in[3, 0] + small_in[3, 1]
    for by in (1, 2, 3):
        copy = small(0, by, small_sum.at[0], spot[0])
        copy.start()
        started.append(copy)

    def small_step(axis):
        for by in (1, 2, 3):
            small(axis, by, small_sum.at[axis], shifted(spot, axis, -by)[axis]).wait_recv()
        small_in[axis, spot[axis]] = small_sum[axis]
        total = small_in[axis, 0] + small_in[axis, 1] + small_in[axis, 2] + small_in[axis, 3]
        if axis == 2:
            total_ref[...] = total
            return
        small_sum[axis + 1] = total
        for by in (1, 2, 3):
            copy = small(axis + 1, by, small_sum.at[axis + 1], spot[axis + 1])
            copy.start()
            started.append(copy)

    for part in range(3):
        first, second, third = PART_ORDER[part]
        for by in (1, 2, 3):
            net(part, 0, by, in_one[part].at[by - 1], in_one[part].at[by - 1]).wait_recv()
        rest = tuple(a for a in (0, 1, 2) if a != third)
        lanes = slice(PART_START[part], PART_START[part] + PART_LANES[part])

        def add_four(index, carry, part=part, third=third, rest=rest, lanes=lanes):
            at = {rest[0]: index // 4, rest[1]: index % 4, third: spot[third]}
            total = held[at[0], at[1], at[2], :, lanes].astype(jnp.float32)
            for by in range(3):
                total = total + in_one[part][by, index // 4, index % 4].astype(jnp.float32)
            sum_one[part][index // 4, index % 4] = total.astype(jnp.bfloat16)
            return carry

        lax.fori_loop(0, 16, add_four, 0, unroll=2)
        for by in (1, 2, 3):
            at = shifted(spot, second, by)[second]
            source = sum_one[part].at[at] if second == rest[0] else sum_one[part].at[:, at]
            copy = net(part, 1, by, source, in_two[part].at[by - 1])
            copy.start()
            started.append(copy)
    small_step(0)

    for copy in kept:
        copy.wait()
    for kind in (0, 1):
        for by in range(1, 8):
            expert(kind, by).wait_recv()

    def sum_eight(source, rows):
        total = source[0, rows].astype(jnp.float32)
        for by in range(1, 8):
            total = total + source[by, rows].astype(jnp.float32)
        return total

    def expert_rows(index, carry):
        rows = pl.ds(pl.multiple_of(index * 16, 16), 16)
        gate_out[rows] = sum_eight(gate_up_in, rows)
        up_out[rows] = sum_eight(gate_up_in, pl.ds(pl.multiple_of(96 + index * 16, 16), 16))
        return carry

    lax.fori_loop(0, 6, expert_rows, 0)

    def down_rows(index, carry):
        rows = pl.ds(pl.multiple_of(index * 16, 16), 16)
        down_out[rows] = sum_eight(down_in, rows)
        return carry

    lax.fori_loop(0, 8, down_rows, 0)

    for part in range(3):
        first, second, third = PART_ORDER[part]
        for by in (1, 2, 3):
            net(part, 1, by, in_two[part].at[by - 1], in_two[part].at[by - 1]).wait_recv()
        rest = tuple(a for a in (0, 1, 2) if a != third)
        for index in range(4):
            if second == rest[0]:
                total = sum_one[part][spot[second], index].astype(jnp.float32)
            else:
                total = sum_one[part][index, spot[second]].astype(jnp.float32)
            for by in range(3):
                total = total + in_two[part][by, index].astype(jnp.float32)
            sum_two[part][index] = total.astype(jnp.bfloat16)
        for by in (1, 2, 3):
            at = shifted(spot, first, by)[first]
            copy = net(part, 2, by, sum_two[part].at[at], in_three[part].at[by - 1])
            copy.start()
            started.append(copy)
    small_step(1)

    for by in range(1, 8):

        @pl.when(ctx + by < 8)
        def _(by=by):
            block_copy(by, ctx).wait_recv()
            own_ref[...] += block_in[by - 1].astype(jnp.float32)

        @pl.when(ctx - by >= 0)
        def _(by=by):
            block_copy(by, ctx - by).wait_send()

    wide = mine_ref[:BLK].astype(jnp.float32)
    scale = rms_rows(wide)
    weighted = own_ref[...] * gain_one
    tokens_grad_ref[...] = (
        state_grad_ref[...]
        + scale * weighted
        - wide * (scale**3 * jnp.mean(weighted * wide, axis=-1, keepdims=True))
    )
    finals = []
    for part in range(3):
        first = PART_ORDER[part][0]
        for by in (1, 2, 3):
            net(part, 2, by, in_three[part].at[by - 1], in_three[part].at[by - 1]).wait_recv()
        total = sum_two[part][spot[first]].astype(jnp.float32)
        for by in range(3):
            total = total + in_three[part][by].astype(jnp.float32)
        finals.append(total)
    final = jnp.concatenate(finals, axis=1)
    sums_ref[:16] = final[:, :768]
    sums_ref[16:] = jnp.concatenate([final[:8, 768:1152], final[8:, 768:1152]], axis=1)
    few_ref[...] = final[:8, 1152:]
    small_step(2)
    for copy in started:
        copy.wait_send()


def run_back(blocks, weights, smalls, prev, wres, routes, cot, kept, back_rows, back_grads, d_gate_up, d_down):
    vmem, anywhere = pl.BlockSpec(memory_space=pltpu.VMEM), pl.BlockSpec(memory_space=pl.ANY)
    shape = jax.ShapeDtypeStruct
    low, wide = jnp.bfloat16, jnp.float32
    dma = pltpu.SemaphoreType.DMA
    left, right, small = (jnp.asarray(t.T, low) for t in placing_tables())
    by_part = lambda *lead: [pltpu.VMEM((*lead, 16, lanes), low) for lanes in PART_LANES]
    return pl.pallas_call(
        back_kernel,
        out_shape=[
            shape((BLK, WIDTH), low),
            shape((16, BLK), wide),
            shape((16, 128), wide),
            shape((BLK, WIDTH), wide),
            shape((24, WIDTH), wide),
            shape((8, 128), wide),
            shape((96, 1024), wide),
            shape((96, 1024), wide),
            shape((128, WIDTH), wide),
        ],
        in_specs=[anywhere] + [vmem] * 18 + [anywhere] * 2 + [vmem] * 4 + [anywhere] * 2,
        out_specs=[vmem] * 9,
        scratch_shapes=[
            pltpu.VMEM((HEADS, 128, BLK), low),
            pltpu.VMEM((HEADS, 128, BLK), low),
            pltpu.VMEM((PAIRS, 2 * BLK, 128), low),
            pltpu.VMEM((PAIRS, 2 * BLK, 128), low),
            pltpu.VMEM((BLK, BLK), wide),
            pltpu.VMEM((16, BLK), wide),
            pltpu.VMEM((WIDTH, BLK), wide),
            pltpu.VMEM((1, WIDTH), wide),
            pltpu.VMEM((BLK, WIDTH), low),
            pltpu.VMEM((BLK, WIDTH), low),
            pltpu.VMEM((128, BLK), wide),
            pltpu.VMEM((128, 128), wide),
            pltpu.VMEM((4, WIDTH, WIDTH), wide),
            pltpu.VMEM((WIDTH, 128), wide),
            pltpu.VMEM((2, 2, PAIRS, BLK, 128), low),
            pltpu.VMEM((2, BLK + 16, WIDTH), low),
            pltpu.VMEM((BLK + 16, WIDTH), low),
            dma((2, 3)),
            pltpu.VMEM((BLK, WIDTH), wide),
            pltpu.VMEM((BLK, WIDTH), wide),
            pltpu.VMEM((8, BLK, WIDTH), low),
            pltpu.VMEM((4, 4, 4, 2, 16, 1280), low),
            pltpu.VMEM((7, BLK, WIDTH), low),
            pltpu.VMEM((8, 192, 1024), low),
            pltpu.VMEM((8, 128, WIDTH), low),
            pltpu.VMEM((4, 4, 16, 128), wide),
            pltpu.VMEM((4, 16, 128), wide),
            dma((7,)),
            dma((7,)),
            dma((2, 7)),
            dma((2, 7)),
            dma((3,)),
            dma((3, 3, 3)),
            dma((3, 3, 3)),
            dma((4,)),
            dma((4,)),
            dma((4, 3)),
            dma((4, 3)),
            pltpu.VMEM((4, 4, 4, 16, 1280), low),
            pltpu.VMEM((4, 4, 4, 16, 1280), low),
            *by_part(3, 4, 4),
            *by_part(3, 4),
            *by_part(3),
            *by_part(4, 4),
            *by_part(4),
        ],
        name="back",
        compiler_params=pltpu.CompilerParams(
            collective_id=2, has_side_effects=True, vmem_limit_bytes=62 * 2**20
        ),
    )(
        blocks, weights, smalls, *rope_tables(), left, right, small, prev, wres, routes, cot,
        *kept, back_rows, back_grads, d_gate_up, d_down,
    )


def finish_kernel(
    out_in, tokens_in, gate_in, up_in, down_in, prev_in, total_in, sums_in, few_in,
    out, tokens_grad, gate, up, down, prev, total, sum_q, sum_k, sum_v, sum_o,
    gain_one, gain_two, router, constant, vectors, prev_at, total_at, sums_at, few_at, sems,
):
    pairs = (
        (prev_in, prev_at), (total_in, total_at), (sums_in, sums_at), (few_in, few_at),
        (tokens_in, tokens_grad), (out_in, out), (gate_in, gate), (up_in, up), (down_in, down),
    )
    copies = [
        pltpu.make_async_copy(source, target, sems.at[index])
        for index, (source, target) in enumerate(pairs)
    ]
    for copy in copies:
        copy.start()
    for copy in copies[:4]:
        copy.wait()
    prev[:, 0, :] = prev_at[:NALL]
    total[...] = total_at[:NALL, :NALL]
    for weight, ref in enumerate((sum_q, sum_k, sum_v, sum_o)):
        ref[...] = sums_at[weight * 6 : weight * 6 + 6]
    few = few_at[...]
    router[...] = few[:6, :NALL]
    tall = jnp.concatenate([few, jnp.zeros((120, 128), jnp.float32)], axis=0).T
    constant[...] = tall[12:16, :6]
    vectors[...] = tall[16:18, :6]
    gain_one[...] = tall[18:19, :6]
    gain_two[...] = tall[19:20, :6]
    for copy in copies[4:]:
        copy.wait()


def finish(out, tokens_grad, gate, up, down, prev, total, sums, few):
    vmem = pl.BlockSpec(memory_space=pltpu.VMEM)
    shape = jax.ShapeDtypeStruct
    wide = jnp.float32
    like = [shape(a.shape, a.dtype) for a in (out, tokens_grad, gate, up, down)]
    few_shapes = [(1, 6), (1, 6), (6, NALL), (4, 6), (2, 6)]
    return pl.pallas_call(
        finish_kernel,
        out_shape=like
        + [shape((NALL, 1, BLK), wide), shape((NALL, NALL), wide)]
        + [shape((6, WIDTH), wide)] * 4
        + [shape(s, wide) for s in few_shapes],
        in_specs=[pl.BlockSpec(memory_space=pl.ANY)] * 9,
        out_specs=[vmem] * 16,
        scratch_shapes=[
            *(pltpu.VMEM(a.shape, a.dtype) for a in (prev, total, sums, few)),
            pltpu.SemaphoreType.DMA((9,)),
        ],
        name="finish",
        compiler_params=pltpu.CompilerParams(vmem_limit_bytes=62 * 2**20),
    )(out, tokens_grad, gate, up, down, prev, total, sums, few)


def on_device(
    tokens, prev_logits, routes, segments, rank_order, norm_first, w_query, w_key, w_value, w_output,
    norm_second, w_router, w_residual, w_constant, v_constant, w_gate, w_up, w_down, cotangent,
):
    few = [w_router, w_constant.T, v_constant.T, norm_first[None], norm_second[None]]
    prev = jnp.transpose(prev_logits, (2, 0, 1))
    (
        state, normed, att, lse, q, keys, values, info, proj, blocks, weights, smalls, _,
        back_rows, back_grads, d_gate_up, d_down,
    ) = run_forward(
        [w_query, w_key, w_value, w_output], few, tokens[0], segments, (w_gate[0], w_up[0], w_down[0]),
        prev, w_residual, routes[0].T, rank_order[0], cotangent[0],
    )
    (
        out, prev_grad, residual, tokens_grad, sums, small, d_gate, d_up, d_down,
    ) = run_back(
        blocks, weights, smalls, prev, w_residual, routes[0].T, cotangent[0],
        (state, normed, att, lse, q, keys, values, info, proj), back_rows, back_grads,
        d_gate_up, d_down,
    )
    (
        out, tokens_grad, d_gate, d_up, d_down, prev_grad, residual, sum_q, sum_k, sum_v, sum_o,
        gain_one, gain_two, router, constant, vectors,
    ) = finish(out, tokens_grad, d_gate, d_up, d_down, prev_grad, residual, sums, small)
    return (
        out[None],
        tokens_grad[None],
        jnp.transpose(prev_grad, (1, 2, 0)),
        gain_one[0],
        sum_q,
        sum_k,
        sum_v,
        sum_o,
        gain_two[0],
        router,
        residual,
        constant.T,
        vectors.T,
        d_gate[None],
        d_up[None],
        d_down[None],
    )


def solution(mesh):
    in_specs = (
        P("fsdp", "ctx", None),
        P("fsdp", "ctx", None),
        P("fsdp", "ctx", None),
        P("fsdp", "ctx"),
        P("fsdp", "ctx", None),
        P(("ctx", "fsdp")),
        P(("ctx", "fsdp"), None),
        P(("ctx", "fsdp"), None),
        P(("ctx", "fsdp"), None),
        P(("ctx", "fsdp"), None),
        P(("ctx", "fsdp")),
        P(("ctx", "fsdp"), None),
        P(),
        P(("ctx", "fsdp"), None),
        P(("ctx", "fsdp"), None),
        P("fsdp", "ctx", None),
        P("fsdp", "ctx", None),
        P("fsdp", "ctx", None),
        P("fsdp", "ctx", None),
    )
    out_specs = (
        P("fsdp", "ctx", None),
        P("fsdp", "ctx", None),
        P("fsdp", "ctx", None),
        P(("ctx", "fsdp")),
        P(("ctx", "fsdp"), None),
        P(("ctx", "fsdp"), None),
        P(("ctx", "fsdp"), None),
        P(("ctx", "fsdp"), None),
        P(("ctx", "fsdp")),
        P(("ctx", "fsdp"), None),
        P(),
        P(("ctx", "fsdp"), None),
        P(("ctx", "fsdp"), None),
        P("fsdp", "ctx", None),
        P("fsdp", "ctx", None),
        P("fsdp", "ctx", None),
    )
    return jax.shard_map(
        on_device, mesh=mesh, in_specs=in_specs, out_specs=out_specs, check_vma=False
    )
```

```python
import functools

import jax
import jax.numpy as jnp
import numpy as np
from jax import lax
from jax.experimental import pallas as pl
from jax.experimental.pallas import tpu as pltpu
from jax.sharding import PartitionSpec as P

HEADS = 12
HDIM = 64
EXPERTS = 8
NALL = 12
CAP = 54
WIDTH = HEADS * HDIM
PAIRS = HEADS // 2
BLK = 256
SLOTS = 64

highest = lax.Precision.HIGHEST
masked_score = -1e30
epsilon = 1e-06

MESH = pl.DeviceIdType.MESH
PART_LANES = (512, 384, 384)
PART_START = (0, 512, 896)
PART_ORDER = ((0, 1, 2), (1, 2, 0), (2, 0, 1))

BLOCK_CUTS = (0, 64, 144, 224, 272)
PAY_CUTS = (0, 64, 144, 224, 288)
SPANS = {"all": (0, 4), "p": (1, 3), "h1": (0, 2), "h2": (2, 4), "q1": (0, 1), "p1": (1, 2), "p2": (2, 3), "q2": (3, 4)}
MESSAGES = (
    (1, (0, 0), "all"), (-1, (0, 0), "all"), (0, (0, 0), "all"),
    (1, (0, 1), "p"), (-1, (0, 1), "p"),
    (1, (-1, 0), "h1"), (-1, (1, 0), "h2"),
    (0, (-1, 0), "q1"), (0, (-1, 0), "q2"), (0, (1, 0), "q1"), (0, (1, 0), "q2"),
    (1, (-1, 1), "p1"), (-1, (1, 1), "p2"),
    (0, (2, 0), "q1"), (0, (2, 0), "q2"),
)


def place():
    ctx = lax.axis_index("ctx")
    fsdp = lax.axis_index("fsdp")
    return ctx // 2, (ctx % 2) * 2 + fsdp // 8, (fsdp // 2) % 4, fsdp % 2


def device_at(x, z, y, core):
    return {"ctx": x * 2 + z // 2, "fsdp": (z % 2) * 8 + y * 2 + core}


def shifted(spot, axis, by):
    moved = list(spot)
    moved[axis] = (moved[axis] + by) % 4
    return tuple(moved)


def greet(devices):
    barrier = pltpu.get_barrier_semaphore()
    for device in devices:
        pl.semaphore_signal(barrier, inc=1, device_id=device, device_id_type=MESH)
    pl.semaphore_wait(barrier, len(devices))


def torus_peers(spot, core):
    peers = [device_at(*shifted(spot, axis, by), core) for axis in range(3) for by in (1, 2, 3)]
    return peers + [device_at(*spot, 1 - core)]


def sequence_peers(spot, core):
    x, z, y = spot
    return [device_at((x + by) % 4, (z + 2) % 4, y, core) for by in (1, 2, 3)]


def region(ref, spot, core, whole):
    return ref.at[
        tuple(slice(None) if axis in whole else spot[axis] for axis in range(3)) + (core,)
    ]


def placing_tables():
    left = np.zeros((192, 256), np.float32)
    right = np.zeros((192, 256), np.float32)
    small = np.zeros((48, 128), np.float32)
    for device in range(8):
        for weight in range(4):
            for row in range(6):
                at, line = weight * 48 + device * 6 + row, weight * 6 + row
                if line < 16:
                    left[at, device * 16 + line] = right[at, device * 16 + line] = 1
                else:
                    left[at, 128 + device * 16 + line - 16] = 1
                    right[at, 128 + device * 16 + line - 8] = 1
        for row in range(6):
            small[device * 6 + row, device * 16 + row] = 1
    return left, right, small


def rope_tables():
    frequency = 10000.0 ** (-2.0 * (np.arange(128) % 32) / HDIM)
    inner = np.arange(BLK)[:, None] * frequency
    outer = (np.arange(8) * BLK)[:, None] * frequency
    return [jnp.asarray(t, jnp.float32) for t in (np.cos(inner), np.sin(inner), np.cos(outer), np.sin(outer))]


def turning(index, tables):
    cos_in, sin_in, cos_out, sin_out = tables
    ca, sa = cos_out[pl.ds(index, 1), :], sin_out[pl.ds(index, 1), :]
    cb, sb = cos_in[...], sin_in[...]
    lower = lax.broadcasted_iota(jnp.int32, (BLK, 128), 1) % HDIM < HDIM // 2
    sine = sa * cb + ca * sb
    return ca * cb - sa * sb, jnp.where(lower, -sine, sine)


def swapped(values):
    lower = lax.broadcasted_iota(jnp.int32, values.shape, 1) % HDIM < HDIM // 2
    return jnp.where(lower, pltpu.roll(values, 96, 1), pltpu.roll(values, 32, 1))


def dot(left, right):
    return jnp.dot(left, right, preferred_element_type=jnp.float32)


def dot_nt(left, right):
    return lax.dot_general(left, right, (((1,), (1,)), ((), ())), preferred_element_type=jnp.float32)


def column(row):
    return jnp.broadcast_to(row, (128, row.shape[1])).T[:, 0:1]


def mask_bias(key_block, query_block, bias_ref, ctx, index):
    key_seg = column(key_block[BLK:, :BLK].astype(jnp.float32)[:1])
    query_seg = query_block[BLK:, :BLK].astype(jnp.float32)[:1]
    key_pos = lax.broadcasted_iota(jnp.int32, (BLK, BLK), 0)
    query_pos = lax.broadcasted_iota(jnp.int32, (BLK, BLK), 1)
    reach = jnp.where(index == ctx, 0, BLK)
    allowed = (key_seg == query_seg) & (key_pos <= query_pos + reach)
    bias_ref[...] = jnp.where(allowed, 0.0, masked_score)


def rms_rows(values):
    return lax.rsqrt(jnp.mean(values * values, axis=-1, keepdims=True) + epsilon)


def pick(onehot, values):
    return jnp.sum(jnp.where(onehot, values, 0.0), axis=1, keepdims=True)


def lane_is(lanes):
    return lax.broadcasted_iota(jnp.int32, (BLK, 128), 1) == lanes


def dot_tn(left, right):
    return lax.dot_general(left, right, (((0,), (0,)), ((), ())), preferred_element_type=jnp.float32)


def row_tile(values):
    *weights, small = values
    rows = jnp.concatenate([w.astype(jnp.float32) for w in weights], axis=0)
    tail = jnp.concatenate([rows[16:, :384], rows[16:, 384:]], axis=0)
    return jnp.concatenate([rows[:16], tail, small], axis=1).astype(jnp.bfloat16)


def forward_kernel(
    wq_ref, wk_ref, wv_ref, wo_ref, router_ref, constant_ref, vector_ref, gain_one_ref, gain_two_ref,
    tokens_ref, segments_in, gate_in, up_in, down_in,
    left_ref, right_ref, place_ref, cos_in, sin_in, cos_out, sin_out,
    prev_ref, wres_ref, routes_ref, rank_ref, cot_ref,
    state_ref, normed_ref, att_ref, lse_ref, q_ref, keys_ref, values_ref,
    info_ref, proj_ref, blocks_ref, w_ref, small_ref, pay_ref,
    back_rows_ref, back_grads_ref, d_pay_ref,
    part_a, part_b, part_c, own_ref, qt_ref, vt_ref, bias_ref, max_ref, sum_ref, acc_ref,
    prev_pad, wres_pad, few_wide, few_tall, kv_ref, rows_ref, grads_ref,
    gate_w, up_w, down_w, x_ref, g_ref, gate_ref, up_ref, hidden_ref, d_gate, d_up,
    mine_ref, twin_out, twin_in,
    net_send, net_recv, twin_send, twin_recv, own_sem, ring_send, ring_recv, kv_sem,
    load_sem, send_sem, recv_sem, share_send, share_recv, half_send, half_recv, ret_send, ret_recv,
    keep_sem,
):
    parts = (part_a, part_b, part_c)
    tables = (cos_in, sin_in, cos_out, sin_out)
    ctx, fsdp = lax.axis_index("ctx"), lax.axis_index("fsdp")
    along, side = ctx // 2, ctx % 2
    *spot, core = place()
    spot = tuple(spot)
    twin = device_at(*spot, 1 - core)
    few_wide[...] = jnp.zeros_like(few_wide)
    few_wide[12:16, :6] = constant_ref[...].astype(jnp.float32)
    few_wide[16:18, :6] = vector_ref[...].astype(jnp.float32)
    few_wide[18:19, :6] = gain_one_ref[...].astype(jnp.float32)
    few_wide[19:20, :6] = gain_two_ref[...].astype(jnp.float32)
    few_tall[...] = few_wide[...].T[:16]
    few_tall[:6, :NALL] = router_ref[...].astype(jnp.float32)
    own_ref[...] = row_tile([wq_ref[...], wk_ref[...], wv_ref[...], wo_ref[...], few_tall[...]])
    marks = jnp.concatenate(
        [segments_in[...].astype(jnp.float32), jnp.zeros((1, WIDTH - BLK), jnp.float32)], axis=1
    )
    blocks_ref[ctx, :BLK] = tokens_ref[...]
    blocks_ref[ctx, BLK:] = jnp.broadcast_to(marks, (16, WIDTH)).astype(jnp.bfloat16)
    chip = fsdp // 2

    def at_expert(where, on):
        return {"ctx": ctx, "fsdp": where * 2 + on}

    greet(
        torus_peers(spot, core)
        + [at_expert((chip + by) % EXPERTS, core) for by in range(1, EXPERTS)]
    )

    def net(part, step, by, source, target):
        axis = PART_ORDER[part][step]
        return pltpu.make_async_remote_copy(
            src_ref=source,
            dst_ref=target,
            send_sem=net_send.at[part, step, by - 1],
            recv_sem=net_recv.at[part, step, by - 1],
            device_id=device_at(*shifted(spot, axis, by), core),
            device_id_type=MESH,
        )

    def share(part, slot, source, target):
        return pltpu.make_async_remote_copy(
            src_ref=source,
            dst_ref=target,
            send_sem=twin_send.at[part, slot],
            recv_sem=twin_recv.at[part, slot],
            device_id=twin,
            device_id_type=MESH,
        )

    payloads = ((blocks_ref, BLOCK_CUTS), (pay_ref, PAY_CUTS))

    def ring(kind, number, arriving=False):
        to, (steps, across_it), rows = MESSAGES[number]
        if arriving:
            steps = steps - to
            across_it = across_it if to else 1 - across_it
        array, cuts = payloads[kind]
        first, last = (cuts[i] for i in SPANS[rows])
        on = side if across_it == 0 else 1 - side
        view = array.at[((along + steps + 4) % 4) * 2 + on, pl.ds(first, last - first)]
        target = ((along + to + 4) % 4) * 2 + (side if to else 1 - side)
        return pltpu.make_async_remote_copy(
            src_ref=view,
            dst_ref=view,
            send_sem=ring_send.at[kind, number],
            recv_sem=ring_recv.at[kind, number],
            device_id={"ctx": target, "fsdp": fsdp},
            device_id_type=MESH,
        )

    def pass_on(kind, stage):
        plan = (
            ((None, (0, 1, 2)),),
            ((2, (3, 4)),),
            ((0, (5, 7, 8)), (1, (6, 9, 10))),
            ((3, (11,)), (4, (12,)), (5, (13,)), (6, (14,))),
            tuple((number, ()) for number in range(7, 15)),
        )[stage]
        for number, then in plan:
            if number is not None:
                ring(kind, number, arriving=True).wait_recv()
            for follow in then:
                ring(kind, follow).start()

    started = []
    kept = []
    for part in range(3):
        own = own_ref.at[:, pl.ds(PART_START[part], PART_LANES[part])]
        mine = region(parts[part], spot, core, ())
        for by in (1, 2, 3):
            copy = net(part, 0, by, own, mine)
            copy.start()
            started.append(copy)
    for part in range(3):
        own = own_ref.at[:, pl.ds(PART_START[part], PART_LANES[part])]
        mine = region(parts[part], spot, core, ())
        copy = pltpu.make_async_copy(own, mine, own_sem.at[part])
        copy.start()
        kept.append(copy)
        copy = share(part, 0, own, mine)
        copy.start()
        started.append(copy)
    tail = [(down_in.at[:96], pay_ref.at[ctx, 192:, pl.ds(0, WIDTH)])] + [
        (down_in.at[96:, pl.ds(256 * m, 256)], pay_ref.at[ctx, pl.ds(192 + 32 * m, 32), pl.ds(WIDTH, 256)])
        for m in range(3)
    ]
    pieces = [(gate_in, pay_ref.at[ctx, :96]), (up_in, pay_ref.at[ctx, 96:192]), *tail]
    own_experts = [
        pltpu.make_async_copy(source, target, own_sem.at[3 + number])
        for number, (source, target) in enumerate(pieces)
    ]
    for copy in own_experts:
        copy.start()
    for copy in kept + own_experts:
        copy.wait()
    for step in range(3):
        for part in range(3):
            order = PART_ORDER[part]
            axis = order[step]
            whole = order[:step]
            for by in (1, 2, 3):
                here = region(parts[part], shifted(spot, axis, -by), core, whole)
                net(part, step, by, here, here).wait_recv()
                copy = share(part, 1 + step * 3 + by - 1, here, here)
                copy.start()
                started.append(copy)
            if step < 2:
                held = region(parts[part], spot, core, order[: step + 1])
                for by in (1, 2, 3):
                    copy = net(part, step + 1, by, held, held)
                    copy.start()
                    started.append(copy)
        if step == 1:
            pass_on(0, 0)
    for part in range(3):
        order = PART_ORDER[part]
        first = region(parts[part], spot, 1 - core, ())
        share(part, 0, first, first).wait_recv()
        for step in range(3):
            for by in (1, 2, 3):
                here = region(
                    parts[part], shifted(spot, order[step], -by), 1 - core, order[:step]
                )
                share(part, 1 + step * 3 + by - 1, here, here).wait_recv()

    def unpack(group, carry):
        a, b, c = (
            part[group // 4, group % 4].reshape(128, lanes)
            for part, lanes in zip(parts, PART_LANES, strict=True)
        )
        tail = jnp.concatenate([b[:, 256:], c[:, :256]], axis=1)
        left = dot(left_ref[...], jnp.concatenate([a[:, :384], tail], axis=0))
        right_rows = jnp.concatenate([a[:, 384:], b[:, :256]], axis=1)
        right = dot(right_ref[...], jnp.concatenate([right_rows, tail], axis=0))
        rows = pl.ds(pl.multiple_of(group * 48, 16), 48)
        for weight in range(4):
            w_ref[weight, rows, :384] = left[weight * 48 : weight * 48 + 48].astype(jnp.bfloat16)
            w_ref[weight, rows, 384:] = right[weight * 48 : weight * 48 + 48].astype(jnp.bfloat16)
        small_ref[rows] = dot(place_ref[...], c[:, 256:]).astype(jnp.bfloat16)
        return carry

    pass_on(0, 1)
    lax.fori_loop(0, 16, unpack, 0)
    pass_on(0, 2)
    across = small_ref[...].astype(jnp.float32).T
    gain_one, gain_two = across[18:19], across[19:20]

    def normed_block(index):
        wide = blocks_ref[index, :BLK].astype(jnp.float32)
        return (wide * rms_rows(wide) * gain_one).astype(jnp.bfloat16)

    query = dot(normed_block(ctx), w_ref[0])
    cosine, sine = turning(ctx, tables)
    for pair in range(PAIRS):
        part = query[:, pair * 128 : pair * 128 + 128]
        turned = (part * cosine + swapped(part) * sine) * (HDIM**-0.5)
        q_ref[pair] = turned.astype(jnp.bfloat16)
        across_q = turned.T.astype(jnp.bfloat16)
        blank = jnp.zeros((HDIM, BLK), jnp.bfloat16)
        qt_ref[2 * pair] = jnp.concatenate([across_q[:HDIM], blank], axis=0)
        qt_ref[2 * pair + 1] = jnp.concatenate([blank, across_q[HDIM:]], axis=0)
    max_ref[...] = jnp.full(max_ref.shape, masked_score, jnp.float32)
    sum_ref[...] = jnp.zeros_like(sum_ref)
    acc_ref[...] = jnp.zeros_like(acc_ref)

    def keep_block(index, slot):
        return [
            pltpu.make_async_copy(kv_ref.at[slot, kind], target.at[index], kv_sem.at[slot, kind])
            for kind, target in enumerate((keys_ref, values_ref))
        ]

    def block_at(step):
        odd = step % 2
        x = along - (step + odd) // 2 + odd * side
        return jnp.where(step == 0, ctx, x * 2 + 1 - odd)

    def block(step, carry):
        index = block_at(step)
        slot = step % 2

        @pl.when(step >= 2)
        def _():
            for copy in keep_block(block_at(step - 2), slot):
                copy.wait()

        normed = normed_block(index)
        key = dot(normed, w_ref[1])
        value = dot(normed, w_ref[2])
        cosine, sine = turning(index, tables)
        for pair in range(PAIRS):
            lanes = slice(pair * 128, pair * 128 + 128)
            part = key[:, lanes]
            kv_ref[slot, 0, pair] = (part * cosine + swapped(part) * sine).astype(jnp.bfloat16)
            kv_ref[slot, 1, pair] = value[:, lanes].astype(jnp.bfloat16)
            vt_ref[lanes, :] = value[:, lanes].T.astype(jnp.bfloat16)
        mask_bias(blocks_ref.at[index], blocks_ref.at[ctx], bias_ref, ctx, index)
        for head in range(HEADS):
            rows = slice(head * HDIM, head * HDIM + HDIM)
            scores = dot(kv_ref[slot, 0, head // 2], qt_ref[head]) + bias_ref[...]
            before = max_ref[head : head + 1]
            top = jnp.maximum(before, jnp.max(scores, axis=0, keepdims=True))
            weights = jnp.exp(scores - top)
            shrink = jnp.exp(before - top)
            sum_ref[head : head + 1] = sum_ref[head : head + 1] * shrink + jnp.sum(
                weights, axis=0, keepdims=True
            )
            max_ref[head : head + 1] = top
            acc_ref[rows] = acc_ref[rows] * shrink + dot(vt_ref[rows, :], weights.astype(jnp.bfloat16))

        for copy in keep_block(index, slot):
            copy.start()
        for when, todo in (
            (0, ((0, 3),)),
            (1, ((0, 4), (1, 0))),
            (4, ((1, 1), (1, 2))),
            (6, ((1, 3),)),
        ):

            @pl.when(step == jnp.minimum(ctx, when))
            def _(todo=todo):
                for kind, stage in todo:
                    pass_on(kind, stage)

        return carry

    lax.fori_loop(0, ctx + 1, block, 0)
    for head in range(HEADS):
        rows = slice(head * HDIM, head * HDIM + HDIM)
        att_ref[rows] = acc_ref[rows] / sum_ref[head : head + 1]
    lse_ref[...] = max_ref[...] + jnp.log(jnp.maximum(sum_ref[...], 1e-30))
    attended = att_ref[...].T.astype(jnp.bfloat16)
    state = blocks_ref[ctx, :BLK].astype(jnp.float32) + dot(attended, w_ref[3])
    state_ref[...] = state
    normed_two = (state * rms_rows(state) * gain_two).astype(jnp.bfloat16)
    normed_ref[...] = normed_two

    proj = dot(normed_two, small_ref[...])
    proj_ref[...] = proj
    pad_routing(prev_ref, wres_ref, prev_pad, wres_pad)
    logits = proj + jnp.dot(
        prev_pad[...].T, wres_pad[...], precision=highest, preferred_element_type=jnp.float32
    )
    lanes = lax.broadcasted_iota(jnp.int32, (BLK, 128), 1).astype(jnp.float32)
    routes = routes_ref[...].astype(jnp.float32)
    route_0, route_1 = column(routes[0:1]), column(routes[1:2])
    hot_0, hot_1 = lanes == route_0, lanes == route_1
    chosen_0, chosen_1 = pick(hot_0, logits), pick(hot_1, logits)
    top = jnp.maximum(chosen_0, chosen_1)
    chosen_0, chosen_1 = jnp.exp(chosen_0 - top), jnp.exp(chosen_1 - top)
    gate_0, gate_1 = chosen_0 / (chosen_0 + chosen_1), chosen_1 / (chosen_0 + chosen_1)
    rank = rank_ref[...].astype(jnp.float32)
    earlier = (rank < column(rank)).astype(jnp.float32).astype(jnp.bfloat16)
    slots = dot(earlier, (hot_0 | hot_1).astype(jnp.float32).astype(jnp.bfloat16))

    def target(route, hot):
        slot = pick(hot, slots)
        return jnp.where(
            (route < EXPERTS) & (slot < CAP), route * SLOTS + slot, -1.0
        )

    target_0, target_1 = target(route_0, hot_0), target(route_1, hot_1)
    info = jnp.where(lanes == 0, gate_0, 0.0) + jnp.where(lanes == 1, gate_1, 0.0)
    info = info + jnp.where(lanes == 2, target_0, 0.0) + jnp.where(lanes == 3, target_1, 0.0)
    info_ref[...] = info
    targets = info.T
    rows = lax.broadcasted_iota(jnp.int32, (EXPERTS * SLOTS, BLK), 0).astype(jnp.float32)
    table_0 = (rows == targets[2:3]).astype(jnp.float32).astype(jnp.bfloat16)
    table_1 = (rows == targets[3:4]).astype(jnp.float32).astype(jnp.bfloat16)
    rows_ref[...] = dot(table_0 + table_1, normed_two).astype(jnp.bfloat16)
    upstream = cot_ref[...].astype(jnp.float32)
    grads_ref[...] = dot(
        jnp.concatenate([table_0, table_1], axis=1),
        jnp.concatenate([gate_0 * upstream, gate_1 * upstream], axis=0).astype(jnp.bfloat16),
    ).astype(jnp.bfloat16)
    for back in (0, 1):

        @pl.when(ctx - back >= 0)
        def _(back=back):
            for copy in keep_block(block_at(ctx - back), (ctx - back) % 2):
                copy.wait()

    other = 1 - core
    half = EXPERTS * SLOTS

    def slots(index, on):
        return pl.ds(pl.multiple_of((on * EXPERTS + index) * SLOTS, SLOTS), SLOTS)

    def chunk(index):
        return pl.ds(pl.multiple_of(index * SLOTS, SLOTS), SLOTS)

    buffers = ((rows_ref, x_ref), (grads_ref, g_ref))

    def dispatch(kind, by):
        source, target = buffers[kind]
        where = (chip + by) % EXPERTS
        return pltpu.make_async_remote_copy(
            src_ref=source.at[chunk(where)],
            dst_ref=target.at[slots(chip, core)],
            send_sem=send_sem.at[kind, by - 1],
            recv_sem=recv_sem.at[kind, by - 1],
            device_id=at_expert(where, core),
            device_id_type=MESH,
        )

    def share(kind, by, on):
        source, target = buffers[kind]
        spot = slots((chip - by) % EXPERTS, on)
        return pltpu.make_async_remote_copy(
            src_ref=target.at[spot],
            dst_ref=target.at[spot],
            send_sem=share_send.at[kind, by],
            recv_sem=share_recv.at[kind, by],
            device_id=at_expert(chip, other),
            device_id_type=MESH,
        )

    def exchange(kind):
        return pltpu.make_async_remote_copy(
            src_ref=twin_out.at[kind],
            dst_ref=twin_in.at[kind],
            send_sem=half_send.at[kind],
            recv_sem=half_recv.at[kind],
            device_id=at_expert(chip, other),
            device_id_type=MESH,
        )

    returned = (back_rows_ref, back_grads_ref)

    def give_back(kind, by):
        where = (chip + by) % EXPERTS
        return pltpu.make_async_remote_copy(
            src_ref=mine_ref.at[kind, chunk(where)],
            dst_ref=returned[kind].at[chunk(chip)],
            send_sem=ret_send.at[kind, by - 1],
            recv_sem=ret_recv.at[kind, by - 1],
            device_id=at_expert(where, core),
            device_id_type=MESH,
        )

    for by in range(1, EXPERTS):
        dispatch(0, by).start()
    for by in range(1, EXPERTS):
        dispatch(0, by).wait_send()
    for by in range(1, EXPERTS):
        copy = dispatch(1, by)
        copy.start()
        started.append(copy)
    for kind in (0, 1):
        source, target = buffers[kind]
        copy = pltpu.make_async_copy(
            source.at[chunk(chip)], target.at[slots(chip, core)], keep_sem.at[kind]
        )
        copy.start()
        copy.wait()
        copy = share(kind, 0, core)
        copy.start()
        started.append(copy)

    def arrive(kind):
        for by in range(1, EXPERTS):
            dispatch(kind, by).wait_recv()
            copy = share(kind, by, core)
            copy.start()
            started.append(copy)

    def arrive_shared(kind):
        for by in range(EXPERTS):
            share(kind, by, other).wait_recv()

    def tiles(on, body):
        def step(index, carry):
            start = pl.multiple_of(on * half + index * 256, 256)
            body(pl.ds(start, 256), pl.ds(pl.multiple_of(index * 256, 256), 256))
            return carry

        lax.fori_loop(0, half // 256, step, 0)

    def forward(on, keep):
        def tile(rows, inner):
            x = x_ref[rows]
            gate, up = dot(x, gate_w[...]), dot(x, up_w[...])
            gate_ref[rows], up_ref[rows] = gate, up
            hidden_ref[rows] = (gate * jax.nn.sigmoid(gate) * up).astype(jnp.bfloat16)

        def result(rows, inner):
            keep(inner, dot(hidden_ref[rows], down_w[...]))

        tiles(on, tile)
        tiles(on, result)

    def backward(on, keep):
        def tile(rows, inner):
            hidden_grad = dot_nt(g_ref[rows], down_w[...])
            gate, up = gate_ref[rows], up_ref[rows]
            sigmoid = jax.nn.sigmoid(gate)
            d_gate[rows] = (
                hidden_grad * up * sigmoid * (1.0 + gate * (1.0 - sigmoid))
            ).astype(jnp.bfloat16)
            d_up[rows] = (hidden_grad * gate * sigmoid).astype(jnp.bfloat16)
            keep(inner, dot_nt(d_gate[rows], gate_w[...]) + dot_nt(d_up[rows], up_w[...]))

        tiles(on, tile)

    def keep_mine(kind):
        def keep(rows, values):
            mine_ref[kind, rows] = values.astype(jnp.bfloat16)

        return keep

    def keep_twin(kind):
        def keep(rows, values):
            twin_out[kind, rows] = values.astype(jnp.bfloat16)

        return keep

    def finish(kind):
        exchange(kind).wait_recv()

        def step(index, carry):
            rows = pl.ds(pl.multiple_of(index * 128, 128), 128)
            mine_ref[kind, rows] = (
                mine_ref[kind, rows].astype(jnp.float32) + twin_in[kind, rows].astype(jnp.float32)
            ).astype(jnp.bfloat16)
            return carry

        lax.fori_loop(0, half // 128, step, 0)
        for by in range(1, EXPERTS):
            copy = give_back(kind, by)
            copy.start()
            started.append(copy)
        copy = pltpu.make_async_copy(
            mine_ref.at[kind, chunk(chip)], returned[kind].at[chunk(chip)], keep_sem.at[kind]
        )
        copy.start()
        copy.wait()

    def load(owner):
        parts = [
            (pay_ref.at[owner, :96], gate_w.at[pl.ds(pl.multiple_of(owner * 96, 16), 96)]),
            (pay_ref.at[owner, 96:192], up_w.at[pl.ds(pl.multiple_of(owner * 96, 16), 96)]),
            (
                pay_ref.at[owner, 192:, pl.ds(0, WIDTH)],
                down_w.at[pl.ds(pl.multiple_of(owner * 128, 16), 96)],
            ),
        ] + [
            (
                pay_ref.at[owner, pl.ds(192 + 32 * m, 32), pl.ds(WIDTH, 256)],
                down_w.at[pl.ds(pl.multiple_of(owner * 128 + 96, 16), 32), pl.ds(256 * m, 256)],
            )
            for m in range(3)
        ]
        return [
            pltpu.make_async_copy(source, target, load_sem.at[owner, number])
            for number, (source, target) in enumerate(parts)
        ]

    pass_on(1, 4)
    for owner in range(8):
        for copy in load(owner):
            copy.start()
    arrive(0)
    for owner in range(8):
        for copy in load(owner):
            copy.wait()
    forward(core, keep_mine(0))
    arrive(1)
    arrive_shared(0)
    forward(other, keep_twin(0))
    copy = exchange(0)
    copy.start()
    started.append(copy)
    backward(core, keep_mine(1))
    finish(0)
    arrive_shared(1)
    backward(other, keep_twin(1))
    copy = exchange(1)
    copy.start()
    started.append(copy)

    def down_tile(index, carry):
        lanes = pl.ds(pl.multiple_of(index * 256, 256), 256)
        part = dot_tn(hidden_ref[:, lanes], g_ref[...]).astype(jnp.bfloat16)
        for piece in (0, 1):
            rows = part[piece * 128 : piece * 128 + 128]
            d_pay_ref[2 * index + piece, 192:, :WIDTH] = rows[:96]
            for m in range(3):
                d_pay_ref[2 * index + piece, 192 + 32 * m : 224 + 32 * m, WIDTH:] = rows[
                    96:, 256 * m : 256 * m + 256
                ]
        return carry

    lax.fori_loop(0, 4, down_tile, 0)
    finish(1)

    def gate_tile(index, carry):
        lanes = pl.ds(pl.multiple_of(index * 256, 256), 256)
        for start, grad in ((0, d_gate), (96, d_up)):
            part = dot_tn(x_ref[...], grad[:, lanes]).astype(jnp.bfloat16)
            for piece in range(8):
                d_pay_ref[piece, start : start + 96, lanes] = part[piece * 96 : piece * 96 + 96]
        return carry

    lax.fori_loop(0, 4, gate_tile, 0)
    for kind in (0, 1):
        for by in range(1, EXPERTS):
            give_back(kind, by).wait_recv()
    for kind in (0, 1):
        for number in range(len(MESSAGES)):
            ring(kind, number).wait_send()
    for copy in started:
        copy.wait_send()


def pad_routing(prev_ref, wres_ref, prev_pad, wres_pad):
    prev_pad[...] = jnp.zeros_like(prev_pad)
    prev_pad[:NALL] = prev_ref[:, 0, :]
    wres_pad[...] = jnp.zeros_like(wres_pad)
    wres_pad[:NALL, :NALL] = wres_ref[...]


def run_forward(weights, few, tokens, segments, experts, prev, wres, routes, rank, cot):
    vmem, anywhere = pl.BlockSpec(memory_space=pltpu.VMEM), pl.BlockSpec(memory_space=pl.ANY)
    shape = jax.ShapeDtypeStruct
    low, wide = jnp.bfloat16, jnp.float32
    dma = pltpu.SemaphoreType.DMA
    half, whole = EXPERTS * SLOTS, 2 * EXPERTS * SLOTS
    left, right, small = (jnp.asarray(t, low) for t in placing_tables())
    return pl.pallas_call(
        forward_kernel,
        out_shape=[
            shape((BLK, WIDTH), wide),
            shape((BLK, WIDTH), low),
            shape((WIDTH, BLK), wide),
            shape((16, BLK), wide),
            shape((PAIRS, BLK, 128), low),
            shape((8, PAIRS, BLK, 128), low),
            shape((8, PAIRS, BLK, 128), low),
            shape((BLK, 128), wide),
            shape((BLK, 128), wide),
            shape((8, BLK + 16, WIDTH), low),
            shape((4, WIDTH, WIDTH), low),
            shape((WIDTH, 128), low),
            shape((8, 288, 1024), low),
            shape((half, WIDTH), low),
            shape((half, WIDTH), low),
            shape((8, 288, 1024), low),
        ],
        in_specs=[vmem] * 26,
        out_specs=[vmem] * 5 + [anywhere] * 2 + [vmem] * 5 + [anywhere] + [vmem] * 3,
        scratch_shapes=[
            *(pltpu.VMEM((4, 4, 4, 2, 16, lanes), low) for lanes in PART_LANES),
            pltpu.VMEM((16, 1280), low),
            pltpu.VMEM((HEADS, 128, BLK), low),
            pltpu.VMEM((WIDTH, BLK), low),
            pltpu.VMEM((BLK, BLK), wide),
            pltpu.VMEM((16, BLK), wide),
            pltpu.VMEM((16, BLK), wide),
            pltpu.VMEM((WIDTH, BLK), wide),
            pltpu.VMEM((128, BLK), wide),
            pltpu.VMEM((128, 128), wide),
            pltpu.VMEM((128, 128), wide),
            pltpu.VMEM((16, 128), wide),
            pltpu.VMEM((2, 2, PAIRS, BLK, 128), low),
            pltpu.VMEM((half, WIDTH), low),
            pltpu.VMEM((half, WIDTH), low),
            pltpu.VMEM((WIDTH, 1024), low),
            pltpu.VMEM((WIDTH, 1024), low),
            pltpu.VMEM((1024, WIDTH), low),
            pltpu.VMEM((whole, WIDTH), low),
            pltpu.VMEM((whole, WIDTH), low),
            pltpu.VMEM((whole, 1024), wide),
            pltpu.VMEM((whole, 1024), wide),
            pltpu.VMEM((whole, 1024), low),
            pltpu.VMEM((whole, 1024), low),
            pltpu.VMEM((whole, 1024), low),
            pltpu.VMEM((2, half, WIDTH), low),
            pltpu.VMEM((2, half, WIDTH), low),
            pltpu.VMEM((2, half, WIDTH), low),
            dma((3, 3, 3)),
            dma((3, 3, 3)),
            dma((3, 10)),
            dma((3, 10)),
            dma((9,)),
            dma((2, 15)),
            dma((2, 15)),
            dma((2, 2)),
            dma((8, 6)),
            dma((2, 7)),
            dma((2, 7)),
            dma((2, 8)),
            dma((2, 8)),
            dma((2,)),
            dma((2,)),
            dma((2, 7)),
            dma((2, 7)),
            dma((2,)),
        ],
        name="forward",
        compiler_params=pltpu.CompilerParams(
            collective_id=1, has_side_effects=True, vmem_limit_bytes=63 * 2**20
        ),
    )(
        *weights, *few, tokens, segments, *experts, left, right, small, *rope_tables(),
        prev, wres, routes, rank, cot,
    )


def split(values):
    high = values.astype(jnp.bfloat16)
    low = (values - high.astype(jnp.float32)).astype(jnp.bfloat16)
    return jnp.concatenate([high, low], axis=1)


def back_kernel(
    blocks_ref, w_ref, small_ref, cos_in, sin_in, cos_out, sin_out, left_ref, right_ref, place_ref,
    prev_ref, wres_ref, routes_ref, cot_ref,
    state_ref, normed_ref, att_ref, lse_ref, q_ref, keys_ref, values_ref, info_ref, proj_ref,
    back_rows_ref, back_grads_ref, d_pay_ref,
    out_ref, prev_grad_ref, total_ref, tokens_grad_ref, sums_ref, few_ref,
    gate_out, up_out, down_out,
    *scratch,
):
    (
        qt_ref, ot_ref, o_ref, qm_ref, bias_ref, inner_ref, dqt_ref, gain_ref, dk_ref, dv_ref,
        prev_pad, wres_pad, dw_ref, dw_low, few_sum, kv_ref, tok_ref, mine_ref, kv_sem, own_ref, state_grad_ref, others_ref, grads_ref, block_in,
        pay_ref, pay_in, small_in, small_sum,
        block_send, block_recv, exp_send, exp_recv, load_sem,
        net_send, net_recv, twin_send, twin_recv, small_send, small_recv,
        *more,
    ) = scratch
    twin_in, in_one, in_two, in_three, sum_one, sum_two = (
        more[0], more[1:4], more[4:7], more[7:10], more[10:13], more[13:16]
    )
    tables = (cos_in, sin_in, cos_out, sin_out)
    ctx, fsdp = lax.axis_index("ctx"), lax.axis_index("fsdp")
    *spot, core = place()
    spot = tuple(spot)
    twin = device_at(*spot, 1 - core)
    started = []
    greet(torus_peers(spot, core) + sequence_peers(spot, core))

    along, side = ctx // 2, ctx % 2

    def rows_of(number):
        first, last = (PAY_CUTS[i] for i in SPANS[MESSAGES[number][2]])
        return first, last - first

    def owner(steps, across_it):
        return ((along + steps + 4) % 4) * 2 + (side if across_it == 0 else 1 - side)

    def expert(number):
        to, (steps, across_it), _ = MESSAGES[number]
        first, count = rows_of(number)
        landing = sum(rows_of(before)[1] for before in range(number))
        return pltpu.make_async_remote_copy(
            src_ref=pay_ref.at[
                owner(steps - to, across_it if to else 1 - across_it), pl.ds(first, count)
            ],
            dst_ref=pay_in.at[pl.ds(landing, count)],
            send_sem=exp_send.at[number],
            recv_sem=exp_recv.at[number],
            device_id={"ctx": owner(-to, 0 if to else 1), "fsdp": fsdp},
            device_id_type=MESH,
        )

    def send_experts(numbers):
        for number in numbers:
            expert(number).start()

    def add_experts(numbers):
        for number in numbers:
            expert(number).wait_recv()
            _, (steps, across_it), _ = MESSAGES[number]
            first, count = rows_of(number)
            landing = sum(rows_of(before)[1] for before in range(number))
            at = owner(steps, across_it)

            def add_rows(index, carry, at=at, first=first, landing=landing):
                here = pl.ds(pl.multiple_of(first + index * 16, 16), 16)
                there = pl.ds(pl.multiple_of(landing + index * 16, 16), 16)
                pay_ref[at, here] = (
                    pay_ref[at, here].astype(jnp.float32) + pay_in[there].astype(jnp.float32)
                ).astype(jnp.bfloat16)
                return carry

            lax.fori_loop(0, count // 16, add_rows, 0)

    loads = [
        pltpu.make_async_copy(d_pay_ref.at[index], pay_ref.at[index], load_sem.at[1 + index])
        for index in range(8)
    ]
    for copy in loads:
        copy.start()
    for copy in loads:
        copy.wait()
    send_experts((13, 14, 11, 12, 7, 8, 9, 10))
    own_block = pltpu.make_async_copy(blocks_ref.at[ctx], mine_ref, load_sem.at[0])
    own_block.start()

    def load_kv(index, slot):
        return [
            pltpu.make_async_copy(source.at[index], kv_ref.at[slot, kind], kv_sem.at[slot, kind])
            for kind, source in enumerate((keys_ref, values_ref))
        ] + [pltpu.make_async_copy(blocks_ref.at[index], tok_ref.at[slot], kv_sem.at[slot, 2])]

    for copy in load_kv(0, 0):
        copy.start()

    def block_copy(by, target):
        return pltpu.make_async_remote_copy(
            src_ref=others_ref.at[target],
            dst_ref=block_in.at[by - 1],
            send_sem=block_send.at[by - 1],
            recv_sem=block_recv.at[by - 1],
            device_id={"ctx": target, "fsdp": fsdp},
            device_id_type=MESH,
        )

    across = small_ref[...].astype(jnp.float32).T
    gain_one, gain_two = across[18:19], across[19:20]
    value_rows = across[16:18]

    lanes = lax.broadcasted_iota(jnp.int32, (BLK, 128), 1)
    info = info_ref[...]
    gates = (info[:, 0:1], info[:, 1:2])
    slots = lax.broadcasted_iota(jnp.int32, (BLK, EXPERTS * SLOTS), 1).astype(jnp.float32)
    tables_of = [
        (slots == info[:, 2 + k : 3 + k]).astype(jnp.float32).astype(jnp.bfloat16) for k in (0, 1)
    ]
    route_rows = routes_ref[...].astype(jnp.float32)
    routes = (column(route_rows[0:1]), column(route_rows[1:2]))
    hots = [lanes.astype(jnp.float32) == routes[k] for k in (0, 1)]
    named = [
        [(routes[k] == EXPERTS + 1 + kind).astype(jnp.float32) for kind in range(3)] for k in (0, 1)
    ]
    proj = proj_ref[...]
    mixes = []
    for c in (0, 1):
        first, second = proj[:, 12 + 2 * c : 13 + 2 * c], proj[:, 13 + 2 * c : 14 + 2 * c]
        top = jnp.maximum(first, second)
        first, second = jnp.exp(first - top), jnp.exp(second - top)
        mixes.append((first / (first + second), second / (first + second)))
    normed_low = normed_ref[...]
    normed_two = normed_low.astype(jnp.float32)
    upstream_low = cot_ref[...]
    upstream = upstream_low.astype(jnp.float32)
    state = state_ref[...]
    back_rows = back_rows_ref[...]
    result = state
    gate_grads = []
    for k in (0, 1):
        copy, one, two = named[k]
        pair = dot(tables_of[k], back_rows)
        pair = pair + (copy + one * mixes[0][0] + two * mixes[1][0]) * normed_two
        pair = pair + (one * mixes[0][1]) * value_rows[0:1] + (two * mixes[1][1]) * value_rows[1:2]
        result = result + gates[k] * pair
        gate_grads.append(jnp.sum(pair * upstream, axis=1, keepdims=True))
    out_ref[...] = result.astype(jnp.bfloat16)
    inner = gates[0] * gate_grads[0] + gates[1] * gate_grads[1]
    logit_grad = jnp.zeros((BLK, 128), jnp.float32)
    for k in (0, 1):
        logit_grad = logit_grad + jnp.where(hots[k], gates[k] * (gate_grads[k] - inner), 0.0)
    pad_routing(prev_ref, wres_ref, prev_pad, wres_pad)
    prev_grad_ref[...] = lax.dot_general(
        wres_pad[...], logit_grad, (((1,), (1,)), ((), ())),
        precision=highest, preferred_element_type=jnp.float32,
    )[:16]
    small_sum[3] = jnp.dot(
        prev_pad[...], logit_grad, precision=highest, preferred_element_type=jnp.float32
    )[:16]
    on_normed = jnp.sum(normed_two * upstream, axis=1, keepdims=True)
    on_vectors = dot(upstream_low, small_ref[...])
    flat = logit_grad
    weight_up = gates[0] * named[0][0] + gates[1] * named[1][0]
    vector_weights = jnp.zeros((BLK, 128), jnp.float32)
    for c in (0, 1):
        scale = gates[0] * named[0][1 + c] + gates[1] * named[1][1 + c]
        mix_0, mix_1 = mixes[c]
        m_0, m_1 = scale * on_normed, scale * on_vectors[:, 16 + c : 17 + c]
        mean = mix_0 * m_0 + mix_1 * m_1
        flat = flat + jnp.where(lanes == 12 + 2 * c, mix_0 * (m_0 - mean), 0.0)
        flat = flat + jnp.where(lanes == 13 + 2 * c, mix_1 * (m_1 - mean), 0.0)
        weight_up = weight_up + mix_0 * scale
        vector_weights = vector_weights + jnp.where(lanes == 16 + c, mix_1 * scale, 0.0)
    flat_split = split(flat)
    normed_grad = dot_nt(flat_split, jnp.concatenate([small_ref[...]] * 2, axis=1))
    normed_grad = normed_grad + weight_up * upstream
    normed_grad = normed_grad + dot(tables_of[0] + tables_of[1], back_grads_ref[...])
    normed_across = normed_two.T.astype(jnp.bfloat16)
    upstream_across = upstream.T.astype(jnp.bfloat16)
    small_grad = dot(normed_across, flat_split)
    small_vector = dot(upstream_across, split(vector_weights))
    small_grad = small_grad[:, :128] + small_grad[:, 128:] + small_vector[:, :128] + small_vector[:, 128:]
    scale_two = rms_rows(state)
    weighted = normed_grad * gain_two
    state_grad = (
        upstream
        + scale_two * weighted
        - state * (scale_two**3 * jnp.mean(weighted * state, axis=-1, keepdims=True))
    )
    state_grad_ref[...] = state_grad
    gain_two_row = jnp.sum(normed_grad * state * scale_two, axis=0, keepdims=True)
    state_low = state_grad.astype(jnp.bfloat16)
    attended = att_ref[...]
    dw_low[1] = dot(attended.astype(jnp.bfloat16), state_low).astype(jnp.bfloat16)
    att_grad = dot_nt(state_low, w_ref[3])
    blank = jnp.zeros((HDIM, BLK), jnp.bfloat16)
    low_half = lax.broadcasted_iota(jnp.int32, (BLK, 128), 1) < HDIM
    none = jnp.zeros((BLK, 128), jnp.bfloat16)
    inner_ref[...] = jnp.zeros_like(inner_ref)
    for pair in range(PAIRS):
        part = att_grad[:, pair * 128 : pair * 128 + 128].astype(jnp.bfloat16)
        across_o = part.astype(jnp.float32).T
        products = across_o * attended[pair * 128 : pair * 128 + 128]
        across_o = across_o.astype(jnp.bfloat16)
        across_q = q_ref[pair].astype(jnp.float32).T.astype(jnp.bfloat16)
        for half in (0, 1):
            head = 2 * pair + half
            rows = slice(half * HDIM, half * HDIM + HDIM)
            inner_ref[head : head + 1] = jnp.sum(products[rows], axis=0, keepdims=True)
            order = (lambda a, b: [a, b]) if half == 0 else (lambda a, b: [b, a])
            ot_ref[head] = jnp.concatenate(order(across_o[rows], blank), axis=0)
            qt_ref[head] = jnp.concatenate(order(across_q[rows], blank), axis=0)
        o_ref[pair, :BLK] = jnp.where(low_half, part, none)
        o_ref[pair, BLK:] = jnp.where(low_half, none, part)
        qm_ref[pair, :BLK] = jnp.where(low_half, q_ref[pair], none)
        qm_ref[pair, BLK:] = jnp.where(low_half, none, q_ref[pair])
    dqt_ref[...] = jnp.zeros_like(dqt_ref)
    dw_ref[...] = jnp.zeros_like(dw_ref)
    gain_ref[...] = jnp.zeros_like(gain_ref)

    own_block.wait()

    def normed_block(array):
        wide = array[:BLK].astype(jnp.float32)
        scaled = wide * rms_rows(wide)
        return scaled, (scaled * gain_one).T.astype(jnp.bfloat16)

    def block(index, carry):
        slot = index % 2
        for copy in load_kv(index, slot):
            copy.wait()

        @pl.when(index < ctx)
        def _():
            for copy in load_kv(index + 1, 1 - slot):
                copy.start()

        mask_bias(tok_ref.at[slot], mine_ref, bias_ref, ctx, index)
        cosine, sine = turning(index, tables)
        for pair in range(PAIRS):
            key, value = kv_ref[slot, 0, pair], kv_ref[slot, 1, pair]
            key_across = key.astype(jnp.float32).T.astype(jnp.bfloat16)
            weights, score_grads = [], []
            for half in (0, 1):
                head = 2 * pair + half
                scores = dot(key, qt_ref[head]) + bias_ref[...]
                weight = jnp.exp(scores - lse_ref[head : head + 1])
                weight_grad = dot(value, ot_ref[head])
                score_grad = (weight * (weight_grad - inner_ref[head : head + 1])).astype(jnp.bfloat16)
                weights.append(weight.astype(jnp.bfloat16))
                score_grads.append(score_grad)
                rows = slice(head * HDIM, head * HDIM + HDIM)
                dqt_ref[rows] += dot(key_across[half * HDIM : half * HDIM + HDIM], score_grad)
            lanes = slice(pair * 128, pair * 128 + 128)
            dv_ref[:, lanes] = dot(jnp.concatenate(weights, axis=1), o_ref[pair]).astype(jnp.bfloat16)
            dk = dot(jnp.concatenate(score_grads, axis=1), qm_ref[pair])
            dk_ref[:, lanes] = (dk * cosine - swapped(dk) * sine).astype(jnp.bfloat16)
        scaled, normed_across = normed_block(tok_ref.at[slot])
        dw_ref[0] += dot(normed_across, dk_ref[...])
        dw_ref[1] += dot(normed_across, dv_ref[...])
        first = dot_nt(dk_ref[...], w_ref[1]) + dot_nt(dv_ref[...], w_ref[2])
        gain_ref[...] += jnp.sum(first * scaled, axis=0, keepdims=True)

        @pl.when(index < ctx)
        def _():
            others_ref[index] = first.astype(jnp.bfloat16)
            block_copy(ctx - index, index).start()

        @pl.when(index == ctx)
        def _():
            own_ref[...] = first

        for when, came, then in (
            (0, (13, 14), (5, 6)),
            (1, (3, 4), (2,)),
            (3, (7, 8, 9, 10, 5, 6), (0, 1)),
        ):

            @pl.when(index == jnp.minimum(ctx, when))
            def _(came=came, then=then):
                add_experts(came)
                send_experts(then)

        return carry

    add_experts((11, 12))
    send_experts((3, 4))
    lax.fori_loop(0, ctx + 1, block, 0)
    cosine, sine = turning(ctx, tables)
    for pair in range(PAIRS):
        lanes = slice(pair * 128, pair * 128 + 128)
        dq = dqt_ref[lanes, :].T * (HDIM**-0.5)
        dk_ref[:, lanes] = (dq * cosine - swapped(dq) * sine).astype(jnp.bfloat16)
    scaled, normed_across = normed_block(mine_ref)
    dw_low[0] = dot(normed_across, dk_ref[...]).astype(jnp.bfloat16)
    first = dot_nt(dk_ref[...], w_ref[0])
    own_ref[...] += first
    gain_one_row = gain_ref[...] + jnp.sum(first * scaled, axis=0, keepdims=True)
    lanes = lax.broadcasted_iota(jnp.int32, (WIDTH, 128), 1)
    ones = jnp.broadcast_to(gain_one_row, (128, WIDTH)).T
    twos = jnp.broadcast_to(gain_two_row, (128, WIDTH)).T
    few = jnp.where(lanes == 18, ones, jnp.where(lanes == 19, twos, small_grad))
    few_sum[...] = few

    def share(x):
        return pltpu.make_async_remote_copy(
            src_ref=grads_ref.at[x, :, :, 1 - core],
            dst_ref=twin_in.at[x],
            send_sem=twin_send.at[x],
            recv_sem=twin_recv.at[x],
            device_id=twin,
            device_id_type=MESH,
        )

    def pack(group, carry):
        rows = pl.ds(pl.multiple_of(group * 48, 16), 48)

        def lane_half(start):
            lanes = slice(start, start + 384)
            query, output = dw_low[0, rows, lanes], dw_low[1, rows, lanes]
            key, value = (dw_ref[w, rows, lanes].astype(jnp.bfloat16) for w in (0, 1))
            return jnp.concatenate([query, key, value, output], axis=0)

        from_left = dot(left_ref[...], lane_half(0))
        from_right = dot(right_ref[...], lane_half(384))
        placed = dot(place_ref[...], few_sum[rows].astype(jnp.bfloat16))
        whole = jnp.concatenate(
            [from_left[:128], from_right[:128], from_left[128:] + from_right[128:], placed], axis=1
        )
        grads_ref[group // 4, group % 4] = whole.astype(jnp.bfloat16).reshape(4, 2, 16, 1280)
        return carry

    for x in range(4):
        lax.fori_loop(4 * x, 4 * x + 4, pack, 0)
        copy = share(x)
        copy.start()
        started.append(copy)

    def net(part, step, by, source, target):
        axis = PART_ORDER[part][2 - step]
        return pltpu.make_async_remote_copy(
            src_ref=source,
            dst_ref=target,
            send_sem=net_send.at[part, step, by - 1],
            recv_sem=net_recv.at[part, step, by - 1],
            device_id=device_at(*shifted(spot, axis, by), core),
            device_id_type=MESH,
        )

    def small(axis, by, source, slot):
        device = twin if axis == 3 else device_at(*shifted(spot, axis, by), core)
        return pltpu.make_async_remote_copy(
            src_ref=source,
            dst_ref=small_in.at[axis, slot],
            send_sem=small_send.at[axis, by - 1],
            recv_sem=small_recv.at[axis, by - 1],
            device_id=device,
            device_id_type=MESH,
        )

    copy = small(3, 1, small_sum.at[3], core)
    copy.start()
    started.append(copy)

    for x in range(4):
        share(x).wait_recv()

        def add_pair(index, carry, x=x):
            z, y = index // 4, index % 4
            grads_ref[x, z, y, core] = (
                grads_ref[x, z, y, core].astype(jnp.float32) + twin_in[x, z, y].astype(jnp.float32)
            ).astype(jnp.bfloat16)
            return carry

        lax.fori_loop(0, 16, add_pair, 0, unroll=2)

    def lanes_of(part):
        return pl.ds(PART_START[part], PART_LANES[part])

    for part in range(3):
        axis = PART_ORDER[part][2]
        for by in (1, 2, 3):
            at = shifted(spot, axis, by)[axis]
            index = tuple(at if a == axis else slice(None) for a in range(3))
            copy = net(
                part, 0, by, grads_ref.at[(*index, core, slice(None), lanes_of(part))], in_one[part].at[by - 1]
            )
            copy.start()
            started.append(copy)

    small(3, 1, small_sum.at[3], 1 - core).wait_recv()
    small_in[3, core] = small_sum[3]
    small_sum[0] = small_in[3, 0] + small_in[3, 1]
    for by in (1, 2, 3):
        copy = small(0, by, small_sum.at[0], spot[0])
        copy.start()
        started.append(copy)

    def small_step(axis):
        for by in (1, 2, 3):
            small(axis, by, small_sum.at[axis], shifted(spot, axis, -by)[axis]).wait_recv()
        small_in[axis, spot[axis]] = small_sum[axis]
        total = small_in[axis, 0] + small_in[axis, 1] + small_in[axis, 2] + small_in[axis, 3]
        if axis == 2:
            total_ref[...] = total
            return
        small_sum[axis + 1] = total
        for by in (1, 2, 3):
            copy = small(axis + 1, by, small_sum.at[axis + 1], spot[axis + 1])
            copy.start()
            started.append(copy)

    for part in range(3):
        first, second, third = PART_ORDER[part]
        for by in (1, 2, 3):
            net(part, 0, by, in_one[part].at[by - 1], in_one[part].at[by - 1]).wait_recv()
        rest = tuple(a for a in (0, 1, 2) if a != third)
        lanes = slice(PART_START[part], PART_START[part] + PART_LANES[part])

        def add_four(index, carry, part=part, third=third, rest=rest, lanes=lanes):
            at = {rest[0]: index // 4, rest[1]: index % 4, third: spot[third]}
            total = grads_ref[at[0], at[1], at[2], core, :, lanes].astype(jnp.float32)
            for by in range(3):
                total = total + in_one[part][by, index // 4, index % 4].astype(jnp.float32)
            sum_one[part][index // 4, index % 4] = total.astype(jnp.bfloat16)
            return carry

        lax.fori_loop(0, 16, add_four, 0, unroll=2)
        for by in (1, 2, 3):
            at = shifted(spot, second, by)[second]
            source = sum_one[part].at[at] if second == rest[0] else sum_one[part].at[:, at]
            copy = net(part, 1, by, source, in_two[part].at[by - 1])
            copy.start()
            started.append(copy)
    small_step(0)

    for number in (0, 1, 2):
        expert(number).wait_recv()
    count = PAY_CUTS[-1]

    def total_rows(start):
        rows = pl.ds(pl.multiple_of(start, 16), 16)
        total = pay_ref[ctx, rows].astype(jnp.float32)
        for number in range(3):
            there = pl.ds(pl.multiple_of(number * count + start, 16), 16)
            total = total + pay_in[there].astype(jnp.float32)
        return total

    def gate_rows(index, carry):
        rows = pl.ds(pl.multiple_of(index * 16, 16), 16)
        gate_out[rows] = total_rows(index * 16)
        up_out[rows] = total_rows(96 + index * 16)
        return carry

    lax.fori_loop(0, 6, gate_rows, 0)
    for index in range(6):
        total = total_rows(192 + 16 * index)
        down_out[16 * index : 16 * index + 16] = total[:, :WIDTH]
        start = 96 + 16 * (index % 2)
        lanes = slice(256 * (index // 2), 256 * (index // 2) + 256)
        down_out[start : start + 16, lanes] = total[:, WIDTH:]

    for part in range(3):
        first, second, third = PART_ORDER[part]
        for by in (1, 2, 3):
            net(part, 1, by, in_two[part].at[by - 1], in_two[part].at[by - 1]).wait_recv()
        rest = tuple(a for a in (0, 1, 2) if a != third)
        for index in range(4):
            if second == rest[0]:
                total = sum_one[part][spot[second], index].astype(jnp.float32)
            else:
                total = sum_one[part][index, spot[second]].astype(jnp.float32)
            for by in range(3):
                total = total + in_two[part][by, index].astype(jnp.float32)
            sum_two[part][index] = total.astype(jnp.bfloat16)
        for by in (1, 2, 3):
            at = shifted(spot, first, by)[first]
            copy = net(part, 2, by, sum_two[part].at[at], in_three[part].at[by - 1])
            copy.start()
            started.append(copy)
    small_step(1)

    for by in range(1, 8):

        @pl.when(ctx + by < 8)
        def _(by=by):
            block_copy(by, ctx).wait_recv()
            own_ref[...] += block_in[by - 1].astype(jnp.float32)

        @pl.when(ctx - by >= 0)
        def _(by=by):
            block_copy(by, ctx - by).wait_send()

    wide = mine_ref[:BLK].astype(jnp.float32)
    scale = rms_rows(wide)
    weighted = own_ref[...] * gain_one
    tokens_grad_ref[...] = (
        state_grad_ref[...]
        + scale * weighted
        - wide * (scale**3 * jnp.mean(weighted * wide, axis=-1, keepdims=True))
    )
    finals = []
    for part in range(3):
        first = PART_ORDER[part][0]
        for by in (1, 2, 3):
            net(part, 2, by, in_three[part].at[by - 1], in_three[part].at[by - 1]).wait_recv()
        total = sum_two[part][spot[first]].astype(jnp.float32)
        for by in range(3):
            total = total + in_three[part][by].astype(jnp.float32)
        finals.append(total)
    final = jnp.concatenate(finals, axis=1)
    sums_ref[:16] = final[:, :768]
    sums_ref[16:] = jnp.concatenate([final[:8, 768:1152], final[8:, 768:1152]], axis=1)
    few_ref[...] = final[:8, 1152:]
    small_step(2)
    for number in range(len(MESSAGES)):
        expert(number).wait_send()
    for copy in started:
        copy.wait_send()


def run_back(blocks, weights, smalls, prev, wres, routes, cot, kept, back_rows, back_grads, d_pay):
    vmem, anywhere = pl.BlockSpec(memory_space=pltpu.VMEM), pl.BlockSpec(memory_space=pl.ANY)
    shape = jax.ShapeDtypeStruct
    low, wide = jnp.bfloat16, jnp.float32
    dma = pltpu.SemaphoreType.DMA
    left, right, small = (jnp.asarray(t.T, low) for t in placing_tables())
    by_part = lambda *lead: [pltpu.VMEM((*lead, 16, lanes), low) for lanes in PART_LANES]
    return pl.pallas_call(
        back_kernel,
        out_shape=[
            shape((BLK, WIDTH), low),
            shape((16, BLK), wide),
            shape((16, 128), wide),
            shape((BLK, WIDTH), wide),
            shape((24, WIDTH), wide),
            shape((8, 128), wide),
            shape((96, 1024), wide),
            shape((96, 1024), wide),
            shape((128, WIDTH), wide),
        ],
        in_specs=[anywhere] + [vmem] * 18 + [anywhere] * 2 + [vmem] * 4 + [anywhere],
        out_specs=[vmem] * 9,
        scratch_shapes=[
            pltpu.VMEM((HEADS, 128, BLK), low),
            pltpu.VMEM((HEADS, 128, BLK), low),
            pltpu.VMEM((PAIRS, 2 * BLK, 128), low),
            pltpu.VMEM((PAIRS, 2 * BLK, 128), low),
            pltpu.VMEM((BLK, BLK), wide),
            pltpu.VMEM((16, BLK), wide),
            pltpu.VMEM((WIDTH, BLK), wide),
            pltpu.VMEM((1, WIDTH), wide),
            pltpu.VMEM((BLK, WIDTH), low),
            pltpu.VMEM((BLK, WIDTH), low),
            pltpu.VMEM((128, BLK), wide),
            pltpu.VMEM((128, 128), wide),
            pltpu.VMEM((2, WIDTH, WIDTH), wide),
            pltpu.VMEM((2, WIDTH, WIDTH), low),
            pltpu.VMEM((WIDTH, 128), wide),
            pltpu.VMEM((2, 2, PAIRS, BLK, 128), low),
            pltpu.VMEM((2, BLK + 16, WIDTH), low),
            pltpu.VMEM((BLK + 16, WIDTH), low),
            dma((2, 3)),
            pltpu.VMEM((BLK, WIDTH), wide),
            pltpu.VMEM((BLK, WIDTH), wide),
            pltpu.VMEM((7, BLK, WIDTH), low),
            pltpu.VMEM((4, 4, 4, 2, 16, 1280), low),
            pltpu.VMEM((7, BLK, WIDTH), low),
            pltpu.VMEM((8, 288, 1024), low),
            pltpu.VMEM((2016, 1024), low),
            pltpu.VMEM((4, 4, 16, 128), wide),
            pltpu.VMEM((4, 16, 128), wide),
            dma((7,)),
            dma((7,)),
            dma((15,)),
            dma((15,)),
            dma((9,)),
            dma((3, 3, 3)),
            dma((3, 3, 3)),
            dma((4,)),
            dma((4,)),
            dma((4, 3)),
            dma((4, 3)),
            pltpu.VMEM((4, 4, 4, 16, 1280), low),
            *by_part(3, 4, 4),
            *by_part(3, 4),
            *by_part(3),
            *by_part(4, 4),
            *by_part(4),
        ],
        name="back",
        compiler_params=pltpu.CompilerParams(
            collective_id=2, has_side_effects=True, vmem_limit_bytes=62 * 2**20
        ),
    )(
        blocks, weights, smalls, *rope_tables(), left, right, small, prev, wres, routes, cot,
        *kept, back_rows, back_grads, d_pay,
    )


def finish_kernel(
    out_in, tokens_in, gate_in, up_in, down_in, prev_in, total_in, sums_in, few_in,
    out, tokens_grad, gate, up, down, prev, total, sum_q, sum_k, sum_v, sum_o,
    gain_one, gain_two, router, constant, vectors, prev_at, total_at, sums_at, few_at, sems,
):
    pairs = (
        (prev_in, prev_at), (total_in, total_at), (sums_in, sums_at), (few_in, few_at),
        (tokens_in, tokens_grad), (out_in, out), (gate_in, gate), (up_in, up), (down_in, down),
    )
    copies = [
        pltpu.make_async_copy(source, target, sems.at[index])
        for index, (source, target) in enumerate(pairs)
    ]
    for copy in copies:
        copy.start()
    for copy in copies[:4]:
        copy.wait()
    prev[:, 0, :] = prev_at[:NALL]
    total[...] = total_at[:NALL, :NALL]
    for weight, ref in enumerate((sum_q, sum_k, sum_v, sum_o)):
        ref[...] = sums_at[weight * 6 : weight * 6 + 6]
    few = few_at[...]
    router[...] = few[:6, :NALL]
    tall = jnp.concatenate([few, jnp.zeros((120, 128), jnp.float32)], axis=0).T
    constant[...] = tall[12:16, :6]
    vectors[...] = tall[16:18, :6]
    gain_one[...] = tall[18:19, :6]
    gain_two[...] = tall[19:20, :6]
    for copy in copies[4:]:
        copy.wait()


def finish(out, tokens_grad, gate, up, down, prev, total, sums, few):
    vmem = pl.BlockSpec(memory_space=pltpu.VMEM)
    shape = jax.ShapeDtypeStruct
    wide = jnp.float32
    like = [shape(a.shape, a.dtype) for a in (out, tokens_grad, gate, up, down)]
    few_shapes = [(1, 6), (1, 6), (6, NALL), (4, 6), (2, 6)]
    return pl.pallas_call(
        finish_kernel,
        out_shape=like
        + [shape((NALL, 1, BLK), wide), shape((NALL, NALL), wide)]
        + [shape((6, WIDTH), wide)] * 4
        + [shape(s, wide) for s in few_shapes],
        in_specs=[pl.BlockSpec(memory_space=pl.ANY)] * 9,
        out_specs=[vmem] * 16,
        scratch_shapes=[
            *(pltpu.VMEM(a.shape, a.dtype) for a in (prev, total, sums, few)),
            pltpu.SemaphoreType.DMA((9,)),
        ],
        name="finish",
        compiler_params=pltpu.CompilerParams(vmem_limit_bytes=62 * 2**20),
    )(out, tokens_grad, gate, up, down, prev, total, sums, few)


def on_device(
    tokens, prev_logits, routes, segments, rank_order, norm_first, w_query, w_key, w_value, w_output,
    norm_second, w_router, w_residual, w_constant, v_constant, w_gate, w_up, w_down, cotangent,
):
    few = [w_router, w_constant.T, v_constant.T, norm_first[None], norm_second[None]]
    prev = jnp.transpose(prev_logits, (2, 0, 1))
    (
        state, normed, att, lse, q, keys, values, info, proj, blocks, weights, smalls, _,
        back_rows, back_grads, d_pay,
    ) = run_forward(
        [w_query, w_key, w_value, w_output], few, tokens[0], segments, (w_gate[0], w_up[0], w_down[0]),
        prev, w_residual, routes[0].T, rank_order[0], cotangent[0],
    )
    (
        out, prev_grad, residual, tokens_grad, sums, small, d_gate, d_up, d_down,
    ) = run_back(
        blocks, weights, smalls, prev, w_residual, routes[0].T, cotangent[0],
        (state, normed, att, lse, q, keys, values, info, proj), back_rows, back_grads, d_pay,
    )
    (
        out, tokens_grad, d_gate, d_up, d_down, prev_grad, residual, sum_q, sum_k, sum_v, sum_o,
        gain_one, gain_two, router, constant, vectors,
    ) = finish(out, tokens_grad, d_gate, d_up, d_down, prev_grad, residual, sums, small)
    return (
        out[None],
        tokens_grad[None],
        jnp.transpose(prev_grad, (1, 2, 0)),
        gain_one[0],
        sum_q,
        sum_k,
        sum_v,
        sum_o,
        gain_two[0],
        router,
        residual,
        constant.T,
        vectors.T,
        d_gate[None],
        d_up[None],
        d_down[None],
    )


def solution(mesh):
    in_specs = (
        P("fsdp", "ctx", None),
        P("fsdp", "ctx", None),
        P("fsdp", "ctx", None),
        P("fsdp", "ctx"),
        P("fsdp", "ctx", None),
        P(("ctx", "fsdp")),
        P(("ctx", "fsdp"), None),
        P(("ctx", "fsdp"), None),
        P(("ctx", "fsdp"), None),
        P(("ctx", "fsdp"), None),
        P(("ctx", "fsdp")),
        P(("ctx", "fsdp"), None),
        P(),
        P(("ctx", "fsdp"), None),
        P(("ctx", "fsdp"), None),
        P("fsdp", "ctx", None),
        P("fsdp", "ctx", None),
        P("fsdp", "ctx", None),
        P("fsdp", "ctx", None),
    )
    out_specs = (
        P("fsdp", "ctx", None),
        P("fsdp", "ctx", None),
        P("fsdp", "ctx", None),
        P(("ctx", "fsdp")),
        P(("ctx", "fsdp"), None),
        P(("ctx", "fsdp"), None),
        P(("ctx", "fsdp"), None),
        P(("ctx", "fsdp"), None),
        P(("ctx", "fsdp")),
        P(("ctx", "fsdp"), None),
        P(),
        P(("ctx", "fsdp"), None),
        P(("ctx", "fsdp"), None),
        P("fsdp", "ctx", None),
        P("fsdp", "ctx", None),
        P("fsdp", "ctx", None),
    )
    return jax.shard_map(
        on_device, mesh=mesh, in_specs=in_specs, out_specs=out_specs, check_vma=False
    )
```

```python
import functools

import jax
import jax.numpy as jnp
import numpy as np
from jax import lax
from jax.experimental import pallas as pl
from jax.experimental.pallas import tpu as pltpu
from jax.sharding import PartitionSpec as P

HEADS = 12
HDIM = 64
EXPERTS = 8
NALL = 12
CAP = 54
WIDTH = HEADS * HDIM
PAIRS = HEADS // 2
BLK = 256
SLOTS = 64

highest = lax.Precision.HIGHEST
masked_score = -1e30
epsilon = 1e-06

MESH = pl.DeviceIdType.MESH
PART_LANES = (512, 384, 384)
PART_START = (0, 512, 896)
PART_ORDER = ((0, 1, 2), (1, 2, 0), (2, 0, 1))

BLOCK_CUTS = (0, 64, 144, 224, 272)
PAY_CUTS = (0, 64, 144, 224, 288)
GRAD_CUTS = (0, 80, 144, 208, 288)
SPANS = {"all": (0, 4), "p": (1, 3), "h1": (0, 2), "h2": (2, 4), "q1": (0, 1), "p1": (1, 2), "p2": (2, 3), "q2": (3, 4)}
MESSAGES = (
    (1, (0, 0), "all"), (-1, (0, 0), "all"), (0, (0, 0), "all"),
    (1, (0, 1), "p"), (-1, (0, 1), "p"),
    (1, (-1, 0), "h1"), (-1, (1, 0), "h2"),
    (0, (-1, 0), "q1"), (0, (-1, 0), "q2"), (0, (1, 0), "q1"), (0, (1, 0), "q2"),
    (1, (-1, 1), "p1"), (-1, (1, 1), "p2"),
    (0, (2, 0), "q1"), (0, (2, 0), "q2"),
)


def place():
    ctx = lax.axis_index("ctx")
    fsdp = lax.axis_index("fsdp")
    return ctx // 2, (ctx % 2) * 2 + fsdp // 8, (fsdp // 2) % 4, fsdp % 2


def device_at(x, z, y, core):
    return {"ctx": x * 2 + z // 2, "fsdp": (z % 2) * 8 + y * 2 + core}


def shifted(spot, axis, by):
    moved = list(spot)
    moved[axis] = (moved[axis] + by) % 4
    return tuple(moved)


def greet(devices):
    barrier = pltpu.get_barrier_semaphore()
    for device in devices:
        pl.semaphore_signal(barrier, inc=1, device_id=device, device_id_type=MESH)
    pl.semaphore_wait(barrier, len(devices))


def torus_peers(spot, core):
    peers = [device_at(*shifted(spot, axis, by), core) for axis in range(3) for by in (1, 2, 3)]
    return peers + [device_at(*spot, 1 - core)]


def sequence_peers(spot, core):
    x, z, y = spot
    return [device_at((x + by) % 4, (z + 2) % 4, y, core) for by in (1, 2, 3)]


def region(ref, spot, core, whole):
    return ref.at[
        tuple(slice(None) if axis in whole else spot[axis] for axis in range(3)) + (core,)
    ]


def placing_tables():
    left = np.zeros((192, 256), np.float32)
    right = np.zeros((192, 256), np.float32)
    small = np.zeros((48, 128), np.float32)
    for device in range(8):
        for weight in range(4):
            for row in range(6):
                at, line = weight * 48 + device * 6 + row, weight * 6 + row
                if line < 16:
                    left[at, device * 16 + line] = right[at, device * 16 + line] = 1
                else:
                    left[at, 128 + device * 16 + line - 16] = 1
                    right[at, 128 + device * 16 + line - 8] = 1
        for row in range(6):
            small[device * 6 + row, device * 16 + row] = 1
    return left, right, small


def rope_tables():
    frequency = 10000.0 ** (-2.0 * (np.arange(128) % 32) / HDIM)
    inner = np.arange(BLK)[:, None] * frequency
    outer = (np.arange(8) * BLK)[:, None] * frequency
    return [jnp.asarray(t, jnp.float32) for t in (np.cos(inner), np.sin(inner), np.cos(outer), np.sin(outer))]


def turning(index, tables):
    cos_in, sin_in, cos_out, sin_out = tables
    ca, sa = cos_out[pl.ds(index, 1), :], sin_out[pl.ds(index, 1), :]
    cb, sb = cos_in[...], sin_in[...]
    lower = lax.broadcasted_iota(jnp.int32, (BLK, 128), 1) % HDIM < HDIM // 2
    sine = sa * cb + ca * sb
    return ca * cb - sa * sb, jnp.where(lower, -sine, sine)


def swapped(values):
    lower = lax.broadcasted_iota(jnp.int32, values.shape, 1) % HDIM < HDIM // 2
    return jnp.where(lower, pltpu.roll(values, 96, 1), pltpu.roll(values, 32, 1))


def dot(left, right):
    return jnp.dot(left, right, preferred_element_type=jnp.float32)


def dot_nt(left, right):
    return lax.dot_general(left, right, (((1,), (1,)), ((), ())), preferred_element_type=jnp.float32)


def column(row):
    return jnp.broadcast_to(row, (128, row.shape[1])).T[:, 0:1]


def mask_bias(key_block, query_block, bias_ref, ctx, index):
    key_seg = column(key_block[BLK:, :BLK].astype(jnp.float32)[:1])
    query_seg = query_block[BLK:, :BLK].astype(jnp.float32)[:1]
    key_pos = lax.broadcasted_iota(jnp.int32, (BLK, BLK), 0)
    query_pos = lax.broadcasted_iota(jnp.int32, (BLK, BLK), 1)
    reach = jnp.where(index == ctx, 0, BLK)
    allowed = (key_seg == query_seg) & (key_pos <= query_pos + reach)
    bias_ref[...] = jnp.where(allowed, 0.0, masked_score)


def rms_rows(values):
    return lax.rsqrt(jnp.mean(values * values, axis=-1, keepdims=True) + epsilon)


def pick(onehot, values):
    return jnp.sum(jnp.where(onehot, values, 0.0), axis=1, keepdims=True)


def lane_is(lanes):
    return lax.broadcasted_iota(jnp.int32, (BLK, 128), 1) == lanes


def dot_tn(left, right):
    return lax.dot_general(left, right, (((0,), (0,)), ((), ())), preferred_element_type=jnp.float32)


def row_tile(values):
    *weights, small = values
    rows = jnp.concatenate([w.astype(jnp.float32) for w in weights], axis=0)
    tail = jnp.concatenate([rows[16:, :384], rows[16:, 384:]], axis=0)
    return jnp.concatenate([rows[:16], tail, small], axis=1).astype(jnp.bfloat16)


def forward_kernel(
    wq_ref, wk_ref, wv_ref, wo_ref, router_ref, constant_ref, vector_ref, gain_one_ref, gain_two_ref,
    tokens_ref, segments_in, gate_in, up_in, down_in,
    left_ref, right_ref, place_ref, cos_in, sin_in, cos_out, sin_out,
    prev_ref, wres_ref, routes_ref, rank_ref, cot_ref,
    state_ref, normed_ref, att_ref, lse_ref, q_ref, keys_ref, values_ref,
    info_ref, proj_ref, blocks_ref, w_ref, small_ref, pay_ref,
    back_rows_ref, back_grads_ref, d_pay_ref,
    part_a, part_b, part_c, own_ref, qt_ref, vt_ref, bias_ref, max_ref, sum_ref, acc_ref,
    prev_pad, wres_pad, few_wide, few_tall, kv_ref, rows_ref, grads_ref,
    gate_w, up_w, down_w, x_ref, g_ref, gate_ref, up_ref, hidden_ref, d_gate, d_up,
    mine_ref, twin_out, twin_in,
    net_send, net_recv, twin_send, twin_recv, own_sem, ring_send, ring_recv, kv_sem,
    load_sem, send_sem, recv_sem, share_send, share_recv, half_send, half_recv, ret_send, ret_recv,
    keep_sem,
):
    parts = (part_a, part_b, part_c)
    tables = (cos_in, sin_in, cos_out, sin_out)
    ctx, fsdp = lax.axis_index("ctx"), lax.axis_index("fsdp")
    along, side = ctx // 2, ctx % 2
    *spot, core = place()
    spot = tuple(spot)
    twin = device_at(*spot, 1 - core)
    few_wide[...] = jnp.zeros_like(few_wide)
    few_wide[12:16, :6] = constant_ref[...].astype(jnp.float32)
    few_wide[16:18, :6] = vector_ref[...].astype(jnp.float32)
    few_wide[18:19, :6] = gain_one_ref[...].astype(jnp.float32)
    few_wide[19:20, :6] = gain_two_ref[...].astype(jnp.float32)
    few_tall[...] = few_wide[...].T[:16]
    few_tall[:6, :NALL] = router_ref[...].astype(jnp.float32)
    own_ref[...] = row_tile([wq_ref[...], wk_ref[...], wv_ref[...], wo_ref[...], few_tall[...]])
    marks = jnp.concatenate(
        [segments_in[...].astype(jnp.float32), jnp.zeros((1, WIDTH - BLK), jnp.float32)], axis=1
    )
    blocks_ref[ctx, :BLK] = tokens_ref[...]
    blocks_ref[ctx, BLK:] = jnp.broadcast_to(marks, (16, WIDTH)).astype(jnp.bfloat16)
    chip = fsdp // 2

    def at_expert(where, on):
        return {"ctx": ctx, "fsdp": where * 2 + on}

    greet(
        torus_peers(spot, core)
        + [at_expert((chip + by) % EXPERTS, core) for by in range(1, EXPERTS)]
    )

    def net(part, step, by, source, target):
        axis = PART_ORDER[part][step]
        return pltpu.make_async_remote_copy(
            src_ref=source,
            dst_ref=target,
            send_sem=net_send.at[part, step, by - 1],
            recv_sem=net_recv.at[part, step, by - 1],
            device_id=device_at(*shifted(spot, axis, by), core),
            device_id_type=MESH,
        )

    def share(part, slot, source, target):
        return pltpu.make_async_remote_copy(
            src_ref=source,
            dst_ref=target,
            send_sem=twin_send.at[part, slot],
            recv_sem=twin_recv.at[part, slot],
            device_id=twin,
            device_id_type=MESH,
        )

    payloads = ((blocks_ref, BLOCK_CUTS), (pay_ref, PAY_CUTS))

    def ring(kind, number, arriving=False):
        to, (steps, across_it), rows = MESSAGES[number]
        if arriving:
            steps = steps - to
            across_it = across_it if to else 1 - across_it
        array, cuts = payloads[kind]
        first, last = (cuts[i] for i in SPANS[rows])
        on = side if across_it == 0 else 1 - side
        view = array.at[((along + steps + 4) % 4) * 2 + on, pl.ds(first, last - first)]
        target = ((along + to + 4) % 4) * 2 + (side if to else 1 - side)
        return pltpu.make_async_remote_copy(
            src_ref=view,
            dst_ref=view,
            send_sem=ring_send.at[kind, number],
            recv_sem=ring_recv.at[kind, number],
            device_id={"ctx": target, "fsdp": fsdp},
            device_id_type=MESH,
        )

    def pass_on(kind, stage):
        plan = (
            ((None, (0, 1, 2)),),
            ((2, (3, 4)),),
            ((0, (5, 7, 8)), (1, (6, 9, 10))),
            ((3, (11,)), (4, (12,)), (5, (13,)), (6, (14,))),
            tuple((number, ()) for number in range(7, 15)),
        )[stage]
        for number, then in plan:
            if number is not None:
                ring(kind, number, arriving=True).wait_recv()
            for follow in then:
                ring(kind, follow).start()

    started = []
    kept = []
    for part in range(3):
        own = own_ref.at[:, pl.ds(PART_START[part], PART_LANES[part])]
        mine = region(parts[part], spot, core, ())
        for by in (1, 2, 3):
            copy = net(part, 0, by, own, mine)
            copy.start()
            started.append(copy)
    for part in range(3):
        own = own_ref.at[:, pl.ds(PART_START[part], PART_LANES[part])]
        mine = region(parts[part], spot, core, ())
        copy = pltpu.make_async_copy(own, mine, own_sem.at[part])
        copy.start()
        kept.append(copy)
        copy = share(part, 0, own, mine)
        copy.start()
        started.append(copy)
    tail = [(down_in.at[:96], pay_ref.at[ctx, 192:, pl.ds(0, WIDTH)])] + [
        (down_in.at[96:, pl.ds(256 * m, 256)], pay_ref.at[ctx, pl.ds(192 + 32 * m, 32), pl.ds(WIDTH, 256)])
        for m in range(3)
    ]
    pieces = [(gate_in, pay_ref.at[ctx, :96]), (up_in, pay_ref.at[ctx, 96:192]), *tail]
    own_experts = [
        pltpu.make_async_copy(source, target, own_sem.at[3 + number])
        for number, (source, target) in enumerate(pieces)
    ]
    for copy in own_experts:
        copy.start()
    for copy in kept + own_experts:
        copy.wait()
    for step in range(3):
        for part in range(3):
            order = PART_ORDER[part]
            axis = order[step]
            whole = order[:step]
            for by in (1, 2, 3):
                here = region(parts[part], shifted(spot, axis, -by), core, whole)
                net(part, step, by, here, here).wait_recv()
                copy = share(part, 1 + step * 3 + by - 1, here, here)
                copy.start()
                started.append(copy)
            if step < 2:
                held = region(parts[part], spot, core, order[: step + 1])
                for by in (1, 2, 3):
                    copy = net(part, step + 1, by, held, held)
                    copy.start()
                    started.append(copy)
        if step == 1:
            pass_on(0, 0)
    for part in range(3):
        order = PART_ORDER[part]
        first = region(parts[part], spot, 1 - core, ())
        share(part, 0, first, first).wait_recv()
        for step in range(3):
            for by in (1, 2, 3):
                here = region(
                    parts[part], shifted(spot, order[step], -by), 1 - core, order[:step]
                )
                share(part, 1 + step * 3 + by - 1, here, here).wait_recv()

    def unpack(group, carry):
        a, b, c = (
            part[group // 4, group % 4].reshape(128, lanes)
            for part, lanes in zip(parts, PART_LANES, strict=True)
        )
        tail = jnp.concatenate([b[:, 256:], c[:, :256]], axis=1)
        left = dot(left_ref[...], jnp.concatenate([a[:, :384], tail], axis=0))
        right_rows = jnp.concatenate([a[:, 384:], b[:, :256]], axis=1)
        right = dot(right_ref[...], jnp.concatenate([right_rows, tail], axis=0))
        rows = pl.ds(pl.multiple_of(group * 48, 16), 48)
        for weight in range(4):
            w_ref[weight, rows, :384] = left[weight * 48 : weight * 48 + 48].astype(jnp.bfloat16)
            w_ref[weight, rows, 384:] = right[weight * 48 : weight * 48 + 48].astype(jnp.bfloat16)
        small_ref[rows] = dot(place_ref[...], c[:, 256:]).astype(jnp.bfloat16)
        return carry

    pass_on(0, 1)
    lax.fori_loop(0, 16, unpack, 0)
    pass_on(0, 2)
    across = small_ref[...].astype(jnp.float32).T
    gain_one, gain_two = across[18:19], across[19:20]

    def normed_block(index):
        wide = blocks_ref[index, :BLK].astype(jnp.float32)
        return (wide * rms_rows(wide) * gain_one).astype(jnp.bfloat16)

    query = dot(normed_block(ctx), w_ref[0])
    cosine, sine = turning(ctx, tables)
    for pair in range(PAIRS):
        part = query[:, pair * 128 : pair * 128 + 128]
        turned = (part * cosine + swapped(part) * sine) * (HDIM**-0.5)
        q_ref[pair] = turned.astype(jnp.bfloat16)
        across_q = turned.T.astype(jnp.bfloat16)
        blank = jnp.zeros((HDIM, BLK), jnp.bfloat16)
        qt_ref[2 * pair] = jnp.concatenate([across_q[:HDIM], blank], axis=0)
        qt_ref[2 * pair + 1] = jnp.concatenate([blank, across_q[HDIM:]], axis=0)
    max_ref[...] = jnp.full(max_ref.shape, masked_score, jnp.float32)
    sum_ref[...] = jnp.zeros_like(sum_ref)
    acc_ref[...] = jnp.zeros_like(acc_ref)

    def keep_block(index, slot):
        return [
            pltpu.make_async_copy(kv_ref.at[slot, kind], target.at[index], kv_sem.at[slot, kind])
            for kind, target in enumerate((keys_ref, values_ref))
        ]

    def block_at(step):
        odd = step % 2
        x = along - (step + odd) // 2 + odd * side
        return jnp.where(step == 0, ctx, x * 2 + 1 - odd)

    def block(step, carry):
        index = block_at(step)
        slot = step % 2

        @pl.when(step >= 2)
        def _():
            for copy in keep_block(block_at(step - 2), slot):
                copy.wait()

        normed = normed_block(index)
        key = dot(normed, w_ref[1])
        value = dot(normed, w_ref[2])
        cosine, sine = turning(index, tables)
        for pair in range(PAIRS):
            lanes = slice(pair * 128, pair * 128 + 128)
            part = key[:, lanes]
            kv_ref[slot, 0, pair] = (part * cosine + swapped(part) * sine).astype(jnp.bfloat16)
            kv_ref[slot, 1, pair] = value[:, lanes].astype(jnp.bfloat16)
            vt_ref[lanes, :] = value[:, lanes].T.astype(jnp.bfloat16)
        mask_bias(blocks_ref.at[index], blocks_ref.at[ctx], bias_ref, ctx, index)
        def score(head):
            return dot(kv_ref[slot, 0, head // 2], qt_ref[head]) + bias_ref[...]

        def soften(head, scores):
            before = max_ref[head : head + 1]
            top = jnp.maximum(before, jnp.max(scores, axis=0, keepdims=True))
            weights = jnp.exp(scores - top)
            shrink = jnp.exp(before - top)
            sum_ref[head : head + 1] = sum_ref[head : head + 1] * shrink + jnp.sum(
                weights, axis=0, keepdims=True
            )
            max_ref[head : head + 1] = top
            return shrink, weights.astype(jnp.bfloat16)

        def gather(head, shrink, weights):
            rows = slice(head * HDIM, head * HDIM + HDIM)
            acc_ref[rows] = acc_ref[rows] * shrink + dot(vt_ref[rows, :], weights)

        ahead = [score(0), score(1)]
        done = None
        for head in range(0, HEADS, 2):
            now = ahead
            if head + 2 < HEADS:
                ahead = [score(head + 2), score(head + 3)]
            if done is not None:
                gather(head - 2, *done[0])
                gather(head - 1, *done[1])
            done = [soften(head, now[0]), soften(head + 1, now[1])]
        gather(HEADS - 2, *done[0])
        gather(HEADS - 1, *done[1])

        for copy in keep_block(index, slot):
            copy.start()
        for when, todo in (
            (0, ((0, 3), (1, 0))),
            (1, ((0, 4),)),
            (5, ((1, 1), (1, 2))),
            (7, ((1, 3),)),
        ):

            @pl.when(step == jnp.minimum(ctx, when))
            def _(todo=todo):
                for kind, stage in todo:
                    pass_on(kind, stage)

        return carry

    lax.fori_loop(0, ctx + 1, block, 0)
    for head in range(HEADS):
        rows = slice(head * HDIM, head * HDIM + HDIM)
        att_ref[rows] = acc_ref[rows] / sum_ref[head : head + 1]
    lse_ref[...] = max_ref[...] + jnp.log(jnp.maximum(sum_ref[...], 1e-30))
    attended = att_ref[...].T.astype(jnp.bfloat16)
    state = blocks_ref[ctx, :BLK].astype(jnp.float32) + dot(attended, w_ref[3])
    state_ref[...] = state
    normed_two = (state * rms_rows(state) * gain_two).astype(jnp.bfloat16)
    normed_ref[...] = normed_two

    proj = dot(normed_two, small_ref[...])
    proj_ref[...] = proj
    pad_routing(prev_ref, wres_ref, prev_pad, wres_pad)
    logits = proj + jnp.dot(
        prev_pad[...].T, wres_pad[...], precision=highest, preferred_element_type=jnp.float32
    )
    lanes = lax.broadcasted_iota(jnp.int32, (BLK, 128), 1).astype(jnp.float32)
    routes = routes_ref[...].astype(jnp.float32)
    route_0, route_1 = column(routes[0:1]), column(routes[1:2])
    hot_0, hot_1 = lanes == route_0, lanes == route_1
    chosen_0, chosen_1 = pick(hot_0, logits), pick(hot_1, logits)
    top = jnp.maximum(chosen_0, chosen_1)
    chosen_0, chosen_1 = jnp.exp(chosen_0 - top), jnp.exp(chosen_1 - top)
    gate_0, gate_1 = chosen_0 / (chosen_0 + chosen_1), chosen_1 / (chosen_0 + chosen_1)
    rank = rank_ref[...].astype(jnp.float32)
    earlier = (rank < column(rank)).astype(jnp.float32).astype(jnp.bfloat16)
    slots = dot(earlier, (hot_0 | hot_1).astype(jnp.float32).astype(jnp.bfloat16))

    def target(route, hot):
        slot = pick(hot, slots)
        return jnp.where(
            (route < EXPERTS) & (slot < CAP), route * SLOTS + slot, -1.0
        )

    target_0, target_1 = target(route_0, hot_0), target(route_1, hot_1)
    info = jnp.where(lanes == 0, gate_0, 0.0) + jnp.where(lanes == 1, gate_1, 0.0)
    info = info + jnp.where(lanes == 2, target_0, 0.0) + jnp.where(lanes == 3, target_1, 0.0)
    info_ref[...] = info
    targets = info.T
    rows = lax.broadcasted_iota(jnp.int32, (EXPERTS * SLOTS, BLK), 0).astype(jnp.float32)
    table_0 = (rows == targets[2:3]).astype(jnp.float32).astype(jnp.bfloat16)
    table_1 = (rows == targets[3:4]).astype(jnp.float32).astype(jnp.bfloat16)
    rows_ref[...] = dot(table_0 + table_1, normed_two).astype(jnp.bfloat16)
    upstream = cot_ref[...].astype(jnp.float32)
    grads_ref[...] = dot(
        jnp.concatenate([table_0, table_1], axis=1),
        jnp.concatenate([gate_0 * upstream, gate_1 * upstream], axis=0).astype(jnp.bfloat16),
    ).astype(jnp.bfloat16)
    for back in (0, 1):

        @pl.when(ctx - back >= 0)
        def _(back=back):
            for copy in keep_block(block_at(ctx - back), (ctx - back) % 2):
                copy.wait()

    other = 1 - core
    half = EXPERTS * SLOTS

    def slots(index, on):
        return pl.ds(pl.multiple_of((on * EXPERTS + index) * SLOTS, SLOTS), SLOTS)

    def chunk(index):
        return pl.ds(pl.multiple_of(index * SLOTS, SLOTS), SLOTS)

    buffers = ((rows_ref, x_ref), (grads_ref, g_ref))

    def dispatch(kind, by):
        source, target = buffers[kind]
        where = (chip + by) % EXPERTS
        return pltpu.make_async_remote_copy(
            src_ref=source.at[chunk(where)],
            dst_ref=target.at[slots(chip, core)],
            send_sem=send_sem.at[kind, by - 1],
            recv_sem=recv_sem.at[kind, by - 1],
            device_id=at_expert(where, core),
            device_id_type=MESH,
        )

    def share(kind, by, on):
        source, target = buffers[kind]
        spot = slots((chip - by) % EXPERTS, on)
        return pltpu.make_async_remote_copy(
            src_ref=target.at[spot],
            dst_ref=target.at[spot],
            send_sem=share_send.at[kind, by],
            recv_sem=share_recv.at[kind, by],
            device_id=at_expert(chip, other),
            device_id_type=MESH,
        )

    def exchange(kind):
        return pltpu.make_async_remote_copy(
            src_ref=twin_out.at[kind],
            dst_ref=twin_in.at[kind],
            send_sem=half_send.at[kind],
            recv_sem=half_recv.at[kind],
            device_id=at_expert(chip, other),
            device_id_type=MESH,
        )

    returned = (back_rows_ref, back_grads_ref)

    def give_back(kind, by):
        where = (chip + by) % EXPERTS
        return pltpu.make_async_remote_copy(
            src_ref=mine_ref.at[kind, chunk(where)],
            dst_ref=returned[kind].at[chunk(chip)],
            send_sem=ret_send.at[kind, by - 1],
            recv_sem=ret_recv.at[kind, by - 1],
            device_id=at_expert(where, core),
            device_id_type=MESH,
        )

    for by in range(1, EXPERTS):
        dispatch(0, by).start()
    for by in range(1, EXPERTS):
        dispatch(0, by).wait_send()
    for by in range(1, EXPERTS):
        copy = dispatch(1, by)
        copy.start()
        started.append(copy)
    for kind in (0, 1):
        source, target = buffers[kind]
        copy = pltpu.make_async_copy(
            source.at[chunk(chip)], target.at[slots(chip, core)], keep_sem.at[kind]
        )
        copy.start()
        copy.wait()
        copy = share(kind, 0, core)
        copy.start()
        started.append(copy)

    def arrive(kind):
        for by in range(1, EXPERTS):
            dispatch(kind, by).wait_recv()
            copy = share(kind, by, core)
            copy.start()
            started.append(copy)

    def arrive_shared(kind):
        for by in range(EXPERTS):
            share(kind, by, other).wait_recv()

    def tiles(on, body):
        def step(index, carry):
            start = pl.multiple_of(on * half + index * 256, 256)
            body(pl.ds(start, 256), pl.ds(pl.multiple_of(index * 256, 256), 256))
            return carry

        lax.fori_loop(0, half // 256, step, 0)

    def forward(on, keep):
        def tile(rows, inner):
            x = x_ref[rows]
            gate, up = dot(x, gate_w[...]), dot(x, up_w[...])
            gate_ref[rows], up_ref[rows] = gate, up
            hidden_ref[rows] = (gate * jax.nn.sigmoid(gate) * up).astype(jnp.bfloat16)

        def result(rows, inner):
            keep(inner, dot(hidden_ref[rows], down_w[...]))

        tiles(on, tile)
        tiles(on, result)

    def backward(on, keep):
        def tile(rows, inner):
            hidden_grad = dot_nt(g_ref[rows], down_w[...])
            gate, up = gate_ref[rows], up_ref[rows]
            sigmoid = jax.nn.sigmoid(gate)
            d_gate[rows] = (
                hidden_grad * up * sigmoid * (1.0 + gate * (1.0 - sigmoid))
            ).astype(jnp.bfloat16)
            d_up[rows] = (hidden_grad * gate * sigmoid).astype(jnp.bfloat16)
            keep(inner, dot_nt(d_gate[rows], gate_w[...]) + dot_nt(d_up[rows], up_w[...]))

        tiles(on, tile)

    def keep_mine(kind):
        def keep(rows, values):
            mine_ref[kind, rows] = values.astype(jnp.bfloat16)

        return keep

    def keep_twin(kind):
        def keep(rows, values):
            twin_out[kind, rows] = values.astype(jnp.bfloat16)

        return keep

    def finish(kind):
        exchange(kind).wait_recv()

        def step(index, carry):
            rows = pl.ds(pl.multiple_of(index * 128, 128), 128)
            mine_ref[kind, rows] = (
                mine_ref[kind, rows].astype(jnp.float32) + twin_in[kind, rows].astype(jnp.float32)
            ).astype(jnp.bfloat16)
            return carry

        lax.fori_loop(0, half // 128, step, 0)
        for by in range(1, EXPERTS):
            copy = give_back(kind, by)
            copy.start()
            started.append(copy)
        copy = pltpu.make_async_copy(
            mine_ref.at[kind, chunk(chip)], returned[kind].at[chunk(chip)], keep_sem.at[kind]
        )
        copy.start()
        copy.wait()

    def load(owner):
        parts = [
            (pay_ref.at[owner, :96], gate_w.at[pl.ds(pl.multiple_of(owner * 96, 16), 96)]),
            (pay_ref.at[owner, 96:192], up_w.at[pl.ds(pl.multiple_of(owner * 96, 16), 96)]),
            (
                pay_ref.at[owner, 192:, pl.ds(0, WIDTH)],
                down_w.at[pl.ds(pl.multiple_of(owner * 128, 16), 96)],
            ),
        ] + [
            (
                pay_ref.at[owner, pl.ds(192 + 32 * m, 32), pl.ds(WIDTH, 256)],
                down_w.at[pl.ds(pl.multiple_of(owner * 128 + 96, 16), 32), pl.ds(256 * m, 256)],
            )
            for m in range(3)
        ]
        return [
            pltpu.make_async_copy(source, target, load_sem.at[owner, number])
            for number, (source, target) in enumerate(parts)
        ]

    pass_on(1, 4)
    for owner in range(8):
        for copy in load(owner):
            copy.start()
    arrive(0)
    for owner in range(8):
        for copy in load(owner):
            copy.wait()
    forward(core, keep_mine(0))
    arrive(1)
    arrive_shared(0)
    forward(other, keep_twin(0))
    copy = exchange(0)
    copy.start()
    started.append(copy)
    backward(core, keep_mine(1))
    finish(0)
    arrive_shared(1)
    backward(other, keep_twin(1))
    copy = exchange(1)
    copy.start()
    started.append(copy)

    def down_tile(index, carry):
        lanes = pl.ds(pl.multiple_of(index * 256, 256), 256)
        part = dot_tn(hidden_ref[:, lanes], g_ref[...]).astype(jnp.bfloat16)
        for piece in (0, 1):
            rows = part[piece * 128 : piece * 128 + 128]
            d_pay_ref[2 * index + piece, 192:, :WIDTH] = rows[:96]
            for m in range(3):
                d_pay_ref[2 * index + piece, 192 + 32 * m : 224 + 32 * m, WIDTH:] = rows[
                    96:, 256 * m : 256 * m + 256
                ]
        return carry

    lax.fori_loop(0, 4, down_tile, 0)
    finish(1)

    def gate_tile(index, carry):
        lanes = pl.ds(pl.multiple_of(index * 256, 256), 256)
        for start, grad in ((0, d_gate), (96, d_up)):
            part = dot_tn(x_ref[...], grad[:, lanes]).astype(jnp.bfloat16)
            for piece in range(8):
                d_pay_ref[piece, start : start + 96, lanes] = part[piece * 96 : piece * 96 + 96]
        return carry

    lax.fori_loop(0, 4, gate_tile, 0)
    for kind in (0, 1):
        for by in range(1, EXPERTS):
            give_back(kind, by).wait_recv()
    for kind in (0, 1):
        for number in range(len(MESSAGES)):
            ring(kind, number).wait_send()
    for copy in started:
        copy.wait_send()


def pad_routing(prev_ref, wres_ref, prev_pad, wres_pad):
    prev_pad[...] = jnp.zeros_like(prev_pad)
    prev_pad[:NALL] = prev_ref[:, 0, :]
    wres_pad[...] = jnp.zeros_like(wres_pad)
    wres_pad[:NALL, :NALL] = wres_ref[...]


def run_forward(weights, few, tokens, segments, experts, prev, wres, routes, rank, cot):
    vmem, anywhere = pl.BlockSpec(memory_space=pltpu.VMEM), pl.BlockSpec(memory_space=pl.ANY)
    shape = jax.ShapeDtypeStruct
    low, wide = jnp.bfloat16, jnp.float32
    dma = pltpu.SemaphoreType.DMA
    half, whole = EXPERTS * SLOTS, 2 * EXPERTS * SLOTS
    left, right, small = (jnp.asarray(t, low) for t in placing_tables())
    return pl.pallas_call(
        forward_kernel,
        out_shape=[
            shape((BLK, WIDTH), wide),
            shape((BLK, WIDTH), low),
            shape((WIDTH, BLK), wide),
            shape((16, BLK), wide),
            shape((PAIRS, BLK, 128), low),
            shape((8, PAIRS, BLK, 128), low),
            shape((8, PAIRS, BLK, 128), low),
            shape((BLK, 128), wide),
            shape((BLK, 128), wide),
            shape((8, BLK + 16, WIDTH), low),
            shape((4, WIDTH, WIDTH), low),
            shape((WIDTH, 128), low),
            shape((8, 288, 1024), low),
            shape((half, WIDTH), low),
            shape((half, WIDTH), low),
            shape((8, 288, 1024), low),
        ],
        in_specs=[vmem] * 26,
        out_specs=[vmem] * 5 + [anywhere] * 2 + [vmem] * 5 + [anywhere] + [vmem] * 3,
        scratch_shapes=[
            *(pltpu.VMEM((4, 4, 4, 2, 16, lanes), low) for lanes in PART_LANES),
            pltpu.VMEM((16, 1280), low),
            pltpu.VMEM((HEADS, 128, BLK), low),
            pltpu.VMEM((WIDTH, BLK), low),
            pltpu.VMEM((BLK, BLK), wide),
            pltpu.VMEM((16, BLK), wide),
            pltpu.VMEM((16, BLK), wide),
            pltpu.VMEM((WIDTH, BLK), wide),
            pltpu.VMEM((128, BLK), wide),
            pltpu.VMEM((128, 128), wide),
            pltpu.VMEM((128, 128), wide),
            pltpu.VMEM((16, 128), wide),
            pltpu.VMEM((2, 2, PAIRS, BLK, 128), low),
            pltpu.VMEM((half, WIDTH), low),
            pltpu.VMEM((half, WIDTH), low),
            pltpu.VMEM((WIDTH, 1024), low),
            pltpu.VMEM((WIDTH, 1024), low),
            pltpu.VMEM((1024, WIDTH), low),
            pltpu.VMEM((whole, WIDTH), low),
            pltpu.VMEM((whole, WIDTH), low),
            pltpu.VMEM((whole, 1024), wide),
            pltpu.VMEM((whole, 1024), wide),
            pltpu.VMEM((whole, 1024), low),
            pltpu.VMEM((whole, 1024), low),
            pltpu.VMEM((whole, 1024), low),
            pltpu.VMEM((2, half, WIDTH), low),
            pltpu.VMEM((2, half, WIDTH), low),
            pltpu.VMEM((2, half, WIDTH), low),
            dma((3, 3, 3)),
            dma((3, 3, 3)),
            dma((3, 10)),
            dma((3, 10)),
            dma((9,)),
            dma((2, 15)),
            dma((2, 15)),
            dma((2, 2)),
            dma((8, 6)),
            dma((2, 7)),
            dma((2, 7)),
            dma((2, 8)),
            dma((2, 8)),
            dma((2,)),
            dma((2,)),
            dma((2, 7)),
            dma((2, 7)),
            dma((2,)),
        ],
        name="forward",
        compiler_params=pltpu.CompilerParams(
            collective_id=1, has_side_effects=True, vmem_limit_bytes=63 * 2**20
        ),
    )(
        *weights, *few, tokens, segments, *experts, left, right, small, *rope_tables(),
        prev, wres, routes, rank, cot,
    )


def split(values):
    high = values.astype(jnp.bfloat16)
    low = (values - high.astype(jnp.float32)).astype(jnp.bfloat16)
    return jnp.concatenate([high, low], axis=1)


def back_kernel(
    blocks_ref, w_ref, small_ref, cos_in, sin_in, cos_out, sin_out, left_ref, right_ref, place_ref,
    prev_ref, wres_ref, routes_ref, cot_ref,
    state_ref, normed_ref, att_ref, lse_ref, q_ref, keys_ref, values_ref, info_ref, proj_ref,
    back_rows_ref, back_grads_ref, d_pay_ref,
    out_ref, prev_grad_ref, total_ref, tokens_grad_ref, sums_ref, few_ref,
    gate_out, up_out, down_out,
    *scratch,
):
    (
        qt_ref, ot_ref, o_ref, qm_ref, bias_ref, inner_ref, dqt_ref, gain_ref, dk_ref, dv_ref,
        prev_pad, wres_pad, dw_ref, dw_low, few_sum, kv_ref, tok_ref, mine_ref, kv_sem, own_ref, state_grad_ref, others_ref, grads_ref, block_in,
        far_in, far_land, far_sum, far_out, far_back, mark_ref, far_send, far_recv,
        pay_ref, pay_in, small_in, small_sum,
        block_send, block_recv, exp_send, exp_recv, load_sem,
        net_send, net_recv, twin_send, twin_recv, small_send, small_recv,
        *more,
    ) = scratch
    twin_in, in_one, in_two, in_three, sum_one, sum_two = (
        more[0], more[1:4], more[4:7], more[7:10], more[10:13], more[13:16]
    )
    tables = (cos_in, sin_in, cos_out, sin_out)
    ctx, fsdp = lax.axis_index("ctx"), lax.axis_index("fsdp")
    *spot, core = place()
    spot = tuple(spot)
    twin = device_at(*spot, 1 - core)
    started = []
    greet(torus_peers(spot, core) + sequence_peers(spot, core))

    along, side = ctx // 2, ctx % 2

    def rows_of(number):
        first, last = (GRAD_CUTS[i] for i in SPANS[MESSAGES[number][2]])
        return first, last - first

    def owner(steps, across_it):
        return ((along + steps + 4) % 4) * 2 + (side if across_it == 0 else 1 - side)

    def expert(number):
        to, (steps, across_it), _ = MESSAGES[number]
        first, count = rows_of(number)
        landing = sum(rows_of(before)[1] for before in range(number))
        return pltpu.make_async_remote_copy(
            src_ref=pay_ref.at[
                owner(steps - to, across_it if to else 1 - across_it), pl.ds(first, count)
            ],
            dst_ref=pay_in.at[pl.ds(landing, count)],
            send_sem=exp_send.at[number],
            recv_sem=exp_recv.at[number],
            device_id={"ctx": owner(-to, 0 if to else 1), "fsdp": fsdp},
            device_id_type=MESH,
        )

    def send_experts(numbers):
        for number in numbers:
            expert(number).start()

    def add_experts(numbers):
        for number in numbers:
            expert(number).wait_recv()
            _, (steps, across_it), _ = MESSAGES[number]
            first, count = rows_of(number)
            landing = sum(rows_of(before)[1] for before in range(number))
            at = owner(steps, across_it)

            def add_rows(index, carry, at=at, first=first, landing=landing):
                here = pl.ds(pl.multiple_of(first + index * 16, 16), 16)
                there = pl.ds(pl.multiple_of(landing + index * 16, 16), 16)
                pay_ref[at, here] = (
                    pay_ref[at, here].astype(jnp.float32) + pay_in[there].astype(jnp.float32)
                ).astype(jnp.bfloat16)
                return carry

            lax.fori_loop(0, count // 16, add_rows, 0)

    loads = [
        pltpu.make_async_copy(d_pay_ref.at[index], pay_ref.at[index], load_sem.at[1 + index])
        for index in range(8)
    ]
    for copy in loads:
        copy.start()
    for copy in loads:
        copy.wait()
    send_experts((13, 14, 11, 12, 7, 8, 9, 10))
    own_block = pltpu.make_async_copy(blocks_ref.at[ctx], mine_ref, load_sem.at[0])
    own_block.start()

    def load_kv(index, slot):
        return [
            pltpu.make_async_copy(source.at[index], kv_ref.at[slot, kind], kv_sem.at[slot, kind])
            for kind, source in enumerate((keys_ref, values_ref))
        ] + [pltpu.make_async_copy(blocks_ref.at[index], tok_ref.at[slot], kv_sem.at[slot, 2])]

    for copy in load_kv(0, 0):
        copy.start()

    mine_half, twin_half = (
        pl.ds(pl.multiple_of(on * 128, 128), 128) for on in (core, 1 - core)
    )
    end_mark = pltpu.make_async_copy(blocks_ref.at[7, pl.ds(BLK, 16)], mark_ref, load_sem.at[9])
    end_mark.start()

    def far_share(index):
        return pltpu.make_async_remote_copy(
            src_ref=others_ref.at[index, twin_half],
            dst_ref=far_in.at[index],
            send_sem=far_send.at[index],
            recv_sem=far_recv.at[index],
            device_id=twin,
            device_id_type=MESH,
        )

    def far_copy(by, target):
        return pltpu.make_async_remote_copy(
            src_ref=others_ref.at[target, mine_half],
            dst_ref=far_land.at[by - 3],
            send_sem=block_send.at[by - 1],
            recv_sem=block_recv.at[by - 1],
            device_id={"ctx": target, "fsdp": fsdp},
            device_id_type=MESH,
        )

    def far_halves():
        return pltpu.make_async_remote_copy(
            src_ref=far_out,
            dst_ref=far_back,
            send_sem=far_send.at[5],
            recv_sem=far_recv.at[5],
            device_id=twin,
            device_id_type=MESH,
        )

    def block_copy(by, target):
        return pltpu.make_async_remote_copy(
            src_ref=others_ref.at[target],
            dst_ref=block_in.at[by - 1],
            send_sem=block_send.at[by - 1],
            recv_sem=block_recv.at[by - 1],
            device_id={"ctx": target, "fsdp": fsdp},
            device_id_type=MESH,
        )

    across = small_ref[...].astype(jnp.float32).T
    gain_one, gain_two = across[18:19], across[19:20]
    value_rows = across[16:18]

    lanes = lax.broadcasted_iota(jnp.int32, (BLK, 128), 1)
    info = info_ref[...]
    gates = (info[:, 0:1], info[:, 1:2])
    slots = lax.broadcasted_iota(jnp.int32, (BLK, EXPERTS * SLOTS), 1).astype(jnp.float32)
    tables_of = [
        (slots == info[:, 2 + k : 3 + k]).astype(jnp.float32).astype(jnp.bfloat16) for k in (0, 1)
    ]
    route_rows = routes_ref[...].astype(jnp.float32)
    routes = (column(route_rows[0:1]), column(route_rows[1:2]))
    hots = [lanes.astype(jnp.float32) == routes[k] for k in (0, 1)]
    named = [
        [(routes[k] == EXPERTS + 1 + kind).astype(jnp.float32) for kind in range(3)] for k in (0, 1)
    ]
    proj = proj_ref[...]
    mixes = []
    for c in (0, 1):
        first, second = proj[:, 12 + 2 * c : 13 + 2 * c], proj[:, 13 + 2 * c : 14 + 2 * c]
        top = jnp.maximum(first, second)
        first, second = jnp.exp(first - top), jnp.exp(second - top)
        mixes.append((first / (first + second), second / (first + second)))
    normed_low = normed_ref[...]
    normed_two = normed_low.astype(jnp.float32)
    upstream_low = cot_ref[...]
    upstream = upstream_low.astype(jnp.float32)
    state = state_ref[...]
    back_rows = back_rows_ref[...]
    result = state
    gate_grads = []
    for k in (0, 1):
        copy, one, two = named[k]
        pair = dot(tables_of[k], back_rows)
        pair = pair + (copy + one * mixes[0][0] + two * mixes[1][0]) * normed_two
        pair = pair + (one * mixes[0][1]) * value_rows[0:1] + (two * mixes[1][1]) * value_rows[1:2]
        result = result + gates[k] * pair
        gate_grads.append(jnp.sum(pair * upstream, axis=1, keepdims=True))
    out_ref[...] = result.astype(jnp.bfloat16)
    inner = gates[0] * gate_grads[0] + gates[1] * gate_grads[1]
    logit_grad = jnp.zeros((BLK, 128), jnp.float32)
    for k in (0, 1):
        logit_grad = logit_grad + jnp.where(hots[k], gates[k] * (gate_grads[k] - inner), 0.0)
    pad_routing(prev_ref, wres_ref, prev_pad, wres_pad)
    prev_grad_ref[...] = lax.dot_general(
        wres_pad[...], logit_grad, (((1,), (1,)), ((), ())),
        precision=highest, preferred_element_type=jnp.float32,
    )[:16]
    small_sum[3] = jnp.dot(
        prev_pad[...], logit_grad, precision=highest, preferred_element_type=jnp.float32
    )[:16]
    on_normed = jnp.sum(normed_two * upstream, axis=1, keepdims=True)
    on_vectors = dot(upstream_low, small_ref[...])
    flat = logit_grad
    weight_up = gates[0] * named[0][0] + gates[1] * named[1][0]
    vector_weights = jnp.zeros((BLK, 128), jnp.float32)
    for c in (0, 1):
        scale = gates[0] * named[0][1 + c] + gates[1] * named[1][1 + c]
        mix_0, mix_1 = mixes[c]
        m_0, m_1 = scale * on_normed, scale * on_vectors[:, 16 + c : 17 + c]
        mean = mix_0 * m_0 + mix_1 * m_1
        flat = flat + jnp.where(lanes == 12 + 2 * c, mix_0 * (m_0 - mean), 0.0)
        flat = flat + jnp.where(lanes == 13 + 2 * c, mix_1 * (m_1 - mean), 0.0)
        weight_up = weight_up + mix_0 * scale
        vector_weights = vector_weights + jnp.where(lanes == 16 + c, mix_1 * scale, 0.0)
    flat_split = split(flat)
    normed_grad = dot_nt(flat_split, jnp.concatenate([small_ref[...]] * 2, axis=1))
    normed_grad = normed_grad + weight_up * upstream
    normed_grad = normed_grad + dot(tables_of[0] + tables_of[1], back_grads_ref[...])
    normed_across = normed_two.T.astype(jnp.bfloat16)
    upstream_across = upstream.T.astype(jnp.bfloat16)
    small_grad = dot(normed_across, flat_split)
    small_vector = dot(upstream_across, split(vector_weights))
    small_grad = small_grad[:, :128] + small_grad[:, 128:] + small_vector[:, :128] + small_vector[:, 128:]
    scale_two = rms_rows(state)
    weighted = normed_grad * gain_two
    state_grad = (
        upstream
        + scale_two * weighted
        - state * (scale_two**3 * jnp.mean(weighted * state, axis=-1, keepdims=True))
    )
    state_grad_ref[...] = state_grad
    gain_two_row = jnp.sum(normed_grad * state * scale_two, axis=0, keepdims=True)
    state_low = state_grad.astype(jnp.bfloat16)
    attended = att_ref[...]
    dw_low[1] = dot(attended.astype(jnp.bfloat16), state_low).astype(jnp.bfloat16)
    att_grad = dot_nt(state_low, w_ref[3])
    blank = jnp.zeros((HDIM, BLK), jnp.bfloat16)
    low_half = lax.broadcasted_iota(jnp.int32, (BLK, 128), 1) < HDIM
    none = jnp.zeros((BLK, 128), jnp.bfloat16)
    inner_ref[...] = jnp.zeros_like(inner_ref)
    for pair in range(PAIRS):
        part = att_grad[:, pair * 128 : pair * 128 + 128].astype(jnp.bfloat16)
        across_o = part.astype(jnp.float32).T
        products = across_o * attended[pair * 128 : pair * 128 + 128]
        across_o = across_o.astype(jnp.bfloat16)
        across_q = q_ref[pair].astype(jnp.float32).T.astype(jnp.bfloat16)
        for half in (0, 1):
            head = 2 * pair + half
            rows = slice(half * HDIM, half * HDIM + HDIM)
            inner_ref[head : head + 1] = jnp.sum(products[rows], axis=0, keepdims=True)
            order = (lambda a, b: [a, b]) if half == 0 else (lambda a, b: [b, a])
            ot_ref[head] = jnp.concatenate(order(across_o[rows], blank), axis=0)
            qt_ref[head] = jnp.concatenate(order(across_q[rows], blank), axis=0)
        o_ref[pair, :BLK] = jnp.where(low_half, part, none)
        o_ref[pair, BLK:] = jnp.where(low_half, none, part)
        qm_ref[pair, :BLK] = jnp.where(low_half, q_ref[pair], none)
        qm_ref[pair, BLK:] = jnp.where(low_half, none, q_ref[pair])
    dqt_ref[...] = jnp.zeros_like(dqt_ref)
    dw_ref[...] = jnp.zeros_like(dw_ref)
    gain_ref[...] = jnp.zeros_like(gain_ref)

    own_block.wait()

    def normed_block(array):
        wide = array[:BLK].astype(jnp.float32)
        scaled = wide * rms_rows(wide)
        return scaled, (scaled * gain_one).T.astype(jnp.bfloat16)

    def block(index, carry):
        slot = index % 2
        for copy in load_kv(index, slot):
            copy.wait()

        @pl.when(index < ctx)
        def _():
            for copy in load_kv(index + 1, 1 - slot):
                copy.start()

        mask_bias(tok_ref.at[slot], mine_ref, bias_ref, ctx, index)
        cosine, sine = turning(index, tables)
        def products(pair):
            key, value = kv_ref[slot, 0, pair], kv_ref[slot, 1, pair]
            return [
                (dot(key, qt_ref[2 * pair + half]) + bias_ref[...], dot(value, ot_ref[2 * pair + half]))
                for half in (0, 1)
            ]

        ahead = products(0)
        for pair in range(PAIRS):
            now = ahead
            if pair + 1 < PAIRS:
                ahead = products(pair + 1)
            key_across = kv_ref[slot, 0, pair].T
            weights, score_grads = [], []
            for half in (0, 1):
                head = 2 * pair + half
                scores, weight_grad = now[half]
                weight = jnp.exp(scores - lse_ref[head : head + 1])
                score_grad = (weight * (weight_grad - inner_ref[head : head + 1])).astype(jnp.bfloat16)
                weights.append(weight.astype(jnp.bfloat16))
                score_grads.append(score_grad)
                rows = slice(head * HDIM, head * HDIM + HDIM)
                dqt_ref[rows] += dot(key_across[half * HDIM : half * HDIM + HDIM], score_grad)
            lanes = slice(pair * 128, pair * 128 + 128)
            dv_ref[:, lanes] = dot(jnp.concatenate(weights, axis=1), o_ref[pair]).astype(jnp.bfloat16)
            dk = dot(jnp.concatenate(score_grads, axis=1), qm_ref[pair])
            dk_ref[:, lanes] = (dk * cosine - swapped(dk) * sine).astype(jnp.bfloat16)
        scaled, normed_across = normed_block(tok_ref.at[slot])
        dw_ref[0] += dot(normed_across, dk_ref[...])
        dw_ref[1] += dot(normed_across, dv_ref[...])
        first = dot_nt(dk_ref[...], w_ref[1]) + dot_nt(dv_ref[...], w_ref[2])
        gain_ref[...] += jnp.sum(first * scaled, axis=0, keepdims=True)

        @pl.when(index < ctx)
        def _():
            others_ref[index] = first.astype(jnp.bfloat16)

        @pl.when((index < ctx) & (index >= ctx - 2))
        def _():
            block_copy(ctx - index, index).start()

        @pl.when(index < ctx - 2)
        def _():
            far_share(index).start()

        @pl.when((index >= 1) & (index - 1 < ctx - 2))
        def _():
            far_share(index - 1).wait_recv()
            others_ref[index - 1, mine_half] = (
                others_ref[index - 1, mine_half].astype(jnp.float32)
                + far_in[index - 1].astype(jnp.float32)
            ).astype(jnp.bfloat16)
            far_copy(ctx - (index - 1), index - 1).start()

        @pl.when(index == ctx)
        def _():
            own_ref[...] = first

        for when, came, then in (
            (0, (13, 14), (5, 6)),
            (1, (3, 4), (2,)),
            (2, (7, 8, 9, 10, 5, 6), (0, 1)),
        ):

            @pl.when(index == jnp.minimum(ctx, when))
            def _(came=came, then=then):
                add_experts(came)
                send_experts(then)

        return carry

    add_experts((11, 12))
    send_experts((3, 4))
    lax.fori_loop(0, ctx + 1, block, 0)
    cosine, sine = turning(ctx, tables)
    for pair in range(PAIRS):
        lanes = slice(pair * 128, pair * 128 + 128)
        dq = dqt_ref[lanes, :].T * (HDIM**-0.5)
        dk_ref[:, lanes] = (dq * cosine - swapped(dq) * sine).astype(jnp.bfloat16)
    scaled, normed_across = normed_block(mine_ref)
    dw_low[0] = dot(normed_across, dk_ref[...]).astype(jnp.bfloat16)
    first = dot_nt(dk_ref[...], w_ref[0])
    own_ref[...] += first
    gain_one_row = gain_ref[...] + jnp.sum(first * scaled, axis=0, keepdims=True)
    lanes = lax.broadcasted_iota(jnp.int32, (WIDTH, 128), 1)
    ones = jnp.broadcast_to(gain_one_row, (128, WIDTH)).T
    twos = jnp.broadcast_to(gain_two_row, (128, WIDTH)).T
    few = jnp.where(lanes == 18, ones, jnp.where(lanes == 19, twos, small_grad))
    few_sum[...] = few

    def share(x):
        return pltpu.make_async_remote_copy(
            src_ref=grads_ref.at[x, :, :, 1 - core],
            dst_ref=twin_in.at[x],
            send_sem=twin_send.at[x],
            recv_sem=twin_recv.at[x],
            device_id=twin,
            device_id_type=MESH,
        )

    def pack(group, carry):
        rows = pl.ds(pl.multiple_of(group * 48, 16), 48)

        def lane_half(start):
            lanes = slice(start, start + 384)
            query, output = dw_low[0, rows, lanes], dw_low[1, rows, lanes]
            key, value = (dw_ref[w, rows, lanes].astype(jnp.bfloat16) for w in (0, 1))
            return jnp.concatenate([query, key, value, output], axis=0)

        from_left = dot(left_ref[...], lane_half(0))
        from_right = dot(right_ref[...], lane_half(384))
        placed = dot(place_ref[...], few_sum[rows].astype(jnp.bfloat16))
        whole = jnp.concatenate(
            [from_left[:128], from_right[:128], from_left[128:] + from_right[128:], placed], axis=1
        )
        grads_ref[group // 4, group % 4] = whole.astype(jnp.bfloat16).reshape(4, 2, 16, 1280)
        return carry

    for x in range(4):
        lax.fori_loop(4 * x, 4 * x + 4, pack, 0)
        copy = share(x)
        copy.start()
        started.append(copy)

    def net(part, step, by, source, target):
        axis = PART_ORDER[part][2 - step]
        return pltpu.make_async_remote_copy(
            src_ref=source,
            dst_ref=target,
            send_sem=net_send.at[part, step, by - 1],
            recv_sem=net_recv.at[part, step, by - 1],
            device_id=device_at(*shifted(spot, axis, by), core),
            device_id_type=MESH,
        )

    def small(axis, by, source, slot):
        device = twin if axis == 3 else device_at(*shifted(spot, axis, by), core)
        return pltpu.make_async_remote_copy(
            src_ref=source,
            dst_ref=small_in.at[axis, slot],
            send_sem=small_send.at[axis, by - 1],
            recv_sem=small_recv.at[axis, by - 1],
            device_id=device,
            device_id_type=MESH,
        )

    copy = small(3, 1, small_sum.at[3], core)
    copy.start()
    started.append(copy)

    for x in range(4):
        share(x).wait_recv()

        def add_pair(index, carry, x=x):
            z, y = index // 4, index % 4
            grads_ref[x, z, y, core] = (
                grads_ref[x, z, y, core].astype(jnp.float32) + twin_in[x, z, y].astype(jnp.float32)
            ).astype(jnp.bfloat16)
            return carry

        lax.fori_loop(0, 16, add_pair, 0, unroll=2)

    def lanes_of(part):
        return pl.ds(PART_START[part], PART_LANES[part])

    for part in range(3):
        axis = PART_ORDER[part][2]
        for by in (1, 2, 3):
            at = shifted(spot, axis, by)[axis]
            index = tuple(at if a == axis else slice(None) for a in range(3))
            copy = net(
                part, 0, by, grads_ref.at[(*index, core, slice(None), lanes_of(part))], in_one[part].at[by - 1]
            )
            copy.start()
            started.append(copy)

    small(3, 1, small_sum.at[3], 1 - core).wait_recv()
    small_in[3, core] = small_sum[3]
    small_sum[0] = small_in[3, 0] + small_in[3, 1]
    for by in (1, 2, 3):
        copy = small(0, by, small_sum.at[0], spot[0])
        copy.start()
        started.append(copy)

    def small_step(axis):
        for by in (1, 2, 3):
            small(axis, by, small_sum.at[axis], shifted(spot, axis, -by)[axis]).wait_recv()
        small_in[axis, spot[axis]] = small_sum[axis]
        total = small_in[axis, 0] + small_in[axis, 1] + small_in[axis, 2] + small_in[axis, 3]
        if axis == 2:
            total_ref[...] = total
            return
        small_sum[axis + 1] = total
        for by in (1, 2, 3):
            copy = small(axis + 1, by, small_sum.at[axis + 1], spot[axis + 1])
            copy.start()
            started.append(copy)

    for part in range(3):
        first, second, third = PART_ORDER[part]
        for by in (1, 2, 3):
            net(part, 0, by, in_one[part].at[by - 1], in_one[part].at[by - 1]).wait_recv()
        rest = tuple(a for a in (0, 1, 2) if a != third)
        lanes = slice(PART_START[part], PART_START[part] + PART_LANES[part])

        def add_four(index, carry, part=part, third=third, rest=rest, lanes=lanes):
            at = {rest[0]: index // 4, rest[1]: index % 4, third: spot[third]}
            total = grads_ref[at[0], at[1], at[2], core, :, lanes].astype(jnp.float32)
            for by in range(3):
                total = total + in_one[part][by, index // 4, index % 4].astype(jnp.float32)
            sum_one[part][index // 4, index % 4] = total.astype(jnp.bfloat16)
            return carry

        lax.fori_loop(0, 16, add_four, 0, unroll=2)
        for by in (1, 2, 3):
            at = shifted(spot, second, by)[second]
            source = sum_one[part].at[at] if second == rest[0] else sum_one[part].at[:, at]
            copy = net(part, 1, by, source, in_two[part].at[by - 1])
            copy.start()
            started.append(copy)
    small_step(0)

    for number in (0, 1, 2):
        expert(number).wait_recv()
    count = PAY_CUTS[-1]

    def total_rows(start):
        rows = pl.ds(pl.multiple_of(start, 16), 16)
        total = pay_ref[ctx, rows].astype(jnp.float32)
        for number in range(3):
            there = pl.ds(pl.multiple_of(number * count + start, 16), 16)
            total = total + pay_in[there].astype(jnp.float32)
        return total

    def gate_rows(index, carry):
        rows = pl.ds(pl.multiple_of(index * 16, 16), 16)
        gate_out[rows] = total_rows(index * 16)
        up_out[rows] = total_rows(96 + index * 16)
        return carry

    lax.fori_loop(0, 6, gate_rows, 0)
    for index in range(6):
        total = total_rows(192 + 16 * index)
        down_out[16 * index : 16 * index + 16] = total[:, :WIDTH]
        start = 96 + 16 * (index % 2)
        lanes = slice(256 * (index // 2), 256 * (index // 2) + 256)
        down_out[start : start + 16, lanes] = total[:, WIDTH:]

    for part in range(3):
        first, second, third = PART_ORDER[part]
        for by in (1, 2, 3):
            net(part, 1, by, in_two[part].at[by - 1], in_two[part].at[by - 1]).wait_recv()
        rest = tuple(a for a in (0, 1, 2) if a != third)
        for index in range(4):
            if second == rest[0]:
                total = sum_one[part][spot[second], index].astype(jnp.float32)
            else:
                total = sum_one[part][index, spot[second]].astype(jnp.float32)
            for by in range(3):
                total = total + in_two[part][by, index].astype(jnp.float32)
            sum_two[part][index] = total.astype(jnp.bfloat16)
        for by in (1, 2, 3):
            at = shifted(spot, first, by)[first]
            copy = net(part, 2, by, sum_two[part].at[at], in_three[part].at[by - 1])
            copy.start()
            started.append(copy)
    small_step(1)

    for by in (1, 2):

        @pl.when(ctx + by < 8)
        def _(by=by):
            block_copy(by, ctx).wait_recv()
            own_ref[...] += block_in[by - 1].astype(jnp.float32)

        @pl.when(ctx - by >= 0)
        def _(by=by):
            block_copy(by, ctx - by).wait_send()

    far_sum[...] = jnp.zeros_like(far_sum)
    for by in range(3, 8):

        @pl.when(ctx + by < 8)
        def _(by=by):
            far_copy(by, ctx).wait_recv()
            far_sum[...] += far_land[by - 3].astype(jnp.float32)

        @pl.when(ctx - by >= 0)
        def _(by=by):
            far_copy(by, ctx - by).wait_send()
            far_share(ctx - by).wait_send()

    far_out[...] = far_sum[...].astype(jnp.bfloat16)
    far_halves().start()
    end_mark.wait()
    single = mark_ref[...].astype(jnp.float32)[0:1, BLK - 1 : BLK] == 0.0
    far_halves().wait_recv()
    own_ref[mine_half] += jnp.where(single, far_sum[...], 0.0)
    own_ref[twin_half] += jnp.where(single, far_back[...].astype(jnp.float32), 0.0)
    far_halves().wait_send()

    wide = mine_ref[:BLK].astype(jnp.float32)
    scale = rms_rows(wide)
    weighted = own_ref[...] * gain_one
    tokens_grad_ref[...] = (
        state_grad_ref[...]
        + scale * weighted
        - wide * (scale**3 * jnp.mean(weighted * wide, axis=-1, keepdims=True))
    )
    finals = []
    for part in range(3):
        first = PART_ORDER[part][0]
        for by in (1, 2, 3):
            net(part, 2, by, in_three[part].at[by - 1], in_three[part].at[by - 1]).wait_recv()
        total = sum_two[part][spot[first]].astype(jnp.float32)
        for by in range(3):
            total = total + in_three[part][by].astype(jnp.float32)
        finals.append(total)
    final = jnp.concatenate(finals, axis=1)
    sums_ref[:16] = final[:, :768]
    sums_ref[16:] = jnp.concatenate([final[:8, 768:1152], final[8:, 768:1152]], axis=1)
    few_ref[...] = final[:8, 1152:]
    small_step(2)
    for number in range(len(MESSAGES)):
        expert(number).wait_send()
    for copy in started:
        copy.wait_send()


def run_back(blocks, weights, smalls, prev, wres, routes, cot, kept, back_rows, back_grads, d_pay):
    vmem, anywhere = pl.BlockSpec(memory_space=pltpu.VMEM), pl.BlockSpec(memory_space=pl.ANY)
    shape = jax.ShapeDtypeStruct
    low, wide = jnp.bfloat16, jnp.float32
    dma = pltpu.SemaphoreType.DMA
    left, right, small = (jnp.asarray(t.T, low) for t in placing_tables())
    by_part = lambda *lead: [pltpu.VMEM((*lead, 16, lanes), low) for lanes in PART_LANES]
    return pl.pallas_call(
        back_kernel,
        out_shape=[
            shape((BLK, WIDTH), low),
            shape((16, BLK), wide),
            shape((16, 128), wide),
            shape((BLK, WIDTH), wide),
            shape((24, WIDTH), wide),
            shape((8, 128), wide),
            shape((96, 1024), wide),
            shape((96, 1024), wide),
            shape((128, WIDTH), wide),
        ],
        in_specs=[anywhere] + [vmem] * 18 + [anywhere] * 2 + [vmem] * 4 + [anywhere],
        out_specs=[vmem] * 9,
        scratch_shapes=[
            pltpu.VMEM((HEADS, 128, BLK), low),
            pltpu.VMEM((HEADS, 128, BLK), low),
            pltpu.VMEM((PAIRS, 2 * BLK, 128), low),
            pltpu.VMEM((PAIRS, 2 * BLK, 128), low),
            pltpu.VMEM((BLK, BLK), wide),
            pltpu.VMEM((16, BLK), wide),
            pltpu.VMEM((WIDTH, BLK), wide),
            pltpu.VMEM((1, WIDTH), wide),
            pltpu.VMEM((BLK, WIDTH), low),
            pltpu.VMEM((BLK, WIDTH), low),
            pltpu.VMEM((128, BLK), wide),
            pltpu.VMEM((128, 128), wide),
            pltpu.VMEM((2, WIDTH, WIDTH), wide),
            pltpu.VMEM((2, WIDTH, WIDTH), low),
            pltpu.VMEM((WIDTH, 128), wide),
            pltpu.VMEM((2, 2, PAIRS, BLK, 128), low),
            pltpu.VMEM((2, BLK + 16, WIDTH), low),
            pltpu.VMEM((BLK + 16, WIDTH), low),
            dma((2, 3)),
            pltpu.VMEM((BLK, WIDTH), wide),
            pltpu.VMEM((BLK, WIDTH), wide),
            pltpu.VMEM((7, BLK, WIDTH), low),
            pltpu.VMEM((4, 4, 4, 2, 16, 1280), low),
            pltpu.VMEM((2, BLK, WIDTH), low),
            pltpu.VMEM((5, 128, WIDTH), low),
            pltpu.VMEM((5, 128, WIDTH), low),
            pltpu.VMEM((128, WIDTH), wide),
            pltpu.VMEM((128, WIDTH), low),
            pltpu.VMEM((128, WIDTH), low),
            pltpu.VMEM((16, WIDTH), low),
            dma((6,)),
            dma((6,)),
            pltpu.VMEM((8, 288, 1024), low),
            pltpu.VMEM((2016, 1024), low),
            pltpu.VMEM((4, 4, 16, 128), wide),
            pltpu.VMEM((4, 16, 128), wide),
            dma((7,)),
            dma((7,)),
            dma((15,)),
            dma((15,)),
            dma((10,)),
            dma((3, 3, 3)),
            dma((3, 3, 3)),
            dma((4,)),
            dma((4,)),
            dma((4, 3)),
            dma((4, 3)),
            pltpu.VMEM((4, 4, 4, 16, 1280), low),
            *by_part(3, 4, 4),
            *by_part(3, 4),
            *by_part(3),
            *by_part(4, 4),
            *by_part(4),
        ],
        name="back",
        compiler_params=pltpu.CompilerParams(
            collective_id=2, has_side_effects=True, vmem_limit_bytes=62 * 2**20
        ),
    )(
        blocks, weights, smalls, *rope_tables(), left, right, small, prev, wres, routes, cot,
        *kept, back_rows, back_grads, d_pay,
    )


def finish_kernel(
    out_in, tokens_in, gate_in, up_in, down_in, prev_in, total_in, sums_in, few_in,
    out, tokens_grad, gate, up, down, prev, total, sum_q, sum_k, sum_v, sum_o,
    gain_one, gain_two, router, constant, vectors, prev_at, total_at, sums_at, few_at, sems,
):
    pairs = (
        (prev_in, prev_at), (total_in, total_at), (sums_in, sums_at), (few_in, few_at),
        (tokens_in, tokens_grad), (out_in, out), (gate_in, gate), (up_in, up), (down_in, down),
    )
    copies = [
        pltpu.make_async_copy(source, target, sems.at[index])
        for index, (source, target) in enumerate(pairs)
    ]
    for copy in copies:
        copy.start()
    for copy in copies[:4]:
        copy.wait()
    prev[:, 0, :] = prev_at[:NALL]
    total[...] = total_at[:NALL, :NALL]
    for weight, ref in enumerate((sum_q, sum_k, sum_v, sum_o)):
        ref[...] = sums_at[weight * 6 : weight * 6 + 6]
    few = few_at[...]
    router[...] = few[:6, :NALL]
    tall = jnp.concatenate([few, jnp.zeros((120, 128), jnp.float32)], axis=0).T
    constant[...] = tall[12:16, :6]
    vectors[...] = tall[16:18, :6]
    gain_one[...] = tall[18:19, :6]
    gain_two[...] = tall[19:20, :6]
    for copy in copies[4:]:
        copy.wait()


def finish(out, tokens_grad, gate, up, down, prev, total, sums, few):
    vmem = pl.BlockSpec(memory_space=pltpu.VMEM)
    shape = jax.ShapeDtypeStruct
    wide = jnp.float32
    like = [shape(a.shape, a.dtype) for a in (out, tokens_grad, gate, up, down)]
    few_shapes = [(1, 6), (1, 6), (6, NALL), (4, 6), (2, 6)]
    return pl.pallas_call(
        finish_kernel,
        out_shape=like
        + [shape((NALL, 1, BLK), wide), shape((NALL, NALL), wide)]
        + [shape((6, WIDTH), wide)] * 4
        + [shape(s, wide) for s in few_shapes],
        in_specs=[pl.BlockSpec(memory_space=pl.ANY)] * 9,
        out_specs=[vmem] * 16,
        scratch_shapes=[
            *(pltpu.VMEM(a.shape, a.dtype) for a in (prev, total, sums, few)),
            pltpu.SemaphoreType.DMA((9,)),
        ],
        name="finish",
        compiler_params=pltpu.CompilerParams(vmem_limit_bytes=62 * 2**20),
    )(out, tokens_grad, gate, up, down, prev, total, sums, few)


def on_device(
    tokens, prev_logits, routes, segments, rank_order, norm_first, w_query, w_key, w_value, w_output,
    norm_second, w_router, w_residual, w_constant, v_constant, w_gate, w_up, w_down, cotangent,
):
    few = [w_router, w_constant.T, v_constant.T, norm_first[None], norm_second[None]]
    prev = jnp.transpose(prev_logits, (2, 0, 1))
    (
        state, normed, att, lse, q, keys, values, info, proj, blocks, weights, smalls, _,
        back_rows, back_grads, d_pay,
    ) = run_forward(
        [w_query, w_key, w_value, w_output], few, tokens[0], segments, (w_gate[0], w_up[0], w_down[0]),
        prev, w_residual, routes[0].T, rank_order[0], cotangent[0],
    )
    (
        out, prev_grad, residual, tokens_grad, sums, small, d_gate, d_up, d_down,
    ) = run_back(
        blocks, weights, smalls, prev, w_residual, routes[0].T, cotangent[0],
        (state, normed, att, lse, q, keys, values, info, proj), back_rows, back_grads, d_pay,
    )
    (
        out, tokens_grad, d_gate, d_up, d_down, prev_grad, residual, sum_q, sum_k, sum_v, sum_o,
        gain_one, gain_two, router, constant, vectors,
    ) = finish(out, tokens_grad, d_gate, d_up, d_down, prev_grad, residual, sums, small)
    return (
        out[None],
        tokens_grad[None],
        jnp.transpose(prev_grad, (1, 2, 0)),
        gain_one[0],
        sum_q,
        sum_k,
        sum_v,
        sum_o,
        gain_two[0],
        router,
        residual,
        constant.T,
        vectors.T,
        d_gate[None],
        d_up[None],
        d_down[None],
    )


def solution(mesh):
    in_specs = (
        P("fsdp", "ctx", None),
        P("fsdp", "ctx", None),
        P("fsdp", "ctx", None),
        P("fsdp", "ctx"),
        P("fsdp", "ctx", None),
        P(("ctx", "fsdp")),
        P(("ctx", "fsdp"), None),
        P(("ctx", "fsdp"), None),
        P(("ctx", "fsdp"), None),
        P(("ctx", "fsdp"), None),
        P(("ctx", "fsdp")),
        P(("ctx", "fsdp"), None),
        P(),
        P(("ctx", "fsdp"), None),
        P(("ctx", "fsdp"), None),
        P("fsdp", "ctx", None),
        P("fsdp", "ctx", None),
        P("fsdp", "ctx", None),
        P("fsdp", "ctx", None),
    )
    out_specs = (
        P("fsdp", "ctx", None),
        P("fsdp", "ctx", None),
        P("fsdp", "ctx", None),
        P(("ctx", "fsdp")),
        P(("ctx", "fsdp"), None),
        P(("ctx", "fsdp"), None),
        P(("ctx", "fsdp"), None),
        P(("ctx", "fsdp"), None),
        P(("ctx", "fsdp")),
        P(("ctx", "fsdp"), None),
        P(),
        P(("ctx", "fsdp"), None),
        P(("ctx", "fsdp"), None),
        P("fsdp", "ctx", None),
        P("fsdp", "ctx", None),
        P("fsdp", "ctx", None),
    )
    return jax.shard_map(
        on_device, mesh=mesh, in_specs=in_specs, out_specs=out_specs, check_vma=False
    )
```

```python
import functools

import jax
import jax.numpy as jnp
import numpy as np
from jax import lax
from jax.experimental import pallas as pl
from jax.experimental.pallas import tpu as pltpu
from jax.sharding import PartitionSpec as P

HEADS = 12
HDIM = 64
EXPERTS = 8
NALL = 12
CAP = 54
WIDTH = HEADS * HDIM
PAIRS = HEADS // 2
BLK = 256
SLOTS = 64

highest = lax.Precision.HIGHEST
masked_score = -1e30
epsilon = 1e-06

MESH = pl.DeviceIdType.MESH
PART_LANES = (512, 384, 384)
PART_START = (0, 512, 896)
PART_ORDER = ((0, 1, 2), (1, 2, 0), (2, 0, 1))

BLOCK_CUTS = (0, 64, 144, 224, 272)
PAY_CUTS = (0, 64, 144, 224, 288)
GRAD_CUTS = (0, 64, 144, 224, 288)
SPANS = {"all": (0, 4), "p": (1, 3), "h1": (0, 2), "h2": (2, 4), "q1": (0, 1), "p1": (1, 2), "p2": (2, 3), "q2": (3, 4)}
MESSAGES = (
    (1, (0, 0), "all"), (-1, (0, 0), "all"), (0, (0, 0), "all"),
    (1, (0, 1), "p"), (-1, (0, 1), "p"),
    (1, (-1, 0), "h1"), (-1, (1, 0), "h2"),
    (0, (-1, 0), "q1"), (0, (-1, 0), "q2"), (0, (1, 0), "q1"), (0, (1, 0), "q2"),
    (1, (-1, 1), "p1"), (-1, (1, 1), "p2"),
    (0, (2, 0), "q1"), (0, (2, 0), "q2"),
)


def place():
    ctx = lax.axis_index("ctx")
    fsdp = lax.axis_index("fsdp")
    return ctx // 2, (ctx % 2) * 2 + fsdp // 8, (fsdp // 2) % 4, fsdp % 2


def device_at(x, z, y, core):
    return {"ctx": x * 2 + z // 2, "fsdp": (z % 2) * 8 + y * 2 + core}


def shifted(spot, axis, by):
    moved = list(spot)
    moved[axis] = (moved[axis] + by) % 4
    return tuple(moved)


def greet(devices):
    barrier = pltpu.get_barrier_semaphore()
    for device in devices:
        pl.semaphore_signal(barrier, inc=1, device_id=device, device_id_type=MESH)
    pl.semaphore_wait(barrier, len(devices))


def torus_peers(spot, core):
    peers = [device_at(*shifted(spot, axis, by), core) for axis in range(3) for by in (1, 2, 3)]
    return peers + [device_at(*spot, 1 - core)]


def sequence_peers(spot, core):
    x, z, y = spot
    return [device_at((x + by) % 4, (z + 2) % 4, y, core) for by in (1, 2, 3)]


def region(ref, spot, core, whole):
    return ref.at[
        tuple(slice(None) if axis in whole else spot[axis] for axis in range(3)) + (core,)
    ]


def placing_tables():
    left = np.zeros((192, 256), np.float32)
    right = np.zeros((192, 256), np.float32)
    small = np.zeros((48, 128), np.float32)
    for device in range(8):
        for weight in range(4):
            for row in range(6):
                at, line = weight * 48 + device * 6 + row, weight * 6 + row
                if line < 16:
                    left[at, device * 16 + line] = right[at, device * 16 + line] = 1
                else:
                    left[at, 128 + device * 16 + line - 16] = 1
                    right[at, 128 + device * 16 + line - 8] = 1
        for row in range(6):
            small[device * 6 + row, device * 16 + row] = 1
    return left, right, small


def rope_tables():
    frequency = 10000.0 ** (-2.0 * (np.arange(128) % 32) / HDIM)
    inner = np.arange(BLK)[:, None] * frequency
    outer = (np.arange(8) * BLK)[:, None] * frequency
    return [jnp.asarray(t, jnp.float32) for t in (np.cos(inner), np.sin(inner), np.cos(outer), np.sin(outer))]


def turning(index, tables):
    cos_in, sin_in, cos_out, sin_out = tables
    ca, sa = cos_out[pl.ds(index, 1), :], sin_out[pl.ds(index, 1), :]
    cb, sb = cos_in[...], sin_in[...]
    lower = lax.broadcasted_iota(jnp.int32, (BLK, 128), 1) % HDIM < HDIM // 2
    sine = sa * cb + ca * sb
    return ca * cb - sa * sb, jnp.where(lower, -sine, sine)


def swapped(values):
    lower = lax.broadcasted_iota(jnp.int32, values.shape, 1) % HDIM < HDIM // 2
    return jnp.where(lower, pltpu.roll(values, 96, 1), pltpu.roll(values, 32, 1))


def dot(left, right):
    return jnp.dot(left, right, preferred_element_type=jnp.float32)


def dot_nt(left, right):
    return lax.dot_general(left, right, (((1,), (1,)), ((), ())), preferred_element_type=jnp.float32)


def column(row):
    return jnp.broadcast_to(row, (128, row.shape[1])).T[:, 0:1]


def mask_bias(key_block, query_block, bias_ref, ctx, index):
    key_seg = column(key_block[BLK:, :BLK].astype(jnp.float32)[:1])
    query_seg = query_block[BLK:, :BLK].astype(jnp.float32)[:1]
    key_pos = lax.broadcasted_iota(jnp.int32, (BLK, BLK), 0)
    query_pos = lax.broadcasted_iota(jnp.int32, (BLK, BLK), 1)
    reach = jnp.where(index == ctx, 0, BLK)
    allowed = (key_seg == query_seg) & (key_pos <= query_pos + reach)
    bias_ref[...] = jnp.where(allowed, 0.0, masked_score)


def rms_rows(values):
    return lax.rsqrt(jnp.mean(values * values, axis=-1, keepdims=True) + epsilon)


def pick(onehot, values):
    return jnp.sum(jnp.where(onehot, values, 0.0), axis=1, keepdims=True)


def lane_is(lanes):
    return lax.broadcasted_iota(jnp.int32, (BLK, 128), 1) == lanes


def dot_tn(left, right):
    return lax.dot_general(left, right, (((0,), (0,)), ((), ())), preferred_element_type=jnp.float32)


def row_tile(values):
    *weights, small = values
    rows = jnp.concatenate([w.astype(jnp.float32) for w in weights], axis=0)
    tail = jnp.concatenate([rows[16:, :384], rows[16:, 384:]], axis=0)
    return jnp.concatenate([rows[:16], tail, small], axis=1).astype(jnp.bfloat16)


def forward_kernel(
    wq_ref, wk_ref, wv_ref, wo_ref, router_ref, constant_ref, vector_ref, gain_one_ref, gain_two_ref,
    tokens_ref, segments_in, gate_in, up_in, down_in,
    left_ref, right_ref, place_ref, cos_in, sin_in, cos_out, sin_out,
    prev_ref, wres_ref, routes_ref, rank_ref, cot_ref,
    state_out, normed_out, att_out, lse_ref, q_out, keys_ref, values_ref,
    info_ref, proj_ref, blocks_out, w_out, small_ref, pay_ref,
    back_rows_ref, back_grads_ref, d_pay_out,
    part_a, part_b, part_c, own_ref, qt_ref, vt_ref, bias_ref, max_ref, sum_ref, acc_ref,
    prev_pad, wres_pad, few_wide, few_tall, kv_ref, rows_ref, grads_ref, blocks_ref, w_ref,
    state_ref, normed_ref, att_ref, q_ref, d_pay_ref,
    gate_w, up_w, down_w, x_ref, g_ref, gate_ref, up_ref, hidden_ref, d_gate, d_up,
    mine_ref, twin_out, twin_in,
    net_send, net_recv, twin_send, twin_recv, own_sem, ring_send, ring_recv, kv_sem,
    load_sem, send_sem, recv_sem, share_send, share_recv, half_send, half_recv, ret_send, ret_recv,
    keep_sem,
):
    parts = (part_a, part_b, part_c)
    tables = (cos_in, sin_in, cos_out, sin_out)
    ctx, fsdp = lax.axis_index("ctx"), lax.axis_index("fsdp")
    along, side = ctx // 2, ctx % 2
    *spot, core = place()
    spot = tuple(spot)
    twin = device_at(*spot, 1 - core)
    few_wide[...] = jnp.zeros_like(few_wide)
    few_wide[12:16, :6] = constant_ref[...].astype(jnp.float32)
    few_wide[16:18, :6] = vector_ref[...].astype(jnp.float32)
    few_wide[18:19, :6] = gain_one_ref[...].astype(jnp.float32)
    few_wide[19:20, :6] = gain_two_ref[...].astype(jnp.float32)
    few_tall[...] = few_wide[...].T[:16]
    few_tall[:6, :NALL] = router_ref[...].astype(jnp.float32)
    own_ref[...] = row_tile([wq_ref[...], wk_ref[...], wv_ref[...], wo_ref[...], few_tall[...]])
    marks = jnp.concatenate(
        [segments_in[...].astype(jnp.float32), jnp.zeros((1, WIDTH - BLK), jnp.float32)], axis=1
    )
    blocks_ref[ctx, :BLK] = tokens_ref[...]
    blocks_ref[ctx, BLK:] = jnp.broadcast_to(marks, (16, WIDTH)).astype(jnp.bfloat16)
    chip = fsdp // 2

    def at_expert(where, on):
        return {"ctx": ctx, "fsdp": where * 2 + on}

    greet(
        torus_peers(spot, core)
        + [at_expert((chip + by) % EXPERTS, core) for by in range(1, EXPERTS)]
    )

    def net(part, step, by, source, target):
        axis = PART_ORDER[part][step]
        return pltpu.make_async_remote_copy(
            src_ref=source,
            dst_ref=target,
            send_sem=net_send.at[part, step, by - 1],
            recv_sem=net_recv.at[part, step, by - 1],
            device_id=device_at(*shifted(spot, axis, by), core),
            device_id_type=MESH,
        )

    def share(part, slot, source, target):
        return pltpu.make_async_remote_copy(
            src_ref=source,
            dst_ref=target,
            send_sem=twin_send.at[part, slot],
            recv_sem=twin_recv.at[part, slot],
            device_id=twin,
            device_id_type=MESH,
        )

    payloads = ((blocks_ref, BLOCK_CUTS), (pay_ref, PAY_CUTS))

    def ring(kind, number, arriving=False):
        to, (steps, across_it), rows = MESSAGES[number]
        if arriving:
            steps = steps - to
            across_it = across_it if to else 1 - across_it
        array, cuts = payloads[kind]
        first, last = (cuts[i] for i in SPANS[rows])
        on = side if across_it == 0 else 1 - side
        view = array.at[((along + steps + 4) % 4) * 2 + on, pl.ds(first, last - first)]
        target = ((along + to + 4) % 4) * 2 + (side if to else 1 - side)
        return pltpu.make_async_remote_copy(
            src_ref=view,
            dst_ref=view,
            send_sem=ring_send.at[kind, number],
            recv_sem=ring_recv.at[kind, number],
            device_id={"ctx": target, "fsdp": fsdp},
            device_id_type=MESH,
        )

    def pass_on(kind, stage):
        plan = (
            ((None, (0, 1, 2)),),
            ((2, (3, 4)),),
            ((0, (5, 7, 8)), (1, (6, 9, 10))),
            ((3, (11,)), (4, (12,)), (5, (13,)), (6, (14,))),
            tuple((number, ()) for number in range(7, 15)),
        )[stage]
        for number, then in plan:
            if number is not None:
                ring(kind, number, arriving=True).wait_recv()
            for follow in then:
                ring(kind, follow).start()

    started = []
    kept = []
    for part in range(3):
        own = own_ref.at[:, pl.ds(PART_START[part], PART_LANES[part])]
        mine = region(parts[part], spot, core, ())
        for by in (1, 2, 3):
            copy = net(part, 0, by, own, mine)
            copy.start()
            started.append(copy)
    for part in range(3):
        own = own_ref.at[:, pl.ds(PART_START[part], PART_LANES[part])]
        mine = region(parts[part], spot, core, ())
        copy = pltpu.make_async_copy(own, mine, own_sem.at[part])
        copy.start()
        kept.append(copy)
        copy = share(part, 0, own, mine)
        copy.start()
        started.append(copy)
    tail = [(down_in.at[:96], pay_ref.at[ctx, 192:, pl.ds(0, WIDTH)])] + [
        (down_in.at[96:, pl.ds(256 * m, 256)], pay_ref.at[ctx, pl.ds(192 + 32 * m, 32), pl.ds(WIDTH, 256)])
        for m in range(3)
    ]
    pieces = [(gate_in, pay_ref.at[ctx, :96]), (up_in, pay_ref.at[ctx, 96:192]), *tail]
    own_experts = [
        pltpu.make_async_copy(source, target, own_sem.at[3 + number])
        for number, (source, target) in enumerate(pieces)
    ]
    for copy in own_experts:
        copy.start()
    for copy in kept + own_experts:
        copy.wait()
    for step in range(3):
        for part in range(3):
            order = PART_ORDER[part]
            axis = order[step]
            whole = order[:step]
            for by in (1, 2, 3):
                here = region(parts[part], shifted(spot, axis, -by), core, whole)
                net(part, step, by, here, here).wait_recv()
                copy = share(part, 1 + step * 3 + by - 1, here, here)
                copy.start()
                started.append(copy)
            if step < 2:
                held = region(parts[part], spot, core, order[: step + 1])
                for by in (1, 2, 3):
                    copy = net(part, step + 1, by, held, held)
                    copy.start()
                    started.append(copy)
        if step == 1:
            pass_on(0, 0)
    for part in range(3):
        order = PART_ORDER[part]
        first = region(parts[part], spot, 1 - core, ())
        share(part, 0, first, first).wait_recv()
        for step in range(3):
            for by in (1, 2, 3):
                here = region(
                    parts[part], shifted(spot, order[step], -by), 1 - core, order[:step]
                )
                share(part, 1 + step * 3 + by - 1, here, here).wait_recv()

    def unpack(group, carry):
        a, b, c = (
            part[group // 4, group % 4].reshape(128, lanes)
            for part, lanes in zip(parts, PART_LANES, strict=True)
        )
        tail = jnp.concatenate([b[:, 256:], c[:, :256]], axis=1)
        left = dot(left_ref[...], jnp.concatenate([a[:, :384], tail], axis=0))
        right_rows = jnp.concatenate([a[:, 384:], b[:, :256]], axis=1)
        right = dot(right_ref[...], jnp.concatenate([right_rows, tail], axis=0))
        rows = pl.ds(pl.multiple_of(group * 48, 16), 48)
        for weight in range(4):
            w_ref[weight, rows, :384] = left[weight * 48 : weight * 48 + 48].astype(jnp.bfloat16)
            w_ref[weight, rows, 384:] = right[weight * 48 : weight * 48 + 48].astype(jnp.bfloat16)
        small_ref[rows] = dot(place_ref[...], c[:, 256:]).astype(jnp.bfloat16)
        return carry

    pass_on(0, 1)
    lax.fori_loop(0, 16, unpack, 0)
    pass_on(0, 2)
    weights_kept = pltpu.make_async_copy(w_ref, w_out, own_sem.at[9])
    weights_kept.start()
    across = small_ref[...].astype(jnp.float32).T
    gain_one, gain_two = across[18:19], across[19:20]

    def normed_block(index):
        wide = blocks_ref[index, :BLK].astype(jnp.float32)
        return (wide * rms_rows(wide) * gain_one).astype(jnp.bfloat16)

    query = dot(normed_block(ctx), w_ref[0])
    cosine, sine = turning(ctx, tables)
    for pair in range(PAIRS):
        part = query[:, pair * 128 : pair * 128 + 128]
        turned = (part * cosine + swapped(part) * sine) * (HDIM**-0.5)
        q_ref[pair] = turned.astype(jnp.bfloat16)
        across_q = turned.T.astype(jnp.bfloat16)
        blank = jnp.zeros((HDIM, BLK), jnp.bfloat16)
        qt_ref[2 * pair] = jnp.concatenate([across_q[:HDIM], blank], axis=0)
        qt_ref[2 * pair + 1] = jnp.concatenate([blank, across_q[HDIM:]], axis=0)
    max_ref[...] = jnp.full(max_ref.shape, masked_score, jnp.float32)
    sum_ref[...] = jnp.zeros_like(sum_ref)
    acc_ref[...] = jnp.zeros_like(acc_ref)

    def keep_block(index, slot):
        return [
            pltpu.make_async_copy(kv_ref.at[slot, kind], target.at[index], kv_sem.at[slot, kind])
            for kind, target in enumerate((keys_ref, values_ref))
        ]

    def block_at(step):
        odd = step % 2
        x = along - (step + odd) // 2 + odd * side
        return jnp.where(step == 0, ctx, x * 2 + 1 - odd)

    def block(step, carry):
        index = block_at(step)
        slot = step % 2

        @pl.when(step >= 2)
        def _():
            for copy in keep_block(block_at(step - 2), slot):
                copy.wait()

        normed = normed_block(index)
        key = dot(normed, w_ref[1])
        value = dot(normed, w_ref[2])
        cosine, sine = turning(index, tables)
        for pair in range(PAIRS):
            lanes = slice(pair * 128, pair * 128 + 128)
            part = key[:, lanes]
            kv_ref[slot, 0, pair] = (part * cosine + swapped(part) * sine).astype(jnp.bfloat16)
            kv_ref[slot, 1, pair] = value[:, lanes].astype(jnp.bfloat16)
            vt_ref[lanes, :] = value[:, lanes].T.astype(jnp.bfloat16)
        mask_bias(blocks_ref.at[index], blocks_ref.at[ctx], bias_ref, ctx, index)
        def score(head):
            return dot(kv_ref[slot, 0, head // 2], qt_ref[head]) + bias_ref[...]

        def soften(head, scores):
            before = max_ref[head : head + 1]
            top = jnp.maximum(before, jnp.max(scores, axis=0, keepdims=True))
            weights = jnp.exp(scores - top)
            shrink = jnp.exp(before - top)
            sum_ref[head : head + 1] = sum_ref[head : head + 1] * shrink + jnp.sum(
                weights, axis=0, keepdims=True
            )
            max_ref[head : head + 1] = top
            return shrink, weights.astype(jnp.bfloat16)

        def gather(head, shrink, weights):
            rows = slice(head * HDIM, head * HDIM + HDIM)
            acc_ref[rows] = acc_ref[rows] * shrink + dot(vt_ref[rows, :], weights)

        ahead = [score(0), score(1)]
        done = None
        for head in range(0, HEADS, 2):
            now = ahead
            if head + 2 < HEADS:
                ahead = [score(head + 2), score(head + 3)]
            if done is not None:
                gather(head - 2, *done[0])
                gather(head - 1, *done[1])
            done = [soften(head, now[0]), soften(head + 1, now[1])]
        gather(HEADS - 2, *done[0])
        gather(HEADS - 1, *done[1])

        for copy in keep_block(index, slot):
            copy.start()
        for when, todo in (
            (0, ((0, 3), (1, 0))),
            (1, ((0, 4),)),
            (5, ((1, 1), (1, 2))),
            (7, ((1, 3),)),
        ):

            @pl.when(step == jnp.minimum(ctx, when))
            def _(todo=todo):
                for kind, stage in todo:
                    pass_on(kind, stage)

        return carry

    lax.fori_loop(0, ctx + 1, block, 0)
    blocks_kept = pltpu.make_async_copy(blocks_ref, blocks_out, own_sem.at[10])
    blocks_kept.start()
    for head in range(HEADS):
        rows = slice(head * HDIM, head * HDIM + HDIM)
        att_ref[rows] = acc_ref[rows] / sum_ref[head : head + 1]
    lse_ref[...] = max_ref[...] + jnp.log(jnp.maximum(sum_ref[...], 1e-30))
    attended = att_ref[...].T.astype(jnp.bfloat16)
    state = blocks_ref[ctx, :BLK].astype(jnp.float32) + dot(attended, w_ref[3])
    state_ref[...] = state
    normed_two = (state * rms_rows(state) * gain_two).astype(jnp.bfloat16)
    normed_ref[...] = normed_two

    proj = dot(normed_two, small_ref[...])
    proj_ref[...] = proj
    pad_routing(prev_ref, wres_ref, prev_pad, wres_pad)
    logits = proj + jnp.dot(
        prev_pad[...].T, wres_pad[...], precision=highest, preferred_element_type=jnp.float32
    )
    lanes = lax.broadcasted_iota(jnp.int32, (BLK, 128), 1).astype(jnp.float32)
    routes = routes_ref[...].astype(jnp.float32)
    route_0, route_1 = column(routes[0:1]), column(routes[1:2])
    hot_0, hot_1 = lanes == route_0, lanes == route_1
    chosen_0, chosen_1 = pick(hot_0, logits), pick(hot_1, logits)
    top = jnp.maximum(chosen_0, chosen_1)
    chosen_0, chosen_1 = jnp.exp(chosen_0 - top), jnp.exp(chosen_1 - top)
    gate_0, gate_1 = chosen_0 / (chosen_0 + chosen_1), chosen_1 / (chosen_0 + chosen_1)
    rank = rank_ref[...].astype(jnp.float32)
    earlier = (rank < column(rank)).astype(jnp.float32).astype(jnp.bfloat16)
    slots = dot(earlier, (hot_0 | hot_1).astype(jnp.float32).astype(jnp.bfloat16))

    def target(route, hot):
        slot = pick(hot, slots)
        return jnp.where(
            (route < EXPERTS) & (slot < CAP), route * SLOTS + slot, -1.0
        )

    target_0, target_1 = target(route_0, hot_0), target(route_1, hot_1)
    info = jnp.where(lanes == 0, gate_0, 0.0) + jnp.where(lanes == 1, gate_1, 0.0)
    info = info + jnp.where(lanes == 2, target_0, 0.0) + jnp.where(lanes == 3, target_1, 0.0)
    info_ref[...] = info
    targets = info.T
    rows = lax.broadcasted_iota(jnp.int32, (EXPERTS * SLOTS, BLK), 0).astype(jnp.float32)
    table_0 = (rows == targets[2:3]).astype(jnp.float32).astype(jnp.bfloat16)
    table_1 = (rows == targets[3:4]).astype(jnp.float32).astype(jnp.bfloat16)
    rows_ref[...] = dot(table_0 + table_1, normed_two).astype(jnp.bfloat16)
    upstream = cot_ref[...].astype(jnp.float32)
    grads_ref[...] = dot(
        jnp.concatenate([table_0, table_1], axis=1),
        jnp.concatenate([gate_0 * upstream, gate_1 * upstream], axis=0).astype(jnp.bfloat16),
    ).astype(jnp.bfloat16)
    for back in (0, 1):

        @pl.when(ctx - back >= 0)
        def _(back=back):
            for copy in keep_block(block_at(ctx - back), (ctx - back) % 2):
                copy.wait()

    other = 1 - core
    half = EXPERTS * SLOTS
    leaving = [
        pltpu.make_async_copy(source, target, own_sem.at[11 + number])
        for number, (source, target) in enumerate(
            ((state_ref, state_out), (normed_ref, normed_out), (att_ref, att_out), (q_ref, q_out))
        )
    ]

    def slots(index, on):
        return pl.ds(pl.multiple_of((on * EXPERTS + index) * SLOTS, SLOTS), SLOTS)

    def chunk(index):
        return pl.ds(pl.multiple_of(index * SLOTS, SLOTS), SLOTS)

    buffers = ((rows_ref, x_ref), (grads_ref, g_ref))

    def dispatch(kind, by):
        source, target = buffers[kind]
        where = (chip + by) % EXPERTS
        return pltpu.make_async_remote_copy(
            src_ref=source.at[chunk(where)],
            dst_ref=target.at[slots(chip, core)],
            send_sem=send_sem.at[kind, by - 1],
            recv_sem=recv_sem.at[kind, by - 1],
            device_id=at_expert(where, core),
            device_id_type=MESH,
        )

    def share(kind, by, on):
        source, target = buffers[kind]
        spot = slots((chip - by) % EXPERTS, on)
        return pltpu.make_async_remote_copy(
            src_ref=target.at[spot],
            dst_ref=target.at[spot],
            send_sem=share_send.at[kind, by],
            recv_sem=share_recv.at[kind, by],
            device_id=at_expert(chip, other),
            device_id_type=MESH,
        )

    def exchange(kind):
        return pltpu.make_async_remote_copy(
            src_ref=twin_out.at[kind],
            dst_ref=twin_in.at[kind],
            send_sem=half_send.at[kind],
            recv_sem=half_recv.at[kind],
            device_id=at_expert(chip, other),
            device_id_type=MESH,
        )

    returned = (back_rows_ref, back_grads_ref)

    def give_back(kind, by):
        where = (chip + by) % EXPERTS
        return pltpu.make_async_remote_copy(
            src_ref=mine_ref.at[kind, chunk(where)],
            dst_ref=returned[kind].at[chunk(chip)],
            send_sem=ret_send.at[kind, by - 1],
            recv_sem=ret_recv.at[kind, by - 1],
            device_id=at_expert(where, core),
            device_id_type=MESH,
        )

    for by in range(1, EXPERTS):
        dispatch(0, by).start()
    for by in range(1, EXPERTS):
        dispatch(0, by).wait_send()
    for by in range(1, EXPERTS):
        copy = dispatch(1, by)
        copy.start()
        started.append(copy)
    for kind in (0, 1):
        source, target = buffers[kind]
        copy = pltpu.make_async_copy(
            source.at[chunk(chip)], target.at[slots(chip, core)], keep_sem.at[kind]
        )
        copy.start()
        copy.wait()
        copy = share(kind, 0, core)
        copy.start()
        started.append(copy)

    def arrive(kind):
        for by in range(1, EXPERTS):
            dispatch(kind, by).wait_recv()
            copy = share(kind, by, core)
            copy.start()
            started.append(copy)

    def arrive_shared(kind):
        for by in range(EXPERTS):
            share(kind, by, other).wait_recv()

    def tiles(on, body):
        def step(index, carry):
            start = pl.multiple_of(on * half + index * 256, 256)
            body(pl.ds(start, 256), pl.ds(pl.multiple_of(index * 256, 256), 256))
            return carry

        lax.fori_loop(0, half // 256, step, 0)

    def forward(on, keep):
        def tile(rows, inner):
            x = x_ref[rows]
            gate, up = dot(x, gate_w[...]), dot(x, up_w[...])
            gate_ref[rows], up_ref[rows] = gate, up
            hidden_ref[rows] = (gate * jax.nn.sigmoid(gate) * up).astype(jnp.bfloat16)

        def result(rows, inner):
            keep(inner, dot(hidden_ref[rows], down_w[...]))

        tiles(on, tile)
        tiles(on, result)

    def backward(on, keep):
        def tile(rows, inner):
            hidden_grad = dot_nt(g_ref[rows], down_w[...])
            gate, up = gate_ref[rows], up_ref[rows]
            sigmoid = jax.nn.sigmoid(gate)
            d_gate[rows] = (
                hidden_grad * up * sigmoid * (1.0 + gate * (1.0 - sigmoid))
            ).astype(jnp.bfloat16)
            d_up[rows] = (hidden_grad * gate * sigmoid).astype(jnp.bfloat16)
            keep(inner, dot_nt(d_gate[rows], gate_w[...]) + dot_nt(d_up[rows], up_w[...]))

        tiles(on, tile)

    def keep_mine(kind):
        def keep(rows, values):
            mine_ref[kind, rows] = values.astype(jnp.bfloat16)

        return keep

    def keep_twin(kind):
        def keep(rows, values):
            twin_out[kind, rows] = values.astype(jnp.bfloat16)

        return keep

    def finish(kind):
        exchange(kind).wait_recv()

        def step(index, carry):
            rows = pl.ds(pl.multiple_of(index * 128, 128), 128)
            mine_ref[kind, rows] = (
                mine_ref[kind, rows].astype(jnp.float32) + twin_in[kind, rows].astype(jnp.float32)
            ).astype(jnp.bfloat16)
            return carry

        lax.fori_loop(0, half // 128, step, 0)
        for by in range(1, EXPERTS):
            copy = give_back(kind, by)
            copy.start()
            started.append(copy)
        copy = pltpu.make_async_copy(
            mine_ref.at[kind, chunk(chip)], returned[kind].at[chunk(chip)], keep_sem.at[kind]
        )
        copy.start()
        copy.wait()

    def load(owner):
        parts = [
            (pay_ref.at[owner, :96], gate_w.at[pl.ds(pl.multiple_of(owner * 96, 16), 96)]),
            (pay_ref.at[owner, 96:192], up_w.at[pl.ds(pl.multiple_of(owner * 96, 16), 96)]),
            (
                pay_ref.at[owner, 192:, pl.ds(0, WIDTH)],
                down_w.at[pl.ds(pl.multiple_of(owner * 128, 16), 96)],
            ),
        ] + [
            (
                pay_ref.at[owner, pl.ds(192 + 32 * m, 32), pl.ds(WIDTH, 256)],
                down_w.at[pl.ds(pl.multiple_of(owner * 128 + 96, 16), 32), pl.ds(256 * m, 256)],
            )
            for m in range(3)
        ]
        return [
            pltpu.make_async_copy(source, target, load_sem.at[owner, number])
            for number, (source, target) in enumerate(parts)
        ]

    pass_on(1, 4)
    for owner in range(8):
        for copy in load(owner):
            copy.start()
    for copy in leaving:
        copy.start()
    arrive(0)
    for owner in range(8):
        for copy in load(owner):
            copy.wait()
    forward(core, keep_mine(0))
    arrive(1)
    arrive_shared(0)
    forward(other, keep_twin(0))
    copy = exchange(0)
    copy.start()
    started.append(copy)
    backward(core, keep_mine(1))
    finish(0)
    arrive_shared(1)
    backward(other, keep_twin(1))
    copy = exchange(1)
    copy.start()
    started.append(copy)

    def down_tile(index, carry):
        lanes = pl.ds(pl.multiple_of(index * 256, 256), 256)
        part = dot_tn(hidden_ref[:, lanes], g_ref[...]).astype(jnp.bfloat16)
        for piece in (0, 1):
            rows = part[piece * 128 : piece * 128 + 128]
            d_pay_ref[2 * index + piece, 192:, :WIDTH] = rows[:96]
            for m in range(3):
                d_pay_ref[2 * index + piece, 192 + 32 * m : 224 + 32 * m, WIDTH:] = rows[
                    96:, 256 * m : 256 * m + 256
                ]
        return carry

    lax.fori_loop(0, 4, down_tile, 0)
    finish(1)

    def gate_tile(index, carry):
        lanes = pl.ds(pl.multiple_of(index * 256, 256), 256)
        for start, grad in ((0, d_gate), (96, d_up)):
            part = dot_tn(x_ref[...], grad[:, lanes]).astype(jnp.bfloat16)
            for piece in range(8):
                d_pay_ref[piece, start : start + 96, lanes] = part[piece * 96 : piece * 96 + 96]
        return carry

    lax.fori_loop(0, 4, gate_tile, 0)
    leaving.append(pltpu.make_async_copy(d_pay_ref, d_pay_out, own_sem.at[15]))
    leaving[-1].start()
    for kind in (0, 1):
        for by in range(1, EXPERTS):
            give_back(kind, by).wait_recv()
    for copy in [weights_kept, blocks_kept, *leaving]:
        copy.wait()
    for kind in (0, 1):
        for number in range(len(MESSAGES)):
            ring(kind, number).wait_send()
    for copy in started:
        copy.wait_send()


def pad_routing(prev_ref, wres_ref, prev_pad, wres_pad):
    prev_pad[...] = jnp.zeros_like(prev_pad)
    prev_pad[:NALL] = prev_ref[:, 0, :]
    wres_pad[...] = jnp.zeros_like(wres_pad)
    wres_pad[:NALL, :NALL] = wres_ref[...]


def run_forward(weights, few, tokens, segments, experts, prev, wres, routes, rank, cot):
    vmem, anywhere = pl.BlockSpec(memory_space=pltpu.VMEM), pl.BlockSpec(memory_space=pl.ANY)
    shape = jax.ShapeDtypeStruct
    low, wide = jnp.bfloat16, jnp.float32
    dma = pltpu.SemaphoreType.DMA
    half, whole = EXPERTS * SLOTS, 2 * EXPERTS * SLOTS
    left, right, small = (jnp.asarray(t, low) for t in placing_tables())
    return pl.pallas_call(
        forward_kernel,
        out_shape=[
            shape((BLK, WIDTH), wide),
            shape((BLK, WIDTH), low),
            shape((WIDTH, BLK), wide),
            shape((16, BLK), wide),
            shape((PAIRS, BLK, 128), low),
            shape((8, PAIRS, BLK, 128), low),
            shape((8, PAIRS, BLK, 128), low),
            shape((BLK, 128), wide),
            shape((BLK, 128), wide),
            shape((8, BLK + 16, WIDTH), low),
            shape((4, WIDTH, WIDTH), low),
            shape((WIDTH, 128), low),
            shape((8, 288, 1024), low),
            shape((half, WIDTH), low),
            shape((half, WIDTH), low),
            shape((8, 288, 1024), low),
        ],
        in_specs=[vmem] * 26,
        out_specs=[anywhere] * 3 + [vmem] + [anywhere] * 3 + [vmem] * 2 + [anywhere] * 2 + [vmem] + [anywhere] + [vmem] * 2 + [anywhere],
        scratch_shapes=[
            *(pltpu.VMEM((4, 4, 4, 2, 16, lanes), low) for lanes in PART_LANES),
            pltpu.VMEM((16, 1280), low),
            pltpu.VMEM((HEADS, 128, BLK), low),
            pltpu.VMEM((WIDTH, BLK), low),
            pltpu.VMEM((BLK, BLK), wide),
            pltpu.VMEM((16, BLK), wide),
            pltpu.VMEM((16, BLK), wide),
            pltpu.VMEM((WIDTH, BLK), wide),
            pltpu.VMEM((128, BLK), wide),
            pltpu.VMEM((128, 128), wide),
            pltpu.VMEM((128, 128), wide),
            pltpu.VMEM((16, 128), wide),
            pltpu.VMEM((2, 2, PAIRS, BLK, 128), low),
            pltpu.VMEM((half, WIDTH), low),
            pltpu.VMEM((half, WIDTH), low),
            pltpu.VMEM((8, BLK + 16, WIDTH), low),
            pltpu.VMEM((4, WIDTH, WIDTH), low),
            pltpu.VMEM((BLK, WIDTH), wide),
            pltpu.VMEM((BLK, WIDTH), low),
            pltpu.VMEM((WIDTH, BLK), wide),
            pltpu.VMEM((PAIRS, BLK, 128), low),
            pltpu.VMEM((8, 288, 1024), low),
            pltpu.VMEM((WIDTH, 1024), low),
            pltpu.VMEM((WIDTH, 1024), low),
            pltpu.VMEM((1024, WIDTH), low),
            pltpu.VMEM((whole, WIDTH), low),
            pltpu.VMEM((whole, WIDTH), low),
            pltpu.VMEM((whole, 1024), wide),
            pltpu.VMEM((whole, 1024), wide),
            pltpu.VMEM((whole, 1024), low),
            pltpu.VMEM((whole, 1024), low),
            pltpu.VMEM((whole, 1024), low),
            pltpu.VMEM((2, half, WIDTH), low),
            pltpu.VMEM((2, half, WIDTH), low),
            pltpu.VMEM((2, half, WIDTH), low),
            dma((3, 3, 3)),
            dma((3, 3, 3)),
            dma((3, 10)),
            dma((3, 10)),
            dma((16,)),
            dma((2, 15)),
            dma((2, 15)),
            dma((2, 2)),
            dma((8, 6)),
            dma((2, 7)),
            dma((2, 7)),
            dma((2, 8)),
            dma((2, 8)),
            dma((2,)),
            dma((2,)),
            dma((2, 7)),
            dma((2, 7)),
            dma((2,)),
        ],
        name="forward",
        compiler_params=pltpu.CompilerParams(
            collective_id=1, has_side_effects=True, vmem_limit_bytes=63 * 2**20
        ),
    )(
        *weights, *few, tokens, segments, *experts, left, right, small, *rope_tables(),
        prev, wres, routes, rank, cot,
    )


def split(values):
    high = values.astype(jnp.bfloat16)
    low = (values - high.astype(jnp.float32)).astype(jnp.bfloat16)
    return jnp.concatenate([high, low], axis=1)


def back_kernel(
    blocks_ref, w_in, small_ref, cos_in, sin_in, cos_out, sin_out, left_ref, right_ref, place_ref,
    prev_ref, wres_ref, routes_ref, cot_ref,
    state_ref, normed_ref, att_ref, lse_ref, q_ref, keys_ref, values_ref, info_ref, proj_ref,
    back_rows_ref, back_grads_ref, d_pay_ref,
    out_ref, prev_grad_ref, total_ref, tokens_grad_ref, sums_ref, few_ref,
    gate_out, up_out, down_out,
    *scratch,
):
    (
        qt_ref, ot_ref, o_ref, qm_ref, bias_ref, inner_ref, dqt_ref, gain_ref, dk_ref, dv_ref,
        prev_pad, wres_pad, dw_ref, dw_low, few_sum, kv_ref, tok_ref, mine_ref, kv_sem, own_ref, state_grad_ref, others_ref, grads_ref, block_in,
        far_in, far_land, far_sum, far_out, far_back, mark_ref, far_send, far_recv,
        w_ref, pay_ref, pay_in, small_in, small_sum,
        block_send, block_recv, exp_send, exp_recv, load_sem,
        net_send, net_recv, twin_send, twin_recv, small_send, small_recv,
        *more,
    ) = scratch
    twin_in, in_one, in_two, in_three, sum_one, sum_two = (
        more[0], more[1:4], more[4:7], more[7:10], more[10:13], more[13:16]
    )
    tables = (cos_in, sin_in, cos_out, sin_out)
    ctx, fsdp = lax.axis_index("ctx"), lax.axis_index("fsdp")
    *spot, core = place()
    spot = tuple(spot)
    twin = device_at(*spot, 1 - core)
    started = []
    greet(torus_peers(spot, core) + sequence_peers(spot, core))

    along, side = ctx // 2, ctx % 2

    def rows_of(number):
        first, last = (GRAD_CUTS[i] for i in SPANS[MESSAGES[number][2]])
        return first, last - first

    def owner(steps, across_it):
        return ((along + steps + 4) % 4) * 2 + (side if across_it == 0 else 1 - side)

    def expert(number):
        to, (steps, across_it), _ = MESSAGES[number]
        first, count = rows_of(number)
        landing = sum(rows_of(before)[1] for before in range(number))
        return pltpu.make_async_remote_copy(
            src_ref=(d_pay_ref if number >= 7 else pay_ref).at[
                owner(steps - to, across_it if to else 1 - across_it), pl.ds(first, count)
            ],
            dst_ref=pay_in.at[pl.ds(landing, count)],
            send_sem=exp_send.at[number],
            recv_sem=exp_recv.at[number],
            device_id={"ctx": owner(-to, 0 if to else 1), "fsdp": fsdp},
            device_id_type=MESH,
        )

    def send_experts(numbers):
        for number in numbers:
            expert(number).start()

    def add_experts(numbers):
        for number in numbers:
            expert(number).wait_recv()
            _, (steps, across_it), _ = MESSAGES[number]
            first, count = rows_of(number)
            landing = sum(rows_of(before)[1] for before in range(number))
            at = owner(steps, across_it)

            def add_rows(index, carry, at=at, first=first, landing=landing):
                here = pl.ds(pl.multiple_of(first + index * 16, 16), 16)
                there = pl.ds(pl.multiple_of(landing + index * 16, 16), 16)
                pay_ref[at, here] = (
                    pay_ref[at, here].astype(jnp.float32) + pay_in[there].astype(jnp.float32)
                ).astype(jnp.bfloat16)
                return carry

            lax.fori_loop(0, count // 16, add_rows, 0)

    loads = [
        pltpu.make_async_copy(d_pay_ref.at[index], pay_ref.at[index], load_sem.at[1 + index])
        for index in range(8)
    ]
    send_experts((13, 14, 11, 12, 7, 8, 9, 10))
    for copy in loads:
        copy.start()
    weights_in = pltpu.make_async_copy(w_in, w_ref, load_sem.at[10])
    weights_in.start()
    own_block = pltpu.make_async_copy(blocks_ref.at[ctx], mine_ref, load_sem.at[0])
    own_block.start()

    def load_kv(index, slot):
        return [
            pltpu.make_async_copy(source.at[index], kv_ref.at[slot, kind], kv_sem.at[slot, kind])
            for kind, source in enumerate((keys_ref, values_ref))
        ] + [pltpu.make_async_copy(blocks_ref.at[index], tok_ref.at[slot], kv_sem.at[slot, 2])]

    for copy in load_kv(0, 0):
        copy.start()

    mine_half, twin_half = (
        pl.ds(pl.multiple_of(on * 128, 128), 128) for on in (core, 1 - core)
    )
    end_mark = pltpu.make_async_copy(blocks_ref.at[7, pl.ds(BLK, 16)], mark_ref, load_sem.at[9])
    end_mark.start()

    def far_share(index):
        return pltpu.make_async_remote_copy(
            src_ref=others_ref.at[index, twin_half],
            dst_ref=far_in.at[index],
            send_sem=far_send.at[index],
            recv_sem=far_recv.at[index],
            device_id=twin,
            device_id_type=MESH,
        )

    def far_copy(by, target):
        return pltpu.make_async_remote_copy(
            src_ref=others_ref.at[target, mine_half],
            dst_ref=far_land.at[by - 3],
            send_sem=block_send.at[by - 1],
            recv_sem=block_recv.at[by - 1],
            device_id={"ctx": target, "fsdp": fsdp},
            device_id_type=MESH,
        )

    def far_halves():
        return pltpu.make_async_remote_copy(
            src_ref=far_out,
            dst_ref=far_back,
            send_sem=far_send.at[5],
            recv_sem=far_recv.at[5],
            device_id=twin,
            device_id_type=MESH,
        )

    def block_copy(by, target):
        return pltpu.make_async_remote_copy(
            src_ref=others_ref.at[target],
            dst_ref=block_in.at[by - 1],
            send_sem=block_send.at[by - 1],
            recv_sem=block_recv.at[by - 1],
            device_id={"ctx": target, "fsdp": fsdp},
            device_id_type=MESH,
        )

    across = small_ref[...].astype(jnp.float32).T
    gain_one, gain_two = across[18:19], across[19:20]
    value_rows = across[16:18]

    lanes = lax.broadcasted_iota(jnp.int32, (BLK, 128), 1)
    info = info_ref[...]
    gates = (info[:, 0:1], info[:, 1:2])
    slots = lax.broadcasted_iota(jnp.int32, (BLK, EXPERTS * SLOTS), 1).astype(jnp.float32)
    tables_of = [
        (slots == info[:, 2 + k : 3 + k]).astype(jnp.float32).astype(jnp.bfloat16) for k in (0, 1)
    ]
    route_rows = routes_ref[...].astype(jnp.float32)
    routes = (column(route_rows[0:1]), column(route_rows[1:2]))
    hots = [lanes.astype(jnp.float32) == routes[k] for k in (0, 1)]
    named = [
        [(routes[k] == EXPERTS + 1 + kind).astype(jnp.float32) for kind in range(3)] for k in (0, 1)
    ]
    proj = proj_ref[...]
    mixes = []
    for c in (0, 1):
        first, second = proj[:, 12 + 2 * c : 13 + 2 * c], proj[:, 13 + 2 * c : 14 + 2 * c]
        top = jnp.maximum(first, second)
        first, second = jnp.exp(first - top), jnp.exp(second - top)
        mixes.append((first / (first + second), second / (first + second)))
    normed_low = normed_ref[...]
    normed_two = normed_low.astype(jnp.float32)
    upstream_low = cot_ref[...]
    upstream = upstream_low.astype(jnp.float32)
    state = state_ref[...]
    back_rows = back_rows_ref[...]
    result = state
    gate_grads = []
    for k in (0, 1):
        copy, one, two = named[k]
        pair = dot(tables_of[k], back_rows)
        pair = pair + (copy + one * mixes[0][0] + two * mixes[1][0]) * normed_two
        pair = pair + (one * mixes[0][1]) * value_rows[0:1] + (two * mixes[1][1]) * value_rows[1:2]
        result = result + gates[k] * pair
        gate_grads.append(jnp.sum(pair * upstream, axis=1, keepdims=True))
    out_ref[...] = result.astype(jnp.bfloat16)
    inner = gates[0] * gate_grads[0] + gates[1] * gate_grads[1]
    logit_grad = jnp.zeros((BLK, 128), jnp.float32)
    for k in (0, 1):
        logit_grad = logit_grad + jnp.where(hots[k], gates[k] * (gate_grads[k] - inner), 0.0)
    pad_routing(prev_ref, wres_ref, prev_pad, wres_pad)
    prev_grad_ref[...] = lax.dot_general(
        wres_pad[...], logit_grad, (((1,), (1,)), ((), ())),
        precision=highest, preferred_element_type=jnp.float32,
    )[:16]
    small_sum[3] = jnp.dot(
        prev_pad[...], logit_grad, precision=highest, preferred_element_type=jnp.float32
    )[:16]
    on_normed = jnp.sum(normed_two * upstream, axis=1, keepdims=True)
    on_vectors = dot(upstream_low, small_ref[...])
    flat = logit_grad
    weight_up = gates[0] * named[0][0] + gates[1] * named[1][0]
    vector_weights = jnp.zeros((BLK, 128), jnp.float32)
    for c in (0, 1):
        scale = gates[0] * named[0][1 + c] + gates[1] * named[1][1 + c]
        mix_0, mix_1 = mixes[c]
        m_0, m_1 = scale * on_normed, scale * on_vectors[:, 16 + c : 17 + c]
        mean = mix_0 * m_0 + mix_1 * m_1
        flat = flat + jnp.where(lanes == 12 + 2 * c, mix_0 * (m_0 - mean), 0.0)
        flat = flat + jnp.where(lanes == 13 + 2 * c, mix_1 * (m_1 - mean), 0.0)
        weight_up = weight_up + mix_0 * scale
        vector_weights = vector_weights + jnp.where(lanes == 16 + c, mix_1 * scale, 0.0)
    flat_split = split(flat)
    normed_grad = dot_nt(flat_split, jnp.concatenate([small_ref[...]] * 2, axis=1))
    normed_grad = normed_grad + weight_up * upstream
    normed_grad = normed_grad + dot(tables_of[0] + tables_of[1], back_grads_ref[...])
    normed_across = normed_two.T.astype(jnp.bfloat16)
    upstream_across = upstream.T.astype(jnp.bfloat16)
    small_grad = dot(normed_across, flat_split)
    small_vector = dot(upstream_across, split(vector_weights))
    small_grad = small_grad[:, :128] + small_grad[:, 128:] + small_vector[:, :128] + small_vector[:, 128:]
    scale_two = rms_rows(state)
    weighted = normed_grad * gain_two
    state_grad = (
        upstream
        + scale_two * weighted
        - state * (scale_two**3 * jnp.mean(weighted * state, axis=-1, keepdims=True))
    )
    state_grad_ref[...] = state_grad
    gain_two_row = jnp.sum(normed_grad * state * scale_two, axis=0, keepdims=True)
    state_low = state_grad.astype(jnp.bfloat16)
    attended = att_ref[...]
    dw_low[1] = dot(attended.astype(jnp.bfloat16), state_low).astype(jnp.bfloat16)
    weights_in.wait()
    att_grad = dot_nt(state_low, w_ref[3])
    blank = jnp.zeros((HDIM, BLK), jnp.bfloat16)
    low_half = lax.broadcasted_iota(jnp.int32, (BLK, 128), 1) < HDIM
    none = jnp.zeros((BLK, 128), jnp.bfloat16)
    inner_ref[...] = jnp.zeros_like(inner_ref)
    for pair in range(PAIRS):
        part = att_grad[:, pair * 128 : pair * 128 + 128].astype(jnp.bfloat16)
        across_o = part.astype(jnp.float32).T
        products = across_o * attended[pair * 128 : pair * 128 + 128]
        across_o = across_o.astype(jnp.bfloat16)
        across_q = q_ref[pair].astype(jnp.float32).T.astype(jnp.bfloat16)
        for half in (0, 1):
            head = 2 * pair + half
            rows = slice(half * HDIM, half * HDIM + HDIM)
            inner_ref[head : head + 1] = jnp.sum(products[rows], axis=0, keepdims=True)
            order = (lambda a, b: [a, b]) if half == 0 else (lambda a, b: [b, a])
            ot_ref[head] = jnp.concatenate(order(across_o[rows], blank), axis=0)
            qt_ref[head] = jnp.concatenate(order(across_q[rows], blank), axis=0)
        o_ref[pair, :BLK] = jnp.where(low_half, part, none)
        o_ref[pair, BLK:] = jnp.where(low_half, none, part)
        qm_ref[pair, :BLK] = jnp.where(low_half, q_ref[pair], none)
        qm_ref[pair, BLK:] = jnp.where(low_half, none, q_ref[pair])
    dqt_ref[...] = jnp.zeros_like(dqt_ref)
    dw_ref[...] = jnp.zeros_like(dw_ref)
    gain_ref[...] = jnp.zeros_like(gain_ref)

    own_block.wait()

    def normed_block(array):
        wide = array[:BLK].astype(jnp.float32)
        scaled = wide * rms_rows(wide)
        return scaled, (scaled * gain_one).T.astype(jnp.bfloat16)

    def block(index, carry):
        slot = index % 2
        for copy in load_kv(index, slot):
            copy.wait()

        @pl.when(index < ctx)
        def _():
            for copy in load_kv(index + 1, 1 - slot):
                copy.start()

        mask_bias(tok_ref.at[slot], mine_ref, bias_ref, ctx, index)
        cosine, sine = turning(index, tables)
        def products(pair):
            key, value = kv_ref[slot, 0, pair], kv_ref[slot, 1, pair]
            return [
                (dot(key, qt_ref[2 * pair + half]) + bias_ref[...], dot(value, ot_ref[2 * pair + half]))
                for half in (0, 1)
            ]

        ahead = products(0)
        for pair in range(PAIRS):
            now = ahead
            if pair + 1 < PAIRS:
                ahead = products(pair + 1)
            key_across = kv_ref[slot, 0, pair].T
            weights, score_grads = [], []
            for half in (0, 1):
                head = 2 * pair + half
                scores, weight_grad = now[half]
                weight = jnp.exp(scores - lse_ref[head : head + 1])
                score_grad = (weight * (weight_grad - inner_ref[head : head + 1])).astype(jnp.bfloat16)
                weights.append(weight.astype(jnp.bfloat16))
                score_grads.append(score_grad)
                rows = slice(head * HDIM, head * HDIM + HDIM)
                dqt_ref[rows] += dot(key_across[half * HDIM : half * HDIM + HDIM], score_grad)
            lanes = slice(pair * 128, pair * 128 + 128)
            dv_ref[:, lanes] = dot(jnp.concatenate(weights, axis=1), o_ref[pair]).astype(jnp.bfloat16)
            dk = dot(jnp.concatenate(score_grads, axis=1), qm_ref[pair])
            dk_ref[:, lanes] = (dk * cosine - swapped(dk) * sine).astype(jnp.bfloat16)
        scaled, normed_across = normed_block(tok_ref.at[slot])
        dw_ref[0] += dot(normed_across, dk_ref[...])
        dw_ref[1] += dot(normed_across, dv_ref[...])
        first = dot_nt(dk_ref[...], w_ref[1]) + dot_nt(dv_ref[...], w_ref[2])
        gain_ref[...] += jnp.sum(first * scaled, axis=0, keepdims=True)

        @pl.when(index < ctx)
        def _():
            others_ref[index] = first.astype(jnp.bfloat16)

        @pl.when((index < ctx) & (index >= ctx - 2))
        def _():
            block_copy(ctx - index, index).start()

        @pl.when(index < ctx - 2)
        def _():
            far_share(index).start()

        @pl.when((index >= 1) & (index - 1 < ctx - 2))
        def _():
            far_share(index - 1).wait_recv()
            others_ref[index - 1, mine_half] = (
                others_ref[index - 1, mine_half].astype(jnp.float32)
                + far_in[index - 1].astype(jnp.float32)
            ).astype(jnp.bfloat16)
            far_copy(ctx - (index - 1), index - 1).start()

        @pl.when(index == ctx)
        def _():
            own_ref[...] = first

        for when, came, then in (
            (0, (13, 14), (5, 6)),
            (2, (3, 4), (2,)),
            (4, (7, 8, 9, 10, 5, 6), (0, 1)),
        ):

            @pl.when(index == jnp.minimum(ctx, when))
            def _(came=came, then=then):
                add_experts(came)
                send_experts(then)

        return carry

    for copy in loads:
        copy.wait()
    add_experts((11, 12))
    send_experts((3, 4))
    lax.fori_loop(0, ctx + 1, block, 0)
    cosine, sine = turning(ctx, tables)
    for pair in range(PAIRS):
        lanes = slice(pair * 128, pair * 128 + 128)
        dq = dqt_ref[lanes, :].T * (HDIM**-0.5)
        dk_ref[:, lanes] = (dq * cosine - swapped(dq) * sine).astype(jnp.bfloat16)
    scaled, normed_across = normed_block(mine_ref)
    dw_low[0] = dot(normed_across, dk_ref[...]).astype(jnp.bfloat16)
    first = dot_nt(dk_ref[...], w_ref[0])
    own_ref[...] += first
    gain_one_row = gain_ref[...] + jnp.sum(first * scaled, axis=0, keepdims=True)
    lanes = lax.broadcasted_iota(jnp.int32, (WIDTH, 128), 1)
    ones = jnp.broadcast_to(gain_one_row, (128, WIDTH)).T
    twos = jnp.broadcast_to(gain_two_row, (128, WIDTH)).T
    few = jnp.where(lanes == 18, ones, jnp.where(lanes == 19, twos, small_grad))
    few_sum[...] = few

    def share(x):
        return pltpu.make_async_remote_copy(
            src_ref=grads_ref.at[x, :, :, 1 - core],
            dst_ref=twin_in.at[x],
            send_sem=twin_send.at[x],
            recv_sem=twin_recv.at[x],
            device_id=twin,
            device_id_type=MESH,
        )

    def pack(group, carry):
        rows = pl.ds(pl.multiple_of(group * 48, 16), 48)

        def lane_half(start):
            lanes = slice(start, start + 384)
            query, output = dw_low[0, rows, lanes], dw_low[1, rows, lanes]
            key, value = (dw_ref[w, rows, lanes].astype(jnp.bfloat16) for w in (0, 1))
            return jnp.concatenate([query, key, value, output], axis=0)

        from_left = dot(left_ref[...], lane_half(0))
        from_right = dot(right_ref[...], lane_half(384))
        placed = dot(place_ref[...], few_sum[rows].astype(jnp.bfloat16))
        whole = jnp.concatenate(
            [from_left[:128], from_right[:128], from_left[128:] + from_right[128:], placed], axis=1
        )
        grads_ref[group // 4, group % 4] = whole.astype(jnp.bfloat16).reshape(4, 2, 16, 1280)
        return carry

    for x in range(4):
        lax.fori_loop(4 * x, 4 * x + 4, pack, 0)
        copy = share(x)
        copy.start()
        started.append(copy)

    def net(part, step, by, source, target):
        axis = PART_ORDER[part][2 - step]
        return pltpu.make_async_remote_copy(
            src_ref=source,
            dst_ref=target,
            send_sem=net_send.at[part, step, by - 1],
            recv_sem=net_recv.at[part, step, by - 1],
            device_id=device_at(*shifted(spot, axis, by), core),
            device_id_type=MESH,
        )

    def small(axis, by, source, slot):
        device = twin if axis == 3 else device_at(*shifted(spot, axis, by), core)
        return pltpu.make_async_remote_copy(
            src_ref=source,
            dst_ref=small_in.at[axis, slot],
            send_sem=small_send.at[axis, by - 1],
            recv_sem=small_recv.at[axis, by - 1],
            device_id=device,
            device_id_type=MESH,
        )

    copy = small(3, 1, small_sum.at[3], core)
    copy.start()
    started.append(copy)

    for x in range(4):
        share(x).wait_recv()

        def add_pair(index, carry, x=x):
            z, y = index // 4, index % 4
            grads_ref[x, z, y, core] = (
                grads_ref[x, z, y, core].astype(jnp.float32) + twin_in[x, z, y].astype(jnp.float32)
            ).astype(jnp.bfloat16)
            return carry

        lax.fori_loop(0, 16, add_pair, 0, unroll=2)

    def lanes_of(part):
        return pl.ds(PART_START[part], PART_LANES[part])

    for part in range(3):
        axis = PART_ORDER[part][2]
        for by in (1, 2, 3):
            at = shifted(spot, axis, by)[axis]
            index = tuple(at if a == axis else slice(None) for a in range(3))
            copy = net(
                part, 0, by, grads_ref.at[(*index, core, slice(None), lanes_of(part))], in_one[part].at[by - 1]
            )
            copy.start()
            started.append(copy)

    small(3, 1, small_sum.at[3], 1 - core).wait_recv()
    small_in[3, core] = small_sum[3]
    small_sum[0] = small_in[3, 0] + small_in[3, 1]
    for by in (1, 2, 3):
        copy = small(0, by, small_sum.at[0], spot[0])
        copy.start()
        started.append(copy)

    def small_step(axis):
        for by in (1, 2, 3):
            small(axis, by, small_sum.at[axis], shifted(spot, axis, -by)[axis]).wait_recv()
        small_in[axis, spot[axis]] = small_sum[axis]
        total = small_in[axis, 0] + small_in[axis, 1] + small_in[axis, 2] + small_in[axis, 3]
        if axis == 2:
            total_ref[...] = total
            return
        small_sum[axis + 1] = total
        for by in (1, 2, 3):
            copy = small(axis + 1, by, small_sum.at[axis + 1], spot[axis + 1])
            copy.start()
            started.append(copy)

    for part in range(3):
        first, second, third = PART_ORDER[part]
        for by in (1, 2, 3):
            net(part, 0, by, in_one[part].at[by - 1], in_one[part].at[by - 1]).wait_recv()
        rest = tuple(a for a in (0, 1, 2) if a != third)
        lanes = slice(PART_START[part], PART_START[part] + PART_LANES[part])

        def add_four(index, carry, part=part, third=third, rest=rest, lanes=lanes):
            at = {rest[0]: index // 4, rest[1]: index % 4, third: spot[third]}
            total = grads_ref[at[0], at[1], at[2], core, :, lanes].astype(jnp.float32)
            for by in range(3):
                total = total + in_one[part][by, index // 4, index % 4].astype(jnp.float32)
            sum_one[part][index // 4, index % 4] = total.astype(jnp.bfloat16)
            return carry

        lax.fori_loop(0, 16, add_four, 0, unroll=2)
        for by in (1, 2, 3):
            at = shifted(spot, second, by)[second]
            source = sum_one[part].at[at] if second == rest[0] else sum_one[part].at[:, at]
            copy = net(part, 1, by, source, in_two[part].at[by - 1])
            copy.start()
            started.append(copy)
    small_step(0)

    for number in (0, 1, 2):
        expert(number).wait_recv()
    count = PAY_CUTS[-1]

    def total_rows(start):
        rows = pl.ds(pl.multiple_of(start, 16), 16)
        total = pay_ref[ctx, rows].astype(jnp.float32)
        for number in range(3):
            there = pl.ds(pl.multiple_of(number * count + start, 16), 16)
            total = total + pay_in[there].astype(jnp.float32)
        return total

    def gate_rows(index, carry):
        rows = pl.ds(pl.multiple_of(index * 16, 16), 16)
        gate_out[rows] = total_rows(index * 16)
        up_out[rows] = total_rows(96 + index * 16)
        return carry

    lax.fori_loop(0, 6, gate_rows, 0)
    for index in range(6):
        total = total_rows(192 + 16 * index)
        down_out[16 * index : 16 * index + 16] = total[:, :WIDTH]
        start = 96 + 16 * (index % 2)
        lanes = slice(256 * (index // 2), 256 * (index // 2) + 256)
        down_out[start : start + 16, lanes] = total[:, WIDTH:]

    for part in range(3):
        first, second, third = PART_ORDER[part]
        for by in (1, 2, 3):
            net(part, 1, by, in_two[part].at[by - 1], in_two[part].at[by - 1]).wait_recv()
        rest = tuple(a for a in (0, 1, 2) if a != third)
        for index in range(4):
            if second == rest[0]:
                total = sum_one[part][spot[second], index].astype(jnp.float32)
            else:
                total = sum_one[part][index, spot[second]].astype(jnp.float32)
            for by in range(3):
                total = total + in_two[part][by, index].astype(jnp.float32)
            sum_two[part][index] = total.astype(jnp.bfloat16)
        for by in (1, 2, 3):
            at = shifted(spot, first, by)[first]
            copy = net(part, 2, by, sum_two[part].at[at], in_three[part].at[by - 1])
            copy.start()
            started.append(copy)
    small_step(1)

    for by in (1, 2):

        @pl.when(ctx + by < 8)
        def _(by=by):
            block_copy(by, ctx).wait_recv()
            own_ref[...] += block_in[by - 1].astype(jnp.float32)

        @pl.when(ctx - by >= 0)
        def _(by=by):
            block_copy(by, ctx - by).wait_send()

    far_sum[...] = jnp.zeros_like(far_sum)
    for by in range(3, 8):

        @pl.when(ctx + by < 8)
        def _(by=by):
            far_copy(by, ctx).wait_recv()
            far_sum[...] += far_land[by - 3].astype(jnp.float32)

        @pl.when(ctx - by >= 0)
        def _(by=by):
            far_copy(by, ctx - by).wait_send()
            far_share(ctx - by).wait_send()

    far_out[...] = far_sum[...].astype(jnp.bfloat16)
    far_halves().start()
    end_mark.wait()
    single = mark_ref[...].astype(jnp.float32)[0:1, BLK - 1 : BLK] == 0.0
    far_halves().wait_recv()
    own_ref[mine_half] += jnp.where(single, far_sum[...], 0.0)
    own_ref[twin_half] += jnp.where(single, far_back[...].astype(jnp.float32), 0.0)
    far_halves().wait_send()

    wide = mine_ref[:BLK].astype(jnp.float32)
    scale = rms_rows(wide)
    weighted = own_ref[...] * gain_one
    tokens_grad_ref[...] = (
        state_grad_ref[...]
        + scale * weighted
        - wide * (scale**3 * jnp.mean(weighted * wide, axis=-1, keepdims=True))
    )
    finals = []
    for part in range(3):
        first = PART_ORDER[part][0]
        for by in (1, 2, 3):
            net(part, 2, by, in_three[part].at[by - 1], in_three[part].at[by - 1]).wait_recv()
        total = sum_two[part][spot[first]].astype(jnp.float32)
        for by in range(3):
            total = total + in_three[part][by].astype(jnp.float32)
        finals.append(total)
    final = jnp.concatenate(finals, axis=1)
    sums_ref[:16] = final[:, :768]
    sums_ref[16:] = jnp.concatenate([final[:8, 768:1152], final[8:, 768:1152]], axis=1)
    few_ref[...] = final[:8, 1152:]
    small_step(2)
    for number in range(len(MESSAGES)):
        expert(number).wait_send()
    for copy in started:
        copy.wait_send()


def run_back(blocks, weights, smalls, prev, wres, routes, cot, kept, back_rows, back_grads, d_pay):
    vmem, anywhere = pl.BlockSpec(memory_space=pltpu.VMEM), pl.BlockSpec(memory_space=pl.ANY)
    shape = jax.ShapeDtypeStruct
    low, wide = jnp.bfloat16, jnp.float32
    dma = pltpu.SemaphoreType.DMA
    left, right, small = (jnp.asarray(t.T, low) for t in placing_tables())
    by_part = lambda *lead: [pltpu.VMEM((*lead, 16, lanes), low) for lanes in PART_LANES]
    return pl.pallas_call(
        back_kernel,
        out_shape=[
            shape((BLK, WIDTH), low),
            shape((16, BLK), wide),
            shape((16, 128), wide),
            shape((BLK, WIDTH), wide),
            shape((24, WIDTH), wide),
            shape((8, 128), wide),
            shape((96, 1024), wide),
            shape((96, 1024), wide),
            shape((128, WIDTH), wide),
        ],
        in_specs=[anywhere] * 2 + [vmem] * 17 + [anywhere] * 2 + [vmem] * 4 + [anywhere],
        out_specs=[vmem] * 9,
        scratch_shapes=[
            pltpu.VMEM((HEADS, 128, BLK), low),
            pltpu.VMEM((HEADS, 128, BLK), low),
            pltpu.VMEM((PAIRS, 2 * BLK, 128), low),
            pltpu.VMEM((PAIRS, 2 * BLK, 128), low),
            pltpu.VMEM((BLK, BLK), wide),
            pltpu.VMEM((16, BLK), wide),
            pltpu.VMEM((WIDTH, BLK), wide),
            pltpu.VMEM((1, WIDTH), wide),
            pltpu.VMEM((BLK, WIDTH), low),
            pltpu.VMEM((BLK, WIDTH), low),
            pltpu.VMEM((128, BLK), wide),
            pltpu.VMEM((128, 128), wide),
            pltpu.VMEM((2, WIDTH, WIDTH), wide),
            pltpu.VMEM((2, WIDTH, WIDTH), low),
            pltpu.VMEM((WIDTH, 128), wide),
            pltpu.VMEM((2, 2, PAIRS, BLK, 128), low),
            pltpu.VMEM((2, BLK + 16, WIDTH), low),
            pltpu.VMEM((BLK + 16, WIDTH), low),
            dma((2, 3)),
            pltpu.VMEM((BLK, WIDTH), wide),
            pltpu.VMEM((BLK, WIDTH), wide),
            pltpu.VMEM((7, BLK, WIDTH), low),
            pltpu.VMEM((4, 4, 4, 2, 16, 1280), low),
            pltpu.VMEM((2, BLK, WIDTH), low),
            pltpu.VMEM((5, 128, WIDTH), low),
            pltpu.VMEM((5, 128, WIDTH), low),
            pltpu.VMEM((128, WIDTH), wide),
            pltpu.VMEM((128, WIDTH), low),
            pltpu.VMEM((128, WIDTH), low),
            pltpu.VMEM((16, WIDTH), low),
            dma((6,)),
            dma((6,)),
            pltpu.VMEM((4, WIDTH, WIDTH), low),
            pltpu.VMEM((8, 288, 1024), low),
            pltpu.VMEM((2016, 1024), low),
            pltpu.VMEM((4, 4, 16, 128), wide),
            pltpu.VMEM((4, 16, 128), wide),
            dma((7,)),
            dma((7,)),
            dma((15,)),
            dma((15,)),
            dma((11,)),
            dma((3, 3, 3)),
            dma((3, 3, 3)),
            dma((4,)),
            dma((4,)),
            dma((4, 3)),
            dma((4, 3)),
            pltpu.VMEM((4, 4, 4, 16, 1280), low),
            *by_part(3, 4, 4),
            *by_part(3, 4),
            *by_part(3),
            *by_part(4, 4),
            *by_part(4),
        ],
        name="back",
        compiler_params=pltpu.CompilerParams(
            collective_id=2, has_side_effects=True, vmem_limit_bytes=62 * 2**20
        ),
    )(
        blocks, weights, smalls, *rope_tables(), left, right, small, prev, wres, routes, cot,
        *kept, back_rows, back_grads, d_pay,
    )


def finish_kernel(
    out_in, tokens_in, gate_in, up_in, down_in, prev_in, total_in, sums_in, few_in,
    out, tokens_grad, gate, up, down, prev, total, sum_q, sum_k, sum_v, sum_o,
    gain_one, gain_two, router, constant, vectors, prev_at, total_at, sums_at, few_at, sems,
):
    pairs = (
        (prev_in, prev_at), (total_in, total_at), (sums_in, sums_at), (few_in, few_at),
        (tokens_in, tokens_grad), (out_in, out), (gate_in, gate), (up_in, up), (down_in, down),
    )
    copies = [
        pltpu.make_async_copy(source, target, sems.at[index])
        for index, (source, target) in enumerate(pairs)
    ]
    for copy in copies:
        copy.start()
    for copy in copies[:4]:
        copy.wait()
    prev[:, 0, :] = prev_at[:NALL]
    total[...] = total_at[:NALL, :NALL]
    for weight, ref in enumerate((sum_q, sum_k, sum_v, sum_o)):
        ref[...] = sums_at[weight * 6 : weight * 6 + 6]
    few = few_at[...]
    router[...] = few[:6, :NALL]
    tall = jnp.concatenate([few, jnp.zeros((120, 128), jnp.float32)], axis=0).T
    constant[...] = tall[12:16, :6]
    vectors[...] = tall[16:18, :6]
    gain_one[...] = tall[18:19, :6]
    gain_two[...] = tall[19:20, :6]
    for copy in copies[4:]:
        copy.wait()


def finish(out, tokens_grad, gate, up, down, prev, total, sums, few):
    vmem = pl.BlockSpec(memory_space=pltpu.VMEM)
    shape = jax.ShapeDtypeStruct
    wide = jnp.float32
    like = [shape(a.shape, a.dtype) for a in (out, tokens_grad, gate, up, down)]
    few_shapes = [(1, 6), (1, 6), (6, NALL), (4, 6), (2, 6)]
    return pl.pallas_call(
        finish_kernel,
        out_shape=like
        + [shape((NALL, 1, BLK), wide), shape((NALL, NALL), wide)]
        + [shape((6, WIDTH), wide)] * 4
        + [shape(s, wide) for s in few_shapes],
        in_specs=[pl.BlockSpec(memory_space=pl.ANY)] * 9,
        out_specs=[vmem] * 16,
        scratch_shapes=[
            *(pltpu.VMEM(a.shape, a.dtype) for a in (prev, total, sums, few)),
            pltpu.SemaphoreType.DMA((9,)),
        ],
        name="finish",
        compiler_params=pltpu.CompilerParams(vmem_limit_bytes=62 * 2**20),
    )(out, tokens_grad, gate, up, down, prev, total, sums, few)


def on_device(
    tokens, prev_logits, routes, segments, rank_order, norm_first, w_query, w_key, w_value, w_output,
    norm_second, w_router, w_residual, w_constant, v_constant, w_gate, w_up, w_down, cotangent,
):
    few = [w_router, w_constant.T, v_constant.T, norm_first[None], norm_second[None]]
    prev = jnp.transpose(prev_logits, (2, 0, 1))
    (
        state, normed, att, lse, q, keys, values, info, proj, blocks, weights, smalls, _,
        back_rows, back_grads, d_pay,
    ) = run_forward(
        [w_query, w_key, w_value, w_output], few, tokens[0], segments, (w_gate[0], w_up[0], w_down[0]),
        prev, w_residual, routes[0].T, rank_order[0], cotangent[0],
    )
    (
        out, prev_grad, residual, tokens_grad, sums, small, d_gate, d_up, d_down,
    ) = run_back(
        blocks, weights, smalls, prev, w_residual, routes[0].T, cotangent[0],
        (state, normed, att, lse, q, keys, values, info, proj), back_rows, back_grads, d_pay,
    )
    (
        out, tokens_grad, d_gate, d_up, d_down, prev_grad, residual, sum_q, sum_k, sum_v, sum_o,
        gain_one, gain_two, router, constant, vectors,
    ) = finish(out, tokens_grad, d_gate, d_up, d_down, prev_grad, residual, sums, small)
    return (
        out[None],
        tokens_grad[None],
        jnp.transpose(prev_grad, (1, 2, 0)),
        gain_one[0],
        sum_q,
        sum_k,
        sum_v,
        sum_o,
        gain_two[0],
        router,
        residual,
        constant.T,
        vectors.T,
        d_gate[None],
        d_up[None],
        d_down[None],
    )


def solution(mesh):
    in_specs = (
        P("fsdp", "ctx", None),
        P("fsdp", "ctx", None),
        P("fsdp", "ctx", None),
        P("fsdp", "ctx"),
        P("fsdp", "ctx", None),
        P(("ctx", "fsdp")),
        P(("ctx", "fsdp"), None),
        P(("ctx", "fsdp"), None),
        P(("ctx", "fsdp"), None),
        P(("ctx", "fsdp"), None),
        P(("ctx", "fsdp")),
        P(("ctx", "fsdp"), None),
        P(),
        P(("ctx", "fsdp"), None),
        P(("ctx", "fsdp"), None),
        P("fsdp", "ctx", None),
        P("fsdp", "ctx", None),
        P("fsdp", "ctx", None),
        P("fsdp", "ctx", None),
    )
    out_specs = (
        P("fsdp", "ctx", None),
        P("fsdp", "ctx", None),
        P("fsdp", "ctx", None),
        P(("ctx", "fsdp")),
        P(("ctx", "fsdp"), None),
        P(("ctx", "fsdp"), None),
        P(("ctx", "fsdp"), None),
        P(("ctx", "fsdp"), None),
        P(("ctx", "fsdp")),
        P(("ctx", "fsdp"), None),
        P(),
        P(("ctx", "fsdp"), None),
        P(("ctx", "fsdp"), None),
        P("fsdp", "ctx", None),
        P("fsdp", "ctx", None),
        P("fsdp", "ctx", None),
    )
    return jax.shard_map(
        on_device, mesh=mesh, in_specs=in_specs, out_specs=out_specs, check_vma=False
    )
```

```python
import functools

import jax
import jax.numpy as jnp
import numpy as np
from jax import lax
from jax.experimental import pallas as pl
from jax.experimental.pallas import tpu as pltpu
from jax.sharding import PartitionSpec as P

HEADS = 12
HDIM = 64
EXPERTS = 8
NALL = 12
CAP = 54
WIDTH = HEADS * HDIM
PAIRS = HEADS // 2
BLK = 256
SLOTS = 64

highest = lax.Precision.HIGHEST
masked_score = -1e30
epsilon = 1e-06

MESH = pl.DeviceIdType.MESH
PART_LANES = (512, 384, 384)
PART_START = (0, 512, 896)
PART_ORDER = ((0, 1, 2), (1, 2, 0), (2, 0, 1))

BLOCK_CUTS = (0, 64, 144, 224, 272)
PAY_CUTS = (0, 64, 144, 224, 288)
GRAD_CUTS = (0, 64, 144, 224, 288)
SPANS = {"all": (0, 4), "p": (1, 3), "h1": (0, 2), "h2": (2, 4), "q1": (0, 1), "p1": (1, 2), "p2": (2, 3), "q2": (3, 4)}
MESSAGES = (
    (1, (0, 0), "all"), (-1, (0, 0), "all"), (0, (0, 0), "all"),
    (1, (0, 1), "p"), (-1, (0, 1), "p"),
    (1, (-1, 0), "h1"), (-1, (1, 0), "h2"),
    (0, (-1, 0), "q1"), (0, (-1, 0), "q2"), (0, (1, 0), "q1"), (0, (1, 0), "q2"),
    (1, (-1, 1), "p1"), (-1, (1, 1), "p2"),
    (0, (2, 0), "q1"), (0, (2, 0), "q2"),
)


def place():
    ctx = lax.axis_index("ctx")
    fsdp = lax.axis_index("fsdp")
    return ctx // 2, (ctx % 2) * 2 + fsdp // 8, (fsdp // 2) % 4, fsdp % 2


def device_at(x, z, y, core):
    return {"ctx": x * 2 + z // 2, "fsdp": (z % 2) * 8 + y * 2 + core}


def shifted(spot, axis, by):
    moved = list(spot)
    moved[axis] = (moved[axis] + by) % 4
    return tuple(moved)


def greet(devices):
    barrier = pltpu.get_barrier_semaphore()
    for device in devices:
        pl.semaphore_signal(barrier, inc=1, device_id=device, device_id_type=MESH)
    pl.semaphore_wait(barrier, len(devices))


def torus_peers(spot, core):
    peers = [device_at(*shifted(spot, axis, by), core) for axis in range(3) for by in (1, 2, 3)]
    return peers + [device_at(*spot, 1 - core)]


def sequence_peers(spot, core):
    x, z, y = spot
    return [device_at((x + by) % 4, (z + 2) % 4, y, core) for by in (1, 2, 3)]


def region(ref, spot, core, whole):
    return ref.at[
        tuple(slice(None) if axis in whole else spot[axis] for axis in range(3)) + (core,)
    ]


def placing_tables():
    left = np.zeros((192, 256), np.float32)
    right = np.zeros((192, 256), np.float32)
    small = np.zeros((48, 128), np.float32)
    for device in range(8):
        for weight in range(4):
            for row in range(6):
                at, line = weight * 48 + device * 6 + row, weight * 6 + row
                if line < 16:
                    left[at, device * 16 + line] = right[at, device * 16 + line] = 1
                else:
                    left[at, 128 + device * 16 + line - 16] = 1
                    right[at, 128 + device * 16 + line - 8] = 1
        for row in range(6):
            small[device * 6 + row, device * 16 + row] = 1
    return left, right, small


def rope_tables():
    frequency = 10000.0 ** (-2.0 * (np.arange(128) % 32) / HDIM)
    inner = np.arange(BLK)[:, None] * frequency
    outer = (np.arange(8) * BLK)[:, None] * frequency
    return [jnp.asarray(t, jnp.float32) for t in (np.cos(inner), np.sin(inner), np.cos(outer), np.sin(outer))]


def turning(index, tables):
    cos_in, sin_in, cos_out, sin_out = tables
    ca, sa = cos_out[pl.ds(index, 1), :], sin_out[pl.ds(index, 1), :]
    cb, sb = cos_in[...], sin_in[...]
    lower = lax.broadcasted_iota(jnp.int32, (BLK, 128), 1) % HDIM < HDIM // 2
    sine = sa * cb + ca * sb
    return ca * cb - sa * sb, jnp.where(lower, -sine, sine)


def swapped(values):
    lower = lax.broadcasted_iota(jnp.int32, values.shape, 1) % HDIM < HDIM // 2
    return jnp.where(lower, pltpu.roll(values, 96, 1), pltpu.roll(values, 32, 1))


def dot(left, right):
    return jnp.dot(left, right, preferred_element_type=jnp.float32)


def dot_nt(left, right):
    return lax.dot_general(left, right, (((1,), (1,)), ((), ())), preferred_element_type=jnp.float32)


def column(row):
    return jnp.broadcast_to(row, (128, row.shape[1])).T[:, 0:1]


def mask_bias(key_block, query_block, bias_ref, ctx, index):
    key_seg = column(key_block[BLK:, :BLK].astype(jnp.float32)[:1])
    query_seg = query_block[BLK:, :BLK].astype(jnp.float32)[:1]
    key_pos = lax.broadcasted_iota(jnp.int32, (BLK, BLK), 0)
    query_pos = lax.broadcasted_iota(jnp.int32, (BLK, BLK), 1)
    reach = jnp.where(index == ctx, 0, BLK)
    allowed = (key_seg == query_seg) & (key_pos <= query_pos + reach)
    bias_ref[...] = jnp.where(allowed, 0.0, masked_score)


def rms_rows(values):
    return lax.rsqrt(jnp.mean(values * values, axis=-1, keepdims=True) + epsilon)


def pick(onehot, values):
    return jnp.sum(jnp.where(onehot, values, 0.0), axis=1, keepdims=True)


def lane_is(lanes):
    return lax.broadcasted_iota(jnp.int32, (BLK, 128), 1) == lanes


def dot_tn(left, right):
    return lax.dot_general(left, right, (((0,), (0,)), ((), ())), preferred_element_type=jnp.float32)


def row_tile(values):
    *weights, small = values
    rows = jnp.concatenate([w.astype(jnp.float32) for w in weights], axis=0)
    tail = jnp.concatenate([rows[16:, :384], rows[16:, 384:]], axis=0)
    return jnp.concatenate([rows[:16], tail, small], axis=1).astype(jnp.bfloat16)


def forward_kernel(
    wq_ref, wk_ref, wv_ref, wo_ref, router_ref, constant_ref, vector_ref, gain_one_ref, gain_two_ref,
    tokens_ref, segments_in, gate_in, up_in, down_in,
    left_ref, right_ref, place_ref, cos_in, sin_in, cos_out, sin_out,
    prev_ref, wres_ref, routes_ref, rank_ref, cot_ref,
    state_out, normed_out, att_out, lse_ref, q_out, keys_ref, values_ref,
    info_ref, proj_ref, blocks_out, w_out, small_ref, pay_ref,
    back_rows_ref, back_grads_ref, d_pay_out,
    part_a, part_b, part_c, own_ref, qt_ref, vt_ref, bias_ref, max_ref, sum_ref, acc_ref,
    prev_pad, wres_pad, few_wide, few_tall, kv_ref, rows_ref, grads_ref, blocks_ref, w_ref,
    state_ref, normed_ref, att_ref, q_ref, d_pay_ref,
    gate_w, up_w, down_w, x_ref, g_ref, gate_ref, up_ref, hidden_ref, d_gate, d_up,
    mine_ref, twin_out, twin_in,
    net_send, net_recv, twin_send, twin_recv, own_sem, ring_send, ring_recv, kv_sem,
    load_sem, send_sem, recv_sem, share_send, share_recv, half_send, half_recv, ret_send, ret_recv,
    keep_sem,
):
    parts = (part_a, part_b, part_c)
    tables = (cos_in, sin_in, cos_out, sin_out)
    ctx, fsdp = lax.axis_index("ctx"), lax.axis_index("fsdp")
    along, side = ctx // 2, ctx % 2
    *spot, core = place()
    spot = tuple(spot)
    twin = device_at(*spot, 1 - core)
    few_wide[...] = jnp.zeros_like(few_wide)
    few_wide[12:16, :6] = constant_ref[...].astype(jnp.float32)
    few_wide[16:18, :6] = vector_ref[...].astype(jnp.float32)
    few_wide[18:19, :6] = gain_one_ref[...].astype(jnp.float32)
    few_wide[19:20, :6] = gain_two_ref[...].astype(jnp.float32)
    few_tall[...] = few_wide[...].T[:16]
    few_tall[:6, :NALL] = router_ref[...].astype(jnp.float32)
    own_ref[...] = row_tile([wq_ref[...], wk_ref[...], wv_ref[...], wo_ref[...], few_tall[...]])
    marks = jnp.concatenate(
        [segments_in[...].astype(jnp.float32), jnp.zeros((1, WIDTH - BLK), jnp.float32)], axis=1
    )
    blocks_ref[ctx, :BLK] = tokens_ref[...]
    blocks_ref[ctx, BLK:] = jnp.broadcast_to(marks, (16, WIDTH)).astype(jnp.bfloat16)
    chip = fsdp // 2

    def at_expert(where, on):
        return {"ctx": ctx, "fsdp": where * 2 + on}

    greet(
        torus_peers(spot, core)
        + [at_expert((chip + by) % EXPERTS, core) for by in range(1, EXPERTS)]
    )

    def net(part, step, by, source, target):
        axis = PART_ORDER[part][step]
        return pltpu.make_async_remote_copy(
            src_ref=source,
            dst_ref=target,
            send_sem=net_send.at[part, step, by - 1],
            recv_sem=net_recv.at[part, step, by - 1],
            device_id=device_at(*shifted(spot, axis, by), core),
            device_id_type=MESH,
        )

    def share(part, slot, source, target):
        return pltpu.make_async_remote_copy(
            src_ref=source,
            dst_ref=target,
            send_sem=twin_send.at[part, slot],
            recv_sem=twin_recv.at[part, slot],
            device_id=twin,
            device_id_type=MESH,
        )

    payloads = ((blocks_ref, BLOCK_CUTS), (pay_ref, PAY_CUTS))

    def ring(kind, number, arriving=False):
        to, (steps, across_it), rows = MESSAGES[number]
        if arriving:
            steps = steps - to
            across_it = across_it if to else 1 - across_it
        array, cuts = payloads[kind]
        first, last = (cuts[i] for i in SPANS[rows])
        on = side if across_it == 0 else 1 - side
        view = array.at[((along + steps + 4) % 4) * 2 + on, pl.ds(first, last - first)]
        target = ((along + to + 4) % 4) * 2 + (side if to else 1 - side)
        return pltpu.make_async_remote_copy(
            src_ref=view,
            dst_ref=view,
            send_sem=ring_send.at[kind, number],
            recv_sem=ring_recv.at[kind, number],
            device_id={"ctx": target, "fsdp": fsdp},
            device_id_type=MESH,
        )

    def pass_on(kind, stage):
        plan = (
            ((None, (0, 1, 2)),),
            ((2, (3, 4)),),
            ((0, (5, 7, 8)), (1, (6, 9, 10))),
            ((3, (11,)), (4, (12,)), (5, (13,)), (6, (14,))),
            tuple((number, ()) for number in range(7, 15)),
        )[stage]
        for number, then in plan:
            if number is not None:
                ring(kind, number, arriving=True).wait_recv()
            for follow in then:
                ring(kind, follow).start()

    started = []
    kept = []
    for part in range(3):
        own = own_ref.at[:, pl.ds(PART_START[part], PART_LANES[part])]
        mine = region(parts[part], spot, core, ())
        for by in (1, 2, 3):
            copy = net(part, 0, by, own, mine)
            copy.start()
            started.append(copy)
    for part in range(3):
        own = own_ref.at[:, pl.ds(PART_START[part], PART_LANES[part])]
        mine = region(parts[part], spot, core, ())
        copy = pltpu.make_async_copy(own, mine, own_sem.at[part])
        copy.start()
        kept.append(copy)
        copy = share(part, 0, own, mine)
        copy.start()
        started.append(copy)
    tail = [(down_in.at[:96], pay_ref.at[ctx, 192:, pl.ds(0, WIDTH)])] + [
        (down_in.at[96:, pl.ds(256 * m, 256)], pay_ref.at[ctx, pl.ds(192 + 32 * m, 32), pl.ds(WIDTH, 256)])
        for m in range(3)
    ]
    pieces = [(gate_in, pay_ref.at[ctx, :96]), (up_in, pay_ref.at[ctx, 96:192]), *tail]
    own_experts = [
        pltpu.make_async_copy(source, target, own_sem.at[3 + number])
        for number, (source, target) in enumerate(pieces)
    ]
    for copy in own_experts:
        copy.start()
    for copy in kept + own_experts:
        copy.wait()
    for step in range(3):
        for part in range(3):
            order = PART_ORDER[part]
            axis = order[step]
            whole = order[:step]
            for by in (1, 2, 3):
                here = region(parts[part], shifted(spot, axis, -by), core, whole)
                net(part, step, by, here, here).wait_recv()
                copy = share(part, 1 + step * 3 + by - 1, here, here)
                copy.start()
                started.append(copy)
            if step < 2:
                held = region(parts[part], spot, core, order[: step + 1])
                for by in (1, 2, 3):
                    copy = net(part, step + 1, by, held, held)
                    copy.start()
                    started.append(copy)
        if step == 1:
            pass_on(0, 0)
    for part in range(3):
        order = PART_ORDER[part]
        first = region(parts[part], spot, 1 - core, ())
        share(part, 0, first, first).wait_recv()
        for step in range(3):
            for by in (1, 2, 3):
                here = region(
                    parts[part], shifted(spot, order[step], -by), 1 - core, order[:step]
                )
                share(part, 1 + step * 3 + by - 1, here, here).wait_recv()

    def unpack(group, carry):
        a, b, c = (
            part[group // 4, group % 4].reshape(128, lanes)
            for part, lanes in zip(parts, PART_LANES, strict=True)
        )
        tail = jnp.concatenate([b[:, 256:], c[:, :256]], axis=1)
        left = dot(left_ref[...], jnp.concatenate([a[:, :384], tail], axis=0))
        right_rows = jnp.concatenate([a[:, 384:], b[:, :256]], axis=1)
        right = dot(right_ref[...], jnp.concatenate([right_rows, tail], axis=0))
        rows = pl.ds(pl.multiple_of(group * 48, 16), 48)
        for weight in range(4):
            w_ref[weight, rows, :384] = left[weight * 48 : weight * 48 + 48].astype(jnp.bfloat16)
            w_ref[weight, rows, 384:] = right[weight * 48 : weight * 48 + 48].astype(jnp.bfloat16)
        small_ref[rows] = dot(place_ref[...], c[:, 256:]).astype(jnp.bfloat16)
        return carry

    pass_on(0, 1)
    lax.fori_loop(0, 16, unpack, 0)
    pass_on(0, 2)
    weights_kept = pltpu.make_async_copy(w_ref, w_out, own_sem.at[9])
    weights_kept.start()
    across = small_ref[...].astype(jnp.float32).T
    gain_one, gain_two = across[18:19], across[19:20]

    def normed_block(index):
        wide = blocks_ref[index, :BLK].astype(jnp.float32)
        return (wide * rms_rows(wide) * gain_one).astype(jnp.bfloat16)

    query = dot(normed_block(ctx), w_ref[0])
    cosine, sine = turning(ctx, tables)
    for pair in range(PAIRS):
        part = query[:, pair * 128 : pair * 128 + 128]
        turned = (part * cosine + swapped(part) * sine) * (HDIM**-0.5)
        q_ref[pair] = turned.astype(jnp.bfloat16)
        across_q = turned.T.astype(jnp.bfloat16)
        blank = jnp.zeros((HDIM, BLK), jnp.bfloat16)
        qt_ref[2 * pair] = jnp.concatenate([across_q[:HDIM], blank], axis=0)
        qt_ref[2 * pair + 1] = jnp.concatenate([blank, across_q[HDIM:]], axis=0)
    max_ref[...] = jnp.full(max_ref.shape, masked_score, jnp.float32)
    sum_ref[...] = jnp.zeros_like(sum_ref)
    acc_ref[...] = jnp.zeros_like(acc_ref)

    def keep_block(index, slot):
        return [
            pltpu.make_async_copy(kv_ref.at[slot, kind], target.at[index], kv_sem.at[slot, kind])
            for kind, target in enumerate((keys_ref, values_ref))
        ]

    def block_at(step):
        odd = step % 2
        x = along - (step + odd) // 2 + odd * side
        return jnp.where(step == 0, ctx, x * 2 + 1 - odd)

    def block(step, carry):
        index = block_at(step)
        slot = step % 2

        @pl.when(step >= 2)
        def _():
            for copy in keep_block(block_at(step - 2), slot):
                copy.wait()

        normed = normed_block(index)
        key = dot(normed, w_ref[1])
        value = dot(normed, w_ref[2])
        cosine, sine = turning(index, tables)
        for pair in range(PAIRS):
            lanes = slice(pair * 128, pair * 128 + 128)
            part = key[:, lanes]
            kv_ref[slot, 0, pair] = (part * cosine + swapped(part) * sine).astype(jnp.bfloat16)
            kv_ref[slot, 1, pair] = value[:, lanes].astype(jnp.bfloat16)
            vt_ref[lanes, :] = value[:, lanes].T.astype(jnp.bfloat16)
        mask_bias(blocks_ref.at[index], blocks_ref.at[ctx], bias_ref, ctx, index)
        def score(head):
            return dot(kv_ref[slot, 0, head // 2], qt_ref[head]) + bias_ref[...]

        def soften(head, scores):
            before = max_ref[head : head + 1]
            top = jnp.maximum(before, jnp.max(scores, axis=0, keepdims=True))
            weights = jnp.exp(scores - top)
            shrink = jnp.exp(before - top)
            sum_ref[head : head + 1] = sum_ref[head : head + 1] * shrink + jnp.sum(
                weights, axis=0, keepdims=True
            )
            max_ref[head : head + 1] = top
            return shrink, weights.astype(jnp.bfloat16)

        def gather(head, shrink, weights):
            rows = slice(head * HDIM, head * HDIM + HDIM)
            acc_ref[rows] = acc_ref[rows] * shrink + dot(vt_ref[rows, :], weights)

        ahead = [score(0), score(1)]
        done = None
        for head in range(0, HEADS, 2):
            now = ahead
            if head + 2 < HEADS:
                ahead = [score(head + 2), score(head + 3)]
            if done is not None:
                gather(head - 2, *done[0])
                gather(head - 1, *done[1])
            done = [soften(head, now[0]), soften(head + 1, now[1])]
        gather(HEADS - 2, *done[0])
        gather(HEADS - 1, *done[1])

        for copy in keep_block(index, slot):
            copy.start()
        for when, todo in (
            (0, ((0, 3), (1, 0))),
            (1, ((0, 4),)),
            (5, ((1, 1), (1, 2))),
            (7, ((1, 3),)),
        ):

            @pl.when(step == jnp.minimum(ctx, when))
            def _(todo=todo):
                for kind, stage in todo:
                    pass_on(kind, stage)

        return carry

    lax.fori_loop(0, ctx + 1, block, 0)
    blocks_kept = pltpu.make_async_copy(blocks_ref, blocks_out, own_sem.at[10])
    blocks_kept.start()
    for head in range(HEADS):
        rows = slice(head * HDIM, head * HDIM + HDIM)
        att_ref[rows] = acc_ref[rows] / sum_ref[head : head + 1]
    lse_ref[...] = max_ref[...] + jnp.log(jnp.maximum(sum_ref[...], 1e-30))
    attended = att_ref[...].T.astype(jnp.bfloat16)
    state = blocks_ref[ctx, :BLK].astype(jnp.float32) + dot(attended, w_ref[3])
    state_ref[...] = state
    normed_two = (state * rms_rows(state) * gain_two).astype(jnp.bfloat16)
    normed_ref[...] = normed_two

    proj = dot(normed_two, small_ref[...])
    proj_ref[...] = proj
    pad_routing(prev_ref, wres_ref, prev_pad, wres_pad)
    logits = proj + jnp.dot(
        prev_pad[...].T, wres_pad[...], precision=highest, preferred_element_type=jnp.float32
    )
    lanes = lax.broadcasted_iota(jnp.int32, (BLK, 128), 1).astype(jnp.float32)
    routes = routes_ref[...].astype(jnp.float32)
    route_0, route_1 = column(routes[0:1]), column(routes[1:2])
    hot_0, hot_1 = lanes == route_0, lanes == route_1
    chosen_0, chosen_1 = pick(hot_0, logits), pick(hot_1, logits)
    top = jnp.maximum(chosen_0, chosen_1)
    chosen_0, chosen_1 = jnp.exp(chosen_0 - top), jnp.exp(chosen_1 - top)
    gate_0, gate_1 = chosen_0 / (chosen_0 + chosen_1), chosen_1 / (chosen_0 + chosen_1)
    rank = rank_ref[...].astype(jnp.float32)
    earlier = (rank < column(rank)).astype(jnp.float32).astype(jnp.bfloat16)
    slots = dot(earlier, (hot_0 | hot_1).astype(jnp.float32).astype(jnp.bfloat16))

    def target(route, hot):
        slot = pick(hot, slots)
        return jnp.where(
            (route < EXPERTS) & (slot < CAP), route * SLOTS + slot, -1.0
        )

    target_0, target_1 = target(route_0, hot_0), target(route_1, hot_1)
    info = jnp.where(lanes == 0, gate_0, 0.0) + jnp.where(lanes == 1, gate_1, 0.0)
    info = info + jnp.where(lanes == 2, target_0, 0.0) + jnp.where(lanes == 3, target_1, 0.0)
    info_ref[...] = info
    targets = info.T
    rows = lax.broadcasted_iota(jnp.int32, (EXPERTS * SLOTS, BLK), 0).astype(jnp.float32)
    table_0 = (rows == targets[2:3]).astype(jnp.float32).astype(jnp.bfloat16)
    table_1 = (rows == targets[3:4]).astype(jnp.float32).astype(jnp.bfloat16)
    rows_ref[...] = dot(table_0 + table_1, normed_two).astype(jnp.bfloat16)
    upstream = cot_ref[...].astype(jnp.float32)
    grads_ref[...] = dot(
        jnp.concatenate([table_0, table_1], axis=1),
        jnp.concatenate([gate_0 * upstream, gate_1 * upstream], axis=0).astype(jnp.bfloat16),
    ).astype(jnp.bfloat16)
    for back in (0, 1):

        @pl.when(ctx - back >= 0)
        def _(back=back):
            for copy in keep_block(block_at(ctx - back), (ctx - back) % 2):
                copy.wait()

    other = 1 - core
    half = EXPERTS * SLOTS
    leaving = [
        pltpu.make_async_copy(source, target, own_sem.at[11 + number])
        for number, (source, target) in enumerate(
            ((state_ref, state_out), (normed_ref, normed_out), (att_ref, att_out), (q_ref, q_out))
        )
    ]

    def slots(index, on):
        return pl.ds(pl.multiple_of((on * EXPERTS + index) * SLOTS, SLOTS), SLOTS)

    def chunk(index):
        return pl.ds(pl.multiple_of(index * SLOTS, SLOTS), SLOTS)

    buffers = ((rows_ref, x_ref), (grads_ref, g_ref))

    def dispatch(kind, by):
        source, target = buffers[kind]
        where = (chip + by) % EXPERTS
        return pltpu.make_async_remote_copy(
            src_ref=source.at[chunk(where)],
            dst_ref=target.at[slots(chip, core)],
            send_sem=send_sem.at[kind, by - 1],
            recv_sem=recv_sem.at[kind, by - 1],
            device_id=at_expert(where, core),
            device_id_type=MESH,
        )

    def share(kind, by, on):
        source, target = buffers[kind]
        spot = slots((chip - by) % EXPERTS, on)
        return pltpu.make_async_remote_copy(
            src_ref=target.at[spot],
            dst_ref=target.at[spot],
            send_sem=share_send.at[kind, by],
            recv_sem=share_recv.at[kind, by],
            device_id=at_expert(chip, other),
            device_id_type=MESH,
        )

    def exchange(kind):
        return pltpu.make_async_remote_copy(
            src_ref=twin_out.at[kind],
            dst_ref=twin_in.at[kind],
            send_sem=half_send.at[kind],
            recv_sem=half_recv.at[kind],
            device_id=at_expert(chip, other),
            device_id_type=MESH,
        )

    returned = (back_rows_ref, back_grads_ref)

    def give_back(kind, by):
        where = (chip + by) % EXPERTS
        return pltpu.make_async_remote_copy(
            src_ref=mine_ref.at[kind, chunk(where)],
            dst_ref=returned[kind].at[chunk(chip)],
            send_sem=ret_send.at[kind, by - 1],
            recv_sem=ret_recv.at[kind, by - 1],
            device_id=at_expert(where, core),
            device_id_type=MESH,
        )

    for by in range(1, EXPERTS):
        dispatch(0, by).start()
    for by in range(1, EXPERTS):
        dispatch(0, by).wait_send()
    for by in range(1, EXPERTS):
        copy = dispatch(1, by)
        copy.start()
        started.append(copy)
    for kind in (0, 1):
        source, target = buffers[kind]
        copy = pltpu.make_async_copy(
            source.at[chunk(chip)], target.at[slots(chip, core)], keep_sem.at[kind]
        )
        copy.start()
        copy.wait()
        copy = share(kind, 0, core)
        copy.start()
        started.append(copy)

    def arrive(kind):
        for by in range(1, EXPERTS):
            dispatch(kind, by).wait_recv()
            copy = share(kind, by, core)
            copy.start()
            started.append(copy)

    def arrive_shared(kind):
        for by in range(EXPERTS):
            share(kind, by, other).wait_recv()

    def tiles(on, body):
        def step(index, carry):
            start = pl.multiple_of(on * half + index * 256, 256)
            body(pl.ds(start, 256), pl.ds(pl.multiple_of(index * 256, 256), 256))
            return carry

        lax.fori_loop(0, half // 256, step, 0)

    def forward(on, keep):
        def tile(rows, inner):
            x = x_ref[rows]
            gate, up = dot(x, gate_w[...]), dot(x, up_w[...])
            gate_ref[rows], up_ref[rows] = gate, up
            hidden_ref[rows] = (gate * jax.nn.sigmoid(gate) * up).astype(jnp.bfloat16)

        def result(rows, inner):
            keep(inner, dot(hidden_ref[rows], down_w[...]))

        tiles(on, tile)
        tiles(on, result)

    def backward(on, keep):
        def tile(rows, inner):
            hidden_grad = dot_nt(g_ref[rows], down_w[...])
            gate, up = gate_ref[rows], up_ref[rows]
            sigmoid = jax.nn.sigmoid(gate)
            d_gate[rows] = (
                hidden_grad * up * sigmoid * (1.0 + gate * (1.0 - sigmoid))
            ).astype(jnp.bfloat16)
            d_up[rows] = (hidden_grad * gate * sigmoid).astype(jnp.bfloat16)
            keep(inner, dot_nt(d_gate[rows], gate_w[...]) + dot_nt(d_up[rows], up_w[...]))

        tiles(on, tile)

    def keep_mine(kind):
        def keep(rows, values):
            mine_ref[kind, rows] = values.astype(jnp.bfloat16)

        return keep

    def keep_twin(kind):
        def keep(rows, values):
            twin_out[kind, rows] = values.astype(jnp.bfloat16)

        return keep

    def finish(kind):
        exchange(kind).wait_recv()

        def step(index, carry):
            rows = pl.ds(pl.multiple_of(index * 128, 128), 128)
            mine_ref[kind, rows] = (
                mine_ref[kind, rows].astype(jnp.float32) + twin_in[kind, rows].astype(jnp.float32)
            ).astype(jnp.bfloat16)
            return carry

        lax.fori_loop(0, half // 128, step, 0)
        for by in range(1, EXPERTS):
            copy = give_back(kind, by)
            copy.start()
            started.append(copy)
        copy = pltpu.make_async_copy(
            mine_ref.at[kind, chunk(chip)], returned[kind].at[chunk(chip)], keep_sem.at[kind]
        )
        copy.start()
        copy.wait()

    def load(owner):
        parts = [
            (pay_ref.at[owner, :96], gate_w.at[pl.ds(pl.multiple_of(owner * 96, 16), 96)]),
            (pay_ref.at[owner, 96:192], up_w.at[pl.ds(pl.multiple_of(owner * 96, 16), 96)]),
            (
                pay_ref.at[owner, 192:, pl.ds(0, WIDTH)],
                down_w.at[pl.ds(pl.multiple_of(owner * 128, 16), 96)],
            ),
        ] + [
            (
                pay_ref.at[owner, pl.ds(192 + 32 * m, 32), pl.ds(WIDTH, 256)],
                down_w.at[pl.ds(pl.multiple_of(owner * 128 + 96, 16), 32), pl.ds(256 * m, 256)],
            )
            for m in range(3)
        ]
        return [
            pltpu.make_async_copy(source, target, load_sem.at[owner, number])
            for number, (source, target) in enumerate(parts)
        ]

    def owner_at(steps, on):
        return ((along + steps + 4) % 4) * 2 + on

    for steps, on in ((0, side), (0, 1 - side), (-1, side), (1, side)):
        for copy in load(owner_at(steps, on)):
            copy.start()
    pass_on(1, 4)
    for steps, on in ((-1, 1 - side), (1, 1 - side), (2, side), (2, 1 - side)):
        for copy in load(owner_at(steps, on)):
            copy.start()
    for copy in leaving:
        copy.start()
    arrive(0)
    for owner in range(8):
        for copy in load(owner):
            copy.wait()
    forward(core, keep_mine(0))
    arrive(1)
    arrive_shared(0)
    forward(other, keep_twin(0))
    copy = exchange(0)
    copy.start()
    started.append(copy)
    backward(core, keep_mine(1))
    finish(0)
    arrive_shared(1)
    backward(other, keep_twin(1))
    copy = exchange(1)
    copy.start()
    started.append(copy)

    def down_tile(index, carry):
        lanes = pl.ds(pl.multiple_of(index * 256, 256), 256)
        part = dot_tn(hidden_ref[:, lanes], g_ref[...]).astype(jnp.bfloat16)
        for piece in (0, 1):
            rows = part[piece * 128 : piece * 128 + 128]
            d_pay_ref[2 * index + piece, 192:, :WIDTH] = rows[:96]
            for m in range(3):
                d_pay_ref[2 * index + piece, 192 + 32 * m : 224 + 32 * m, WIDTH:] = rows[
                    96:, 256 * m : 256 * m + 256
                ]
        return carry

    lax.fori_loop(0, 4, down_tile, 0)
    finish(1)

    def gate_tile(index, carry):
        lanes = pl.ds(pl.multiple_of(index * 256, 256), 256)
        for start, grad in ((0, d_gate), (96, d_up)):
            part = dot_tn(x_ref[...], grad[:, lanes]).astype(jnp.bfloat16)
            for piece in range(8):
                d_pay_ref[piece, start : start + 96, lanes] = part[piece * 96 : piece * 96 + 96]
        return carry

    lax.fori_loop(0, 4, gate_tile, 0)
    leaving.append(pltpu.make_async_copy(d_pay_ref, d_pay_out, own_sem.at[15]))
    leaving[-1].start()
    for kind in (0, 1):
        for by in range(1, EXPERTS):
            give_back(kind, by).wait_recv()
    for copy in [weights_kept, blocks_kept, *leaving]:
        copy.wait()
    for kind in (0, 1):
        for number in range(len(MESSAGES)):
            ring(kind, number).wait_send()
    for copy in started:
        copy.wait_send()


def pad_routing(prev_ref, wres_ref, prev_pad, wres_pad):
    prev_pad[...] = jnp.zeros_like(prev_pad)
    prev_pad[:NALL] = prev_ref[:, 0, :]
    wres_pad[...] = jnp.zeros_like(wres_pad)
    wres_pad[:NALL, :NALL] = wres_ref[...]


def run_forward(weights, few, tokens, segments, experts, prev, wres, routes, rank, cot):
    vmem, anywhere = pl.BlockSpec(memory_space=pltpu.VMEM), pl.BlockSpec(memory_space=pl.ANY)
    shape = jax.ShapeDtypeStruct
    low, wide = jnp.bfloat16, jnp.float32
    dma = pltpu.SemaphoreType.DMA
    half, whole = EXPERTS * SLOTS, 2 * EXPERTS * SLOTS
    left, right, small = (jnp.asarray(t, low) for t in placing_tables())
    return pl.pallas_call(
        forward_kernel,
        out_shape=[
            shape((BLK, WIDTH), wide),
            shape((BLK, WIDTH), low),
            shape((WIDTH, BLK), wide),
            shape((16, BLK), wide),
            shape((PAIRS, BLK, 128), low),
            shape((8, PAIRS, BLK, 128), low),
            shape((8, PAIRS, BLK, 128), low),
            shape((BLK, 128), wide),
            shape((BLK, 128), wide),
            shape((8, BLK + 16, WIDTH), low),
            shape((4, WIDTH, WIDTH), low),
            shape((WIDTH, 128), low),
            shape((8, 288, 1024), low),
            shape((half, WIDTH), low),
            shape((half, WIDTH), low),
            shape((8, 288, 1024), low),
        ],
        in_specs=[vmem] * 26,
        out_specs=[anywhere] * 3 + [vmem] + [anywhere] * 3 + [vmem] * 2 + [anywhere] * 2 + [vmem] + [anywhere] + [vmem] * 2 + [anywhere],
        scratch_shapes=[
            *(pltpu.VMEM((4, 4, 4, 2, 16, lanes), low) for lanes in PART_LANES),
            pltpu.VMEM((16, 1280), low),
            pltpu.VMEM((HEADS, 128, BLK), low),
            pltpu.VMEM((WIDTH, BLK), low),
            pltpu.VMEM((BLK, BLK), wide),
            pltpu.VMEM((16, BLK), wide),
            pltpu.VMEM((16, BLK), wide),
            pltpu.VMEM((WIDTH, BLK), wide),
            pltpu.VMEM((128, BLK), wide),
            pltpu.VMEM((128, 128), wide),
            pltpu.VMEM((128, 128), wide),
            pltpu.VMEM((16, 128), wide),
            pltpu.VMEM((2, 2, PAIRS, BLK, 128), low),
            pltpu.VMEM((half, WIDTH), low),
            pltpu.VMEM((half, WIDTH), low),
            pltpu.VMEM((8, BLK + 16, WIDTH), low),
            pltpu.VMEM((4, WIDTH, WIDTH), low),
            pltpu.VMEM((BLK, WIDTH), wide),
            pltpu.VMEM((BLK, WIDTH), low),
            pltpu.VMEM((WIDTH, BLK), wide),
            pltpu.VMEM((PAIRS, BLK, 128), low),
            pltpu.VMEM((8, 288, 1024), low),
            pltpu.VMEM((WIDTH, 1024), low),
            pltpu.VMEM((WIDTH, 1024), low),
            pltpu.VMEM((1024, WIDTH), low),
            pltpu.VMEM((whole, WIDTH), low),
            pltpu.VMEM((whole, WIDTH), low),
            pltpu.VMEM((whole, 1024), wide),
            pltpu.VMEM((whole, 1024), wide),
            pltpu.VMEM((whole, 1024), low),
            pltpu.VMEM((whole, 1024), low),
            pltpu.VMEM((whole, 1024), low),
            pltpu.VMEM((2, half, WIDTH), low),
            pltpu.VMEM((2, half, WIDTH), low),
            pltpu.VMEM((2, half, WIDTH), low),
            dma((3, 3, 3)),
            dma((3, 3, 3)),
            dma((3, 10)),
            dma((3, 10)),
            dma((16,)),
            dma((2, 15)),
            dma((2, 15)),
            dma((2, 2)),
            dma((8, 6)),
            dma((2, 7)),
            dma((2, 7)),
            dma((2, 8)),
            dma((2, 8)),
            dma((2,)),
            dma((2,)),
            dma((2, 7)),
            dma((2, 7)),
            dma((2,)),
        ],
        name="forward",
        compiler_params=pltpu.CompilerParams(
            collective_id=1, has_side_effects=True, vmem_limit_bytes=63 * 2**20
        ),
    )(
        *weights, *few, tokens, segments, *experts, left, right, small, *rope_tables(),
        prev, wres, routes, rank, cot,
    )


def split(values):
    high = values.astype(jnp.bfloat16)
    low = (values - high.astype(jnp.float32)).astype(jnp.bfloat16)
    return jnp.concatenate([high, low], axis=1)


def back_kernel(
    blocks_ref, w_in, small_ref, cos_in, sin_in, cos_out, sin_out, left_ref, right_ref, place_ref,
    prev_ref, wres_ref, routes_ref, cot_ref,
    state_ref, normed_ref, att_ref, lse_ref, q_ref, keys_ref, values_ref, info_ref, proj_ref,
    back_rows_ref, back_grads_ref, d_pay_ref,
    out_ref, prev_grad_ref, total_ref, tokens_grad_ref, sums_ref, few_ref,
    gate_out, up_out, down_out,
    *scratch,
):
    (
        qt_ref, ot_ref, o_ref, qm_ref, bias_ref, inner_ref, dqt_ref, gain_ref, dk_ref, dv_ref,
        prev_pad, wres_pad, dw_ref, dw_low, few_sum, kv_ref, tok_ref, mine_ref, kv_sem, own_ref, state_grad_ref, others_ref, grads_ref, block_in,
        far_in, far_land, far_sum, far_out, far_back, mark_ref, far_send, far_recv,
        w_ref, pay_ref, pay_in, small_in, small_sum,
        block_send, block_recv, exp_send, exp_recv, load_sem,
        net_send, net_recv, twin_send, twin_recv, small_send, small_recv,
        *more,
    ) = scratch
    twin_in, in_one, in_two, in_three, sum_one, sum_two = (
        more[0], more[1:4], more[4:7], more[7:10], more[10:13], more[13:16]
    )
    tables = (cos_in, sin_in, cos_out, sin_out)
    ctx, fsdp = lax.axis_index("ctx"), lax.axis_index("fsdp")
    *spot, core = place()
    spot = tuple(spot)
    twin = device_at(*spot, 1 - core)
    started = []
    greet(torus_peers(spot, core) + sequence_peers(spot, core))

    along, side = ctx // 2, ctx % 2

    def rows_of(number):
        first, last = (GRAD_CUTS[i] for i in SPANS[MESSAGES[number][2]])
        return first, last - first

    def owner(steps, across_it):
        return ((along + steps + 4) % 4) * 2 + (side if across_it == 0 else 1 - side)

    def expert(number):
        to, (steps, across_it), _ = MESSAGES[number]
        first, count = rows_of(number)
        landing = sum(rows_of(before)[1] for before in range(number))
        return pltpu.make_async_remote_copy(
            src_ref=(d_pay_ref if number >= 7 else pay_ref).at[
                owner(steps - to, across_it if to else 1 - across_it), pl.ds(first, count)
            ],
            dst_ref=pay_in.at[pl.ds(landing, count)],
            send_sem=exp_send.at[number],
            recv_sem=exp_recv.at[number],
            device_id={"ctx": owner(-to, 0 if to else 1), "fsdp": fsdp},
            device_id_type=MESH,
        )

    def send_experts(numbers):
        for number in numbers:
            expert(number).start()

    def add_experts(numbers):
        for number in numbers:
            expert(number).wait_recv()
            _, (steps, across_it), _ = MESSAGES[number]
            first, count = rows_of(number)
            landing = sum(rows_of(before)[1] for before in range(number))
            at = owner(steps, across_it)

            def add_rows(index, carry, at=at, first=first, landing=landing):
                here = pl.ds(pl.multiple_of(first + index * 16, 16), 16)
                there = pl.ds(pl.multiple_of(landing + index * 16, 16), 16)
                pay_ref[at, here] = (
                    pay_ref[at, here].astype(jnp.float32) + pay_in[there].astype(jnp.float32)
                ).astype(jnp.bfloat16)
                return carry

            lax.fori_loop(0, count // 16, add_rows, 0)

    loads = [
        pltpu.make_async_copy(d_pay_ref.at[index], pay_ref.at[index], load_sem.at[1 + index])
        for index in range(8)
    ]
    send_experts((13, 14, 11, 12, 7, 8, 9, 10))
    for copy in loads:
        copy.start()
    weights_in = pltpu.make_async_copy(w_in, w_ref, load_sem.at[10])
    weights_in.start()
    own_block = pltpu.make_async_copy(blocks_ref.at[ctx], mine_ref, load_sem.at[0])
    own_block.start()

    def load_kv(index, slot):
        return [
            pltpu.make_async_copy(source.at[index], kv_ref.at[slot, kind], kv_sem.at[slot, kind])
            for kind, source in enumerate((keys_ref, values_ref))
        ] + [pltpu.make_async_copy(blocks_ref.at[index], tok_ref.at[slot], kv_sem.at[slot, 2])]

    for copy in load_kv(0, 0):
        copy.start()

    mine_half, twin_half = (
        pl.ds(pl.multiple_of(on * 128, 128), 128) for on in (core, 1 - core)
    )
    end_mark = pltpu.make_async_copy(blocks_ref.at[7, pl.ds(BLK, 16)], mark_ref, load_sem.at[9])
    end_mark.start()

    def far_share(index):
        return pltpu.make_async_remote_copy(
            src_ref=others_ref.at[index, twin_half],
            dst_ref=far_in.at[index],
            send_sem=far_send.at[index],
            recv_sem=far_recv.at[index],
            device_id=twin,
            device_id_type=MESH,
        )

    def far_copy(by, target):
        return pltpu.make_async_remote_copy(
            src_ref=others_ref.at[target, mine_half],
            dst_ref=far_land.at[by - 3],
            send_sem=block_send.at[by - 1],
            recv_sem=block_recv.at[by - 1],
            device_id={"ctx": target, "fsdp": fsdp},
            device_id_type=MESH,
        )

    def far_halves():
        return pltpu.make_async_remote_copy(
            src_ref=far_out,
            dst_ref=far_back,
            send_sem=far_send.at[5],
            recv_sem=far_recv.at[5],
            device_id=twin,
            device_id_type=MESH,
        )

    def block_copy(by, target):
        return pltpu.make_async_remote_copy(
            src_ref=others_ref.at[target],
            dst_ref=block_in.at[by - 1],
            send_sem=block_send.at[by - 1],
            recv_sem=block_recv.at[by - 1],
            device_id={"ctx": target, "fsdp": fsdp},
            device_id_type=MESH,
        )

    across = small_ref[...].astype(jnp.float32).T
    gain_one, gain_two = across[18:19], across[19:20]
    value_rows = across[16:18]

    lanes = lax.broadcasted_iota(jnp.int32, (BLK, 128), 1)
    info = info_ref[...]
    gates = (info[:, 0:1], info[:, 1:2])
    slots = lax.broadcasted_iota(jnp.int32, (BLK, EXPERTS * SLOTS), 1).astype(jnp.float32)
    tables_of = [
        (slots == info[:, 2 + k : 3 + k]).astype(jnp.float32).astype(jnp.bfloat16) for k in (0, 1)
    ]
    route_rows = routes_ref[...].astype(jnp.float32)
    routes = (column(route_rows[0:1]), column(route_rows[1:2]))
    hots = [lanes.astype(jnp.float32) == routes[k] for k in (0, 1)]
    named = [
        [(routes[k] == EXPERTS + 1 + kind).astype(jnp.float32) for kind in range(3)] for k in (0, 1)
    ]
    proj = proj_ref[...]
    mixes = []
    for c in (0, 1):
        first, second = proj[:, 12 + 2 * c : 13 + 2 * c], proj[:, 13 + 2 * c : 14 + 2 * c]
        top = jnp.maximum(first, second)
        first, second = jnp.exp(first - top), jnp.exp(second - top)
        mixes.append((first / (first + second), second / (first + second)))
    normed_low = normed_ref[...]
    normed_two = normed_low.astype(jnp.float32)
    upstream_low = cot_ref[...]
    upstream = upstream_low.astype(jnp.float32)
    state = state_ref[...]
    back_rows = back_rows_ref[...]
    result = state
    gate_grads = []
    for k in (0, 1):
        copy, one, two = named[k]
        pair = dot(tables_of[k], back_rows)
        pair = pair + (copy + one * mixes[0][0] + two * mixes[1][0]) * normed_two
        pair = pair + (one * mixes[0][1]) * value_rows[0:1] + (two * mixes[1][1]) * value_rows[1:2]
        result = result + gates[k] * pair
        gate_grads.append(jnp.sum(pair * upstream, axis=1, keepdims=True))
    out_ref[...] = result.astype(jnp.bfloat16)
    inner = gates[0] * gate_grads[0] + gates[1] * gate_grads[1]
    logit_grad = jnp.zeros((BLK, 128), jnp.float32)
    for k in (0, 1):
        logit_grad = logit_grad + jnp.where(hots[k], gates[k] * (gate_grads[k] - inner), 0.0)
    pad_routing(prev_ref, wres_ref, prev_pad, wres_pad)
    prev_grad_ref[...] = lax.dot_general(
        wres_pad[...], logit_grad, (((1,), (1,)), ((), ())),
        precision=highest, preferred_element_type=jnp.float32,
    )[:16]
    small_sum[3] = jnp.dot(
        prev_pad[...], logit_grad, precision=highest, preferred_element_type=jnp.float32
    )[:16]
    on_normed = jnp.sum(normed_two * upstream, axis=1, keepdims=True)
    on_vectors = dot(upstream_low, small_ref[...])
    flat = logit_grad
    weight_up = gates[0] * named[0][0] + gates[1] * named[1][0]
    vector_weights = jnp.zeros((BLK, 128), jnp.float32)
    for c in (0, 1):
        scale = gates[0] * named[0][1 + c] + gates[1] * named[1][1 + c]
        mix_0, mix_1 = mixes[c]
        m_0, m_1 = scale * on_normed, scale * on_vectors[:, 16 + c : 17 + c]
        mean = mix_0 * m_0 + mix_1 * m_1
        flat = flat + jnp.where(lanes == 12 + 2 * c, mix_0 * (m_0 - mean), 0.0)
        flat = flat + jnp.where(lanes == 13 + 2 * c, mix_1 * (m_1 - mean), 0.0)
        weight_up = weight_up + mix_0 * scale
        vector_weights = vector_weights + jnp.where(lanes == 16 + c, mix_1 * scale, 0.0)
    flat_split = split(flat)
    normed_grad = dot_nt(flat_split, jnp.concatenate([small_ref[...]] * 2, axis=1))
    normed_grad = normed_grad + weight_up * upstream
    normed_grad = normed_grad + dot(tables_of[0] + tables_of[1], back_grads_ref[...])
    normed_across = normed_two.T.astype(jnp.bfloat16)
    upstream_across = upstream.T.astype(jnp.bfloat16)
    small_grad = dot(normed_across, flat_split)
    small_vector = dot(upstream_across, split(vector_weights))
    small_grad = small_grad[:, :128] + small_grad[:, 128:] + small_vector[:, :128] + small_vector[:, 128:]
    scale_two = rms_rows(state)
    weighted = normed_grad * gain_two
    state_grad = (
        upstream
        + scale_two * weighted
        - state * (scale_two**3 * jnp.mean(weighted * state, axis=-1, keepdims=True))
    )
    state_grad_ref[...] = state_grad
    gain_two_row = jnp.sum(normed_grad * state * scale_two, axis=0, keepdims=True)
    state_low = state_grad.astype(jnp.bfloat16)
    attended = att_ref[...]
    dw_low[1] = dot(attended.astype(jnp.bfloat16), state_low).astype(jnp.bfloat16)
    weights_in.wait()
    att_grad = dot_nt(state_low, w_ref[3])
    blank = jnp.zeros((HDIM, BLK), jnp.bfloat16)
    low_half = lax.broadcasted_iota(jnp.int32, (BLK, 128), 1) < HDIM
    none = jnp.zeros((BLK, 128), jnp.bfloat16)
    inner_ref[...] = jnp.zeros_like(inner_ref)
    for pair in range(PAIRS):
        part = att_grad[:, pair * 128 : pair * 128 + 128].astype(jnp.bfloat16)
        across_o = part.astype(jnp.float32).T
        products = across_o * attended[pair * 128 : pair * 128 + 128]
        across_o = across_o.astype(jnp.bfloat16)
        across_q = q_ref[pair].astype(jnp.float32).T.astype(jnp.bfloat16)
        for half in (0, 1):
            head = 2 * pair + half
            rows = slice(half * HDIM, half * HDIM + HDIM)
            inner_ref[head : head + 1] = jnp.sum(products[rows], axis=0, keepdims=True)
            order = (lambda a, b: [a, b]) if half == 0 else (lambda a, b: [b, a])
            ot_ref[head] = jnp.concatenate(order(across_o[rows], blank), axis=0)
            qt_ref[head] = jnp.concatenate(order(across_q[rows], blank), axis=0)
        o_ref[pair, :BLK] = jnp.where(low_half, part, none)
        o_ref[pair, BLK:] = jnp.where(low_half, none, part)
        qm_ref[pair, :BLK] = jnp.where(low_half, q_ref[pair], none)
        qm_ref[pair, BLK:] = jnp.where(low_half, none, q_ref[pair])
    dqt_ref[...] = jnp.zeros_like(dqt_ref)
    dw_ref[...] = jnp.zeros_like(dw_ref)
    gain_ref[...] = jnp.zeros_like(gain_ref)

    own_block.wait()

    def normed_block(array):
        wide = array[:BLK].astype(jnp.float32)
        scaled = wide * rms_rows(wide)
        return scaled, (scaled * gain_one).T.astype(jnp.bfloat16)

    def block(index, carry):
        slot = index % 2
        for copy in load_kv(index, slot):
            copy.wait()

        @pl.when(index < ctx)
        def _():
            for copy in load_kv(index + 1, 1 - slot):
                copy.start()

        mask_bias(tok_ref.at[slot], mine_ref, bias_ref, ctx, index)
        cosine, sine = turning(index, tables)
        def products(pair):
            key, value = kv_ref[slot, 0, pair], kv_ref[slot, 1, pair]
            return [
                (dot(key, qt_ref[2 * pair + half]) + bias_ref[...], dot(value, ot_ref[2 * pair + half]))
                for half in (0, 1)
            ]

        ahead = products(0)
        for pair in range(PAIRS):
            now = ahead
            if pair + 1 < PAIRS:
                ahead = products(pair + 1)
            key_across = kv_ref[slot, 0, pair].T
            weights, score_grads = [], []
            for half in (0, 1):
                head = 2 * pair + half
                scores, weight_grad = now[half]
                weight = jnp.exp(scores - lse_ref[head : head + 1])
                score_grad = (weight * (weight_grad - inner_ref[head : head + 1])).astype(jnp.bfloat16)
                weights.append(weight.astype(jnp.bfloat16))
                score_grads.append(score_grad)
                rows = slice(head * HDIM, head * HDIM + HDIM)
                dqt_ref[rows] += dot(key_across[half * HDIM : half * HDIM + HDIM], score_grad)
            lanes = slice(pair * 128, pair * 128 + 128)
            dv_ref[:, lanes] = dot(jnp.concatenate(weights, axis=1), o_ref[pair]).astype(jnp.bfloat16)
            dk = dot(jnp.concatenate(score_grads, axis=1), qm_ref[pair])
            dk_ref[:, lanes] = (dk * cosine - swapped(dk) * sine).astype(jnp.bfloat16)
        scaled, normed_across = normed_block(tok_ref.at[slot])
        dw_ref[0] += dot(normed_across, dk_ref[...])
        dw_ref[1] += dot(normed_across, dv_ref[...])
        first = dot_nt(dk_ref[...], w_ref[1]) + dot_nt(dv_ref[...], w_ref[2])
        gain_ref[...] += jnp.sum(first * scaled, axis=0, keepdims=True)

        @pl.when(index < ctx)
        def _():
            others_ref[index] = first.astype(jnp.bfloat16)

        @pl.when((index < ctx) & (index >= ctx - 2))
        def _():
            block_copy(ctx - index, index).start()

        @pl.when(index < ctx - 2)
        def _():
            far_share(index).start()

        @pl.when((index >= 1) & (index - 1 < ctx - 2))
        def _():
            far_share(index - 1).wait_recv()
            others_ref[index - 1, mine_half] = (
                others_ref[index - 1, mine_half].astype(jnp.float32)
                + far_in[index - 1].astype(jnp.float32)
            ).astype(jnp.bfloat16)
            far_copy(ctx - (index - 1), index - 1).start()

        @pl.when(index == ctx)
        def _():
            own_ref[...] = first

        for when, came, then in (
            (0, (13, 14), (5, 6)),
            (2, (3, 4), (2,)),
            (4, (7, 8, 9, 10, 5, 6), (0, 1)),
        ):

            @pl.when(index == jnp.minimum(ctx, when))
            def _(came=came, then=then):
                add_experts(came)
                send_experts(then)

        return carry

    for copy in loads:
        copy.wait()
    add_experts((11, 12))
    send_experts((3, 4))
    lax.fori_loop(0, ctx + 1, block, 0)
    cosine, sine = turning(ctx, tables)
    for pair in range(PAIRS):
        lanes = slice(pair * 128, pair * 128 + 128)
        dq = dqt_ref[lanes, :].T * (HDIM**-0.5)
        dk_ref[:, lanes] = (dq * cosine - swapped(dq) * sine).astype(jnp.bfloat16)
    scaled, normed_across = normed_block(mine_ref)
    dw_low[0] = dot(normed_across, dk_ref[...]).astype(jnp.bfloat16)
    first = dot_nt(dk_ref[...], w_ref[0])
    own_ref[...] += first
    gain_one_row = gain_ref[...] + jnp.sum(first * scaled, axis=0, keepdims=True)
    lanes = lax.broadcasted_iota(jnp.int32, (WIDTH, 128), 1)
    ones = jnp.broadcast_to(gain_one_row, (128, WIDTH)).T
    twos = jnp.broadcast_to(gain_two_row, (128, WIDTH)).T
    few = jnp.where(lanes == 18, ones, jnp.where(lanes == 19, twos, small_grad))
    few_sum[...] = few

    def share(x):
        return pltpu.make_async_remote_copy(
            src_ref=grads_ref.at[x, :, :, 1 - core],
            dst_ref=twin_in.at[x],
            send_sem=twin_send.at[x],
            recv_sem=twin_recv.at[x],
            device_id=twin,
            device_id_type=MESH,
        )

    def pack(group, carry):
        rows = pl.ds(pl.multiple_of(group * 48, 16), 48)

        def lane_half(start):
            lanes = slice(start, start + 384)
            query, output = dw_low[0, rows, lanes], dw_low[1, rows, lanes]
            key, value = (dw_ref[w, rows, lanes].astype(jnp.bfloat16) for w in (0, 1))
            return jnp.concatenate([query, key, value, output], axis=0)

        from_left = dot(left_ref[...], lane_half(0))
        from_right = dot(right_ref[...], lane_half(384))
        placed = dot(place_ref[...], few_sum[rows].astype(jnp.bfloat16))
        whole = jnp.concatenate(
            [from_left[:128], from_right[:128], from_left[128:] + from_right[128:], placed], axis=1
        )
        grads_ref[group // 4, group % 4] = whole.astype(jnp.bfloat16).reshape(4, 2, 16, 1280)
        return carry

    for x in range(4):
        lax.fori_loop(4 * x, 4 * x + 4, pack, 0)
        copy = share(x)
        copy.start()
        started.append(copy)

    def net(part, step, by, source, target):
        axis = PART_ORDER[part][2 - step]
        return pltpu.make_async_remote_copy(
            src_ref=source,
            dst_ref=target,
            send_sem=net_send.at[part, step, by - 1],
            recv_sem=net_recv.at[part, step, by - 1],
            device_id=device_at(*shifted(spot, axis, by), core),
            device_id_type=MESH,
        )

    def small(axis, by, source, slot):
        device = twin if axis == 3 else device_at(*shifted(spot, axis, by), core)
        return pltpu.make_async_remote_copy(
            src_ref=source,
            dst_ref=small_in.at[axis, slot],
            send_sem=small_send.at[axis, by - 1],
            recv_sem=small_recv.at[axis, by - 1],
            device_id=device,
            device_id_type=MESH,
        )

    copy = small(3, 1, small_sum.at[3], core)
    copy.start()
    started.append(copy)

    def lanes_of(part):
        return pl.ds(PART_START[part], PART_LANES[part])

    for x in range(4):
        share(x).wait_recv()

        def add_pair(index, carry, x=x):
            z, y = index // 4, index % 4
            grads_ref[x, z, y, core] = (
                grads_ref[x, z, y, core].astype(jnp.float32) + twin_in[x, z, y].astype(jnp.float32)
            ).astype(jnp.bfloat16)
            return carry

        lax.fori_loop(0, 16, add_pair, 0, unroll=2)

        @pl.when(spot[0] != x)
        def _(x=x):
            by = (x - spot[0] + 4) % 4
            net(1, 0, by, grads_ref.at[x, :, :, core, :, lanes_of(1)], in_one[1].at[by - 1]).start()

    for part in range(3):
        axis = PART_ORDER[part][2]
        for by in (1, 2, 3):
            at = shifted(spot, axis, by)[axis]
            index = tuple(at if a == axis else slice(None) for a in range(3))
            copy = net(
                part, 0, by, grads_ref.at[(*index, core, slice(None), lanes_of(part))], in_one[part].at[by - 1]
            )
            if part != 1:
                copy.start()
            started.append(copy)

    small(3, 1, small_sum.at[3], 1 - core).wait_recv()
    small_in[3, core] = small_sum[3]
    small_sum[0] = small_in[3, 0] + small_in[3, 1]
    for by in (1, 2, 3):
        copy = small(0, by, small_sum.at[0], spot[0])
        copy.start()
        started.append(copy)

    def small_step(axis):
        for by in (1, 2, 3):
            small(axis, by, small_sum.at[axis], shifted(spot, axis, -by)[axis]).wait_recv()
        small_in[axis, spot[axis]] = small_sum[axis]
        total = small_in[axis, 0] + small_in[axis, 1] + small_in[axis, 2] + small_in[axis, 3]
        if axis == 2:
            total_ref[...] = total
            return
        small_sum[axis + 1] = total
        for by in (1, 2, 3):
            copy = small(axis + 1, by, small_sum.at[axis + 1], spot[axis + 1])
            copy.start()
            started.append(copy)

    for part in range(3):
        first, second, third = PART_ORDER[part]
        for by in (1, 2, 3):
            net(part, 0, by, in_one[part].at[by - 1], in_one[part].at[by - 1]).wait_recv()
        rest = tuple(a for a in (0, 1, 2) if a != third)
        lanes = slice(PART_START[part], PART_START[part] + PART_LANES[part])

        def add_four(index, carry, part=part, third=third, rest=rest, lanes=lanes):
            at = {rest[0]: index // 4, rest[1]: index % 4, third: spot[third]}
            total = grads_ref[at[0], at[1], at[2], core, :, lanes].astype(jnp.float32)
            for by in range(3):
                total = total + in_one[part][by, index // 4, index % 4].astype(jnp.float32)
            sum_one[part][index // 4, index % 4] = total.astype(jnp.bfloat16)
            return carry

        lax.fori_loop(0, 16, add_four, 0, unroll=2)
        for by in (1, 2, 3):
            at = shifted(spot, second, by)[second]
            source = sum_one[part].at[at] if second == rest[0] else sum_one[part].at[:, at]
            copy = net(part, 1, by, source, in_two[part].at[by - 1])
            copy.start()
            started.append(copy)
    small_step(0)

    for number in (0, 1, 2):
        expert(number).wait_recv()
    count = PAY_CUTS[-1]

    def total_rows(start):
        rows = pl.ds(pl.multiple_of(start, 16), 16)
        total = pay_ref[ctx, rows].astype(jnp.float32)
        for number in range(3):
            there = pl.ds(pl.multiple_of(number * count + start, 16), 16)
            total = total + pay_in[there].astype(jnp.float32)
        return total

    def gate_rows(index, carry):
        rows = pl.ds(pl.multiple_of(index * 16, 16), 16)
        gate_out[rows] = total_rows(index * 16)
        up_out[rows] = total_rows(96 + index * 16)
        return carry

    lax.fori_loop(0, 6, gate_rows, 0)
    for index in range(6):
        total = total_rows(192 + 16 * index)
        down_out[16 * index : 16 * index + 16] = total[:, :WIDTH]
        start = 96 + 16 * (index % 2)
        lanes = slice(256 * (index // 2), 256 * (index // 2) + 256)
        down_out[start : start + 16, lanes] = total[:, WIDTH:]

    for part in range(3):
        first, second, third = PART_ORDER[part]
        for by in (1, 2, 3):
            net(part, 1, by, in_two[part].at[by - 1], in_two[part].at[by - 1]).wait_recv()
        rest = tuple(a for a in (0, 1, 2) if a != third)
        for index in range(4):
            if second == rest[0]:
                total = sum_one[part][spot[second], index].astype(jnp.float32)
            else:
                total = sum_one[part][index, spot[second]].astype(jnp.float32)
            for by in range(3):
                total = total + in_two[part][by, index].astype(jnp.float32)
            sum_two[part][index] = total.astype(jnp.bfloat16)
        for by in (1, 2, 3):
            at = shifted(spot, first, by)[first]
            copy = net(part, 2, by, sum_two[part].at[at], in_three[part].at[by - 1])
            copy.start()
            started.append(copy)
    small_step(1)

    for by in (1, 2):

        @pl.when(ctx + by < 8)
        def _(by=by):
            block_copy(by, ctx).wait_recv()
            own_ref[...] += block_in[by - 1].astype(jnp.float32)

        @pl.when(ctx - by >= 0)
        def _(by=by):
            block_copy(by, ctx - by).wait_send()

    far_sum[...] = jnp.zeros_like(far_sum)
    for by in range(3, 8):

        @pl.when(ctx + by < 8)
        def _(by=by):
            far_copy(by, ctx).wait_recv()
            far_sum[...] += far_land[by - 3].astype(jnp.float32)

        @pl.when(ctx - by >= 0)
        def _(by=by):
            far_copy(by, ctx - by).wait_send()
            far_share(ctx - by).wait_send()

    far_out[...] = far_sum[...].astype(jnp.bfloat16)
    far_halves().start()
    end_mark.wait()
    single = mark_ref[...].astype(jnp.float32)[0:1, BLK - 1 : BLK] == 0.0
    far_halves().wait_recv()
    own_ref[mine_half] += jnp.where(single, far_sum[...], 0.0)
    own_ref[twin_half] += jnp.where(single, far_back[...].astype(jnp.float32), 0.0)
    far_halves().wait_send()

    wide = mine_ref[:BLK].astype(jnp.float32)
    scale = rms_rows(wide)
    weighted = own_ref[...] * gain_one
    tokens_grad_ref[...] = (
        state_grad_ref[...]
        + scale * weighted
        - wide * (scale**3 * jnp.mean(weighted * wide, axis=-1, keepdims=True))
    )
    finals = []
    for part in range(3):
        first = PART_ORDER[part][0]
        for by in (1, 2, 3):
            net(part, 2, by, in_three[part].at[by - 1], in_three[part].at[by - 1]).wait_recv()
        total = sum_two[part][spot[first]].astype(jnp.float32)
        for by in range(3):
            total = total + in_three[part][by].astype(jnp.float32)
        finals.append(total)
    final = jnp.concatenate(finals, axis=1)
    sums_ref[:16] = final[:, :768]
    sums_ref[16:] = jnp.concatenate([final[:8, 768:1152], final[8:, 768:1152]], axis=1)
    few_ref[...] = final[:8, 1152:]
    small_step(2)
    for number in range(len(MESSAGES)):
        expert(number).wait_send()
    for copy in started:
        copy.wait_send()


def run_back(blocks, weights, smalls, prev, wres, routes, cot, kept, back_rows, back_grads, d_pay):
    vmem, anywhere = pl.BlockSpec(memory_space=pltpu.VMEM), pl.BlockSpec(memory_space=pl.ANY)
    shape = jax.ShapeDtypeStruct
    low, wide = jnp.bfloat16, jnp.float32
    dma = pltpu.SemaphoreType.DMA
    left, right, small = (jnp.asarray(t.T, low) for t in placing_tables())
    by_part = lambda *lead: [pltpu.VMEM((*lead, 16, lanes), low) for lanes in PART_LANES]
    return pl.pallas_call(
        back_kernel,
        out_shape=[
            shape((BLK, WIDTH), low),
            shape((16, BLK), wide),
            shape((16, 128), wide),
            shape((BLK, WIDTH), wide),
            shape((24, WIDTH), wide),
            shape((8, 128), wide),
            shape((96, 1024), wide),
            shape((96, 1024), wide),
            shape((128, WIDTH), wide),
        ],
        in_specs=[anywhere] * 2 + [vmem] * 17 + [anywhere] * 2 + [vmem] * 4 + [anywhere],
        out_specs=[vmem] * 9,
        scratch_shapes=[
            pltpu.VMEM((HEADS, 128, BLK), low),
            pltpu.VMEM((HEADS, 128, BLK), low),
            pltpu.VMEM((PAIRS, 2 * BLK, 128), low),
            pltpu.VMEM((PAIRS, 2 * BLK, 128), low),
            pltpu.VMEM((BLK, BLK), wide),
            pltpu.VMEM((16, BLK), wide),
            pltpu.VMEM((WIDTH, BLK), wide),
            pltpu.VMEM((1, WIDTH), wide),
            pltpu.VMEM((BLK, WIDTH), low),
            pltpu.VMEM((BLK, WIDTH), low),
            pltpu.VMEM((128, BLK), wide),
            pltpu.VMEM((128, 128), wide),
            pltpu.VMEM((2, WIDTH, WIDTH), wide),
            pltpu.VMEM((2, WIDTH, WIDTH), low),
            pltpu.VMEM((WIDTH, 128), wide),
            pltpu.VMEM((2, 2, PAIRS, BLK, 128), low),
            pltpu.VMEM((2, BLK + 16, WIDTH), low),
            pltpu.VMEM((BLK + 16, WIDTH), low),
            dma((2, 3)),
            pltpu.VMEM((BLK, WIDTH), wide),
            pltpu.VMEM((BLK, WIDTH), wide),
            pltpu.VMEM((7, BLK, WIDTH), low),
            pltpu.VMEM((4, 4, 4, 2, 16, 1280), low),
            pltpu.VMEM((2, BLK, WIDTH), low),
            pltpu.VMEM((5, 128, WIDTH), low),
            pltpu.VMEM((5, 128, WIDTH), low),
            pltpu.VMEM((128, WIDTH), wide),
            pltpu.VMEM((128, WIDTH), low),
            pltpu.VMEM((128, WIDTH), low),
            pltpu.VMEM((16, WIDTH), low),
            dma((6,)),
            dma((6,)),
            pltpu.VMEM((4, WIDTH, WIDTH), low),
            pltpu.VMEM((8, 288, 1024), low),
            pltpu.VMEM((2016, 1024), low),
            pltpu.VMEM((4, 4, 16, 128), wide),
            pltpu.VMEM((4, 16, 128), wide),
            dma((7,)),
            dma((7,)),
            dma((15,)),
            dma((15,)),
            dma((11,)),
            dma((3, 3, 3)),
            dma((3, 3, 3)),
            dma((4,)),
            dma((4,)),
            dma((4, 3)),
            dma((4, 3)),
            pltpu.VMEM((4, 4, 4, 16, 1280), low),
            *by_part(3, 4, 4),
            *by_part(3, 4),
            *by_part(3),
            *by_part(4, 4),
            *by_part(4),
        ],
        name="back",
        compiler_params=pltpu.CompilerParams(
            collective_id=2, has_side_effects=True, vmem_limit_bytes=62 * 2**20
        ),
    )(
        blocks, weights, smalls, *rope_tables(), left, right, small, prev, wres, routes, cot,
        *kept, back_rows, back_grads, d_pay,
    )


def finish_kernel(
    out_in, tokens_in, gate_in, up_in, down_in, prev_in, total_in, sums_in, few_in,
    out, tokens_grad, gate, up, down, prev, total, sum_q, sum_k, sum_v, sum_o,
    gain_one, gain_two, router, constant, vectors, prev_at, total_at, sums_at, few_at, sems,
):
    pairs = (
        (prev_in, prev_at), (total_in, total_at), (sums_in, sums_at), (few_in, few_at),
        (tokens_in, tokens_grad), (out_in, out), (gate_in, gate), (up_in, up), (down_in, down),
    )
    copies = [
        pltpu.make_async_copy(source, target, sems.at[index])
        for index, (source, target) in enumerate(pairs)
    ]
    for copy in copies:
        copy.start()
    for copy in copies[:4]:
        copy.wait()
    prev[:, 0, :] = prev_at[:NALL]
    total[...] = total_at[:NALL, :NALL]
    for weight, ref in enumerate((sum_q, sum_k, sum_v, sum_o)):
        ref[...] = sums_at[weight * 6 : weight * 6 + 6]
    few = few_at[...]
    router[...] = few[:6, :NALL]
    tall = jnp.concatenate([few, jnp.zeros((120, 128), jnp.float32)], axis=0).T
    constant[...] = tall[12:16, :6]
    vectors[...] = tall[16:18, :6]
    gain_one[...] = tall[18:19, :6]
    gain_two[...] = tall[19:20, :6]
    for copy in copies[4:]:
        copy.wait()


def finish(out, tokens_grad, gate, up, down, prev, total, sums, few):
    vmem = pl.BlockSpec(memory_space=pltpu.VMEM)
    shape = jax.ShapeDtypeStruct
    wide = jnp.float32
    like = [shape(a.shape, a.dtype) for a in (out, tokens_grad, gate, up, down)]
    few_shapes = [(1, 6), (1, 6), (6, NALL), (4, 6), (2, 6)]
    return pl.pallas_call(
        finish_kernel,
        out_shape=like
        + [shape((NALL, 1, BLK), wide), shape((NALL, NALL), wide)]
        + [shape((6, WIDTH), wide)] * 4
        + [shape(s, wide) for s in few_shapes],
        in_specs=[pl.BlockSpec(memory_space=pl.ANY)] * 9,
        out_specs=[vmem] * 16,
        scratch_shapes=[
            *(pltpu.VMEM(a.shape, a.dtype) for a in (prev, total, sums, few)),
            pltpu.SemaphoreType.DMA((9,)),
        ],
        name="finish",
        compiler_params=pltpu.CompilerParams(vmem_limit_bytes=62 * 2**20),
    )(out, tokens_grad, gate, up, down, prev, total, sums, few)


def on_device(
    tokens, prev_logits, routes, segments, rank_order, norm_first, w_query, w_key, w_value, w_output,
    norm_second, w_router, w_residual, w_constant, v_constant, w_gate, w_up, w_down, cotangent,
):
    few = [w_router, w_constant.T, v_constant.T, norm_first[None], norm_second[None]]
    prev = jnp.transpose(prev_logits, (2, 0, 1))
    (
        state, normed, att, lse, q, keys, values, info, proj, blocks, weights, smalls, _,
        back_rows, back_grads, d_pay,
    ) = run_forward(
        [w_query, w_key, w_value, w_output], few, tokens[0], segments, (w_gate[0], w_up[0], w_down[0]),
        prev, w_residual, routes[0].T, rank_order[0], cotangent[0],
    )
    (
        out, prev_grad, residual, tokens_grad, sums, small, d_gate, d_up, d_down,
    ) = run_back(
        blocks, weights, smalls, prev, w_residual, routes[0].T, cotangent[0],
        (state, normed, att, lse, q, keys, values, info, proj), back_rows, back_grads, d_pay,
    )
    (
        out, tokens_grad, d_gate, d_up, d_down, prev_grad, residual, sum_q, sum_k, sum_v, sum_o,
        gain_one, gain_two, router, constant, vectors,
    ) = finish(out, tokens_grad, d_gate, d_up, d_down, prev_grad, residual, sums, small)
    return (
        out[None],
        tokens_grad[None],
        jnp.transpose(prev_grad, (1, 2, 0)),
        gain_one[0],
        sum_q,
        sum_k,
        sum_v,
        sum_o,
        gain_two[0],
        router,
        residual,
        constant.T,
        vectors.T,
        d_gate[None],
        d_up[None],
        d_down[None],
    )


def solution(mesh):
    in_specs = (
        P("fsdp", "ctx", None),
        P("fsdp", "ctx", None),
        P("fsdp", "ctx", None),
        P("fsdp", "ctx"),
        P("fsdp", "ctx", None),
        P(("ctx", "fsdp")),
        P(("ctx", "fsdp"), None),
        P(("ctx", "fsdp"), None),
        P(("ctx", "fsdp"), None),
        P(("ctx", "fsdp"), None),
        P(("ctx", "fsdp")),
        P(("ctx", "fsdp"), None),
        P(),
        P(("ctx", "fsdp"), None),
        P(("ctx", "fsdp"), None),
        P("fsdp", "ctx", None),
        P("fsdp", "ctx", None),
        P("fsdp", "ctx", None),
        P("fsdp", "ctx", None),
    )
    out_specs = (
        P("fsdp", "ctx", None),
        P("fsdp", "ctx", None),
        P("fsdp", "ctx", None),
        P(("ctx", "fsdp")),
        P(("ctx", "fsdp"), None),
        P(("ctx", "fsdp"), None),
        P(("ctx", "fsdp"), None),
        P(("ctx", "fsdp"), None),
        P(("ctx", "fsdp")),
        P(("ctx", "fsdp"), None),
        P(),
        P(("ctx", "fsdp"), None),
        P(("ctx", "fsdp"), None),
        P("fsdp", "ctx", None),
        P("fsdp", "ctx", None),
        P("fsdp", "ctx", None),
    )
    return jax.shard_map(
        on_device, mesh=mesh, in_specs=in_specs, out_specs=out_specs, check_vma=False
    )
```
